32 devices in a mesh: grp: 2 (over y), seq: 4 (over z), head: 2 (over x), sub: 2 (over core).
Axes of the slice: x: 2, y: 2, z: 4, core: 2. Of those that a mesh axis runs over, the one named last changes fastest.
Arguments:
- tokens_in: bfloat16 [16384, 1024], P(('grp', 'seq', 'sub')), parts along dimension 0, may hold values from -16 to 16
- w_query: bfloat16 [1024, 1024], P(None, 'head'), may hold values from -0.1875 to 0.1875
- w_value: bfloat16 [1024, 1024], P(None, 'head'), may hold values from -0.1875 to 0.1875
- cotangent: bfloat16 [16384, 1024], P(('grp', 'seq', 'sub'), 'head'), parts along dimension 0, may hold values from -6 to 6
- assignment: int32 [16384, 1], P(('grp', 'seq', 'sub')), parts along dimension 0, may hold values from 0 to 63; in each aligned block of 1024 rows (0 to 1023, 1024 to 2047, ...) at most 32 rows name the same one
Outputs:
- grad_input: bfloat16 [16384, 1024], P(('grp', 'seq', 'sub'), 'head'), parts along dimension 0
- grad_wq: float32 [2048, 1024], P(('grp', 'seq', 'sub'), 'head'), parts along dimension 0
- grad_wv: float32 [2048, 1024], P(('grp', 'seq', 'sub'), 'head'), parts along dimension 0
- centroid_grad: float32 [128, 1024], P('grp', 'head'), parts along dimension 0
The draws below stay inside these ranges and needn't reach their ends.
There are 2 independent parts, one for each index of `grp`. The reference program is written for one: setup_inputs(seed, part) draws one part's arguments, and reference() takes and returns one part's arrays. A program takes and returns all parts, laid end to end along the dimension named above; an argument that names none is the same for every part. Nothing has to cross between parts.
Inputs may be any that keep to these rules, and one draw needn't show every extreme that they name: `assignment`: in each device's aligned block of 1024 rows no cluster holds more than 32 tokens, and some cluster holds exactly 32.
All inputs are finite; a program needn't handle non-finite values.
Results may differ from the reference program's by a relative error of at most 0.018.
The reference program's roundings to bfloat16 on the way (of `queries`, `values`, `probs_half`, `grad_scores`, `grad_q` and `grad_v`) count: a program that leaves them out, or rounds other values in their place, can miss the bound.
Values may be sent and summed in bfloat16 or wider, within the bound.
No kernel may reach another device: no remote copies, remote signals or barrier semaphores. Data moves between devices by JAX's collectives and lax.ppermute only.
A program may use at most 64 MiB of HBM per device.

```python
import math
import jax
import jax.numpy as jnp
import numpy as np
from jax import lax

D = 1024
H = 16
HD = 64
CLUSTERS = 64
BLOCK_ROWS = 128
TOK_DEV = 1024
TOKENS = 8192
M = 32
N_SEQ = 4
N_HEAD = 2
N_SUB = 2


def draw_tokens_in(key, part):
    key = jax.random.fold_in(key, 11)
    key_base = jax.random.fold_in(key, 0)
    scaled = jnp.clip(jax.random.normal(key_base, (TOKENS, D), jnp.float32), -6.0, 6.0)
    return scaled.astype(jnp.bfloat16)


def steps_of(stream_key, dims, shards, low, high):
    def one(dim, shards_of):
        steps = jax.random.uniform(jax.random.fold_in(jax.random.fold_in(stream_key, 6), dim), (shards_of,), jnp.float32, low / len(shards), high / len(shards))
        return jnp.repeat(jnp.exp(steps), dims[dim] // shards_of).reshape((-1,) + (1,) * (len(dims) - dim - 1))

    level = one(*shards[0])
    for cut in shards[1:]:
        level = level * one(*cut)
    return level


def shared_out(key, own, number, rows, amount, top, reach, skew):
    order = jax.random.permutation(key, amount)
    packed, common = load_shares(amount, rows * top, reach, skew, True), load_shares(amount, rows * top, reach, skew, False)
    places = jnp.arange(amount)

    def named(tallies, offset_by):
        used = int((tallies > 0).sum())
        fixed = max(1, used // 4)
        shifted = fixed + (places - fixed + offset_by * (used - fixed)) % max(1, amount - fixed)
        return jnp.zeros((amount,), jnp.int32).at[order[jnp.where(places < fixed, places, shifted)]].set(jnp.asarray(tallies, jnp.int32))

    tallies = jnp.where(number % 4 == 0, named(packed, number // 4), named(common, number - number // 4 - 1))
    mixed = jax.random.permutation(jax.random.fold_in(own, 3), amount)
    giver, receiver = mixed[0:amount // 2 * 2:2], mixed[1:amount // 2 * 2:2]
    margin = jnp.minimum(tallies[giver] - 1, reach - tallies[receiver]) // 2
    margin = jnp.where((giver == order[0]) | (receiver == order[0]) | (tallies[receiver] == 0), 0, jnp.maximum(margin, 0))
    shifted = jax.random.randint(jax.random.fold_in(own, 4), (amount // 2,), 0, 1 << 20) % (margin + 1)
    tallies = tallies.at[giver].add(-shifted).at[receiver].add(shifted)
    members = jnp.searchsorted(jnp.cumsum(tallies), jnp.arange(rows * top), side="right").astype(jnp.int32)
    grid = members.reshape(top, rows).T
    grid = grid[jax.random.permutation(jax.random.fold_in(own, 1), rows)]
    offset_by = jax.random.randint(jax.random.fold_in(own, 2), (rows, 1), 0, top)
    return jnp.take_along_axis(grid, (jnp.arange(top)[None, :] + offset_by) % top, axis=1)


def load_shares(count, total, limit, slope, full):
    portions = [(1 << 20) // math.isqrt(rank ** slope) + 1 for rank in range(1, count + 1)]
    largest = limit if full else min(limit, max(-(-total // count), total * portions[0] // sum(portions)))
    least = 1 if total - largest >= count - 1 else 0
    holding, rest = [largest] + [least] * (count - 1), total - largest - least * (count - 1)
    while rest > 0:
        movable = [i for i in range(1, count) if holding[i] < largest] or [i for i in range(1, count) if holding[i] < limit]
        pool, left = sum([portions[i] for i in movable]), rest
        for i in movable:
            addition = min(limit - holding[i], max(1, left * portions[i] // pool), rest)
            holding[i] = holding[i] + addition
            rest = rest - addition
    return np.array(holding)


def bell_draw(stream_key, dims, deviation, reach, pieces=(), held_as=jnp.bfloat16):
    loudness = steps_of(stream_key, dims, pieces, -0.22, 0.18) if pieces else 1.0
    drawn = jax.random.normal(stream_key, dims, jnp.float32) * deviation * loudness
    return jnp.minimum(jnp.maximum(drawn, -reach), reach).astype(held_as)


def setup_inputs(seed: int = 0, part: int = 0) -> dict:
    key_of = jax.random.split(jax.random.key(seed), 6)
    part_splits = jax.random.split(jax.random.fold_in(key_of[5], part), 6)
    tokens_in = draw_tokens_in(jax.random.fold_in(jax.random.fold_in(key_of[5], part), 71), part)
    w_query = bell_draw(key_of[1], (D, H * HD), D ** -0.5, 0.1875, ((1, 2),))
    w_value = bell_draw(key_of[2], (D, H * HD), D ** -0.5, 0.1875, ((1, 2),))
    cotangent = bell_draw(part_splits[3], (TOKENS, H * HD), 1.0, 6.0, ((0, 8), (1, 2)))
    assignment_keys = jax.random.split(jax.random.fold_in(part_splits[4], 1), TOKENS // TOK_DEV)
    assignment_turns = jax.random.permutation(jax.random.fold_in(part_splits[4], 3), TOKENS // TOK_DEV)
    assignment = jax.vmap(lambda own, number: shared_out(jax.random.fold_in(part_splits[4], 2), own, number, TOK_DEV, CLUSTERS, 1, M, 2))(assignment_keys, assignment_turns).reshape((TOKENS, 1))
    return dict(tokens_in=tokens_in, w_query=w_query, w_value=w_value, cotangent=cotangent, assignment=assignment)


def block_backward(queries, values, cotangent):
    score_scale = 0.5 * HD ** -0.5
    query_full = queries.astype(jnp.float32)
    value_full = values.astype(jnp.float32)
    cot_full = cotangent.astype(jnp.float32)
    scores = jnp.einsum("bihd,bjhd->bhij", query_full, query_full) * score_scale
    length = queries.shape[1]
    lower = jnp.tril(jnp.ones((length, length), dtype=bool))
    scores = jnp.where(lower, scores, -jnp.inf)
    highest = jnp.max(scores, axis=-1, keepdims=True)
    raised = jnp.exp(scores - highest)
    probs = raised / jnp.sum(raised, axis=-1, keepdims=True)
    probs_half = probs.astype(jnp.bfloat16).astype(jnp.float32)
    output = jnp.einsum("bhij,bjhd->bihd", probs_half, value_full)
    grad_probs = jnp.einsum("bihd,bjhd->bhij", cot_full, value_full)
    row_dot = jnp.transpose(jnp.sum(cot_full * output, axis=-1), (0, 2, 1))[..., None]
    grad_scores = (probs * (grad_probs - row_dot)).astype(jnp.bfloat16).astype(jnp.float32)
    grad_query = score_scale * (jnp.einsum("bhij,bjhd->bihd", grad_scores, query_full)
                                + jnp.einsum("bhij,bihd->bjhd", grad_scores, query_full))
    grad_value = jnp.einsum("bhij,bihd->bjhd", probs_half, cot_full)
    return grad_query.astype(jnp.bfloat16), grad_value.astype(jnp.bfloat16)


def reference(tokens_in, w_query, w_value, cotangent, assignment):
    queries = jnp.dot(tokens_in, w_query, preferred_element_type=jnp.float32).astype(jnp.bfloat16)
    values = jnp.dot(tokens_in, w_value, preferred_element_type=jnp.float32).astype(jnp.bfloat16)
    cluster = assignment[:, 0].astype(jnp.int32)
    positions = jnp.arange(TOKENS, dtype=jnp.int32)
    sorting = jnp.argsort(cluster * TOKENS + positions).astype(jnp.int32)
    counts = jnp.zeros((CLUSTERS,), jnp.int32).at[cluster].add(1)
    starts = counts.cumsum() - counts
    sorted_cluster = cluster[sorting]
    ranking = positions - starts[sorted_cluster]
    capacity = ((M * N_SEQ * N_SUB + BLOCK_ROWS - 1) // BLOCK_ROWS) * BLOCK_ROWS
    target_sorted = (sorted_cluster * capacity + ranking).astype(jnp.int32)
    target_row = jnp.zeros((TOKENS,), jnp.int32).at[sorting].set(target_sorted)
    block_shape = (CLUSTERS, capacity // BLOCK_ROWS, BLOCK_ROWS, H, HD)

    def place(rows):
        filled = jnp.zeros((CLUSTERS * capacity, rows.shape[1]), rows.dtype).at[target_row].set(rows)
        return filled.reshape(block_shape)

    def per_cluster(items):
        return block_backward(items[0], items[1], items[2])

    grad_q_blocks, grad_v_blocks = lax.map(per_cluster, (place(queries), place(values), place(cotangent)))
    grad_q = grad_q_blocks.reshape(CLUSTERS * capacity, H * HD)[target_row]
    grad_v = grad_v_blocks.reshape(CLUSTERS * capacity, H * HD)[target_row]
    width_dev = H * HD // N_HEAD
    total = jnp.zeros((TOKENS, D), jnp.float32)
    for group in range(N_HEAD):
        low = group * width_dev
        high = low + width_dev
        partial_sum = jnp.dot(grad_q[:, low:high], w_query[:, low:high].T, preferred_element_type=jnp.float32)
        partial_sum = partial_sum + jnp.dot(grad_v[:, low:high], w_value[:, low:high].T, preferred_element_type=jnp.float32)
        total = total + lax.optimization_barrier(partial_sum.astype(jnp.bfloat16)).astype(jnp.float32)
    grad_input = total.astype(jnp.bfloat16)
    grad_wq = jnp.dot(tokens_in.T, grad_q, preferred_element_type=jnp.float32)
    grad_wv = jnp.dot(tokens_in.T, grad_v, preferred_element_type=jnp.float32)
    centroid_grad = jax.ops.segment_sum(grad_q.astype(jnp.float32), cluster, CLUSTERS) * (CLUSTERS / TOKENS) ** 0.5
    return grad_input, grad_wq, grad_wv, centroid_grad
```

```python
import functools

import jax
import jax.numpy as jnp
from jax import lax
from jax.experimental import pallas as pl
from jax.experimental.pallas import tpu as pltpu
from jax.sharding import PartitionSpec as P

HD = 64
CLUSTERS = 64
BLOCK_ROWS = 128
LANES = 128
SCALE = 0.5 * HD ** (-0.5)
F32 = jnp.float32
BF16 = jnp.bfloat16
VMEM_LIMIT = 56 * 1024 * 1024
OWNERS = ("seq", "sub")


def iota(shape, dim):
    return lax.broadcasted_iota(jnp.int32, shape, dim)


def low_half(shape):
    return iota(shape, 1) < HD


def swap_halves(tile):
    return pltpu.roll(tile, HD, 1)


def dot(a, b):
    return jnp.dot(a, b, preferred_element_type=F32)


def dot_nt(a, b):
    return lax.dot_general(a, b, (((1,), (1,)), ((), ())), preferred_element_type=F32)


def ones_where(condition):
    return jnp.where(condition, 1.0, 0.0).astype(BF16)


def project_query_kernel(
    groups, rows, assign_ref, tokens_ref, weight_ref, cotan_ref, out_ref, slot_ref, counts_ref, mixed_ref
):
    toks = tokens_ref.shape[0]
    per_group = CLUSTERS // groups
    heads = weight_ref.shape[1] // HD
    member = iota((CLUSTERS, toks), 0) == assign_ref[...]
    member_f = jnp.where(member, 1.0, 0.0)
    member_b = member_f.astype(BF16)
    upto = ones_where(iota((toks, toks), 0) <= iota((toks, toks), 1))
    running = dot(member_b, upto)
    counts = jnp.broadcast_to(jnp.sum(member_f, axis=1, keepdims=True), (CLUSTERS, LANES))
    here, other = iota((CLUSTERS, CLUSTERS), 0), iota((CLUSTERS, CLUSTERS), 1)
    group_of = lambda index: lax.div(index, jnp.int32(per_group))
    earlier = ones_where((other < here) & (group_of(other) == group_of(here)))
    base = dot(earlier, counts.astype(BF16))[:, :1]
    base = base + (group_of(iota((CLUSTERS, 1), 0)) * rows).astype(F32)
    slot = jnp.sum(member_f * (running - 1.0 + base), axis=0, keepdims=True).astype(jnp.int32)
    slot_ref[...] = slot
    counts_ref[...] = dot_nt(jnp.ones((8, toks), BF16), member_b).astype(jnp.int32)

    step = min(256, toks)

    @pl.loop(0, toks // step)
    def _(i):
        where = pl.ds(pl.multiple_of(i * step, step), step)
        query = dot(tokens_ref[where, :], weight_ref[...])
        cotan = cotan_ref[where, :].astype(F32)
        low = low_half((step, LANES))
        for pair in range(heads // 2):
            q_tile = query[:, pair * LANES : (pair + 1) * LANES]
            c_tile = cotan[:, pair * LANES : (pair + 1) * LANES]
            even = jnp.where(low, q_tile, swap_halves(c_tile)).astype(BF16)
            odd = jnp.where(low, swap_halves(q_tile), c_tile).astype(BF16)
            mixed_ref[where, 2 * pair * LANES : (2 * pair + 1) * LANES] = even
            mixed_ref[where, (2 * pair + 1) * LANES : (2 * pair + 2) * LANES] = odd

    part = min(256, rows)
    pieces = rows // part

    @pl.loop(0, groups * pieces)
    def _(i):
        group, piece = lax.div(i, jnp.int32(pieces)), lax.rem(i, jnp.int32(pieces))
        first = pl.multiple_of(piece * part, part)
        pick = ones_where(iota((part, toks), 0) + i * part == slot_ref[...])
        sorted_rows = dot(pick, mixed_ref[...]).astype(BF16)
        for head in range(heads):
            out_ref[group * heads + head, pl.ds(first, part), :] = sorted_rows[
                :, head * LANES : (head + 1) * LANES
            ]


def project_value_kernel(groups, rows, slot_ref, tokens_ref, weight_ref, out_ref, value_ref):
    toks = tokens_ref.shape[0]
    heads = weight_ref.shape[1] // HD
    step = min(256, toks)

    @pl.loop(0, toks // step)
    def _(i):
        where = pl.ds(pl.multiple_of(i * step, step), step)
        value_ref[where, :] = dot(tokens_ref[where, :], weight_ref[...]).astype(BF16)

    half = rows // 2
    part = min(256, half)
    pieces = half // part

    @pl.loop(0, groups * pieces)
    def _(i):
        group, piece = lax.div(i, jnp.int32(pieces)), lax.rem(i, jnp.int32(pieces))
        first = pl.multiple_of(piece * part, part)
        index = iota((part, toks), 0) + group * rows + first
        upper = dot(ones_where(index == slot_ref[...]), value_ref[...])
        lower = dot(ones_where(index + half == slot_ref[...]), value_ref[...])
        low = low_half((part, LANES))
        for pair in range(heads // 2):
            up = upper[:, pair * LANES : (pair + 1) * LANES]
            down = lower[:, pair * LANES : (pair + 1) * LANES]
            even = jnp.where(low, up, swap_halves(down)).astype(BF16)
            odd = jnp.where(low, swap_halves(up), down).astype(BF16)
            out_ref[group * heads + 2 * pair, pl.ds(first, part), :] = even
            out_ref[group * heads + 2 * pair + 1, pl.ds(first, part), :] = odd


def sort_tokens_kernel(slot_ref, tokens_ref, out_ref):
    toks = tokens_ref.shape[0]
    slots = out_ref.shape[1]
    turned = tokens_ref[...].T
    part = min(256, slots)

    for i in range(slots // part):
        pick = ones_where(iota((part, toks), 0) + i * part == slot_ref[...])
        out_ref[:, i * part : (i + 1) * part] = dot_nt(turned, pick).astype(BF16)


def softmax_turned(mixed, query):
    scores = dot_nt(query, mixed) * SCALE
    shape = scores.shape
    seen = iota(shape, 0) <= iota(shape, 1)
    scores = jnp.where(seen, scores, -jnp.inf)
    raised = jnp.exp(scores - jnp.max(scores, axis=0, keepdims=True))
    return raised * (1.0 / jnp.sum(raised, axis=0, keepdims=True))


def for_each_cluster(counts_ref, first_ref, place_ref, owners, per_group, slot_rows, body):
    for source in range(owners):
        place_ref[source] = 0

    @pl.loop(0, per_group)
    def _(cluster):
        runs = []
        total = 0
        for source in range(owners):
            count = counts_ref[source * 8, first_ref[0] + cluster]
            start = place_ref[source]
            runs.append((source, start, total))
            place_ref[source] = start + count
            total = total + count
        body(cluster, runs, total)


def value_grad_kernel(
    per_group, slot_rows, first_ref, counts_ref, mixed_ref, out_ref, place_ref, wide_ref, block_ref, grad_ref, home_ref
):
    owners, rows, _ = mixed_ref.shape
    capacity = block_ref.shape[0] - slot_rows
    for source in range(owners):
        wide_ref[source, :rows, :] = mixed_ref[source].astype(F32)
        wide_ref[source, rows:, :] = jnp.zeros((slot_rows, LANES), F32)

    def body(cluster, runs, total):
        for source, start, before in runs:
            block_ref[pl.ds(before, slot_rows), :] = wide_ref[source, pl.ds(start, slot_rows), :]
        low = low_half((BLOCK_ROWS, LANES))
        for first in range(0, capacity, BLOCK_ROWS):
            filled = iota((BLOCK_ROWS, LANES), 0) + first < total
            mixed = jnp.where(filled, block_ref[first : first + BLOCK_ROWS, :], 0.0)
            query = jnp.where(low, mixed, 0.0).astype(BF16)
            mixed = mixed.astype(BF16)
            probs_half = softmax_turned(mixed, query).astype(BF16)
            grad_ref[first : first + BLOCK_ROWS, :] = dot(probs_half, mixed)
        for source, start, before in runs:
            home_ref[source, pl.ds(start, slot_rows), :] = grad_ref[pl.ds(before, slot_rows), :]

    for_each_cluster(counts_ref, first_ref, place_ref, owners, per_group, slot_rows, body)
    half = rows // 2
    for source in range(owners):
        up, down = home_ref[source, :half, :], home_ref[source, half:rows, :]
        out_ref[source] = jnp.where(low_half((half, LANES)), swap_halves(up), down).astype(BF16)


def query_grad_kernel(
    per_group,
    slot_rows,
    first_ref,
    counts_ref,
    mixed_ref,
    value_in_ref,
    out_ref,
    sums_ref,
    place_ref,
    wide_ref,
    value_ref,
    block_ref,
    value_block_ref,
    grad_ref,
    home_ref,
):
    owners, rows, _ = mixed_ref.shape
    half = rows // 2
    capacity = block_ref.shape[0] - slot_rows
    for source in range(owners):
        wide_ref[source, :rows, :] = mixed_ref[source].astype(F32)
        wide_ref[source, rows:, :] = jnp.zeros((slot_rows, LANES), F32)
        value = value_in_ref[source].astype(F32)
        value_ref[source, :half, :] = swap_halves(value)
        value_ref[source, half:rows, :] = value
        value_ref[source, rows:, :] = jnp.zeros((slot_rows, LANES), F32)

    def body(cluster, runs, total):
        for source, start, before in runs:
            block_ref[pl.ds(before, slot_rows), :] = wide_ref[source, pl.ds(start, slot_rows), :]
            value_block_ref[pl.ds(before, slot_rows), :] = value_ref[source, pl.ds(start, slot_rows), :]
        low = low_half((BLOCK_ROWS, LANES))
        sums = jnp.zeros((1, LANES), F32)
        for first in range(0, capacity, BLOCK_ROWS):
            filled = iota((BLOCK_ROWS, LANES), 0) + first < total
            mixed = jnp.where(filled, block_ref[first : first + BLOCK_ROWS, :], 0.0)
            value = jnp.where(filled, value_block_ref[first : first + BLOCK_ROWS, :], 0.0).astype(BF16)
            query = jnp.where(low, mixed, 0.0).astype(BF16)
            cotan = jnp.where(low, 0.0, mixed).astype(BF16)
            probs = softmax_turned(mixed.astype(BF16), query)
            grad_probs = dot_nt(value, cotan)
            probs_half = probs.astype(BF16).astype(F32)
            row_dot = jnp.sum(probs_half * grad_probs, axis=0, keepdims=True)
            grad_scores = (probs * (grad_probs - row_dot)).astype(BF16).astype(F32)
            both = (grad_scores + grad_scores.T).astype(BF16)
            grad = (dot(both, query) * SCALE).astype(BF16).astype(F32)
            grad_ref[first : first + BLOCK_ROWS, :] = grad
            sums = sums + jnp.sum(grad, axis=0, keepdims=True)
        sums_ref[pl.ds(cluster, 1), :] = sums
        for source, start, before in runs:
            home_ref[source, pl.ds(start, slot_rows), :] = grad_ref[pl.ds(before, slot_rows), :]

    for_each_cluster(counts_ref, first_ref, place_ref, owners, per_group, slot_rows, body)
    for source in range(owners):
        up, down = home_ref[source, :half, :], home_ref[source, half:rows, :]
        out_ref[source] = jnp.where(low_half((half, LANES)), up, swap_halves(down)).astype(BF16)


def unfold(home_ref, out_ref, heads):
    owners, half, _ = home_ref.shape
    low = low_half((half, LANES))
    for group in range(owners // heads):
        first = group * 2 * half
        for pair in range(heads // 2):
            even = home_ref[group * heads + 2 * pair].astype(F32)
            odd = home_ref[group * heads + 2 * pair + 1].astype(F32)
            columns = slice(pair * LANES, (pair + 1) * LANES)
            out_ref[first : first + half, columns] = jnp.where(low, even, swap_halves(odd)).astype(BF16)
            out_ref[first + half : first + 2 * half, columns] = jnp.where(
                low, swap_halves(even), odd
            ).astype(BF16)


def weight_grad_kernel(heads, home_ref, turned_ref, out_ref, rows_ref):
    unfold(home_ref, rows_ref, heads)
    width = turned_ref.shape[0]
    step = min(256, width)

    @pl.loop(0, width // step)
    def _(i):
        where = pl.ds(pl.multiple_of(i * step, step), step)
        out_ref[where, :] = dot(turned_ref[where, :], rows_ref[...]).astype(BF16)


def input_grad_kernel(
    heads, me_ref, query_home_ref, value_rows_ref, w_query_ref, w_value_ref, turned_ref, *rest
):
    out_refs, weight_out_ref, rows_ref = rest[:-2], rest[-2], rest[-1]
    unfold(query_home_ref, rows_ref, heads)
    parts = len(out_refs)
    slots = rows_ref.shape[0]
    columns = w_query_ref.shape[0] // parts
    step = min(256, slots)
    for ahead, out_ref in enumerate(out_refs):
        dest = lax.rem(me_ref[0] + ahead, jnp.int32(parts))
        mine = pl.ds(pl.multiple_of(dest * columns, columns), columns)

        @pl.loop(0, slots // step)
        def _(i):
            where = pl.ds(pl.multiple_of(i * step, step), step)
            total = dot_nt(rows_ref[where, :], w_query_ref[mine, :])
            total = total + dot_nt(value_rows_ref[where, :], w_value_ref[mine, :])
            out_ref[where, :] = total.astype(BF16)

    width = turned_ref.shape[0]
    step_w = min(256, width)

    @pl.loop(0, width // step_w)
    def _(i):
        where = pl.ds(pl.multiple_of(i * step_w, step_w), step_w)
        weight_out_ref[where, :] = dot(turned_ref[where, :], rows_ref[...]).astype(BF16)


def unsort_kernel(slot_ref, *refs):
    part_refs, out_ref, total_ref = refs[:-2], refs[-2], refs[-1]
    total = part_refs[0][...].astype(F32)
    for part_ref in part_refs[1:]:
        total = total + part_ref[...].astype(F32)
    total_ref[...] = total.astype(BF16)
    toks = out_ref.shape[0]
    slots = total_ref.shape[0]
    step = min(256, toks)

    @pl.loop(0, toks // step)
    def _(i):
        where = pl.ds(pl.multiple_of(i * step, step), step)
        pick = ones_where(iota((step, slots), 1) == slot_ref[where, :])
        out_ref[where, :] = dot(pick, total_ref[...]).astype(BF16)


def call(kernel, outs, inputs, smem=(), scratch=(), flops=0, name=None):
    specs = [
        pl.BlockSpec(memory_space=pltpu.SMEM if i in smem else pltpu.VMEM) for i in range(len(inputs))
    ]
    moved = sum(x.size * x.dtype.itemsize for x in inputs) + sum(
        x.size * x.dtype.itemsize for x in jax.tree.leaves(outs)
    )
    return pl.pallas_call(
        kernel,
        out_shape=outs,
        in_specs=specs,
        out_specs=jax.tree.map(lambda _: pl.BlockSpec(memory_space=pltpu.VMEM), outs),
        scratch_shapes=list(scratch),
        compiler_params=pltpu.CompilerParams(vmem_limit_bytes=VMEM_LIMIT),
        cost_estimate=pl.CostEstimate(flops=flops, bytes_accessed=moved, transcendentals=0),
        name=name,
    )(*inputs)


def exchange(rows):
    return lax.all_to_all(rows, OWNERS, split_axis=0, concat_axis=0, tiled=True)


def on_device(tokens_in, w_query, w_value, cotangent, assignment):
    owners = lax.axis_size(OWNERS)
    parts = lax.axis_size("head")
    toks, width = tokens_in.shape
    width_dev = cotangent.shape[1]
    heads = width_dev // HD
    slot_rows = 2 * toks // CLUSTERS
    assert owners % heads == 0 and heads % 2 == 0
    groups = owners // heads
    per_group = CLUSTERS // groups
    rows = toks if groups == 1 else per_group * slot_rows
    half = rows // 2
    slots = groups * rows
    capacity = (slot_rows * owners + BLOCK_ROWS - 1) // BLOCK_ROWS * BLOCK_ROWS
    shape = jax.ShapeDtypeStruct

    assign_row = assignment.reshape(1, toks)
    send_mixed, slot_row, counts = call(
        functools.partial(project_query_kernel, groups, rows),
        (
            shape((owners, rows, LANES), BF16),
            shape((1, toks), jnp.int32),
            shape((8, CLUSTERS), jnp.int32),
        ),
        (assign_row, tokens_in, w_query, cotangent),
        scratch=[pltpu.VMEM((toks, 2 * width_dev), BF16)],
        flops=2 * toks * width * width_dev + 4 * slots * toks * width_dev,
        name="project_query",
    )
    got_mixed = exchange(send_mixed)
    all_counts = lax.all_gather(counts, OWNERS, axis=0, tiled=True)
    send_value = call(
        functools.partial(project_value_kernel, groups, rows),
        shape((owners, half, LANES), BF16),
        (slot_row, tokens_in, w_value),
        scratch=[pltpu.VMEM((toks, width_dev), BF16)],
        flops=2 * toks * width * width_dev + 2 * slots * toks * width_dev,
        name="project_value",
    )
    got_value = exchange(send_value)
    turned = call(
        sort_tokens_kernel,
        shape((width, slots), BF16),
        (slot_row, tokens_in),
        flops=2 * slots * toks * width,
        name="sort_tokens",
    )
    owner = lax.axis_index(OWNERS)
    first = (lax.div(owner, jnp.int32(heads)) * per_group).astype(jnp.int32).reshape(1)
    blocks = per_group * capacity // BLOCK_ROWS
    block_flops = 2 * BLOCK_ROWS * BLOCK_ROWS * LANES
    tall = pltpu.VMEM((owners, rows + slot_rows, LANES), F32)
    block = pltpu.VMEM((capacity + slot_rows, LANES), F32)
    place = pltpu.SMEM((owners,), jnp.int32)
    back_value = call(
        functools.partial(value_grad_kernel, per_group, slot_rows),
        shape((owners, half, LANES), BF16),
        (first, all_counts, got_mixed),
        smem=(0, 1),
        scratch=[place, tall, block, block, tall],
        flops=8 * blocks * block_flops,
        name="value_grad",
    )
    home_value = exchange(back_value)
    back_query, sums = call(
        functools.partial(query_grad_kernel, per_group, slot_rows),
        (shape((owners, half, LANES), BF16), shape((per_group, LANES), F32)),
        (first, all_counts, got_mixed, got_value),
        smem=(0, 1),
        scratch=[place, tall, tall, block, block, block, tall],
        flops=12 * blocks * block_flops,
        name="query_grad",
    )
    home_query = exchange(back_query)
    weight_flops = 2 * slots * width * width_dev
    partial_wv, value_rows = call(
        functools.partial(weight_grad_kernel, heads),
        (shape((width, width_dev), BF16), shape((slots, width_dev), BF16)),
        (home_value, turned),
        flops=weight_flops,
        name="weight_grad",
    )
    grad_wv = lax.psum_scatter(partial_wv, OWNERS, scatter_dimension=0, tiled=True).astype(F32)
    me = lax.axis_index("head").astype(jnp.int32).reshape(1)
    *partials, partial_wq = call(
        functools.partial(input_grad_kernel, heads),
        tuple([shape((slots, width // parts), BF16)] * parts + [shape((width, width_dev), BF16)]),
        (me, home_query, value_rows, w_query, w_value, turned),
        smem=(0,),
        scratch=[pltpu.VMEM((slots, width_dev), BF16)],
        flops=3 * weight_flops,
        name="input_grad",
    )
    arrived = [partials[0]]
    for ahead in range(1, parts):
        arrived.append(
            lax.ppermute(partials[ahead], "head", [(i, (i + ahead) % parts) for i in range(parts)])
        )
    grad_wq = lax.psum_scatter(partial_wq, OWNERS, scatter_dimension=0, tiled=True).astype(F32)
    grad_input = call(
        unsort_kernel,
        shape((toks, width // parts), BF16),
        (slot_row.reshape(toks, 1), *arrived),
        scratch=[pltpu.VMEM((slots, width // parts), BF16)],
        flops=2 * slots * toks * width // parts,
        name="unsort",
    )
    factor = (CLUSTERS / (toks * owners)) ** 0.5
    gathered = lax.all_gather(sums[:, :HD].astype(BF16), OWNERS, axis=0, tiled=False)
    gathered = gathered.reshape(groups, heads, per_group, HD).transpose(0, 2, 1, 3)
    centroid_grad = gathered.reshape(CLUSTERS, width_dev).astype(F32) * factor
    return (grad_input, grad_wq, grad_wv, centroid_grad)


def solution(mesh):
    return jax.shard_map(
        on_device,
        mesh=mesh,
        in_specs=(
            P(("grp", "seq", "sub"), None),
            P(None, "head"),
            P(None, "head"),
            P(("grp", "seq", "sub"), "head"),
            P(("grp", "seq", "sub"), None),
        ),
        out_specs=(
            P(("grp", "seq", "sub"), "head"),
            P(("grp", "seq", "sub"), "head"),
            P(("grp", "seq", "sub"), "head"),
            P("grp", "head"),
        ),
        check_vma=False,
    )
```

```python
import functools

import jax
import jax.numpy as jnp
from jax import lax
from jax.experimental import pallas as pl
from jax.experimental.pallas import tpu as pltpu
from jax.sharding import PartitionSpec as P

HD = 64
CLUSTERS = 64
BLOCK_ROWS = 128
LANES = 128
UNROLL = 4
COUNT_ROWS = 16
SCALE = 0.5 * HD ** (-0.5)
F32 = jnp.float32
BF16 = jnp.bfloat16
VMEM_LIMIT = 56 * 1024 * 1024
OWNERS = ("seq", "sub")


def iota(shape, dim):
    return lax.broadcasted_iota(jnp.int32, shape, dim)


def low_half(shape):
    return iota(shape, 1) < HD


def swap_halves(tile):
    return pltpu.roll(tile, HD, 1)


def dot(a, b):
    return jnp.dot(a, b, preferred_element_type=F32)


def dot_nt(a, b):
    return lax.dot_general(a, b, (((1,), (1,)), ((), ())), preferred_element_type=F32)


def ones_where(condition):
    return jnp.where(condition, 1.0, 0.0).astype(BF16)


def project_query_kernel(
    groups, rows, assign_ref, tokens_ref, weight_ref, cotan_ref, out_ref, slot_ref, mixed_ref
):
    toks = tokens_ref.shape[0]
    per_group = CLUSTERS // groups
    heads = weight_ref.shape[1] // HD
    member = iota((CLUSTERS, toks), 0) == assign_ref[...]
    member_f = jnp.where(member, 1.0, 0.0)
    member_b = member_f.astype(BF16)
    upto = ones_where(iota((toks, toks), 0) <= iota((toks, toks), 1))
    running = dot(member_b, upto)
    counts = jnp.broadcast_to(jnp.sum(member_f, axis=1, keepdims=True), (CLUSTERS, LANES))
    here, other = iota((CLUSTERS, CLUSTERS), 0), iota((CLUSTERS, CLUSTERS), 1)
    group_of = lambda index: lax.div(index, jnp.int32(per_group))
    earlier = ones_where((other < here) & (group_of(other) == group_of(here)))
    base = dot(earlier, counts.astype(BF16))[:, :1]
    base = base + (group_of(iota((CLUSTERS, 1), 0)) * rows).astype(F32)
    slot = jnp.sum(member_f * (running - 1.0 + base), axis=0, keepdims=True).astype(jnp.int32)
    slot_ref[...] = slot
    spread = jnp.concatenate([member_b, jnp.zeros((LANES - CLUSTERS, toks), BF16)], axis=0)
    tallies = dot_nt(jnp.ones((COUNT_ROWS, toks), BF16), spread).astype(BF16)
    for owner in range(out_ref.shape[0]):
        out_ref[owner, rows:, :] = tallies

    step = min(256, toks)

    @pl.loop(0, toks // step)
    def _(i):
        where = pl.ds(pl.multiple_of(i * step, step), step)
        query = dot(tokens_ref[where, :], weight_ref[...])
        cotan = cotan_ref[where, :].astype(F32)
        low = low_half((step, LANES))
        for pair in range(heads // 2):
            q_tile = query[:, pair * LANES : (pair + 1) * LANES]
            c_tile = cotan[:, pair * LANES : (pair + 1) * LANES]
            even = jnp.where(low, q_tile, swap_halves(c_tile)).astype(BF16)
            odd = jnp.where(low, swap_halves(q_tile), c_tile).astype(BF16)
            mixed_ref[where, 2 * pair * LANES : (2 * pair + 1) * LANES] = even
            mixed_ref[where, (2 * pair + 1) * LANES : (2 * pair + 2) * LANES] = odd

    part = min(256, rows)
    pieces = rows // part

    @pl.loop(0, groups * pieces)
    def _(i):
        group, piece = lax.div(i, jnp.int32(pieces)), lax.rem(i, jnp.int32(pieces))
        first = pl.multiple_of(piece * part, part)
        pick = ones_where(iota((part, toks), 0) + i * part == slot_ref[...])
        sorted_rows = dot(pick, mixed_ref[...]).astype(BF16)
        for head in range(heads):
            out_ref[group * heads + head, pl.ds(first, part), :] = sorted_rows[
                :, head * LANES : (head + 1) * LANES
            ]


def project_value_kernel(groups, rows, slot_ref, tokens_ref, weight_ref, out_ref, value_ref):
    toks = tokens_ref.shape[0]
    heads = weight_ref.shape[1] // HD
    step = min(256, toks)

    @pl.loop(0, toks // step)
    def _(i):
        where = pl.ds(pl.multiple_of(i * step, step), step)
        value_ref[where, :] = dot(tokens_ref[where, :], weight_ref[...]).astype(BF16)

    half = rows // 2
    part = min(256, half)
    pieces = half // part

    @pl.loop(0, groups * pieces)
    def _(i):
        group, piece = lax.div(i, jnp.int32(pieces)), lax.rem(i, jnp.int32(pieces))
        first = pl.multiple_of(piece * part, part)
        index = iota((part, toks), 0) + group * rows + first
        upper = dot(ones_where(index == slot_ref[...]), value_ref[...])
        lower = dot(ones_where(index + half == slot_ref[...]), value_ref[...])
        low = low_half((part, LANES))
        for pair in range(heads // 2):
            up = upper[:, pair * LANES : (pair + 1) * LANES]
            down = lower[:, pair * LANES : (pair + 1) * LANES]
            even = jnp.where(low, up, swap_halves(down)).astype(BF16)
            odd = jnp.where(low, swap_halves(up), down).astype(BF16)
            out_ref[group * heads + 2 * pair, pl.ds(first, part), :] = even
            out_ref[group * heads + 2 * pair + 1, pl.ds(first, part), :] = odd


def sort_tokens_kernel(slot_ref, tokens_ref, out_ref):
    toks = tokens_ref.shape[0]
    slots = out_ref.shape[1]
    turned = tokens_ref[...].T
    part = min(256, slots)

    for i in range(slots // part):
        pick = ones_where(iota((part, toks), 0) + i * part == slot_ref[...])
        out_ref[:, i * part : (i + 1) * part] = dot_nt(turned, pick).astype(BF16)


def softmax_turned(mixed):
    query = jnp.where(low_half(mixed.shape), mixed.astype(F32) * SCALE, 0.0).astype(BF16)
    scores = dot_nt(query, mixed)
    shape = scores.shape
    seen = iota(shape, 0) <= iota(shape, 1)
    scores = jnp.where(seen, scores, -jnp.inf)
    raised = jnp.exp(scores - jnp.max(scores, axis=0, keepdims=True))
    return raised * (1.0 / jnp.sum(raised, axis=0, keepdims=True))


def load_counts(mixed_ref, rows, wide_counts_ref, counts_ref):
    for source in range(mixed_ref.shape[0]):
        tail = mixed_ref[source, rows:, :].astype(F32).astype(jnp.int32)
        wide_counts_ref[source : source + 1, :] = tail[:1, :]
    pltpu.sync_copy(wide_counts_ref, counts_ref)


def for_each_cluster(counts_ref, first_ref, place_ref, owners, per_group, body):
    for source in range(owners):
        place_ref[source] = 0

    def step(cluster, block):
        runs = []
        total = 0
        base = block * BLOCK_ROWS
        for source in range(owners):
            count = counts_ref[source, first_ref[0] + cluster]
            start = place_ref[source]
            runs.append((source, start, base + total))
            place_ref[source] = start + count
            total = total + count
        body(cluster, block, runs, base + total)
        return block + lax.shift_right_logical(total + (BLOCK_ROWS - 1), jnp.int32(7))

    return lax.fori_loop(0, per_group, step, jnp.int32(0))


def for_each_block(blocks, body):
    def step(i, carry):
        for ahead in range(UNROLL):
            body(i * UNROLL + ahead)
        return carry

    lax.fori_loop(0, lax.div(blocks + (UNROLL - 1), jnp.int32(UNROLL)), step, 0)


def block_rows(block):
    return pl.ds(pl.multiple_of(block * BLOCK_ROWS, BLOCK_ROWS), BLOCK_ROWS)


def value_grad_kernel(
    per_group,
    slot_rows,
    first_ref,
    mixed_ref,
    out_ref,
    dense_ref,
    wide_counts_ref,
    counts_ref,
    place_ref,
    wide_ref,
    block_ref,
):
    owners = mixed_ref.shape[0]
    rows = 2 * out_ref.shape[1]
    load_counts(mixed_ref, rows, wide_counts_ref, counts_ref)
    for source in range(owners):
        wide_ref[source, :rows, :] = mixed_ref[source, :rows, :].astype(F32)
        wide_ref[source, rows:, :] = jnp.zeros((slot_rows, LANES), F32)

    def gather(cluster, block, runs, end):
        for source, start, row in runs:
            block_ref[pl.ds(row, slot_rows), :] = wide_ref[source, pl.ds(start, slot_rows), :]
        block_ref[pl.ds(end, BLOCK_ROWS), :] = jnp.zeros((BLOCK_ROWS, LANES), F32)

    blocks = for_each_cluster(counts_ref, first_ref, place_ref, owners, per_group, gather)
    spare = pl.ds(pl.multiple_of(blocks * BLOCK_ROWS, BLOCK_ROWS), UNROLL * BLOCK_ROWS)
    block_ref[spare, :] = jnp.zeros((UNROLL * BLOCK_ROWS, LANES), F32)

    def one_block(block):
        where = block_rows(block)
        mixed = block_ref[where, :].astype(BF16)
        dense_ref[where, :] = mixed
        probs_half = softmax_turned(mixed).astype(BF16)
        block_ref[where, :] = dot(probs_half, mixed)

    for_each_block(blocks, one_block)

    def scatter(cluster, block, runs, end):
        for source, start, row in runs:
            wide_ref[source, pl.ds(start, slot_rows), :] = block_ref[pl.ds(row, slot_rows), :]

    for_each_cluster(counts_ref, first_ref, place_ref, owners, per_group, scatter)
    half = rows // 2
    for source in range(owners):
        up, down = wide_ref[source, :half, :], wide_ref[source, half:rows, :]
        out_ref[source] = jnp.where(low_half((half, LANES)), swap_halves(up), down).astype(BF16)


def query_grad_kernel(
    per_group,
    slot_rows,
    first_ref,
    counts_in_ref,
    dense_ref,
    value_in_ref,
    out_ref,
    wide_counts_ref,
    counts_ref,
    place_ref,
    wide_ref,
    block_ref,
    sums_ref,
    centroid_ref,
):
    owners, half, _ = value_in_ref.shape
    rows = 2 * half
    load_counts(counts_in_ref, 0, wide_counts_ref, counts_ref)
    for source in range(owners):
        value = value_in_ref[source].astype(F32)
        wide_ref[source, :half, :] = swap_halves(value)
        wide_ref[source, half:rows, :] = value
        wide_ref[source, rows:, :] = jnp.zeros((slot_rows, LANES), F32)

    def gather(cluster, block, runs, end):
        for source, start, row in runs:
            block_ref[pl.ds(row, slot_rows), :] = wide_ref[source, pl.ds(start, slot_rows), :]
        block_ref[pl.ds(end, BLOCK_ROWS), :] = jnp.zeros((BLOCK_ROWS, LANES), F32)

    blocks = for_each_cluster(counts_ref, first_ref, place_ref, owners, per_group, gather)
    spare = pl.ds(pl.multiple_of(blocks * BLOCK_ROWS, BLOCK_ROWS), UNROLL * BLOCK_ROWS)
    block_ref[spare, :] = jnp.zeros((UNROLL * BLOCK_ROWS, LANES), F32)

    def one_block(block):
        where = block_rows(block)
        mixed = dense_ref[where, :]
        value = block_ref[where, :].astype(BF16)
        low = low_half((BLOCK_ROWS, LANES))
        cotan = jnp.where(low, jnp.zeros_like(mixed), mixed)
        probs = softmax_turned(mixed)
        grad_probs = dot_nt(value, cotan)
        probs_half = probs.astype(BF16).astype(F32)
        row_dot = jnp.sum(probs_half * grad_probs, axis=0, keepdims=True)
        grad_scores = (probs * (grad_probs - row_dot)).astype(BF16).astype(F32)
        both = (grad_scores + grad_scores.T).astype(BF16)
        grad = (dot(both, mixed) * SCALE).astype(BF16).astype(F32)
        block_ref[where, :] = grad
        sums_ref[pl.ds(block, 1), :] = jnp.sum(grad, axis=0, keepdims=True)

    for_each_block(blocks, one_block)

    most = owners * slot_rows // BLOCK_ROWS if owners * slot_rows >= BLOCK_ROWS else 1

    def scatter(cluster, block, runs, end):
        total = jnp.zeros((1, LANES), F32)
        for ahead in range(most):
            here = block + ahead
            total = total + jnp.where(here * BLOCK_ROWS < end, sums_ref[pl.ds(here, 1), :], 0.0)
        centroid_ref[pl.ds(cluster, 1), :] = total
        for source, start, row in runs:
            wide_ref[source, pl.ds(start, slot_rows), :] = block_ref[pl.ds(row, slot_rows), :]

    for_each_cluster(counts_ref, first_ref, place_ref, owners, per_group, scatter)
    extra = out_ref.shape[1] - half
    centroid = jnp.where(
        low_half((extra, LANES)), centroid_ref[:extra, :], swap_halves(centroid_ref[extra:, :])
    ).astype(BF16)
    for source in range(owners):
        up, down = wide_ref[source, :half, :], wide_ref[source, half:rows, :]
        out_ref[source, :half, :] = jnp.where(low_half((half, LANES)), up, swap_halves(down)).astype(BF16)
        out_ref[source, half:, :] = centroid


def unfold(home_ref, out_ref, heads, start, half, finish):
    low = low_half((half, LANES))
    for group in range(home_ref.shape[0] // heads):
        first = group * 2 * half
        for pair in range(heads // 2):
            even = home_ref[group * heads + 2 * pair, start : start + half, :].astype(F32)
            odd = home_ref[group * heads + 2 * pair + 1, start : start + half, :].astype(F32)
            columns = slice(pair * LANES, (pair + 1) * LANES)
            out_ref[first : first + half, columns] = finish(jnp.where(low, even, swap_halves(odd)))
            out_ref[first + half : first + 2 * half, columns] = finish(
                jnp.where(low, swap_halves(even), odd)
            )


def to_half(x):
    return x.astype(BF16)


def unfold_kernel(heads, home_ref, out_ref):
    unfold(home_ref, out_ref, heads, 0, home_ref.shape[1], to_half)


def weight_grad_kernel(me_ref, turned_ref, rows_ref, *out_refs):
    subs = len(out_refs)
    seqs, piece, _ = out_refs[0].shape
    for ahead, out_ref in enumerate(out_refs):
        sub = lax.rem(me_ref[0] + ahead, jnp.int32(subs))

        @pl.loop(0, seqs)
        def _(seq):
            where = pl.ds(pl.multiple_of((seq * subs + sub) * piece, piece), piece)
            out_ref[seq] = dot(turned_ref[where, :], rows_ref[...]).astype(BF16)


def fold_subs_kernel(me_ref, *refs):
    seqs = refs[0].shape[0]
    terms, out_refs = refs[:-seqs], refs[-seqs:]
    for ahead, out_ref in enumerate(out_refs):
        seq = lax.rem(me_ref[0] + ahead, jnp.int32(seqs))
        total = terms[0][seq].astype(F32)
        for term in terms[1:]:
            total = total + term[seq].astype(F32)
        out_ref[...] = total.astype(BF16)


def sum_kernel(*refs):
    total = refs[0][...].astype(F32)
    for ref in refs[1:-1]:
        total = total + ref[...].astype(F32)
    refs[-1][...] = total


def input_grad_kernel(
    heads, factor, me_ref, query_home_ref, value_rows_ref, w_query_ref, w_value_ref, *rest
):
    out_refs, rows_ref, centroid_ref = rest[:-2], rest[-2], rest[-1]
    parts = len(out_refs)
    slots = rows_ref.shape[0]
    half = slots * heads // query_home_ref.shape[0] // 2
    unfold(query_home_ref, rows_ref, heads, 0, half, to_half)
    extra = query_home_ref.shape[1] - half
    unfold(query_home_ref, centroid_ref, heads, half, extra, lambda x: x * factor)
    columns = w_query_ref.shape[0] // parts
    step = min(256, slots)
    for ahead, out_ref in enumerate(out_refs):
        dest = lax.rem(me_ref[0] + ahead, jnp.int32(parts))
        mine = pl.ds(pl.multiple_of(dest * columns, columns), columns)

        @pl.loop(0, slots // step)
        def _(i):
            where = pl.ds(pl.multiple_of(i * step, step), step)
            total = dot_nt(rows_ref[where, :], w_query_ref[mine, :])
            total = total + dot_nt(value_rows_ref[where, :], w_value_ref[mine, :])
            out_ref[where, :] = total.astype(BF16)


def unsort_kernel(slot_ref, *refs):
    part_refs, out_ref, total_ref = refs[:-2], refs[-2], refs[-1]
    total = part_refs[0][...].astype(F32)
    for part_ref in part_refs[1:]:
        total = total + part_ref[...].astype(F32)
    total_ref[...] = total.astype(BF16)
    toks = out_ref.shape[0]
    slots = total_ref.shape[0]
    step = min(256, toks)

    @pl.loop(0, toks // step)
    def _(i):
        where = pl.ds(pl.multiple_of(i * step, step), step)
        pick = ones_where(iota((step, slots), 1) == slot_ref[where, :])
        out_ref[where, :] = dot(pick, total_ref[...]).astype(BF16)


def call(kernel, outs, inputs, smem=(), scratch=(), flops=0, name=None):
    specs = [
        pl.BlockSpec(memory_space=pltpu.SMEM if i in smem else pltpu.VMEM) for i in range(len(inputs))
    ]
    moved = sum(x.size * x.dtype.itemsize for x in inputs) + sum(
        x.size * x.dtype.itemsize for x in jax.tree.leaves(outs)
    )
    return pl.pallas_call(
        kernel,
        out_shape=outs,
        in_specs=specs,
        out_specs=jax.tree.map(lambda _: pl.BlockSpec(memory_space=pltpu.VMEM), outs),
        scratch_shapes=list(scratch),
        compiler_params=pltpu.CompilerParams(vmem_limit_bytes=VMEM_LIMIT),
        cost_estimate=pl.CostEstimate(flops=flops, bytes_accessed=moved, transcendentals=0),
        name=name,
    )(*inputs)


def exchange(rows):
    return lax.all_to_all(rows, OWNERS, split_axis=0, concat_axis=0, tiled=True)


def pass_round(parts, axis):
    size = len(parts)
    return [parts[0]] + [
        lax.ppermute(parts[ahead], axis, [(i, (i + ahead) % size) for i in range(size)])
        for ahead in range(1, size)
    ]


def index_of(axis):
    return lax.axis_index(axis).astype(jnp.int32).reshape(1)


def weight_grad(turned, rows, name):
    seqs, subs = lax.axis_size("seq"), lax.axis_size("sub")
    width, slots = turned.shape
    columns = rows.shape[1]
    piece = width // (seqs * subs)
    shape = jax.ShapeDtypeStruct
    by_sub = call(
        weight_grad_kernel,
        (shape((seqs, piece, columns), BF16),) * subs,
        (index_of("sub"), turned, rows),
        smem=(0,),
        flops=2 * slots * width * columns,
        name=name,
    )
    by_seq = call(
        fold_subs_kernel,
        (shape((piece, columns), BF16),) * seqs,
        (index_of("seq"), *pass_round(by_sub, "sub")),
        smem=(0,),
        name=name + "_subs",
    )
    return call(
        sum_kernel, shape((piece, columns), F32), tuple(pass_round(by_seq, "seq")), name=name + "_sum"
    )


def on_device(tokens_in, w_query, w_value, cotangent, assignment):
    owners = lax.axis_size(OWNERS)
    parts = lax.axis_size("head")
    toks, width = tokens_in.shape
    width_dev = cotangent.shape[1]
    heads = width_dev // HD
    slot_rows = 2 * toks // CLUSTERS
    assert owners % heads == 0 and heads % 2 == 0
    groups = owners // heads
    per_group = CLUSTERS // groups
    rows = toks if groups == 1 else per_group * slot_rows
    half = rows // 2
    slots = groups * rows
    capacity = (slot_rows * owners + BLOCK_ROWS - 1) // BLOCK_ROWS * BLOCK_ROWS
    extra = max(per_group // 2, 16)
    shape = jax.ShapeDtypeStruct

    assign_row = assignment.reshape(1, toks)
    send_mixed, slot_row = call(
        functools.partial(project_query_kernel, groups, rows),
        (shape((owners, rows + COUNT_ROWS, LANES), BF16), shape((1, toks), jnp.int32)),
        (assign_row, tokens_in, w_query, cotangent),
        scratch=[pltpu.VMEM((toks, 2 * width_dev), BF16)],
        flops=2 * toks * width * width_dev + 4 * slots * toks * width_dev,
        name="project_query",
    )
    got_mixed = exchange(send_mixed)
    send_value = call(
        functools.partial(project_value_kernel, groups, rows),
        shape((owners, half, LANES), BF16),
        (slot_row, tokens_in, w_value),
        scratch=[pltpu.VMEM((toks, width_dev), BF16)],
        flops=2 * toks * width * width_dev + 2 * slots * toks * width_dev,
        name="project_value",
    )
    got_value = exchange(send_value)
    turned = call(
        sort_tokens_kernel,
        shape((width, slots), BF16),
        (slot_row, tokens_in),
        flops=2 * slots * toks * width,
        name="sort_tokens",
    )
    owner = lax.axis_index(OWNERS)
    first = (lax.div(owner, jnp.int32(heads)) * per_group).astype(jnp.int32).reshape(1)
    blocks = per_group * capacity // BLOCK_ROWS
    dense_rows = blocks * BLOCK_ROWS
    block_flops = 2 * BLOCK_ROWS * BLOCK_ROWS * LANES
    common = [
        pltpu.VMEM((owners, LANES), jnp.int32),
        pltpu.SMEM((owners, LANES), jnp.int32),
        pltpu.SMEM((owners,), jnp.int32),
        pltpu.VMEM((owners, rows + slot_rows, LANES), F32),
        pltpu.VMEM((dense_rows + UNROLL * BLOCK_ROWS, LANES), F32),
    ]
    back_value, dense = call(
        functools.partial(value_grad_kernel, per_group, slot_rows),
        (shape((owners, half, LANES), BF16), shape((dense_rows, LANES), BF16)),
        (first, got_mixed),
        smem=(0,),
        scratch=common,
        flops=4 * blocks * block_flops,
        name="value_grad",
    )
    home_value = exchange(back_value)
    back_query = call(
        functools.partial(query_grad_kernel, per_group, slot_rows),
        shape((owners, half + extra, LANES), BF16),
        (first, got_mixed[:, rows:, :], dense, got_value),
        smem=(0,),
        scratch=common + [pltpu.VMEM((blocks + 8, LANES), F32), pltpu.VMEM((2 * extra, LANES), F32)],
        flops=6 * blocks * block_flops,
        name="query_grad",
    )
    home_query = exchange(back_query)
    weight_flops = 2 * slots * width * width_dev
    value_rows = call(
        functools.partial(unfold_kernel, heads), shape((slots, width_dev), BF16), (home_value,), name="unfold"
    )
    grad_wv = weight_grad(turned, value_rows, "value_weight")
    *partials, query_rows, centroid_grad = call(
        functools.partial(input_grad_kernel, heads, (CLUSTERS / (toks * owners)) ** 0.5),
        (shape((slots, width // parts), BF16),) * parts
        + (shape((slots, width_dev), BF16), shape((groups * 2 * extra, width_dev), F32)),
        (index_of("head"), home_query, value_rows, w_query, w_value),
        smem=(0,),
        flops=2 * weight_flops,
        name="input_grad",
    )
    arrived = pass_round(partials, "head")
    grad_wq = weight_grad(turned, query_rows, "query_weight")
    grad_input = call(
        unsort_kernel,
        shape((toks, width // parts), BF16),
        (slot_row.reshape(toks, 1), *arrived),
        scratch=[pltpu.VMEM((slots, width // parts), BF16)],
        flops=2 * slots * toks * width // parts,
        name="unsort",
    )
    if groups > 1:
        centroid_grad = centroid_grad.reshape(groups, 2 * extra, width_dev)[:, :per_group]
        centroid_grad = centroid_grad.reshape(CLUSTERS, width_dev)
    return (grad_input, grad_wq, grad_wv, centroid_grad)


def solution(mesh):
    return jax.shard_map(
        on_device,
        mesh=mesh,
        in_specs=(
            P(("grp", "seq", "sub"), None),
            P(None, "head"),
            P(None, "head"),
            P(("grp", "seq", "sub"), "head"),
            P(("grp", "seq", "sub"), None),
        ),
        out_specs=(
            P(("grp", "seq", "sub"), "head"),
            P(("grp", "seq", "sub"), "head"),
            P(("grp", "seq", "sub"), "head"),
            P("grp", "head"),
        ),
        check_vma=False,
    )
```

```python
import functools

import jax
import jax.numpy as jnp
from jax import lax
from jax.experimental import pallas as pl
from jax.experimental.pallas import tpu as pltpu
from jax.sharding import PartitionSpec as P

HD = 64
CLUSTERS = 64
BLOCK_ROWS = 128
LANES = 128
UNROLL = 4
COUNT_ROWS = 16
SCALE = 0.5 * HD ** (-0.5)
F32 = jnp.float32
BF16 = jnp.bfloat16
VMEM_LIMIT = 56 * 1024 * 1024
OWNERS = ("seq", "sub")
GROUP_ROWS = UNROLL * BLOCK_ROWS
LEAD = 2


def iota(shape, dim):
    return lax.broadcasted_iota(jnp.int32, shape, dim)


def low_half(shape):
    return iota(shape, 1) < HD


def swap_halves(tile):
    return pltpu.roll(tile, HD, 1)


def dot(a, b):
    return jnp.dot(a, b, preferred_element_type=F32)


def dot_nt(a, b):
    return lax.dot_general(a, b, (((1,), (1,)), ((), ())), preferred_element_type=F32)


def ones_where(condition):
    return jnp.where(condition, 1.0, 0.0).astype(BF16)


def owner_of(me_ref, ahead, sizes):
    seq = lax.rem(me_ref[0] + ahead[0], jnp.int32(sizes[0]))
    sub = lax.rem(me_ref[1] + ahead[1], jnp.int32(sizes[1]))
    return seq * sizes[1] + sub


def source_of(me_ref, ahead, sizes):
    return owner_of(me_ref, ((sizes[0] - ahead[0]) % sizes[0], (sizes[1] - ahead[1]) % sizes[1]), sizes)


def steps_of(sizes):
    return [(seq, sub) for seq in range(sizes[0]) for sub in range(sizes[1])]


def hand_out(by_owner_ref, out_refs, me_ref, sizes):
    for ahead, out_ref in zip(steps_of(sizes), out_refs):
        out_ref[...] = by_owner_ref[owner_of(me_ref, ahead, sizes)]


def project_query_kernel(sizes, groups, rows, me_ref, assign_ref, tokens_ref, weight_ref, cotan_ref, *rest):
    out_refs, (slot_ref, mixed_ref, sorted_ref) = rest[:-3], rest[-3:]
    toks = tokens_ref.shape[0]
    per_group = CLUSTERS // groups
    heads = weight_ref.shape[1] // HD
    member = iota((CLUSTERS, toks), 0) == assign_ref[...]
    member_f = jnp.where(member, 1.0, 0.0)
    member_b = member_f.astype(BF16)
    upto = ones_where(iota((toks, toks), 0) <= iota((toks, toks), 1))
    running = dot(member_b, upto)
    counts = jnp.broadcast_to(jnp.sum(member_f, axis=1, keepdims=True), (CLUSTERS, LANES))
    here, other = iota((CLUSTERS, CLUSTERS), 0), iota((CLUSTERS, CLUSTERS), 1)
    group_of = lambda index: lax.div(index, jnp.int32(per_group))
    earlier = ones_where((other < here) & (group_of(other) == group_of(here)))
    base = dot(earlier, counts.astype(BF16))[:, :1]
    base = base + (group_of(iota((CLUSTERS, 1), 0)) * rows).astype(F32)
    slot = jnp.sum(member_f * (running - 1.0 + base), axis=0, keepdims=True).astype(jnp.int32)
    slot_ref[...] = slot
    spread = jnp.concatenate([member_b, jnp.zeros((LANES - CLUSTERS, toks), BF16)], axis=0)
    tallies = dot_nt(jnp.ones((COUNT_ROWS, toks), BF16), spread).astype(BF16)
    for owner in range(sorted_ref.shape[0]):
        sorted_ref[owner, rows:, :] = tallies

    step = min(512, toks)

    @pl.loop(0, toks // step)
    def _(i):
        where = pl.ds(pl.multiple_of(i * step, step), step)
        query = dot(tokens_ref[where, :], weight_ref[...])
        cotan = cotan_ref[where, :].astype(F32)
        low = low_half((step, LANES))
        for pair in range(heads // 2):
            q_tile = query[:, pair * LANES : (pair + 1) * LANES]
            c_tile = cotan[:, pair * LANES : (pair + 1) * LANES]
            even = jnp.where(low, q_tile, swap_halves(c_tile)).astype(BF16)
            odd = jnp.where(low, swap_halves(q_tile), c_tile).astype(BF16)
            mixed_ref[where, 2 * pair * LANES : (2 * pair + 1) * LANES] = even
            mixed_ref[where, (2 * pair + 1) * LANES : (2 * pair + 2) * LANES] = odd

    part = min(512, rows)
    pieces = rows // part

    @pl.loop(0, groups * pieces)
    def _(i):
        group, piece = lax.div(i, jnp.int32(pieces)), lax.rem(i, jnp.int32(pieces))
        first = pl.multiple_of(piece * part, part)
        pick = ones_where(iota((part, toks), 0) + i * part == slot_ref[...])
        sorted_rows = dot(pick, mixed_ref[...]).astype(BF16)
        for head in range(heads):
            sorted_ref[group * heads + head, pl.ds(first, part), :] = sorted_rows[
                :, head * LANES : (head + 1) * LANES
            ]

    hand_out(sorted_ref, out_refs, me_ref, sizes)


def project_value_kernel(
    sizes, groups, rows, parts, me_ref, slot_ref, tokens_ref, w_value_ref, w_query_ref, *rest
):
    owners = sizes[0] * sizes[1]
    out_refs, weight_refs, (turned_ref, value_ref, sorted_ref) = (
        rest[:owners],
        rest[owners : owners + parts],
        rest[owners + parts :],
    )
    toks = tokens_ref.shape[0]
    heads = w_value_ref.shape[1] // HD
    step = min(512, toks)

    @pl.loop(0, toks // step)
    def _(i):
        where = pl.ds(pl.multiple_of(i * step, step), step)
        value_ref[where, :] = dot(tokens_ref[where, :], w_value_ref[...]).astype(BF16)

    half = rows // 2
    part = min(256, half)
    pieces = half // part

    @pl.loop(0, groups * pieces)
    def _(i):
        group, piece = lax.div(i, jnp.int32(pieces)), lax.rem(i, jnp.int32(pieces))
        first = pl.multiple_of(piece * part, part)
        index = iota((part, toks), 0) + group * rows + first
        upper = dot(ones_where(index == slot_ref[...]), value_ref[...])
        lower = dot(ones_where(index + half == slot_ref[...]), value_ref[...])
        low = low_half((part, LANES))
        for pair in range(heads // 2):
            up = upper[:, pair * LANES : (pair + 1) * LANES]
            down = lower[:, pair * LANES : (pair + 1) * LANES]
            even = jnp.where(low, up, swap_halves(down)).astype(BF16)
            odd = jnp.where(low, swap_halves(up), down).astype(BF16)
            sorted_ref[group * heads + 2 * pair, pl.ds(first, part), :] = even
            sorted_ref[group * heads + 2 * pair + 1, pl.ds(first, part), :] = odd

    hand_out(sorted_ref, out_refs, me_ref, sizes)
    columns = w_query_ref.shape[0] // parts
    for ahead, weight_out_ref in enumerate(weight_refs):
        dest = lax.rem(me_ref[2] + ahead, jnp.int32(parts))
        mine = pl.ds(pl.multiple_of(dest * columns, columns), columns)
        weight_out_ref[0] = w_query_ref[mine, :]
        weight_out_ref[1] = w_value_ref[mine, :]
    turned = tokens_ref[...].T
    slots = turned_ref.shape[1]
    part = min(256, slots)
    for i in range(slots // part):
        pick = ones_where(iota((part, toks), 0) + i * part == slot_ref[...])
        turned_ref[:, i * part : (i + 1) * part] = dot_nt(turned, pick).astype(BF16)


def score(mixed):
    query = jnp.where(low_half(mixed.shape), mixed.astype(F32) * SCALE, 0.0).astype(BF16)
    return dot_nt(query, mixed)


def softmax_turned(scores):
    shape = scores.shape
    seen = iota(shape, 0) <= iota(shape, 1)
    scores = jnp.where(seen, scores, -jnp.inf)
    raised = jnp.exp(scores - jnp.max(scores, axis=0, keepdims=True))
    return raised * (1.0 / jnp.sum(raised, axis=0, keepdims=True))


def for_each_cluster(counts_ref, me_ref, place_ref, owners, per_group, body):
    for source in range(owners):
        place_ref[source] = 0

    def step(cluster, block):
        runs = []
        total = 0
        base = block * BLOCK_ROWS
        for source in range(owners):
            count = counts_ref[source, me_ref[3] + cluster]
            start = place_ref[source]
            runs.append((source, start, base + total))
            place_ref[source] = start + count
            total = total + count
        body(cluster, block, runs, base + total)
        return block + lax.shift_right_logical(total + (BLOCK_ROWS - 1), jnp.int32(7))

    return lax.fori_loop(0, per_group, step, jnp.int32(LEAD * UNROLL))


def gather_blocks(counts_ref, me_ref, place_ref, owners, per_group, slot_rows, wide_ref, block_ref):
    def body(cluster, block, runs, end):
        for source, start, row in runs:
            block_ref[pl.ds(row, slot_rows), :] = wide_ref[source, pl.ds(start, slot_rows), :]
        block_ref[pl.ds(end, BLOCK_ROWS), :] = jnp.zeros((BLOCK_ROWS, LANES), F32)

    blocks = for_each_cluster(counts_ref, me_ref, place_ref, owners, per_group, body)
    spare = pl.ds(pl.multiple_of(blocks * BLOCK_ROWS, BLOCK_ROWS), GROUP_ROWS)
    block_ref[spare, :] = jnp.zeros((GROUP_ROWS, LANES), F32)
    return blocks


def for_each_group(blocks, stages):
    first, second, third = stages
    groups = lax.div(blocks + (UNROLL - 1), jnp.int32(UNROLL))

    def step(i, carry):
        for slot in range(2):
            group = LEAD + 2 * i + slot
            third(group - 2, slot)
            second(group - 1, 1 - slot)
            first(group, slot)
        return carry

    lax.fori_loop(0, lax.shift_right_logical(groups + 1, jnp.int32(1)), step, 0)


def block_rows(group, ahead):
    return pl.ds(pl.multiple_of((group * UNROLL + ahead) * BLOCK_ROWS, BLOCK_ROWS), BLOCK_ROWS)


def tile_rows(ahead):
    return slice(ahead * BLOCK_ROWS, (ahead + 1) * BLOCK_ROWS)


def value_grad_kernel(sizes, per_group, slot_rows, me_ref, *refs):
    owners = sizes[0] * sizes[1]
    mixed_refs, out_refs, rest = refs[:owners], refs[owners : 2 * owners], refs[2 * owners :]
    dense_ref, counts_out_ref, counts_ref, place_ref, wide_ref, block_ref, home_ref = rest[:7]
    score_refs, probs_refs = rest[7:9], rest[9:11]
    half = out_refs[0].shape[0]
    rows = 2 * half
    for ahead, mixed_ref in zip(steps_of(sizes), mixed_refs):
        source = source_of(me_ref, ahead, sizes)
        tail = mixed_ref[rows:, :].astype(F32).astype(jnp.int32)
        counts_out_ref[pl.ds(source, 1), :] = tail[:1, :]
        wide_ref[source, :rows, :] = mixed_ref[:rows, :].astype(F32)
        wide_ref[source, rows:, :] = jnp.zeros((slot_rows, LANES), F32)
    pltpu.sync_copy(counts_out_ref, counts_ref)
    blocks = gather_blocks(counts_ref, me_ref, place_ref, owners, per_group, slot_rows, wide_ref, block_ref)

    def first(group, slot):
        for ahead in range(UNROLL):
            where = block_rows(group, ahead)
            mixed = block_ref[where, :].astype(BF16)
            dense_ref[where, :] = mixed
            score_refs[slot][tile_rows(ahead), :] = score(mixed)

    def second(group, slot):
        for ahead in range(UNROLL):
            tile = tile_rows(ahead)
            probs_refs[slot][tile, :] = softmax_turned(score_refs[slot][tile, :]).astype(BF16)

    def third(group, slot):
        for ahead in range(UNROLL):
            where = block_rows(group, ahead)
            block_ref[where, :] = dot(probs_refs[slot][tile_rows(ahead), :], dense_ref[where, :])

    for_each_group(blocks, (first, second, third))

    def scatter(cluster, block, runs, end):
        for source, start, row in runs:
            wide_ref[source, pl.ds(start, slot_rows), :] = block_ref[pl.ds(row, slot_rows), :]

    for_each_cluster(counts_ref, me_ref, place_ref, owners, per_group, scatter)
    for ahead, out_ref in zip(steps_of(sizes), out_refs):
        source = owner_of(me_ref, ahead, sizes)
        up, down = wide_ref[source, :half, :], wide_ref[source, half:rows, :]
        out_ref[...] = jnp.where(low_half((half, LANES)), swap_halves(up), down).astype(BF16)


def query_grad_kernel(sizes, per_group, slot_rows, me_ref, counts_ref, dense_ref, *refs):
    owners = sizes[0] * sizes[1]
    value_refs, out_refs, rest = refs[:owners], refs[owners : 2 * owners], refs[2 * owners :]
    place_ref, wide_ref, block_ref, sums_ref, centroid_ref = rest[:5]
    score_refs, grad_probs_refs, both_refs = rest[5:7], rest[7:9], rest[9:11]
    half = value_refs[0].shape[0]
    rows = 2 * half
    for ahead, value_ref in zip(steps_of(sizes), value_refs):
        source = source_of(me_ref, ahead, sizes)
        value = value_ref[...].astype(F32)
        wide_ref[source, :half, :] = swap_halves(value)
        wide_ref[source, half:rows, :] = value
        wide_ref[source, rows:, :] = jnp.zeros((slot_rows, LANES), F32)
    blocks = gather_blocks(counts_ref, me_ref, place_ref, owners, per_group, slot_rows, wide_ref, block_ref)

    def first(group, slot):
        for ahead in range(UNROLL):
            where, tile = block_rows(group, ahead), tile_rows(ahead)
            mixed = dense_ref[where, :]
            value = block_ref[where, :].astype(BF16)
            cotan = jnp.where(low_half(mixed.shape), jnp.zeros_like(mixed), mixed)
            score_refs[slot][tile, :] = score(mixed)
            grad_probs_refs[slot][tile, :] = dot_nt(value, cotan)

    def second(group, slot):
        for ahead in range(UNROLL):
            tile = tile_rows(ahead)
            probs = softmax_turned(score_refs[slot][tile, :])
            grad_probs = grad_probs_refs[slot][tile, :]
            probs_half = probs.astype(BF16).astype(F32)
            row_dot = jnp.sum(probs_half * grad_probs, axis=0, keepdims=True)
            grad_scores = (probs * (grad_probs - row_dot)).astype(BF16).astype(F32)
            both_refs[slot][tile, :] = (grad_scores + grad_scores.T).astype(BF16)

    def third(group, slot):
        for ahead in range(UNROLL):
            where = block_rows(group, ahead)
            grad = dot(both_refs[slot][tile_rows(ahead), :], dense_ref[where, :]) * SCALE
            grad = grad.astype(BF16).astype(F32)
            block_ref[where, :] = grad
            sums_ref[pl.ds(group * UNROLL + ahead, 1), :] = jnp.sum(grad, axis=0, keepdims=True)

    for_each_group(blocks, (first, second, third))
    most = (owners * slot_rows + BLOCK_ROWS - 1) // BLOCK_ROWS

    def scatter(cluster, block, runs, end):
        total = jnp.zeros((1, LANES), F32)
        for ahead in range(most):
            here = block + ahead
            total = total + jnp.where(here * BLOCK_ROWS < end, sums_ref[pl.ds(here, 1), :], 0.0)
        centroid_ref[pl.ds(cluster, 1), :] = total
        for source, start, row in runs:
            wide_ref[source, pl.ds(start, slot_rows), :] = block_ref[pl.ds(row, slot_rows), :]

    for_each_cluster(counts_ref, me_ref, place_ref, owners, per_group, scatter)
    extra = out_refs[0].shape[0] - half
    centroid = jnp.where(
        low_half((extra, LANES)), centroid_ref[:extra, :], swap_halves(centroid_ref[extra:, :])
    ).astype(BF16)
    for ahead, out_ref in zip(steps_of(sizes), out_refs):
        source = owner_of(me_ref, ahead, sizes)
        up, down = wide_ref[source, :half, :], wide_ref[source, half:rows, :]
        out_ref[:half, :] = jnp.where(low_half((half, LANES)), up, swap_halves(down)).astype(BF16)
        out_ref[half:, :] = centroid


def unfold(home_ref, out_ref, heads, start, half, finish):
    low = low_half((half, LANES))
    for group in range(home_ref.shape[0] // heads):
        first = group * 2 * half
        for pair in range(heads // 2):
            even = home_ref[group * heads + 2 * pair, start : start + half, :].astype(F32)
            odd = home_ref[group * heads + 2 * pair + 1, start : start + half, :].astype(F32)
            columns = slice(pair * LANES, (pair + 1) * LANES)
            out_ref[first : first + half, columns] = finish(jnp.where(low, even, swap_halves(odd)))
            out_ref[first + half : first + 2 * half, columns] = finish(
                jnp.where(low, swap_halves(even), odd)
            )


def to_half(x):
    return x.astype(BF16)


def weight_grad_kernel(sizes, heads, factor, me_ref, turned_ref, *refs):
    owners = sizes[0] * sizes[1]
    home_refs, rows_ref, sub_refs, rest = (
        refs[:owners],
        refs[owners],
        refs[owners + 1 : owners + 1 + sizes[1]],
        refs[owners + 1 + sizes[1] :],
    )
    home_ref, whole_ref = rest[-2:]
    for ahead, part_ref in zip(steps_of(sizes), home_refs):
        home_ref[source_of(me_ref, ahead, sizes)] = part_ref[...]
    slots = rows_ref.shape[0]
    half = slots * heads // owners // 2
    unfold(home_ref, rows_ref, heads, 0, half, to_half)
    if factor is not None:
        unfold(home_ref, rest[0], heads, half, home_ref.shape[1] - half, lambda x: x * factor)
    width = turned_ref.shape[0]
    step = min(512, width)

    @pl.loop(0, width // step)
    def _(i):
        where = pl.ds(pl.multiple_of(i * step, step), step)
        whole_ref[where, :] = dot(turned_ref[where, :], rows_ref[...]).astype(BF16)

    piece = width // owners
    for ahead, sub_ref in enumerate(sub_refs):
        sub = lax.rem(me_ref[1] + ahead, jnp.int32(sizes[1]))
        for seq in range(sizes[0]):
            first = pl.multiple_of((seq * sizes[1] + sub) * piece, piece)
            sub_ref[seq] = whole_ref[pl.ds(first, piece), :]


def fold_subs_kernel(me_ref, *refs):
    seqs = refs[0].shape[0]
    terms, out_refs = refs[:-seqs], refs[-seqs:]
    for ahead, out_ref in enumerate(out_refs):
        seq = lax.rem(me_ref[0] + ahead, jnp.int32(seqs))
        total = terms[0][seq].astype(F32)
        for term in terms[1:]:
            total = total + term[seq].astype(F32)
        out_ref[...] = total.astype(BF16)


def sum_kernel(*refs):
    total = refs[0][...].astype(F32)
    for ref in refs[1:-1]:
        total = total + ref[...].astype(F32)
    refs[-1][...] = total


def input_grad_kernel(sizes, heads, parts, me_ref, slot_ref, *refs):
    value_refs, weight_refs, query_refs = refs[:parts], refs[parts : 2 * parts], refs[2 * parts : -5]
    out_ref, home_ref, rows_ref, sum_ref, total_ref = refs[-5:]
    owners = sizes[0] * sizes[1]
    slots = rows_ref.shape[0]
    step = min(512, slots)
    each = (len(query_refs) - 1) // max(parts - 1, 1)
    for group in range(parts):
        if group == 0:
            source_ref = query_refs[0]
        else:
            pieces = query_refs[1 + (group - 1) * each : 1 + group * each]
            for index, ahead in enumerate(steps_of(sizes)):
                piece = pieces[index][...] if each > 1 else pieces[0][index]
                home_ref[source_of(me_ref, ahead, sizes)] = piece
            unfold(home_ref, rows_ref, heads, 0, slots * heads // owners // 2, to_half)
            source_ref = rows_ref

        @pl.loop(0, slots // step)
        def _(i):
            where = pl.ds(pl.multiple_of(i * step, step), step)
            total = dot_nt(source_ref[where, :], weight_refs[group][0])
            total = total + dot_nt(value_refs[group][where, :], weight_refs[group][1])
            total = total.astype(BF16).astype(F32)
            if group > 0:
                total = sum_ref[where, :] + total
            if group == parts - 1:
                total_ref[where, :] = total.astype(BF16)
            else:
                sum_ref[where, :] = total

    toks = out_ref.shape[0]
    step_t = min(512, toks)

    @pl.loop(0, toks // step_t)
    def _(i):
        where = pl.ds(pl.multiple_of(i * step_t, step_t), step_t)
        pick = ones_where(iota((step_t, slots), 1) == slot_ref[where, :])
        out_ref[where, :] = dot(pick, total_ref[...]).astype(BF16)


def call(kernel, outs, inputs, smem=(0,), scratch=(), flops=0, name=None):
    specs = [
        pl.BlockSpec(memory_space=pltpu.SMEM if i in smem else pltpu.VMEM) for i in range(len(inputs))
    ]
    moved = sum(x.size * x.dtype.itemsize for x in inputs) + sum(
        x.size * x.dtype.itemsize for x in jax.tree.leaves(outs)
    )
    return pl.pallas_call(
        kernel,
        out_shape=outs,
        in_specs=specs,
        out_specs=jax.tree.map(lambda _: pl.BlockSpec(memory_space=pltpu.VMEM), outs),
        scratch_shapes=list(scratch),
        compiler_params=pltpu.CompilerParams(vmem_limit_bytes=VMEM_LIMIT),
        cost_estimate=pl.CostEstimate(flops=flops, bytes_accessed=moved, transcendentals=0),
        name=name,
    )(*inputs)


def exchange(parts, sizes):
    out = []
    for ahead, part in zip(steps_of(sizes), parts):
        moves = [
            (
                seq * sizes[1] + sub,
                (seq + ahead[0]) % sizes[0] * sizes[1] + (sub + ahead[1]) % sizes[1],
            )
            for seq, sub in steps_of(sizes)
        ]
        out.append(part if ahead == (0, 0) else lax.ppermute(part, OWNERS, moves))
    return out


def shift(part, axis, ahead):
    size = lax.axis_size(axis)
    return lax.ppermute(part, axis, [(i, (i + ahead) % size) for i in range(size)])


def pass_round(parts, axis):
    return [parts[0]] + [shift(parts[ahead], axis, ahead) for ahead in range(1, len(parts))]


def reduce_weight(me, by_sub, name):
    seqs, piece, columns = by_sub[0].shape
    shape = jax.ShapeDtypeStruct
    by_seq = call(
        fold_subs_kernel,
        (shape((piece, columns), BF16),) * seqs,
        (me, *pass_round(by_sub, "sub")),
        name=name + "_subs",
    )
    return call(
        sum_kernel,
        shape((piece, columns), F32),
        tuple(pass_round(by_seq, "seq")),
        smem=(),
        name=name + "_sum",
    )


def on_device(tokens_in, w_query, w_value, cotangent, assignment):
    sizes = (lax.axis_size("seq"), lax.axis_size("sub"))
    owners = sizes[0] * sizes[1]
    parts = lax.axis_size("head")
    toks, width = tokens_in.shape
    width_dev = cotangent.shape[1]
    heads = width_dev // HD
    slot_rows = 2 * toks // CLUSTERS
    assert owners % heads == 0 and heads % 2 == 0
    groups = owners // heads
    per_group = CLUSTERS // groups
    rows = toks if groups == 1 else per_group * slot_rows
    half = rows // 2
    slots = groups * rows
    columns = width // parts
    capacity = (slot_rows * owners + BLOCK_ROWS - 1) // BLOCK_ROWS * BLOCK_ROWS
    extra = max(per_group // 2, 16)
    shape = jax.ShapeDtypeStruct
    seq, sub = lax.axis_index("seq"), lax.axis_index("sub")
    first = lax.div(seq * sizes[1] + sub, jnp.int32(heads)) * per_group
    me = jnp.stack([seq, sub, lax.axis_index("head"), first]).astype(jnp.int32)

    def several(count, *dims):
        return (shape(dims, BF16),) * count

    *send_mixed, slot_row = call(
        functools.partial(project_query_kernel, sizes, groups, rows),
        several(owners, rows + COUNT_ROWS, LANES) + (shape((1, toks), jnp.int32),),
        (me, assignment.reshape(1, toks), tokens_in, w_query, cotangent),
        scratch=[pltpu.VMEM((toks, 2 * width_dev), BF16), pltpu.VMEM((owners, rows + COUNT_ROWS, LANES), BF16)],
        flops=2 * toks * width * width_dev + 4 * slots * toks * width_dev,
        name="project_query",
    )
    got_mixed = exchange(send_mixed, sizes)
    sent = call(
        functools.partial(project_value_kernel, sizes, groups, rows, parts),
        several(owners, half, LANES) + several(parts, 2, columns, width_dev) + several(1, width, slots),
        (me, slot_row, tokens_in, w_value, w_query),
        scratch=[pltpu.VMEM((toks, width_dev), BF16), pltpu.VMEM((owners, half, LANES), BF16)],
        flops=2 * toks * width * width_dev + 2 * slots * toks * (width_dev + width),
        name="project_value",
    )
    got_value = exchange(sent[:owners], sizes)
    weights = pass_round(sent[owners:-1], "head")
    turned = sent[-1]
    blocks = per_group * capacity // BLOCK_ROWS
    held = blocks + (LEAD + 4) * UNROLL
    block_flops = 2 * BLOCK_ROWS * BLOCK_ROWS * LANES
    tall = pltpu.VMEM((owners, rows + slot_rows, LANES), F32)
    dense_rows = pltpu.VMEM((held * BLOCK_ROWS, LANES), F32)
    group_f32 = pltpu.VMEM((GROUP_ROWS, BLOCK_ROWS), F32)
    group_b16 = pltpu.VMEM((GROUP_ROWS, BLOCK_ROWS), BF16)
    place = pltpu.SMEM((owners,), jnp.int32)
    *back_value, dense, counts = call(
        functools.partial(value_grad_kernel, sizes, per_group, slot_rows),
        several(owners, half, LANES)
        + several(1, held * BLOCK_ROWS, LANES)
        + (shape((owners, LANES), jnp.int32),),
        (me, *got_mixed),
        scratch=[pltpu.SMEM((owners, LANES), jnp.int32), place, tall, dense_rows, tall]
        + [group_f32] * 2
        + [group_b16] * 2,
        flops=4 * blocks * block_flops,
        name="value_grad",
    )
    home_value = exchange(back_value, sizes)
    back_query = call(
        functools.partial(query_grad_kernel, sizes, per_group, slot_rows),
        several(owners, half + extra, LANES),
        (me, counts, dense, *got_value),
        smem=(0, 1),
        scratch=[place, tall, dense_rows, pltpu.VMEM((held, LANES), F32), pltpu.VMEM((2 * extra, LANES), F32)]
        + [group_f32] * 4
        + [group_b16] * 2,
        flops=6 * blocks * block_flops,
        name="query_grad",
    )
    home_query = exchange(back_query, sizes)
    weight_flops = 2 * slots * width * width_dev
    weight_outs = several(1, slots, width_dev) + several(sizes[1], sizes[0], width // owners, width_dev)
    value_rows, *value_weight = call(
        functools.partial(weight_grad_kernel, sizes, heads, None),
        weight_outs,
        (me, turned, *home_value),
        scratch=[pltpu.VMEM((owners, half, LANES), BF16), pltpu.VMEM((width, width_dev), BF16)],
        flops=weight_flops,
        name="value_weight",
    )
    all_value_rows = pass_round([value_rows] * parts, "head")
    grad_wv = reduce_weight(me, value_weight, "value_weight")
    if parts == 2:
        others = [shift(piece, "head", 1) for piece in home_query]
    else:
        stacked = jnp.stack(home_query)
        others = [shift(stacked, "head", ahead) for ahead in range(1, parts)]
    query_rows, *query_weight, centroid_grad = call(
        functools.partial(weight_grad_kernel, sizes, heads, (CLUSTERS / (toks * owners)) ** 0.5),
        weight_outs + (shape((groups * 2 * extra, width_dev), F32),),
        (me, turned, *home_query),
        scratch=[pltpu.VMEM((owners, half + extra, LANES), BF16), pltpu.VMEM((width, width_dev), BF16)],
        flops=weight_flops,
        name="query_weight",
    )
    grad_wq = reduce_weight(me, query_weight, "query_weight")
    grad_input = call(
        functools.partial(input_grad_kernel, sizes, heads, parts),
        shape((toks, columns), BF16),
        (me, slot_row.reshape(toks, 1), *all_value_rows, *weights, query_rows, *others),
        scratch=[
            pltpu.VMEM((owners, half + extra, LANES), BF16),
            pltpu.VMEM((slots, width_dev), BF16),
            pltpu.VMEM((slots, columns), F32),
            pltpu.VMEM((slots, columns), BF16),
        ],
        flops=2 * weight_flops + 2 * slots * toks * columns,
        name="input_grad",
    )
    if groups > 1:
        centroid_grad = centroid_grad.reshape(groups, 2 * extra, width_dev)[:, :per_group]
        centroid_grad = centroid_grad.reshape(CLUSTERS, width_dev)
    return (grad_input, grad_wq, grad_wv, centroid_grad)


def solution(mesh):
    return jax.shard_map(
        on_device,
        mesh=mesh,
        in_specs=(
            P(("grp", "seq", "sub"), None),
            P(None, "head"),
            P(None, "head"),
            P(("grp", "seq", "sub"), "head"),
            P(("grp", "seq", "sub"), None),
        ),
        out_specs=(
            P(("grp", "seq", "sub"), "head"),
            P(("grp", "seq", "sub"), "head"),
            P(("grp", "seq", "sub"), "head"),
            P("grp", "head"),
        ),
        check_vma=False,
    )
```

```python
import functools

import jax
import jax.numpy as jnp
from jax import lax
from jax.experimental import pallas as pl
from jax.experimental.pallas import tpu as pltpu
from jax.sharding import PartitionSpec as P

HD = 64
CLUSTERS = 64
BLOCK_ROWS = 128
LANES = 128
UNROLL = 4
COUNT_ROWS = 16
SCALE = 0.5 * HD ** (-0.5)
F32 = jnp.float32
BF16 = jnp.bfloat16
OWNERS = ("seq", "sub")
GROUP_ROWS = UNROLL * BLOCK_ROWS
LEAD = 2


def iota(shape, dim):
    return lax.broadcasted_iota(jnp.int32, shape, dim)


def low_half(shape):
    return iota(shape, 1) < HD


def swap_halves(tile):
    return pltpu.roll(tile, HD, 1)


def dot(a, b):
    return jnp.dot(a, b, preferred_element_type=F32)


def dot_nt(a, b):
    return lax.dot_general(a, b, (((1,), (1,)), ((), ())), preferred_element_type=F32)


def ones_where(condition):
    return jnp.where(condition, 1.0, 0.0).astype(BF16)


def owner_of(me_ref, ahead, sizes):
    seq = lax.rem(me_ref[0] + ahead[0], jnp.int32(sizes[0]))
    sub = lax.rem(me_ref[1] + ahead[1], jnp.int32(sizes[1]))
    return seq * sizes[1] + sub


def source_of(me_ref, ahead, sizes):
    return owner_of(me_ref, ((sizes[0] - ahead[0]) % sizes[0], (sizes[1] - ahead[1]) % sizes[1]), sizes)


def steps_of(sizes):
    return [(seq, sub) for seq in range(sizes[0]) for sub in range(sizes[1])]


def hand_out(by_owner_ref, out_refs, me_ref, sizes):
    for ahead, out_ref in zip(steps_of(sizes), out_refs):
        out_ref[...] = by_owner_ref[owner_of(me_ref, ahead, sizes)]


def project_query_kernel(sizes, groups, rows, me_ref, assign_ref, tokens_ref, weight_ref, cotan_ref, *rest):
    out_refs, (slot_ref, mixed_ref, sorted_ref) = rest[:-3], rest[-3:]
    toks = tokens_ref.shape[0]
    per_group = CLUSTERS // groups
    heads = weight_ref.shape[1] // HD
    member = iota((CLUSTERS, toks), 0) == assign_ref[...]
    member_f = jnp.where(member, 1.0, 0.0)
    member_b = member_f.astype(BF16)
    upto = ones_where(iota((toks, toks), 0) <= iota((toks, toks), 1))
    running = dot(member_b, upto)
    counts = jnp.broadcast_to(jnp.sum(member_f, axis=1, keepdims=True), (CLUSTERS, LANES))
    here, other = iota((CLUSTERS, CLUSTERS), 0), iota((CLUSTERS, CLUSTERS), 1)
    group_of = lambda index: lax.div(index, jnp.int32(per_group))
    earlier = ones_where((other < here) & (group_of(other) == group_of(here)))
    base = dot(earlier, counts.astype(BF16))[:, :1]
    base = base + (group_of(iota((CLUSTERS, 1), 0)) * rows).astype(F32)
    slot = jnp.sum(member_f * (running - 1.0 + base), axis=0, keepdims=True).astype(jnp.int32)
    slot_ref[...] = slot
    spread = jnp.concatenate([member_b, jnp.zeros((LANES - CLUSTERS, toks), BF16)], axis=0)
    tallies = dot_nt(jnp.ones((COUNT_ROWS, toks), BF16), spread).astype(BF16)
    for owner in range(sorted_ref.shape[0]):
        sorted_ref[owner, rows:, :] = tallies

    step = min(512, toks)

    @pl.loop(0, toks // step)
    def _(i):
        where = pl.ds(pl.multiple_of(i * step, step), step)
        query = dot(tokens_ref[where, :], weight_ref[...])
        cotan = cotan_ref[where, :].astype(F32)
        low = low_half((step, LANES))
        for pair in range(heads // 2):
            q_tile = query[:, pair * LANES : (pair + 1) * LANES]
            c_tile = cotan[:, pair * LANES : (pair + 1) * LANES]
            even = jnp.where(low, q_tile, swap_halves(c_tile)).astype(BF16)
            odd = jnp.where(low, swap_halves(q_tile), c_tile).astype(BF16)
            mixed_ref[where, 2 * pair * LANES : (2 * pair + 1) * LANES] = even
            mixed_ref[where, (2 * pair + 1) * LANES : (2 * pair + 2) * LANES] = odd

    part = min(512, rows)
    pieces = rows // part

    @pl.loop(0, groups * pieces)
    def _(i):
        group, piece = lax.div(i, jnp.int32(pieces)), lax.rem(i, jnp.int32(pieces))
        first = pl.multiple_of(piece * part, part)
        pick = ones_where(iota((part, toks), 0) + i * part == slot_ref[...])
        sorted_rows = dot(pick, mixed_ref[...]).astype(BF16)
        for head in range(heads):
            sorted_ref[group * heads + head, pl.ds(first, part), :] = sorted_rows[
                :, head * LANES : (head + 1) * LANES
            ]

    hand_out(sorted_ref, out_refs, me_ref, sizes)


def project_value_kernel(sizes, groups, rows, me_ref, slot_ref, tokens_ref, weight_ref, *rest):
    out_refs, (turned_ref, unsort_ref, value_ref, sorted_ref) = rest[:-4], rest[-4:]
    toks = tokens_ref.shape[0]
    heads = weight_ref.shape[1] // HD
    step = min(512, toks)

    @pl.loop(0, toks // step)
    def _(i):
        where = pl.ds(pl.multiple_of(i * step, step), step)
        value_ref[where, :] = dot(tokens_ref[where, :], weight_ref[...]).astype(BF16)

    half = rows // 2
    part = min(256, half)
    pieces = half // part

    @pl.loop(0, groups * pieces)
    def _(i):
        group, piece = lax.div(i, jnp.int32(pieces)), lax.rem(i, jnp.int32(pieces))
        first = pl.multiple_of(piece * part, part)
        index = iota((part, toks), 0) + group * rows + first
        upper = dot(ones_where(index == slot_ref[...]), value_ref[...])
        lower = dot(ones_where(index + half == slot_ref[...]), value_ref[...])
        low = low_half((part, LANES))
        for pair in range(heads // 2):
            up = upper[:, pair * LANES : (pair + 1) * LANES]
            down = lower[:, pair * LANES : (pair + 1) * LANES]
            even = jnp.where(low, up, swap_halves(down)).astype(BF16)
            odd = jnp.where(low, swap_halves(up), down).astype(BF16)
            sorted_ref[group * heads + 2 * pair, pl.ds(first, part), :] = even
            sorted_ref[group * heads + 2 * pair + 1, pl.ds(first, part), :] = odd

    hand_out(sorted_ref, out_refs, me_ref, sizes)
    turned_ref[...] = tokens_ref[...].T
    slots = unsort_ref.shape[1]
    part = min(256, slots)
    for i in range(slots // part):
        pick = ones_where(iota((part, toks), 0) + i * part == slot_ref[...])
        unsort_ref[:, i * part : (i + 1) * part] = pick.T


def score(mixed):
    query = jnp.where(low_half(mixed.shape), mixed.astype(F32) * SCALE, 0.0).astype(BF16)
    return dot_nt(query, mixed)


def softmax_turned(scores):
    shape = scores.shape
    seen = iota(shape, 0) <= iota(shape, 1)
    scores = jnp.where(seen, scores, -jnp.inf)
    raised = jnp.exp(scores - jnp.max(scores, axis=0, keepdims=True))
    return raised * (1.0 / jnp.sum(raised, axis=0, keepdims=True))


def for_each_cluster(counts_ref, me_ref, place_ref, owners, per_group, body):
    for source in range(owners):
        place_ref[source] = 0

    def step(cluster, block):
        runs = []
        total = 0
        base = block * BLOCK_ROWS
        for source in range(owners):
            count = counts_ref[source, me_ref[3] + cluster]
            start = place_ref[source]
            runs.append((source, start, base + total))
            place_ref[source] = start + count
            total = total + count
        body(cluster, block, runs, base + total)
        return block + lax.shift_right_logical(total + (BLOCK_ROWS - 1), jnp.int32(7))

    return lax.fori_loop(0, per_group, step, jnp.int32(LEAD * UNROLL))


def gather_blocks(counts_ref, me_ref, place_ref, owners, per_group, slot_rows, wide_ref, block_ref):
    def body(cluster, block, runs, end):
        for source, start, row in runs:
            block_ref[pl.ds(row, slot_rows), :] = wide_ref[source, pl.ds(start, slot_rows), :]
        block_ref[pl.ds(end, BLOCK_ROWS), :] = jnp.zeros((BLOCK_ROWS, LANES), F32)

    blocks = for_each_cluster(counts_ref, me_ref, place_ref, owners, per_group, body)
    spare = pl.ds(pl.multiple_of(blocks * BLOCK_ROWS, BLOCK_ROWS), GROUP_ROWS)
    block_ref[spare, :] = jnp.zeros((GROUP_ROWS, LANES), F32)
    return blocks


def for_each_group(blocks, stages):
    first, second, third = stages
    groups = lax.div(blocks + (UNROLL - 1), jnp.int32(UNROLL))

    def step(i, carry):
        for slot in range(2):
            group = LEAD + 2 * i + slot
            third(group - 2, slot)
            second(group - 1, 1 - slot)
            first(group, slot)
        return carry

    lax.fori_loop(0, lax.shift_right_logical(groups + 1, jnp.int32(1)), step, 0)


def block_rows(group, ahead):
    return pl.ds(pl.multiple_of((group * UNROLL + ahead) * BLOCK_ROWS, BLOCK_ROWS), BLOCK_ROWS)


def tile_rows(ahead):
    return slice(ahead * BLOCK_ROWS, (ahead + 1) * BLOCK_ROWS)


def value_grad_kernel(sizes, per_group, slot_rows, me_ref, *refs):
    owners = sizes[0] * sizes[1]
    mixed_refs, out_refs, rest = refs[:owners], refs[owners : 2 * owners], refs[2 * owners :]
    dense_ref, counts_out_ref, counts_ref, place_ref, wide_ref, block_ref, home_ref = rest[:7]
    score_refs, probs_refs = rest[7:9], rest[9:11]
    half = out_refs[0].shape[0]
    rows = 2 * half
    for ahead, mixed_ref in zip(steps_of(sizes), mixed_refs):
        source = source_of(me_ref, ahead, sizes)
        tail = mixed_ref[rows:, :].astype(F32).astype(jnp.int32)
        counts_out_ref[pl.ds(source, 1), :] = tail[:1, :]
        wide_ref[source, :rows, :] = mixed_ref[:rows, :].astype(F32)
        wide_ref[source, rows:, :] = jnp.zeros((slot_rows, LANES), F32)
    pltpu.sync_copy(counts_out_ref, counts_ref)
    blocks = gather_blocks(counts_ref, me_ref, place_ref, owners, per_group, slot_rows, wide_ref, block_ref)

    def first(group, slot):
        for ahead in range(UNROLL):
            where = block_rows(group, ahead)
            mixed = block_ref[where, :].astype(BF16)
            dense_ref[where, :] = mixed
            score_refs[slot][tile_rows(ahead), :] = score(mixed)

    def second(group, slot):
        for ahead in range(UNROLL):
            tile = tile_rows(ahead)
            probs_refs[slot][tile, :] = softmax_turned(score_refs[slot][tile, :]).astype(BF16)

    def third(group, slot):
        for ahead in range(UNROLL):
            where = block_rows(group, ahead)
            block_ref[where, :] = dot(probs_refs[slot][tile_rows(ahead), :], dense_ref[where, :])

    for_each_group(blocks, (first, second, third))

    def scatter(cluster, block, runs, end):
        for source, start, row in runs:
            wide_ref[source, pl.ds(start, slot_rows), :] = block_ref[pl.ds(row, slot_rows), :]

    for_each_cluster(counts_ref, me_ref, place_ref, owners, per_group, scatter)
    for ahead, out_ref in zip(steps_of(sizes), out_refs):
        source = owner_of(me_ref, ahead, sizes)
        up, down = wide_ref[source, :half, :], wide_ref[source, half:rows, :]
        out_ref[...] = jnp.where(low_half((half, LANES)), swap_halves(up), down).astype(BF16)


def query_grad_kernel(sizes, per_group, slot_rows, me_ref, counts_ref, dense_ref, *refs):
    owners = sizes[0] * sizes[1]
    value_refs, out_refs, rest = refs[:owners], refs[owners : 2 * owners], refs[2 * owners :]
    place_ref, wide_ref, block_ref, sums_ref, centroid_ref = rest[:5]
    score_refs, grad_probs_refs, both_refs = rest[5:7], rest[7:9], rest[9:11]
    half = value_refs[0].shape[0]
    rows = 2 * half
    for ahead, value_ref in zip(steps_of(sizes), value_refs):
        source = source_of(me_ref, ahead, sizes)
        value = value_ref[...].astype(F32)
        wide_ref[source, :half, :] = swap_halves(value)
        wide_ref[source, half:rows, :] = value
        wide_ref[source, rows:, :] = jnp.zeros((slot_rows, LANES), F32)
    blocks = gather_blocks(counts_ref, me_ref, place_ref, owners, per_group, slot_rows, wide_ref, block_ref)

    def first(group, slot):
        for ahead in range(UNROLL):
            where, tile = block_rows(group, ahead), tile_rows(ahead)
            mixed = dense_ref[where, :]
            value = block_ref[where, :].astype(BF16)
            cotan = jnp.where(low_half(mixed.shape), jnp.zeros_like(mixed), mixed)
            score_refs[slot][tile, :] = score(mixed)
            grad_probs_refs[slot][tile, :] = dot_nt(value, cotan)

    def second(group, slot):
        for ahead in range(UNROLL):
            tile = tile_rows(ahead)
            probs = softmax_turned(score_refs[slot][tile, :])
            grad_probs = grad_probs_refs[slot][tile, :]
            probs_half = probs.astype(BF16).astype(F32)
            row_dot = jnp.sum(probs_half * grad_probs, axis=0, keepdims=True)
            grad_scores = (probs * (grad_probs - row_dot)).astype(BF16).astype(F32)
            both_refs[slot][tile, :] = (grad_scores + grad_scores.T).astype(BF16)

    def third(group, slot):
        for ahead in range(UNROLL):
            where = block_rows(group, ahead)
            grad = dot(both_refs[slot][tile_rows(ahead), :], dense_ref[where, :]) * SCALE
            grad = grad.astype(BF16).astype(F32)
            block_ref[where, :] = grad
            sums_ref[pl.ds(group * UNROLL + ahead, 1), :] = jnp.sum(grad, axis=0, keepdims=True)

    for_each_group(blocks, (first, second, third))
    most = (owners * slot_rows + BLOCK_ROWS - 1) // BLOCK_ROWS

    def scatter(cluster, block, runs, end):
        total = jnp.zeros((1, LANES), F32)
        for ahead in range(most):
            here = block + ahead
            total = total + jnp.where(here * BLOCK_ROWS < end, sums_ref[pl.ds(here, 1), :], 0.0)
        centroid_ref[pl.ds(cluster, 1), :] = total
        for source, start, row in runs:
            wide_ref[source, pl.ds(start, slot_rows), :] = block_ref[pl.ds(row, slot_rows), :]

    for_each_cluster(counts_ref, me_ref, place_ref, owners, per_group, scatter)
    extra = out_refs[0].shape[0] - half
    centroid = jnp.where(
        low_half((extra, LANES)), centroid_ref[:extra, :], swap_halves(centroid_ref[extra:, :])
    ).astype(BF16)
    for ahead, out_ref in zip(steps_of(sizes), out_refs):
        source = owner_of(me_ref, ahead, sizes)
        up, down = wide_ref[source, :half, :], wide_ref[source, half:rows, :]
        out_ref[:half, :] = jnp.where(low_half((half, LANES)), up, swap_halves(down)).astype(BF16)
        out_ref[half:, :] = centroid


def unfold(home_ref, out_ref, heads, start, half, finish):
    low = low_half((half, LANES))
    for group in range(home_ref.shape[0] // heads):
        first = group * 2 * half
        for pair in range(heads // 2):
            even = home_ref[group * heads + 2 * pair, start : start + half, :].astype(F32)
            odd = home_ref[group * heads + 2 * pair + 1, start : start + half, :].astype(F32)
            columns = slice(pair * LANES, (pair + 1) * LANES)
            out_ref[first : first + half, columns] = finish(jnp.where(low, even, swap_halves(odd)))
            out_ref[first + half : first + 2 * half, columns] = finish(
                jnp.where(low, swap_halves(even), odd)
            )


def to_half(x):
    return x.astype(BF16)


def bring_home(sizes, heads, me_ref, part_refs, unsort_ref, home_ref, sorted_ref, rows_ref):
    for ahead, part_ref in zip(steps_of(sizes), part_refs):
        home_ref[source_of(me_ref, ahead, sizes)] = part_ref[...]
    half = sorted_ref.shape[0] * heads // (sizes[0] * sizes[1]) // 2
    unfold(home_ref, sorted_ref, heads, 0, half, to_half)
    toks = rows_ref.shape[0]
    step = min(512, toks)

    @pl.loop(0, toks // step)
    def _(i):
        where = pl.ds(pl.multiple_of(i * step, step), step)
        rows_ref[where, :] = dot(unsort_ref[where, :], sorted_ref[...]).astype(BF16)


def weight_partial(sizes, me_ref, turned_ref, rows_ref, whole_ref, sub_refs):
    width = turned_ref.shape[0]
    step = min(512, width)

    @pl.loop(0, width // step)
    def _(i):
        where = pl.ds(pl.multiple_of(i * step, step), step)
        whole_ref[where, :] = dot(turned_ref[where, :], rows_ref[...]).astype(BF16)

    piece = width // (sizes[0] * sizes[1])
    for ahead, sub_ref in enumerate(sub_refs):
        sub = lax.rem(me_ref[1] + ahead, jnp.int32(sizes[1]))
        for seq in range(sizes[0]):
            first = pl.multiple_of((seq * sizes[1] + sub) * piece, piece)
            sub_ref[seq] = whole_ref[pl.ds(first, piece), :]


def value_home_kernel(sizes, heads, me_ref, turned_ref, unsort_ref, *refs):
    part_refs, rows_ref, sub_refs = refs[: -4 - sizes[1]], refs[-4 - sizes[1]], refs[-3 - sizes[1] : -3]
    home_ref, sorted_ref, whole_ref = refs[-3:]
    bring_home(sizes, heads, me_ref, part_refs, unsort_ref, home_ref, sorted_ref, rows_ref)
    weight_partial(sizes, me_ref, turned_ref, rows_ref, whole_ref, sub_refs)


def query_home_kernel(
    sizes, heads, factor, parts, me_ref, unsort_ref, value_rows_ref, w_query_ref, w_value_ref, *refs
):
    part_refs, out_refs, (rows_ref, centroid_ref, home_ref, sorted_ref) = (
        refs[: -4 - parts],
        refs[-4 - parts : -4],
        refs[-4:],
    )
    bring_home(sizes, heads, me_ref, part_refs, unsort_ref, home_ref, sorted_ref, rows_ref)
    half = sorted_ref.shape[0] * heads // (sizes[0] * sizes[1]) // 2
    unfold(home_ref, centroid_ref, heads, half, home_ref.shape[1] - half, lambda x: x * factor)
    toks = rows_ref.shape[0]
    columns = w_query_ref.shape[0] // parts
    step = min(512, toks)
    for ahead, out_ref in enumerate(out_refs):
        dest = lax.rem(me_ref[2] + ahead, jnp.int32(parts))
        mine = pl.ds(pl.multiple_of(dest * columns, columns), columns)

        @pl.loop(0, toks // step)
        def _(i):
            where = pl.ds(pl.multiple_of(i * step, step), step)
            total = dot_nt(rows_ref[where, :], w_query_ref[mine, :])
            total = total + dot_nt(value_rows_ref[where, :], w_value_ref[mine, :])
            out_ref[where, :] = total.astype(BF16)


def query_weight_kernel(sizes, me_ref, turned_ref, rows_ref, *refs):
    weight_partial(sizes, me_ref, turned_ref, rows_ref, refs[-1], refs[:-1])


def fold_subs_kernel(me_ref, *refs):
    seqs = refs[0].shape[0]
    terms, out_refs = refs[:-seqs], refs[-seqs:]
    for ahead, out_ref in enumerate(out_refs):
        seq = lax.rem(me_ref[0] + ahead, jnp.int32(seqs))
        total = terms[0][seq].astype(F32)
        for term in terms[1:]:
            total = total + term[seq].astype(F32)
        out_ref[...] = total.astype(BF16)


def sum_kernel(*refs):
    total = refs[0][...].astype(F32)
    for ref in refs[1:-1]:
        total = total + ref[...].astype(F32)
    refs[-1][...] = total.astype(refs[-1].dtype)


def call(kernel, outs, inputs, smem=(0,), scratch=(), flops=0, vmem=24, name=None):
    specs = [
        pl.BlockSpec(memory_space=pltpu.SMEM if i in smem else pltpu.VMEM) for i in range(len(inputs))
    ]
    moved = sum(x.size * x.dtype.itemsize for x in inputs) + sum(
        x.size * x.dtype.itemsize for x in jax.tree.leaves(outs)
    )
    return pl.pallas_call(
        kernel,
        out_shape=outs,
        in_specs=specs,
        out_specs=jax.tree.map(lambda _: pl.BlockSpec(memory_space=pltpu.VMEM), outs),
        scratch_shapes=list(scratch),
        compiler_params=pltpu.CompilerParams(vmem_limit_bytes=vmem * 2**20),
        cost_estimate=pl.CostEstimate(flops=flops, bytes_accessed=moved, transcendentals=0),
        name=name,
    )(*inputs)


def exchange(parts, sizes):
    out = []
    for ahead, part in zip(steps_of(sizes), parts):
        moves = [
            (
                seq * sizes[1] + sub,
                (seq + ahead[0]) % sizes[0] * sizes[1] + (sub + ahead[1]) % sizes[1],
            )
            for seq, sub in steps_of(sizes)
        ]
        out.append(part if ahead == (0, 0) else lax.ppermute(part, OWNERS, moves))
    return out


def shift(part, axis, ahead):
    size = lax.axis_size(axis)
    return lax.ppermute(part, axis, [(i, (i + ahead) % size) for i in range(size)])


def pass_round(parts, axis):
    return [parts[0]] + [shift(parts[ahead], axis, ahead) for ahead in range(1, len(parts))]


def fold_subs(me, by_sub, name):
    seqs, piece, columns = by_sub[0].shape
    return call(
        fold_subs_kernel,
        (jax.ShapeDtypeStruct((piece, columns), BF16),) * seqs,
        (me, *pass_round(by_sub, "sub")),
        name=name,
    )


def add_up(terms, dtype, name):
    return call(sum_kernel, jax.ShapeDtypeStruct(terms[0].shape, dtype), tuple(terms), smem=(), name=name)


def on_device(tokens_in, w_query, w_value, cotangent, assignment):
    sizes = (lax.axis_size("seq"), lax.axis_size("sub"))
    owners = sizes[0] * sizes[1]
    parts = lax.axis_size("head")
    toks, width = tokens_in.shape
    width_dev = cotangent.shape[1]
    heads = width_dev // HD
    slot_rows = 2 * toks // CLUSTERS
    assert owners % heads == 0 and heads % 2 == 0
    groups = owners // heads
    per_group = CLUSTERS // groups
    rows = toks if groups == 1 else per_group * slot_rows
    half = rows // 2
    slots = groups * rows
    columns = width // parts
    capacity = (slot_rows * owners + BLOCK_ROWS - 1) // BLOCK_ROWS * BLOCK_ROWS
    extra = max(per_group // 2, 16)
    shape = jax.ShapeDtypeStruct
    seq, sub = lax.axis_index("seq"), lax.axis_index("sub")
    first = lax.div(seq * sizes[1] + sub, jnp.int32(heads)) * per_group
    me = jnp.stack([seq, sub, lax.axis_index("head"), first]).astype(jnp.int32)

    def several(count, *dims):
        return (shape(dims, BF16),) * count

    *send_mixed, slot_row = call(
        functools.partial(project_query_kernel, sizes, groups, rows),
        several(owners, rows + COUNT_ROWS, LANES) + (shape((1, toks), jnp.int32),),
        (me, assignment.reshape(1, toks), tokens_in, w_query, cotangent),
        scratch=[pltpu.VMEM((toks, 2 * width_dev), BF16), pltpu.VMEM((owners, rows + COUNT_ROWS, LANES), BF16)],
        flops=2 * toks * width * width_dev + 4 * slots * toks * width_dev,
        name="project_query",
    )
    got_mixed = exchange(send_mixed, sizes)
    *send_value, turned, unsort = call(
        functools.partial(project_value_kernel, sizes, groups, rows),
        several(owners, half, LANES) + several(1, width, toks) + several(1, toks, slots),
        (me, slot_row, tokens_in, w_value),
        scratch=[pltpu.VMEM((toks, width_dev), BF16), pltpu.VMEM((owners, half, LANES), BF16)],
        flops=2 * toks * width * width_dev + 2 * slots * toks * width_dev,
        name="project_value",
    )
    got_value = exchange(send_value, sizes)
    blocks = per_group * capacity // BLOCK_ROWS
    held = blocks + (LEAD + 4) * UNROLL
    block_flops = 2 * BLOCK_ROWS * BLOCK_ROWS * LANES
    tall = pltpu.VMEM((owners, rows + slot_rows, LANES), F32)
    dense_rows = pltpu.VMEM((held * BLOCK_ROWS, LANES), F32)
    group_f32 = pltpu.VMEM((GROUP_ROWS, BLOCK_ROWS), F32)
    group_b16 = pltpu.VMEM((GROUP_ROWS, BLOCK_ROWS), BF16)
    place = pltpu.SMEM((owners,), jnp.int32)
    *back_value, dense, counts = call(
        functools.partial(value_grad_kernel, sizes, per_group, slot_rows),
        several(owners, half, LANES)
        + several(1, held * BLOCK_ROWS, LANES)
        + (shape((owners, LANES), jnp.int32),),
        (me, *got_mixed),
        scratch=[pltpu.SMEM((owners, LANES), jnp.int32), place, tall, dense_rows, tall]
        + [group_f32] * 2
        + [group_b16] * 2,
        flops=4 * blocks * block_flops,
        vmem=48,
        name="value_grad",
    )
    home_value = exchange(back_value, sizes)
    back_query = call(
        functools.partial(query_grad_kernel, sizes, per_group, slot_rows),
        several(owners, half + extra, LANES),
        (me, counts, dense, *got_value),
        smem=(0, 1),
        scratch=[place, tall, dense_rows, pltpu.VMEM((held, LANES), F32), pltpu.VMEM((2 * extra, LANES), F32)]
        + [group_f32] * 4
        + [group_b16] * 2,
        flops=6 * blocks * block_flops,
        vmem=48,
        name="query_grad",
    )
    home_query = exchange(back_query, sizes)
    weight_flops = 2 * toks * width * width_dev
    home_flops = 2 * slots * toks * width_dev
    sub_shapes = several(sizes[1], sizes[0], width // owners, width_dev)
    whole = pltpu.VMEM((width, width_dev), BF16)
    sorted_rows = pltpu.VMEM((slots, width_dev), BF16)
    value_rows, *value_weight = call(
        functools.partial(value_home_kernel, sizes, heads),
        several(1, toks, width_dev) + sub_shapes,
        (me, turned, unsort, *home_value),
        scratch=[pltpu.VMEM((owners, half, LANES), BF16), sorted_rows, whole],
        flops=weight_flops + home_flops,
        name="value_home",
    )
    value_weight = fold_subs(me, value_weight, "value_subs")
    *partials, query_rows, centroid_grad = call(
        functools.partial(query_home_kernel, sizes, heads, (CLUSTERS / (toks * owners)) ** 0.5, parts),
        several(parts, toks, columns)
        + several(1, toks, width_dev)
        + (shape((groups * 2 * extra, width_dev), F32),),
        (me, unsort, value_rows, w_query, w_value, *home_query),
        scratch=[pltpu.VMEM((owners, half + extra, LANES), BF16), sorted_rows],
        flops=2 * weight_flops + home_flops,
        name="query_home",
    )
    arrived = pass_round(partials, "head")
    value_weight, _ = lax.optimization_barrier((value_weight, home_query))
    value_weight = pass_round(value_weight, "seq")
    query_weight = call(
        functools.partial(query_weight_kernel, sizes),
        sub_shapes,
        (me, turned, query_rows),
        scratch=[whole],
        flops=weight_flops,
        name="query_weight",
    )
    query_weight = pass_round(fold_subs(me, query_weight, "query_subs"), "seq")
    grad_wv = add_up(value_weight, F32, "value_sum")
    grad_wq = add_up(query_weight, F32, "query_sum")
    grad_input = add_up(arrived, BF16, "input_sum")
    if groups > 1:
        centroid_grad = centroid_grad.reshape(groups, 2 * extra, width_dev)[:, :per_group]
        centroid_grad = centroid_grad.reshape(CLUSTERS, width_dev)
    return (grad_input, grad_wq, grad_wv, centroid_grad)


def solution(mesh):
    return jax.shard_map(
        on_device,
        mesh=mesh,
        in_specs=(
            P(("grp", "seq", "sub"), None),
            P(None, "head"),
            P(None, "head"),
            P(("grp", "seq", "sub"), "head"),
            P(("grp", "seq", "sub"), None),
        ),
        out_specs=(
            P(("grp", "seq", "sub"), "head"),
            P(("grp", "seq", "sub"), "head"),
            P(("grp", "seq", "sub"), "head"),
            P("grp", "head"),
        ),
        check_vma=False,
    )
```

```python
import functools

import jax
import jax.numpy as jnp
from jax import lax
from jax.experimental import pallas as pl
from jax.experimental.pallas import tpu as pltpu
from jax.sharding import PartitionSpec as P

HD = 64
CLUSTERS = 64
BLOCK_ROWS = 128
LANES = 128
UNROLL = 4
COUNT_ROWS = 16
SCALE = 0.5 * HD ** (-0.5)
F32 = jnp.float32
BF16 = jnp.bfloat16
OWNERS = ("seq", "sub")
GROUP_ROWS = UNROLL * BLOCK_ROWS
LEAD = 2


def iota(shape, dim):
    return lax.broadcasted_iota(jnp.int32, shape, dim)


def low_half(shape):
    return iota(shape, 1) < HD


def swap_halves(tile):
    return pltpu.roll(tile, HD, 1)


def dot(a, b):
    return jnp.dot(a, b, preferred_element_type=F32)


def dot_nt(a, b):
    return lax.dot_general(a, b, (((1,), (1,)), ((), ())), preferred_element_type=F32)


def ones_where(condition):
    return jnp.where(condition, 1.0, 0.0).astype(BF16)


def owner_of(me_ref, ahead, sizes):
    seq = lax.rem(me_ref[0] + ahead[0], jnp.int32(sizes[0]))
    sub = lax.rem(me_ref[1] + ahead[1], jnp.int32(sizes[1]))
    return seq * sizes[1] + sub


def source_of(me_ref, ahead, sizes):
    return owner_of(me_ref, ((sizes[0] - ahead[0]) % sizes[0], (sizes[1] - ahead[1]) % sizes[1]), sizes)


def steps_of(sizes):
    return [(seq, sub) for seq in range(sizes[0]) for sub in range(sizes[1])]


def arrivals(sizes, me_ref, refs):
    seqs, subs = sizes
    for ahead in steps_of(sizes):
        if ahead[1] == 0:
            piece = refs[ahead[0]][me_ref[1]]
        else:
            piece = refs[seqs + ahead[1] - 1][ahead[0]]
        yield source_of(me_ref, ahead, sizes), piece


def swap_kernel(sizes, me_ref, *refs):
    for k, out_ref in enumerate(refs[sizes[0] :]):
        sub = lax.rem(me_ref[1] + (k + 1), jnp.int32(sizes[1]))
        for seq in range(sizes[0]):
            out_ref[seq] = refs[seq][sub]


def project_query_kernel(sizes, groups, rows, me_ref, assign_ref, tokens_hbm, weight_hbm, cotan_hbm, *rest):
    out_refs, rest = rest[:-8], rest[-8:]
    slot_ref, tokens_ref, weight_ref, cotan_ref, mixed_ref, sorted_ref, in_sems, out_sems = rest
    toks = tokens_ref.shape[0]
    step = min(512, toks)
    load_weight = pltpu.make_async_copy(weight_hbm, weight_ref, in_sems.at[0])
    load_weight.start()

    def load(i):
        where = pl.ds(i * step, step)
        return (
            pltpu.make_async_copy(tokens_hbm.at[where, :], tokens_ref.at[where, :], in_sems.at[1 + 2 * i]),
            pltpu.make_async_copy(cotan_hbm.at[where, :], cotan_ref.at[where, :], in_sems.at[2 + 2 * i]),
        )

    for i in range(toks // step):
        for copy in load(i):
            copy.start()
    per_group = CLUSTERS // groups
    heads = weight_ref.shape[1] // HD
    member = iota((CLUSTERS, toks), 0) == assign_ref[...]
    member_f = jnp.where(member, 1.0, 0.0)
    member_b = member_f.astype(BF16)
    upto = ones_where(iota((toks, toks), 0) <= iota((toks, toks), 1))
    running = dot(member_b, upto)
    counts = jnp.broadcast_to(jnp.sum(member_f, axis=1, keepdims=True), (CLUSTERS, LANES))
    here, other = iota((CLUSTERS, CLUSTERS), 0), iota((CLUSTERS, CLUSTERS), 1)
    group_of = lambda index: lax.div(index, jnp.int32(per_group))
    earlier = ones_where((other < here) & (group_of(other) == group_of(here)))
    base = dot(earlier, counts.astype(BF16))[:, :1]
    base = base + (group_of(iota((CLUSTERS, 1), 0)) * rows).astype(F32)
    slot = jnp.sum(member_f * (running - 1.0 + base), axis=0, keepdims=True).astype(jnp.int32)
    slot_ref[...] = slot
    spread = jnp.concatenate([member_b, jnp.zeros((LANES - CLUSTERS, toks), BF16)], axis=0)
    tallies = dot_nt(jnp.ones((COUNT_ROWS, toks), BF16), spread).astype(BF16)
    for owner in range(sorted_ref.shape[0]):
        sorted_ref[owner, rows:, :] = tallies

    load_weight.wait()
    for i in range(toks // step):
        for copy in load(i):
            copy.wait()
        where = slice(i * step, (i + 1) * step)
        query = dot(tokens_ref[where, :], weight_ref[...])
        cotan = cotan_ref[where, :].astype(F32)
        low = low_half((step, LANES))
        for pair in range(heads // 2):
            q_tile = query[:, pair * LANES : (pair + 1) * LANES]
            c_tile = cotan[:, pair * LANES : (pair + 1) * LANES]
            even = jnp.where(low, q_tile, swap_halves(c_tile)).astype(BF16)
            odd = jnp.where(low, swap_halves(q_tile), c_tile).astype(BF16)
            mixed_ref[where, 2 * pair * LANES : (2 * pair + 1) * LANES] = even
            mixed_ref[where, (2 * pair + 1) * LANES : (2 * pair + 2) * LANES] = odd

    part = min(512, rows)
    pieces = rows // part

    @pl.loop(0, groups * pieces)
    def _(i):
        group, piece = lax.div(i, jnp.int32(pieces)), lax.rem(i, jnp.int32(pieces))
        first = pl.multiple_of(piece * part, part)
        pick = ones_where(iota((part, toks), 0) + i * part == slot_ref[...])
        sorted_rows = dot(pick, mixed_ref[...]).astype(BF16)
        for head in range(heads):
            sorted_ref[group * heads + head, pl.ds(first, part), :] = sorted_rows[
                :, head * LANES : (head + 1) * LANES
            ]

    copies = [
        pltpu.make_async_copy(sorted_ref.at[owner_of(me_ref, ahead, sizes)], out_ref, out_sems.at[k])
        for k, (ahead, out_ref) in enumerate(zip(steps_of(sizes), out_refs))
    ]
    for copy in copies:
        copy.start()
    for copy in copies:
        copy.wait()


def project_value_kernel(sizes, groups, rows, me_ref, slot_ref, tokens_ref, weight_ref, *rest):
    out_refs, (turned_ref, unsort_ref, value_ref, sorted_ref) = rest[:-4], rest[-4:]
    toks = tokens_ref.shape[0]
    heads = weight_ref.shape[1] // HD
    step = min(512, toks)

    @pl.loop(0, toks // step)
    def _(i):
        where = pl.ds(pl.multiple_of(i * step, step), step)
        value_ref[where, :] = dot(tokens_ref[where, :], weight_ref[...]).astype(BF16)

    half = rows // 2
    part = min(256, half)
    pieces = half // part

    @pl.loop(0, groups * pieces)
    def _(i):
        group, piece = lax.div(i, jnp.int32(pieces)), lax.rem(i, jnp.int32(pieces))
        first = pl.multiple_of(piece * part, part)
        index = iota((part, toks), 0) + group * rows + first
        upper = dot(ones_where(index == slot_ref[...]), value_ref[...])
        lower = dot(ones_where(index + half == slot_ref[...]), value_ref[...])
        low = low_half((part, LANES))
        for pair in range(heads // 2):
            up = upper[:, pair * LANES : (pair + 1) * LANES]
            down = lower[:, pair * LANES : (pair + 1) * LANES]
            even = jnp.where(low, up, swap_halves(down)).astype(BF16)
            odd = jnp.where(low, swap_halves(up), down).astype(BF16)
            sorted_ref[group * heads + 2 * pair, pl.ds(first, part), :] = even
            sorted_ref[group * heads + 2 * pair + 1, pl.ds(first, part), :] = odd

    for ahead, out_ref in enumerate(out_refs):
        for sub in range(sizes[1]):
            out_ref[sub] = sorted_ref[owner_of(me_ref, (ahead, 0), sizes) - me_ref[1] + sub]
    turned_ref[...] = tokens_ref[...].T
    slots = unsort_ref.shape[1]
    part = min(256, slots)
    for i in range(slots // part):
        pick = ones_where(iota((part, toks), 0) + i * part == slot_ref[...])
        unsort_ref[:, i * part : (i + 1) * part] = pick.T


def score(mixed):
    query = jnp.where(low_half(mixed.shape), mixed.astype(F32) * SCALE, 0.0).astype(BF16)
    return dot_nt(query, mixed)


def softmax_turned(scores):
    shape = scores.shape
    seen = iota(shape, 0) <= iota(shape, 1)
    scores = jnp.where(seen, scores, -jnp.inf)
    raised = jnp.exp(scores - jnp.max(scores, axis=0, keepdims=True))
    return raised * (1.0 / jnp.sum(raised, axis=0, keepdims=True))


def for_each_cluster(counts_ref, me_ref, place_ref, owners, per_group, body):
    for source in range(owners):
        place_ref[source] = 0

    def step(cluster, block):
        runs = []
        total = 0
        base = block * BLOCK_ROWS
        for source in range(owners):
            count = counts_ref[source, me_ref[3] + cluster]
            start = place_ref[source]
            runs.append((source, start, base + total))
            place_ref[source] = start + count
            total = total + count
        body(cluster, block, runs, base + total)
        return block + lax.shift_right_logical(total + (BLOCK_ROWS - 1), jnp.int32(7))

    return lax.fori_loop(0, per_group, step, jnp.int32(LEAD * UNROLL))


def gather_blocks(counts_ref, me_ref, place_ref, owners, per_group, slot_rows, wide_ref, block_ref):
    def body(cluster, block, runs, end):
        for source, start, row in runs:
            block_ref[pl.ds(row, slot_rows), :] = wide_ref[source, pl.ds(start, slot_rows), :]
        block_ref[pl.ds(end, BLOCK_ROWS), :] = jnp.zeros((BLOCK_ROWS, LANES), F32)

    blocks = for_each_cluster(counts_ref, me_ref, place_ref, owners, per_group, body)
    spare = pl.ds(pl.multiple_of(blocks * BLOCK_ROWS, BLOCK_ROWS), GROUP_ROWS)
    block_ref[spare, :] = jnp.zeros((GROUP_ROWS, LANES), F32)
    return blocks


def for_each_group(blocks, stages):
    first, second, third = stages
    groups = lax.div(blocks + (UNROLL - 1), jnp.int32(UNROLL))

    def step(i, carry):
        for slot in range(2):
            group = LEAD + 2 * i + slot
            third(group - 2, slot)
            second(group - 1, 1 - slot)
            first(group, slot)
        return carry

    lax.fori_loop(0, lax.shift_right_logical(groups + 1, jnp.int32(1)), step, 0)


def block_rows(group, ahead):
    return pl.ds(pl.multiple_of((group * UNROLL + ahead) * BLOCK_ROWS, BLOCK_ROWS), BLOCK_ROWS)


def tile_rows(ahead):
    return slice(ahead * BLOCK_ROWS, (ahead + 1) * BLOCK_ROWS)


def value_grad_kernel(sizes, per_group, slot_rows, me_ref, *refs):
    owners = sizes[0] * sizes[1]
    mixed_refs, out_refs, rest = refs[:owners], refs[owners : owners + sizes[0]], refs[owners + sizes[0] :]
    dense_ref, counts_out_ref, counts_ref, place_ref, wide_ref, block_ref, home_ref = rest[:7]
    score_refs, probs_refs = rest[7:9], rest[9:11]
    half = out_refs[0].shape[1]
    rows = 2 * half
    for ahead, mixed_ref in zip(steps_of(sizes), mixed_refs):
        source = source_of(me_ref, ahead, sizes)
        tail = mixed_ref[rows:, :].astype(F32).astype(jnp.int32)
        counts_out_ref[pl.ds(source, 1), :] = tail[:1, :]
        wide_ref[source, :rows, :] = mixed_ref[:rows, :].astype(F32)
        wide_ref[source, rows:, :] = jnp.zeros((slot_rows, LANES), F32)
    pltpu.sync_copy(counts_out_ref, counts_ref)
    blocks = gather_blocks(counts_ref, me_ref, place_ref, owners, per_group, slot_rows, wide_ref, block_ref)

    def first(group, slot):
        for ahead in range(UNROLL):
            where = block_rows(group, ahead)
            mixed = block_ref[where, :].astype(BF16)
            dense_ref[where, :] = mixed
            score_refs[slot][tile_rows(ahead), :] = score(mixed)

    def second(group, slot):
        for ahead in range(UNROLL):
            tile = tile_rows(ahead)
            probs_refs[slot][tile, :] = softmax_turned(score_refs[slot][tile, :]).astype(BF16)

    def third(group, slot):
        for ahead in range(UNROLL):
            where = block_rows(group, ahead)
            block_ref[where, :] = dot(probs_refs[slot][tile_rows(ahead), :], dense_ref[where, :])

    for_each_group(blocks, (first, second, third))

    def scatter(cluster, block, runs, end):
        for source, start, row in runs:
            wide_ref[source, pl.ds(start, slot_rows), :] = block_ref[pl.ds(row, slot_rows), :]

    for_each_cluster(counts_ref, me_ref, place_ref, owners, per_group, scatter)
    for ahead, out_ref in enumerate(out_refs):
        for sub in range(sizes[1]):
            source = owner_of(me_ref, (ahead, 0), sizes) - me_ref[1] + sub
            up, down = wide_ref[source, :half, :], wide_ref[source, half:rows, :]
            out_ref[sub] = jnp.where(low_half((half, LANES)), swap_halves(up), down).astype(BF16)


def query_grad_kernel(sizes, per_group, slot_rows, me_ref, counts_ref, dense_ref, *refs):
    owners = sizes[0] * sizes[1]
    values = sizes[0] + sizes[1] - 1
    value_refs, out_refs, rest = refs[:values], refs[values : values + owners], refs[values + owners :]
    place_ref, wide_ref, block_ref, sums_ref, centroid_ref = rest[:5]
    score_refs, grad_probs_refs, both_refs = rest[5:7], rest[7:9], rest[9:11]
    half = value_refs[0].shape[1]
    rows = 2 * half
    for source, value in arrivals(sizes, me_ref, value_refs):
        value = value.astype(F32)
        wide_ref[source, :half, :] = swap_halves(value)
        wide_ref[source, half:rows, :] = value
        wide_ref[source, rows:, :] = jnp.zeros((slot_rows, LANES), F32)
    blocks = gather_blocks(counts_ref, me_ref, place_ref, owners, per_group, slot_rows, wide_ref, block_ref)

    def first(group, slot):
        for ahead in range(UNROLL):
            where, tile = block_rows(group, ahead), tile_rows(ahead)
            mixed = dense_ref[where, :]
            value = block_ref[where, :].astype(BF16)
            cotan = jnp.where(low_half(mixed.shape), jnp.zeros_like(mixed), mixed)
            score_refs[slot][tile, :] = score(mixed)
            grad_probs_refs[slot][tile, :] = dot_nt(value, cotan)

    def second(group, slot):
        for ahead in range(UNROLL):
            tile = tile_rows(ahead)
            probs = softmax_turned(score_refs[slot][tile, :])
            grad_probs = grad_probs_refs[slot][tile, :]
            probs_half = probs.astype(BF16).astype(F32)
            row_dot = jnp.sum(probs_half * grad_probs, axis=0, keepdims=True)
            grad_scores = (probs * (grad_probs - row_dot)).astype(BF16).astype(F32)
            both_refs[slot][tile, :] = (grad_scores + grad_scores.T).astype(BF16)

    def third(group, slot):
        for ahead in range(UNROLL):
            where = block_rows(group, ahead)
            grad = dot(both_refs[slot][tile_rows(ahead), :], dense_ref[where, :]) * SCALE
            grad = grad.astype(BF16).astype(F32)
            block_ref[where, :] = grad
            sums_ref[pl.ds(group * UNROLL + ahead, 1), :] = jnp.sum(grad, axis=0, keepdims=True)

    for_each_group(blocks, (first, second, third))
    most = (owners * slot_rows + BLOCK_ROWS - 1) // BLOCK_ROWS

    def scatter(cluster, block, runs, end):
        total = jnp.zeros((1, LANES), F32)
        for ahead in range(most):
            here = block + ahead
            total = total + jnp.where(here * BLOCK_ROWS < end, sums_ref[pl.ds(here, 1), :], 0.0)
        centroid_ref[pl.ds(cluster, 1), :] = total
        for source, start, row in runs:
            wide_ref[source, pl.ds(start, slot_rows), :] = block_ref[pl.ds(row, slot_rows), :]

    for_each_cluster(counts_ref, me_ref, place_ref, owners, per_group, scatter)
    extra = out_refs[0].shape[0] - half
    centroid = jnp.where(
        low_half((extra, LANES)), centroid_ref[:extra, :], swap_halves(centroid_ref[extra:, :])
    ).astype(BF16)
    for ahead, out_ref in zip(steps_of(sizes), out_refs):
        source = owner_of(me_ref, ahead, sizes)
        up, down = wide_ref[source, :half, :], wide_ref[source, half:rows, :]
        out_ref[:half, :] = jnp.where(low_half((half, LANES)), up, swap_halves(down)).astype(BF16)
        out_ref[half:, :] = centroid


def unfold(home_ref, out_ref, heads, start, half, finish):
    low = low_half((half, LANES))
    for group in range(home_ref.shape[0] // heads):
        first = group * 2 * half
        for pair in range(heads // 2):
            even = home_ref[group * heads + 2 * pair, start : start + half, :].astype(F32)
            odd = home_ref[group * heads + 2 * pair + 1, start : start + half, :].astype(F32)
            columns = slice(pair * LANES, (pair + 1) * LANES)
            out_ref[first : first + half, columns] = finish(jnp.where(low, even, swap_halves(odd)))
            out_ref[first + half : first + 2 * half, columns] = finish(
                jnp.where(low, swap_halves(even), odd)
            )


def to_half(x):
    return x.astype(BF16)


def bring_home(sizes, heads, pieces, unsort_ref, home_ref, sorted_ref, rows_ref):
    for source, piece in pieces:
        home_ref[source] = piece
    half = sorted_ref.shape[0] * heads // (sizes[0] * sizes[1]) // 2
    unfold(home_ref, sorted_ref, heads, 0, half, to_half)
    toks = rows_ref.shape[0]
    step = min(512, toks)

    @pl.loop(0, toks // step)
    def _(i):
        where = pl.ds(pl.multiple_of(i * step, step), step)
        rows_ref[where, :] = dot(unsort_ref[where, :], sorted_ref[...]).astype(BF16)


def weight_partial(sizes, me_ref, turned_ref, rows_ref, whole_ref, sub_refs):
    width = turned_ref.shape[0]
    step = min(512, width)

    @pl.loop(0, width // step)
    def _(i):
        where = pl.ds(pl.multiple_of(i * step, step), step)
        whole_ref[where, :] = dot(turned_ref[where, :], rows_ref[...]).astype(BF16)

    piece = width // (sizes[0] * sizes[1])
    for ahead, sub_ref in enumerate(sub_refs):
        sub = lax.rem(me_ref[1] + ahead, jnp.int32(sizes[1]))
        for seq in range(sizes[0]):
            first = pl.multiple_of((seq * sizes[1] + sub) * piece, piece)
            sub_ref[seq] = whole_ref[pl.ds(first, piece), :]


def value_home_kernel(sizes, heads, me_ref, turned_ref, unsort_ref, *refs):
    part_refs, rows_ref, sub_refs = refs[: -4 - sizes[1]], refs[-4 - sizes[1]], refs[-3 - sizes[1] : -3]
    home_ref, sorted_ref, whole_ref = refs[-3:]
    pieces = arrivals(sizes, me_ref, part_refs)
    bring_home(sizes, heads, pieces, unsort_ref, home_ref, sorted_ref, rows_ref)
    weight_partial(sizes, me_ref, turned_ref, rows_ref, whole_ref, sub_refs)


def input_partial(me_ref, ahead, parts, rows_ref, value_rows_ref, w_query_ref, w_value_ref, out_ref):
    toks = rows_ref.shape[0]
    columns = w_query_ref.shape[0] // parts
    step = min(512, toks)
    dest = lax.rem(me_ref[2] + ahead, jnp.int32(parts))
    mine = pl.ds(pl.multiple_of(dest * columns, columns), columns)

    @pl.loop(0, toks // step)
    def _(i):
        where = pl.ds(pl.multiple_of(i * step, step), step)
        total = dot_nt(rows_ref[where, :], w_query_ref[mine, :])
        total = total + dot_nt(value_rows_ref[where, :], w_value_ref[mine, :])
        out_ref[where, :] = total.astype(BF16)


def query_home_kernel(
    sizes, heads, factor, parts, me_ref, unsort_ref, value_rows_ref, w_query_ref, w_value_ref, *refs
):
    part_refs, out_refs, (rows_ref, centroid_ref, home_ref, sorted_ref) = (
        refs[: -3 - parts],
        refs[-3 - parts : -4],
        refs[-4:],
    )
    pieces = [
        (source_of(me_ref, ahead, sizes), part_ref[...]) for ahead, part_ref in zip(steps_of(sizes), part_refs)
    ]
    bring_home(sizes, heads, pieces, unsort_ref, home_ref, sorted_ref, rows_ref)
    half = sorted_ref.shape[0] * heads // (sizes[0] * sizes[1]) // 2
    unfold(home_ref, centroid_ref, heads, half, home_ref.shape[1] - half, lambda x: x * factor)
    for ahead, out_ref in enumerate(out_refs):
        input_partial(me_ref, ahead + 1, parts, rows_ref, value_rows_ref, w_query_ref, w_value_ref, out_ref)


def query_weight_kernel(
    sizes, parts, me_ref, turned_ref, rows_ref, value_rows_ref, w_query_ref, w_value_ref, *refs
):
    sub_refs, out_ref, whole_ref = refs[:-2], refs[-2], refs[-1]
    weight_partial(sizes, me_ref, turned_ref, rows_ref, whole_ref, sub_refs)
    input_partial(me_ref, 0, parts, rows_ref, value_rows_ref, w_query_ref, w_value_ref, out_ref)


def fold_subs_kernel(me_ref, *refs):
    seqs = refs[0].shape[0]
    terms, out_refs = refs[:-seqs], refs[-seqs:]
    for ahead, out_ref in enumerate(out_refs):
        seq = lax.rem(me_ref[0] + ahead, jnp.int32(seqs))
        total = terms[0][seq].astype(F32)
        for term in terms[1:]:
            total = total + term[seq].astype(F32)
        out_ref[...] = total.astype(BF16)


def sum_kernel(*refs):
    total = refs[0][...].astype(F32)
    for ref in refs[1:-1]:
        total = total + ref[...].astype(F32)
    refs[-1][...] = total.astype(refs[-1].dtype)


def call(kernel, outs, inputs, smem=(0,), in_place=(), after=(), scratch=(), flops=0, vmem=24, name=None):
    def body(*refs):
        kernel(*refs[: len(inputs)], *refs[len(inputs) + len(after) :])

    def space(i):
        return pltpu.SMEM if i in smem else pl.ANY if i in in_place else pltpu.VMEM

    specs = [pl.BlockSpec(memory_space=space(i)) for i in range(len(inputs))]
    specs += [pl.BlockSpec(memory_space=pl.ANY)] * len(after)
    moved = sum(x.size * x.dtype.itemsize for x in inputs) + sum(
        x.size * x.dtype.itemsize for x in jax.tree.leaves(outs)
    )
    out_space = lambda x: pl.ANY if in_place and x.dtype == BF16 else pltpu.VMEM
    return pl.pallas_call(
        body,
        out_shape=outs,
        in_specs=specs,
        out_specs=jax.tree.map(lambda x: pl.BlockSpec(memory_space=out_space(x)), outs),
        scratch_shapes=list(scratch),
        compiler_params=pltpu.CompilerParams(vmem_limit_bytes=vmem * 2**20),
        cost_estimate=pl.CostEstimate(flops=flops, bytes_accessed=moved, transcendentals=0),
        name=name,
    )(*inputs, *after)


def exchange(parts, sizes):
    out = []
    for ahead, part in zip(steps_of(sizes), parts):
        moves = [
            (
                seq * sizes[1] + sub,
                (seq + ahead[0]) % sizes[0] * sizes[1] + (sub + ahead[1]) % sizes[1],
            )
            for seq, sub in steps_of(sizes)
        ]
        out.append(part if ahead == (0, 0) else lax.ppermute(part, OWNERS, moves))
    return out


def shift(part, axis, ahead):
    size = lax.axis_size(axis)
    return lax.ppermute(part, axis, [(i, (i + ahead) % size) for i in range(size)])


def pass_round(parts, axis):
    return [parts[0]] + [shift(parts[ahead], axis, ahead) for ahead in range(1, len(parts))]


def fold_subs(me, by_sub, name, after=()):
    seqs, piece, columns = by_sub[0].shape
    return call(
        fold_subs_kernel,
        (jax.ShapeDtypeStruct((piece, columns), BF16),) * seqs,
        (me, *pass_round(by_sub, "sub")),
        after=after,
        name=name,
    )


def exchange_by_chip(me, parts, sizes, name):
    came = pass_round(parts, "seq")
    swapped = call(
        functools.partial(swap_kernel, sizes),
        (jax.ShapeDtypeStruct((sizes[0], *parts[0].shape[1:]), BF16),) * (sizes[1] - 1),
        (me, *came),
        name=name,
    )
    return came + [shift(part, "sub", k + 1) for k, part in enumerate(swapped)]


def add_up(terms, dtype, name):
    return call(sum_kernel, jax.ShapeDtypeStruct(terms[0].shape, dtype), tuple(terms), smem=(), name=name)


def on_device(tokens_in, w_query, w_value, cotangent, assignment):
    sizes = (lax.axis_size("seq"), lax.axis_size("sub"))
    owners = sizes[0] * sizes[1]
    parts = lax.axis_size("head")
    toks, width = tokens_in.shape
    width_dev = cotangent.shape[1]
    heads = width_dev // HD
    slot_rows = 2 * toks // CLUSTERS
    assert owners % heads == 0 and heads % 2 == 0
    groups = owners // heads
    per_group = CLUSTERS // groups
    rows = toks if groups == 1 else per_group * slot_rows
    half = rows // 2
    slots = groups * rows
    columns = width // parts
    capacity = (slot_rows * owners + BLOCK_ROWS - 1) // BLOCK_ROWS * BLOCK_ROWS
    extra = max(per_group // 2, 16)
    shape = jax.ShapeDtypeStruct
    seq, sub = lax.axis_index("seq"), lax.axis_index("sub")
    first = lax.div(seq * sizes[1] + sub, jnp.int32(heads)) * per_group
    me = jnp.stack([seq, sub, lax.axis_index("head"), first]).astype(jnp.int32)

    def several(count, *dims):
        return (shape(dims, BF16),) * count

    *send_mixed, slot_row = call(
        functools.partial(project_query_kernel, sizes, groups, rows),
        several(owners, rows + COUNT_ROWS, LANES) + (shape((1, toks), jnp.int32),),
        (me, assignment.reshape(1, toks), tokens_in, w_query, cotangent),
        in_place=(2, 3, 4),
        scratch=[
            pltpu.VMEM((toks, width), BF16),
            pltpu.VMEM((width, width_dev), BF16),
            pltpu.VMEM((toks, width_dev), BF16),
            pltpu.VMEM((toks, 2 * width_dev), BF16),
            pltpu.VMEM((owners, rows + COUNT_ROWS, LANES), BF16),
            pltpu.SemaphoreType.DMA((1 + 2 * (toks // min(512, toks)),)),
            pltpu.SemaphoreType.DMA((owners,)),
        ],
        vmem=60,
        flops=2 * toks * width * width_dev + 4 * slots * toks * width_dev,
        name="project_query",
    )
    got_mixed = exchange(send_mixed, sizes)
    *send_value, turned, unsort = call(
        functools.partial(project_value_kernel, sizes, groups, rows),
        several(sizes[0], sizes[1], half, LANES) + several(1, width, toks) + several(1, toks, slots),
        (me, slot_row, tokens_in, w_value),
        scratch=[pltpu.VMEM((toks, width_dev), BF16), pltpu.VMEM((owners, half, LANES), BF16)],
        flops=2 * toks * width * width_dev + 2 * slots * toks * width_dev,
        name="project_value",
    )
    send_value, _ = lax.optimization_barrier((send_value, got_mixed[1:4]))
    got_value = exchange_by_chip(me, send_value, sizes, "swap_value")
    blocks = per_group * capacity // BLOCK_ROWS
    held = blocks + (LEAD + 4) * UNROLL
    block_flops = 2 * BLOCK_ROWS * BLOCK_ROWS * LANES
    tall = pltpu.VMEM((owners, rows + slot_rows, LANES), F32)
    dense_rows = pltpu.VMEM((held * BLOCK_ROWS, LANES), F32)
    group_f32 = pltpu.VMEM((GROUP_ROWS, BLOCK_ROWS), F32)
    group_b16 = pltpu.VMEM((GROUP_ROWS, BLOCK_ROWS), BF16)
    place = pltpu.SMEM((owners,), jnp.int32)
    *back_value, dense, counts = call(
        functools.partial(value_grad_kernel, sizes, per_group, slot_rows),
        several(sizes[0], sizes[1], half, LANES)
        + several(1, held * BLOCK_ROWS, LANES)
        + (shape((owners, LANES), jnp.int32),),
        (me, *got_mixed),
        scratch=[pltpu.SMEM((owners, LANES), jnp.int32), place, tall, dense_rows, tall]
        + [group_f32] * 2
        + [group_b16] * 2,
        flops=4 * blocks * block_flops,
        vmem=48,
        name="value_grad",
    )
    home_value = exchange_by_chip(me, back_value, sizes, "swap_value_grad")
    back_query = call(
        functools.partial(query_grad_kernel, sizes, per_group, slot_rows),
        several(owners, half + extra, LANES),
        (me, counts, dense, *got_value),
        smem=(0, 1),
        scratch=[place, tall, dense_rows, pltpu.VMEM((held, LANES), F32), pltpu.VMEM((2 * extra, LANES), F32)]
        + [group_f32] * 4
        + [group_b16] * 2,
        flops=6 * blocks * block_flops,
        vmem=48,
        name="query_grad",
    )
    home_query = exchange(back_query, sizes)
    weight_flops = 2 * toks * width * width_dev
    home_flops = 2 * slots * toks * width_dev
    sub_shapes = several(sizes[1], sizes[0], width // owners, width_dev)
    whole = pltpu.VMEM((width, width_dev), BF16)
    sorted_rows = pltpu.VMEM((slots, width_dev), BF16)
    value_rows, *value_weight = call(
        functools.partial(value_home_kernel, sizes, heads),
        several(1, toks, width_dev) + sub_shapes,
        (me, turned, unsort, *home_value),
        scratch=[pltpu.VMEM((owners, half, LANES), BF16), sorted_rows, whole],
        flops=weight_flops + home_flops,
        name="value_home",
    )
    value_weight = fold_subs(me, value_weight, "value_subs")
    *partials, query_rows, centroid_grad = call(
        functools.partial(query_home_kernel, sizes, heads, (CLUSTERS / (toks * owners)) ** 0.5, parts),
        several(parts - 1, toks, columns)
        + several(1, toks, width_dev)
        + (shape((groups * 2 * extra, width_dev), F32),),
        (me, unsort, value_rows, w_query, w_value, *home_query),
        after=value_weight,
        scratch=[pltpu.VMEM((owners, half + extra, LANES), BF16), sorted_rows],
        flops=weight_flops + home_flops,
        name="query_home",
    )
    arrived = [shift(partial, "head", k + 1) for k, partial in enumerate(partials)]
    value_weight, _ = lax.optimization_barrier((value_weight, home_query))
    value_weight = pass_round(value_weight, "seq")
    *query_weight, own = call(
        functools.partial(query_weight_kernel, sizes, parts),
        sub_shapes + several(1, toks, columns),
        (me, turned, query_rows, value_rows, w_query, w_value),
        after=value_weight[1:2],
        scratch=[whole],
        flops=2 * weight_flops,
        name="query_weight",
    )
    query_weight = pass_round(fold_subs(me, query_weight, "query_subs", value_weight[2:]), "seq")
    grad_wv = add_up(value_weight, F32, "value_sum")
    grad_wq = add_up(query_weight, F32, "query_sum")
    grad_input = add_up([own] + arrived, BF16, "input_sum")
    if groups > 1:
        centroid_grad = centroid_grad.reshape(groups, 2 * extra, width_dev)[:, :per_group]
        centroid_grad = centroid_grad.reshape(CLUSTERS, width_dev)
    return (grad_input, grad_wq, grad_wv, centroid_grad)


def solution(mesh):
    return jax.shard_map(
        on_device,
        mesh=mesh,
        in_specs=(
            P(("grp", "seq", "sub"), None),
            P(None, "head"),
            P(None, "head"),
            P(("grp", "seq", "sub"), "head"),
            P(("grp", "seq", "sub"), None),
        ),
        out_specs=(
            P(("grp", "seq", "sub"), "head"),
            P(("grp", "seq", "sub"), "head"),
            P(("grp", "seq", "sub"), "head"),
            P("grp", "head"),
        ),
        check_vma=False,
    )
```

```python
import functools

import jax
import jax.numpy as jnp
from jax import lax
from jax.experimental import pallas as pl
from jax.experimental.pallas import tpu as pltpu
from jax.sharding import PartitionSpec as P

HD = 64
CLUSTERS = 64
BLOCK_ROWS = 128
LANES = 128
UNROLL = 4
COUNT_ROWS = 16
SCALE = 0.5 * HD ** (-0.5)
F32 = jnp.float32
BF16 = jnp.bfloat16
OWNERS = ("seq", "sub")
GROUP_ROWS = UNROLL * BLOCK_ROWS
LEAD = 2


def iota(shape, dim):
    return lax.broadcasted_iota(jnp.int32, shape, dim)


def low_half(shape):
    return iota(shape, 1) < HD


def swap_halves(tile):
    return pltpu.roll(tile, HD, 1)


def dot(a, b):
    return jnp.dot(a, b, preferred_element_type=F32)


def dot_nt(a, b):
    return lax.dot_general(a, b, (((1,), (1,)), ((), ())), preferred_element_type=F32)


def ones_where(condition):
    return jnp.where(condition, 1.0, 0.0).astype(BF16)


def owner_of(me_ref, ahead, sizes):
    seq = lax.rem(me_ref[0] + ahead[0], jnp.int32(sizes[0]))
    sub = lax.rem(me_ref[1] + ahead[1], jnp.int32(sizes[1]))
    return seq * sizes[1] + sub


def source_of(me_ref, ahead, sizes):
    return owner_of(me_ref, ((sizes[0] - ahead[0]) % sizes[0], (sizes[1] - ahead[1]) % sizes[1]), sizes)


def steps_of(sizes):
    return [(seq, sub) for seq in range(sizes[0]) for sub in range(sizes[1])]


def arrivals(sizes, me_ref, refs):
    seqs, subs = sizes
    for ahead in steps_of(sizes):
        if ahead[1] == 0:
            piece = refs[ahead[0]][me_ref[1]]
        else:
            piece = refs[seqs + ahead[1] - 1][ahead[0]]
        yield source_of(me_ref, ahead, sizes), piece


def swap_kernel(sizes, me_ref, *refs):
    for k, out_ref in enumerate(refs[sizes[0] :]):
        sub = lax.rem(me_ref[1] + (k + 1), jnp.int32(sizes[1]))
        for seq in range(sizes[0]):
            out_ref[seq] = refs[seq][sub]


def project_query_kernel(sizes, groups, rows, me_ref, assign_ref, tokens_hbm, weight_hbm, cotan_hbm, *rest):
    out_refs, rest = rest[:-8], rest[-8:]
    slot_ref, tokens_ref, weight_ref, cotan_ref, mixed_ref, sorted_ref, in_sems, out_sems = rest
    toks = tokens_ref.shape[0]
    step = min(512, toks)
    fine = min(128, toks)

    def load(kind, first, last):
        source, target = ((weight_hbm, weight_ref), (tokens_hbm, tokens_ref), (cotan_hbm, cotan_ref))[kind]
        return [
            pltpu.make_async_copy(
                source.at[pl.ds(row, fine), :], target.at[pl.ds(row, fine), :], in_sems.at[kind, row // fine]
            )
            for row in range(first, last, fine)
        ]

    width = weight_ref.shape[0]
    for copy in load(0, 0, width) + load(1, 0, toks) + load(2, 0, toks):
        copy.start()
    per_group = CLUSTERS // groups
    heads = weight_ref.shape[1] // HD
    member = iota((CLUSTERS, toks), 0) == assign_ref[...]
    member_f = jnp.where(member, 1.0, 0.0)
    member_b = member_f.astype(BF16)
    upto = ones_where(iota((toks, toks), 0) <= iota((toks, toks), 1))
    running = dot(member_b, upto)
    counts = jnp.broadcast_to(jnp.sum(member_f, axis=1, keepdims=True), (CLUSTERS, LANES))
    here, other = iota((CLUSTERS, CLUSTERS), 0), iota((CLUSTERS, CLUSTERS), 1)
    group_of = lambda index: lax.div(index, jnp.int32(per_group))
    earlier = ones_where((other < here) & (group_of(other) == group_of(here)))
    base = dot(earlier, counts.astype(BF16))[:, :1]
    base = base + (group_of(iota((CLUSTERS, 1), 0)) * rows).astype(F32)
    slot = jnp.sum(member_f * (running - 1.0 + base), axis=0, keepdims=True).astype(jnp.int32)
    slot_ref[...] = slot
    spread = jnp.concatenate([member_b, jnp.zeros((LANES - CLUSTERS, toks), BF16)], axis=0)
    tallies = dot_nt(jnp.ones((COUNT_ROWS, toks), BF16), spread).astype(BF16)
    for owner in range(sorted_ref.shape[0]):
        sorted_ref[owner, rows:, :] = tallies

    for copy in load(0, 0, width):
        copy.wait()
    for i in range(toks // step):
        for copy in load(1, i * step, (i + 1) * step) + load(2, i * step, (i + 1) * step):
            copy.wait()
        where = slice(i * step, (i + 1) * step)
        query = dot(tokens_ref[where, :], weight_ref[...])
        cotan = cotan_ref[where, :].astype(F32)
        low = low_half((step, LANES))
        for pair in range(heads // 2):
            q_tile = query[:, pair * LANES : (pair + 1) * LANES]
            c_tile = cotan[:, pair * LANES : (pair + 1) * LANES]
            even = jnp.where(low, q_tile, swap_halves(c_tile)).astype(BF16)
            odd = jnp.where(low, swap_halves(q_tile), c_tile).astype(BF16)
            mixed_ref[where, 2 * pair * LANES : (2 * pair + 1) * LANES] = even
            mixed_ref[where, (2 * pair + 1) * LANES : (2 * pair + 2) * LANES] = odd

    part = min(512, rows)
    pieces = rows // part

    @pl.loop(0, groups * pieces)
    def _(i):
        group, piece = lax.div(i, jnp.int32(pieces)), lax.rem(i, jnp.int32(pieces))
        first = pl.multiple_of(piece * part, part)
        pick = ones_where(iota((part, toks), 0) + i * part == slot_ref[...])
        sorted_rows = dot(pick, mixed_ref[...]).astype(BF16)
        for head in range(heads):
            sorted_ref[group * heads + head, pl.ds(first, part), :] = sorted_rows[
                :, head * LANES : (head + 1) * LANES
            ]

    copies = [
        pltpu.make_async_copy(sorted_ref.at[owner_of(me_ref, ahead, sizes)], out_ref, out_sems.at[k])
        for k, (ahead, out_ref) in enumerate(zip(steps_of(sizes), out_refs))
    ]
    for copy in copies:
        copy.start()
    for copy in copies:
        copy.wait()


def project_value_kernel(sizes, groups, rows, me_ref, slot_ref, tokens_ref, weight_ref, *rest):
    out_refs, (turned_ref, unsort_ref, value_ref, sorted_ref) = rest[:-4], rest[-4:]
    toks = tokens_ref.shape[0]
    heads = weight_ref.shape[1] // HD
    step = min(512, toks)

    @pl.loop(0, toks // step)
    def _(i):
        where = pl.ds(pl.multiple_of(i * step, step), step)
        value_ref[where, :] = dot(tokens_ref[where, :], weight_ref[...]).astype(BF16)

    half = rows // 2
    part = min(256, half)
    pieces = half // part

    @pl.loop(0, groups * pieces)
    def _(i):
        group, piece = lax.div(i, jnp.int32(pieces)), lax.rem(i, jnp.int32(pieces))
        first = pl.multiple_of(piece * part, part)
        index = iota((part, toks), 0) + group * rows + first
        upper = dot(ones_where(index == slot_ref[...]), value_ref[...])
        lower = dot(ones_where(index + half == slot_ref[...]), value_ref[...])
        low = low_half((part, LANES))
        for pair in range(heads // 2):
            up = upper[:, pair * LANES : (pair + 1) * LANES]
            down = lower[:, pair * LANES : (pair + 1) * LANES]
            even = jnp.where(low, up, swap_halves(down)).astype(BF16)
            odd = jnp.where(low, swap_halves(up), down).astype(BF16)
            sorted_ref[group * heads + 2 * pair, pl.ds(first, part), :] = even
            sorted_ref[group * heads + 2 * pair + 1, pl.ds(first, part), :] = odd

    for ahead, out_ref in enumerate(out_refs):
        for sub in range(sizes[1]):
            out_ref[sub] = sorted_ref[owner_of(me_ref, (ahead, 0), sizes) - me_ref[1] + sub]
    turned_ref[...] = tokens_ref[...].T
    slots = unsort_ref.shape[1]
    part = min(256, slots)
    for i in range(slots // part):
        pick = ones_where(iota((part, toks), 0) + i * part == slot_ref[...])
        unsort_ref[:, i * part : (i + 1) * part] = pick.T


def score(mixed):
    query = jnp.where(low_half(mixed.shape), mixed.astype(F32) * SCALE, 0.0).astype(BF16)
    return dot_nt(query, mixed)


def softmax_turned(scores):
    shape = scores.shape
    seen = iota(shape, 0) <= iota(shape, 1)
    scores = jnp.where(seen, scores, -jnp.inf)
    raised = jnp.exp(scores - jnp.max(scores, axis=0, keepdims=True))
    return raised * (1.0 / jnp.sum(raised, axis=0, keepdims=True))


def for_each_cluster(counts_ref, me_ref, place_ref, owners, per_group, body):
    for source in range(owners):
        place_ref[source] = 0

    def step(cluster, block):
        runs = []
        total = 0
        base = block * BLOCK_ROWS
        for source in range(owners):
            count = counts_ref[source, me_ref[3] + cluster]
            start = place_ref[source]
            runs.append((source, start, base + total))
            place_ref[source] = start + count
            total = total + count
        body(cluster, block, runs, base + total)
        return block + lax.shift_right_logical(total + (BLOCK_ROWS - 1), jnp.int32(7))

    return lax.fori_loop(0, per_group, step, jnp.int32(LEAD * UNROLL))


def gather_blocks(counts_ref, me_ref, place_ref, owners, per_group, slot_rows, wide_ref, block_ref):
    def body(cluster, block, runs, end):
        for source, start, row in runs:
            block_ref[pl.ds(row, slot_rows), :] = wide_ref[source, pl.ds(start, slot_rows), :]
        block_ref[pl.ds(end, BLOCK_ROWS), :] = jnp.zeros((BLOCK_ROWS, LANES), F32)

    blocks = for_each_cluster(counts_ref, me_ref, place_ref, owners, per_group, body)
    spare = pl.ds(pl.multiple_of(blocks * BLOCK_ROWS, BLOCK_ROWS), GROUP_ROWS)
    block_ref[spare, :] = jnp.zeros((GROUP_ROWS, LANES), F32)
    return blocks


def for_each_group(blocks, stages):
    first, second, third = stages
    groups = lax.div(blocks + (UNROLL - 1), jnp.int32(UNROLL))

    def step(i, carry):
        for slot in range(2):
            group = LEAD + 2 * i + slot
            third(group - 2, slot)
            second(group - 1, 1 - slot)
            first(group, slot)
        return carry

    lax.fori_loop(0, lax.shift_right_logical(groups + 1, jnp.int32(1)), step, 0)


def block_rows(group, ahead):
    return pl.ds(pl.multiple_of((group * UNROLL + ahead) * BLOCK_ROWS, BLOCK_ROWS), BLOCK_ROWS)


def tile_rows(ahead):
    return slice(ahead * BLOCK_ROWS, (ahead + 1) * BLOCK_ROWS)


def value_grad_kernel(sizes, per_group, slot_rows, me_ref, *refs):
    owners = sizes[0] * sizes[1]
    mixed_refs, out_refs, rest = refs[:owners], refs[owners : owners + sizes[0]], refs[owners + sizes[0] :]
    dense_ref, counts_out_ref, counts_ref, place_ref, wide_ref, block_ref, home_ref = rest[:7]
    score_refs, probs_refs = rest[7:9], rest[9:11]
    half = out_refs[0].shape[1]
    rows = 2 * half
    for ahead, mixed_ref in zip(steps_of(sizes), mixed_refs):
        source = source_of(me_ref, ahead, sizes)
        tail = mixed_ref[rows:, :].astype(F32).astype(jnp.int32)
        counts_out_ref[pl.ds(source, 1), :] = tail[:1, :]
        wide_ref[source, :rows, :] = mixed_ref[:rows, :].astype(F32)
        wide_ref[source, rows:, :] = jnp.zeros((slot_rows, LANES), F32)
    pltpu.sync_copy(counts_out_ref, counts_ref)
    blocks = gather_blocks(counts_ref, me_ref, place_ref, owners, per_group, slot_rows, wide_ref, block_ref)

    def first(group, slot):
        for ahead in range(UNROLL):
            where = block_rows(group, ahead)
            mixed = block_ref[where, :].astype(BF16)
            dense_ref[where, :] = mixed
            score_refs[slot][tile_rows(ahead), :] = score(mixed)

    def second(group, slot):
        for ahead in range(UNROLL):
            tile = tile_rows(ahead)
            probs_refs[slot][tile, :] = softmax_turned(score_refs[slot][tile, :]).astype(BF16)

    def third(group, slot):
        for ahead in range(UNROLL):
            where = block_rows(group, ahead)
            block_ref[where, :] = dot(probs_refs[slot][tile_rows(ahead), :], dense_ref[where, :])

    for_each_group(blocks, (first, second, third))

    def scatter(cluster, block, runs, end):
        for source, start, row in runs:
            wide_ref[source, pl.ds(start, slot_rows), :] = block_ref[pl.ds(row, slot_rows), :]

    for_each_cluster(counts_ref, me_ref, place_ref, owners, per_group, scatter)
    for ahead, out_ref in enumerate(out_refs):
        for sub in range(sizes[1]):
            source = owner_of(me_ref, (ahead, 0), sizes) - me_ref[1] + sub
            up, down = wide_ref[source, :half, :], wide_ref[source, half:rows, :]
            out_ref[sub] = jnp.where(low_half((half, LANES)), swap_halves(up), down).astype(BF16)


def query_grad_kernel(sizes, per_group, slot_rows, me_ref, counts_ref, dense_ref, *refs):
    owners = sizes[0] * sizes[1]
    values = sizes[0] + sizes[1] - 1
    value_refs, out_refs, rest = refs[:values], refs[values : values + owners], refs[values + owners :]
    place_ref, wide_ref, block_ref, sums_ref, centroid_ref = rest[:5]
    score_refs, grad_probs_refs, both_refs = rest[5:7], rest[7:9], rest[9:11]
    half = value_refs[0].shape[1]
    rows = 2 * half
    for source, value in arrivals(sizes, me_ref, value_refs):
        value = value.astype(F32)
        wide_ref[source, :half, :] = swap_halves(value)
        wide_ref[source, half:rows, :] = value
        wide_ref[source, rows:, :] = jnp.zeros((slot_rows, LANES), F32)
    blocks = gather_blocks(counts_ref, me_ref, place_ref, owners, per_group, slot_rows, wide_ref, block_ref)

    def first(group, slot):
        for ahead in range(UNROLL):
            where, tile = block_rows(group, ahead), tile_rows(ahead)
            mixed = dense_ref[where, :]
            value = block_ref[where, :].astype(BF16)
            cotan = jnp.where(low_half(mixed.shape), jnp.zeros_like(mixed), mixed)
            score_refs[slot][tile, :] = score(mixed)
            grad_probs_refs[slot][tile, :] = dot_nt(value, cotan)

    def second(group, slot):
        for ahead in range(UNROLL):
            tile = tile_rows(ahead)
            probs = softmax_turned(score_refs[slot][tile, :])
            grad_probs = grad_probs_refs[slot][tile, :]
            probs_half = probs.astype(BF16).astype(F32)
            row_dot = jnp.sum(probs_half * grad_probs, axis=0, keepdims=True)
            grad_scores = (probs * (grad_probs - row_dot)).astype(BF16).astype(F32)
            both_refs[slot][tile, :] = (grad_scores + grad_scores.T).astype(BF16)

    def third(group, slot):
        for ahead in range(UNROLL):
            where = block_rows(group, ahead)
            grad = dot(both_refs[slot][tile_rows(ahead), :], dense_ref[where, :]) * SCALE
            grad = grad.astype(BF16).astype(F32)
            block_ref[where, :] = grad
            sums_ref[pl.ds(group * UNROLL + ahead, 1), :] = jnp.sum(grad, axis=0, keepdims=True)

    for_each_group(blocks, (first, second, third))
    most = (owners * slot_rows + BLOCK_ROWS - 1) // BLOCK_ROWS

    def scatter(cluster, block, runs, end):
        total = jnp.zeros((1, LANES), F32)
        for ahead in range(most):
            here = block + ahead
            total = total + jnp.where(here * BLOCK_ROWS < end, sums_ref[pl.ds(here, 1), :], 0.0)
        centroid_ref[pl.ds(cluster, 1), :] = total
        for source, start, row in runs:
            wide_ref[source, pl.ds(start, slot_rows), :] = block_ref[pl.ds(row, slot_rows), :]

    for_each_cluster(counts_ref, me_ref, place_ref, owners, per_group, scatter)
    extra = out_refs[0].shape[0] - half
    centroid = jnp.where(
        low_half((extra, LANES)), centroid_ref[:extra, :], swap_halves(centroid_ref[extra:, :])
    ).astype(BF16)
    for ahead, out_ref in zip(steps_of(sizes), out_refs):
        source = owner_of(me_ref, ahead, sizes)
        up, down = wide_ref[source, :half, :], wide_ref[source, half:rows, :]
        out_ref[:half, :] = jnp.where(low_half((half, LANES)), up, swap_halves(down)).astype(BF16)
        out_ref[half:, :] = centroid


def unfold(home_ref, out_ref, heads, start, half, finish):
    low = low_half((half, LANES))
    for group in range(home_ref.shape[0] // heads):
        first = group * 2 * half
        for pair in range(heads // 2):
            even = home_ref[group * heads + 2 * pair, start : start + half, :].astype(F32)
            odd = home_ref[group * heads + 2 * pair + 1, start : start + half, :].astype(F32)
            columns = slice(pair * LANES, (pair + 1) * LANES)
            out_ref[first : first + half, columns] = finish(jnp.where(low, even, swap_halves(odd)))
            out_ref[first + half : first + 2 * half, columns] = finish(
                jnp.where(low, swap_halves(even), odd)
            )


def to_half(x):
    return x.astype(BF16)


def bring_home(sizes, heads, pieces, unsort_ref, home_ref, sorted_ref, rows_ref):
    for source, piece in pieces:
        home_ref[source] = piece
    half = sorted_ref.shape[0] * heads // (sizes[0] * sizes[1]) // 2
    unfold(home_ref, sorted_ref, heads, 0, half, to_half)
    toks = rows_ref.shape[0]
    step = min(512, toks)

    @pl.loop(0, toks // step)
    def _(i):
        where = pl.ds(pl.multiple_of(i * step, step), step)
        rows_ref[where, :] = dot(unsort_ref[where, :], sorted_ref[...]).astype(BF16)


def weight_partial(sizes, me_ref, turned_ref, rows_ref, whole_ref, sub_refs):
    width = turned_ref.shape[0]
    step = min(512, width)

    @pl.loop(0, width // step)
    def _(i):
        where = pl.ds(pl.multiple_of(i * step, step), step)
        whole_ref[where, :] = dot(turned_ref[where, :], rows_ref[...]).astype(BF16)

    piece = width // (sizes[0] * sizes[1])
    for ahead, sub_ref in enumerate(sub_refs):
        sub = lax.rem(me_ref[1] + ahead, jnp.int32(sizes[1]))
        for seq in range(sizes[0]):
            first = pl.multiple_of((seq * sizes[1] + sub) * piece, piece)
            sub_ref[seq] = whole_ref[pl.ds(first, piece), :]


def value_home_kernel(sizes, heads, me_ref, turned_ref, unsort_ref, *refs):
    part_refs, rows_ref, sub_refs = refs[: -4 - sizes[1]], refs[-4 - sizes[1]], refs[-3 - sizes[1] : -3]
    home_ref, sorted_ref, whole_ref = refs[-3:]
    pieces = arrivals(sizes, me_ref, part_refs)
    bring_home(sizes, heads, pieces, unsort_ref, home_ref, sorted_ref, rows_ref)
    weight_partial(sizes, me_ref, turned_ref, rows_ref, whole_ref, sub_refs)


def input_partial(me_ref, ahead, parts, rows_ref, value_rows_ref, w_query_ref, w_value_ref, out_ref):
    toks = rows_ref.shape[0]
    columns = w_query_ref.shape[0] // parts
    step = min(512, toks)
    dest = lax.rem(me_ref[2] + ahead, jnp.int32(parts))
    mine = pl.ds(pl.multiple_of(dest * columns, columns), columns)

    @pl.loop(0, toks // step)
    def _(i):
        where = pl.ds(pl.multiple_of(i * step, step), step)
        total = dot_nt(rows_ref[where, :], w_query_ref[mine, :])
        total = total + dot_nt(value_rows_ref[where, :], w_value_ref[mine, :])
        out_ref[where, :] = total.astype(BF16)


def query_home_kernel(
    sizes, heads, factor, parts, me_ref, unsort_ref, value_rows_ref, w_query_ref, w_value_ref, *refs
):
    part_refs, out_refs, (rows_ref, centroid_ref, home_ref, sorted_ref) = (
        refs[: -3 - parts],
        refs[-3 - parts : -4],
        refs[-4:],
    )
    pieces = [
        (source_of(me_ref, ahead, sizes), part_ref[...]) for ahead, part_ref in zip(steps_of(sizes), part_refs)
    ]
    bring_home(sizes, heads, pieces, unsort_ref, home_ref, sorted_ref, rows_ref)
    half = sorted_ref.shape[0] * heads // (sizes[0] * sizes[1]) // 2
    unfold(home_ref, centroid_ref, heads, half, home_ref.shape[1] - half, lambda x: x * factor)
    for ahead, out_ref in enumerate(out_refs):
        input_partial(me_ref, ahead + 1, parts, rows_ref, value_rows_ref, w_query_ref, w_value_ref, out_ref)


def query_weight_kernel(
    sizes, parts, me_ref, turned_ref, rows_ref, value_rows_ref, w_query_ref, w_value_ref, *refs
):
    sub_refs, out_ref, whole_ref = refs[:-2], refs[-2], refs[-1]
    weight_partial(sizes, me_ref, turned_ref, rows_ref, whole_ref, sub_refs)
    input_partial(me_ref, 0, parts, rows_ref, value_rows_ref, w_query_ref, w_value_ref, out_ref)


def fold_subs_kernel(me_ref, *refs):
    seqs = refs[0].shape[0]
    terms, out_refs = refs[:-seqs], refs[-seqs:]
    for ahead, out_ref in enumerate(out_refs):
        seq = lax.rem(me_ref[0] + ahead, jnp.int32(seqs))
        total = terms[0][seq].astype(F32)
        for term in terms[1:]:
            total = total + term[seq].astype(F32)
        out_ref[...] = total.astype(BF16)


def sum_kernel(*refs):
    total = refs[0][...].astype(F32)
    for ref in refs[1:-1]:
        total = total + ref[...].astype(F32)
    refs[-1][...] = total.astype(refs[-1].dtype)


def call(kernel, outs, inputs, smem=(0,), in_place=(), after=(), scratch=(), flops=0, vmem=24, name=None):
    def body(*refs):
        kernel(*refs[: len(inputs)], *refs[len(inputs) + len(after) :])

    def space(i):
        return pltpu.SMEM if i in smem else pl.ANY if i in in_place else pltpu.VMEM

    specs = [pl.BlockSpec(memory_space=space(i)) for i in range(len(inputs))]
    specs += [pl.BlockSpec(memory_space=pl.ANY)] * len(after)
    moved = sum(x.size * x.dtype.itemsize for x in inputs) + sum(
        x.size * x.dtype.itemsize for x in jax.tree.leaves(outs)
    )
    out_space = lambda x: pl.ANY if in_place and x.dtype == BF16 else pltpu.VMEM
    return pl.pallas_call(
        body,
        out_shape=outs,
        in_specs=specs,
        out_specs=jax.tree.map(lambda x: pl.BlockSpec(memory_space=out_space(x)), outs),
        scratch_shapes=list(scratch),
        compiler_params=pltpu.CompilerParams(vmem_limit_bytes=vmem * 2**20),
        cost_estimate=pl.CostEstimate(flops=flops, bytes_accessed=moved, transcendentals=0),
        name=name,
    )(*inputs, *after)


def exchange(parts, sizes):
    out = []
    for ahead, part in zip(steps_of(sizes), parts):
        moves = [
            (
                seq * sizes[1] + sub,
                (seq + ahead[0]) % sizes[0] * sizes[1] + (sub + ahead[1]) % sizes[1],
            )
            for seq, sub in steps_of(sizes)
        ]
        out.append(part if ahead == (0, 0) else lax.ppermute(part, OWNERS, moves))
    return out


def shift(part, axis, ahead):
    size = lax.axis_size(axis)
    return lax.ppermute(part, axis, [(i, (i + ahead) % size) for i in range(size)])


def pass_round(parts, axis):
    return [parts[0]] + [shift(parts[ahead], axis, ahead) for ahead in range(1, len(parts))]


def fold_subs(me, by_sub, name, after=()):
    seqs, piece, columns = by_sub[0].shape
    return call(
        fold_subs_kernel,
        (jax.ShapeDtypeStruct((piece, columns), BF16),) * seqs,
        (me, *pass_round(by_sub, "sub")),
        after=after,
        name=name,
    )


def exchange_by_chip(me, parts, sizes, name, after=()):
    came = pass_round(parts, "seq")
    swapped = call(
        functools.partial(swap_kernel, sizes),
        (jax.ShapeDtypeStruct((sizes[0], *parts[0].shape[1:]), BF16),) * (sizes[1] - 1),
        (me, *came),
        after=after,
        name=name,
    )
    return came + [shift(part, "sub", k + 1) for k, part in enumerate(swapped)]


def add_up(terms, dtype, name):
    return call(sum_kernel, jax.ShapeDtypeStruct(terms[0].shape, dtype), tuple(terms), smem=(), name=name)


def on_device(tokens_in, w_query, w_value, cotangent, assignment):
    sizes = (lax.axis_size("seq"), lax.axis_size("sub"))
    owners = sizes[0] * sizes[1]
    parts = lax.axis_size("head")
    toks, width = tokens_in.shape
    width_dev = cotangent.shape[1]
    heads = width_dev // HD
    slot_rows = 2 * toks // CLUSTERS
    assert owners % heads == 0 and heads % 2 == 0
    groups = owners // heads
    per_group = CLUSTERS // groups
    rows = toks if groups == 1 else per_group * slot_rows
    half = rows // 2
    slots = groups * rows
    columns = width // parts
    capacity = (slot_rows * owners + BLOCK_ROWS - 1) // BLOCK_ROWS * BLOCK_ROWS
    extra = max(per_group // 2, 16)
    shape = jax.ShapeDtypeStruct
    seq, sub = lax.axis_index("seq"), lax.axis_index("sub")
    first = lax.div(seq * sizes[1] + sub, jnp.int32(heads)) * per_group
    me = jnp.stack([seq, sub, lax.axis_index("head"), first]).astype(jnp.int32)

    def several(count, *dims):
        return (shape(dims, BF16),) * count

    *send_mixed, slot_row = call(
        functools.partial(project_query_kernel, sizes, groups, rows),
        several(owners, rows + COUNT_ROWS, LANES) + (shape((1, toks), jnp.int32),),
        (me, assignment.reshape(1, toks), tokens_in, w_query, cotangent),
        in_place=(2, 3, 4),
        scratch=[
            pltpu.VMEM((toks, width), BF16),
            pltpu.VMEM((width, width_dev), BF16),
            pltpu.VMEM((toks, width_dev), BF16),
            pltpu.VMEM((toks, 2 * width_dev), BF16),
            pltpu.VMEM((owners, rows + COUNT_ROWS, LANES), BF16),
            pltpu.SemaphoreType.DMA((3, max(toks, width) // min(128, toks))),
            pltpu.SemaphoreType.DMA((owners,)),
        ],
        vmem=60,
        flops=2 * toks * width * width_dev + 4 * slots * toks * width_dev,
        name="project_query",
    )
    got_mixed = exchange(send_mixed, sizes)
    *send_value, turned, unsort = call(
        functools.partial(project_value_kernel, sizes, groups, rows),
        several(sizes[0], sizes[1], half, LANES) + several(1, width, toks) + several(1, toks, slots),
        (me, slot_row, tokens_in, w_value),
        scratch=[pltpu.VMEM((toks, width_dev), BF16), pltpu.VMEM((owners, half, LANES), BF16)],
        flops=2 * toks * width * width_dev + 2 * slots * toks * width_dev,
        name="project_value",
    )
    send_value, _ = lax.optimization_barrier((send_value, got_mixed[1:4]))
    blocks = per_group * capacity // BLOCK_ROWS
    held = blocks + (LEAD + 4) * UNROLL
    block_flops = 2 * BLOCK_ROWS * BLOCK_ROWS * LANES
    tall = pltpu.VMEM((owners, rows + slot_rows, LANES), F32)
    dense_rows = pltpu.VMEM((held * BLOCK_ROWS, LANES), F32)
    group_f32 = pltpu.VMEM((GROUP_ROWS, BLOCK_ROWS), F32)
    group_b16 = pltpu.VMEM((GROUP_ROWS, BLOCK_ROWS), BF16)
    place = pltpu.SMEM((owners,), jnp.int32)
    *back_value, dense, counts = call(
        functools.partial(value_grad_kernel, sizes, per_group, slot_rows),
        several(sizes[0], sizes[1], half, LANES)
        + several(1, held * BLOCK_ROWS, LANES)
        + (shape((owners, LANES), jnp.int32),),
        (me, *got_mixed),
        after=[unsort],
        scratch=[pltpu.SMEM((owners, LANES), jnp.int32), place, tall, dense_rows, tall]
        + [group_f32] * 2
        + [group_b16] * 2,
        flops=4 * blocks * block_flops,
        vmem=48,
        name="value_grad",
    )
    got_value = exchange_by_chip(me, send_value, sizes, "swap_value", [dense])
    back_query = call(
        functools.partial(query_grad_kernel, sizes, per_group, slot_rows),
        several(owners, half + extra, LANES),
        (me, counts, dense, *got_value),
        smem=(0, 1),
        scratch=[place, tall, dense_rows, pltpu.VMEM((held, LANES), F32), pltpu.VMEM((2 * extra, LANES), F32)]
        + [group_f32] * 4
        + [group_b16] * 2,
        flops=6 * blocks * block_flops,
        vmem=48,
        name="query_grad",
    )
    home_query = exchange(back_query, sizes)
    home_value = exchange_by_chip(me, back_value, sizes, "swap_value_grad", home_query[1:3])
    weight_flops = 2 * toks * width * width_dev
    home_flops = 2 * slots * toks * width_dev
    sub_shapes = several(sizes[1], sizes[0], width // owners, width_dev)
    whole = pltpu.VMEM((width, width_dev), BF16)
    sorted_rows = pltpu.VMEM((slots, width_dev), BF16)
    value_rows, *value_weight = call(
        functools.partial(value_home_kernel, sizes, heads),
        several(1, toks, width_dev) + sub_shapes,
        (me, turned, unsort, *home_value),
        after=home_query[3:5],
        scratch=[pltpu.VMEM((owners, half, LANES), BF16), sorted_rows, whole],
        flops=weight_flops + home_flops,
        name="value_home",
    )
    value_weight = fold_subs(me, value_weight, "value_subs")
    *partials, query_rows, centroid_grad = call(
        functools.partial(query_home_kernel, sizes, heads, (CLUSTERS / (toks * owners)) ** 0.5, parts),
        several(parts - 1, toks, columns)
        + several(1, toks, width_dev)
        + (shape((groups * 2 * extra, width_dev), F32),),
        (me, unsort, value_rows, w_query, w_value, *home_query),
        after=value_weight,
        scratch=[pltpu.VMEM((owners, half + extra, LANES), BF16), sorted_rows],
        flops=weight_flops + home_flops,
        name="query_home",
    )
    arrived = [shift(partial, "head", k + 1) for k, partial in enumerate(partials)]
    value_weight, _ = lax.optimization_barrier((value_weight, home_query))
    value_weight = pass_round(value_weight, "seq")
    *query_weight, own = call(
        functools.partial(query_weight_kernel, sizes, parts),
        sub_shapes + several(1, toks, columns),
        (me, turned, query_rows, value_rows, w_query, w_value),
        scratch=[whole],
        flops=2 * weight_flops,
        name="query_weight",
    )
    query_weight = pass_round(fold_subs(me, query_weight, "query_subs", value_weight[1:]), "seq")
    grad_wv = add_up(value_weight, F32, "value_sum")
    grad_wq = add_up(query_weight, F32, "query_sum")
    grad_input = add_up([own] + arrived, BF16, "input_sum")
    if groups > 1:
        centroid_grad = centroid_grad.reshape(groups, 2 * extra, width_dev)[:, :per_group]
        centroid_grad = centroid_grad.reshape(CLUSTERS, width_dev)
    return (grad_input, grad_wq, grad_wv, centroid_grad)


def solution(mesh):
    return jax.shard_map(
        on_device,
        mesh=mesh,
        in_specs=(
            P(("grp", "seq", "sub"), None),
            P(None, "head"),
            P(None, "head"),
            P(("grp", "seq", "sub"), "head"),
            P(("grp", "seq", "sub"), None),
        ),
        out_specs=(
            P(("grp", "seq", "sub"), "head"),
            P(("grp", "seq", "sub"), "head"),
            P(("grp", "seq", "sub"), "head"),
            P("grp", "head"),
        ),
        check_vma=False,
    )
```

```python
import functools

import jax
import jax.numpy as jnp
from jax import lax
from jax.experimental import pallas as pl
from jax.experimental.pallas import tpu as pltpu
from jax.sharding import PartitionSpec as P

HD = 64
CLUSTERS = 64
BLOCK_ROWS = 128
LANES = 128
UNROLL = 4
COUNT_ROWS = 16
SCALE = 0.5 * HD ** (-0.5)
F32 = jnp.float32
BF16 = jnp.bfloat16
OWNERS = ("seq", "sub")
GROUP_ROWS = UNROLL * BLOCK_ROWS
LEAD = 2


def iota(shape, dim):
    return lax.broadcasted_iota(jnp.int32, shape, dim)


def low_half(shape):
    return iota(shape, 1) < HD


def swap_halves(tile):
    return pltpu.roll(tile, HD, 1)


def dot(a, b):
    return jnp.dot(a, b, preferred_element_type=F32)


def dot_nt(a, b):
    return lax.dot_general(a, b, (((1,), (1,)), ((), ())), preferred_element_type=F32)


def ones_where(condition):
    return jnp.where(condition, 1.0, 0.0).astype(BF16)


def owner_of(me_ref, ahead, sizes):
    seq = lax.rem(me_ref[0] + ahead[0], jnp.int32(sizes[0]))
    sub = lax.rem(me_ref[1] + ahead[1], jnp.int32(sizes[1]))
    return seq * sizes[1] + sub


def source_of(me_ref, ahead, sizes):
    return owner_of(me_ref, ((sizes[0] - ahead[0]) % sizes[0], (sizes[1] - ahead[1]) % sizes[1]), sizes)


def steps_of(sizes):
    return [(seq, sub) for seq in range(sizes[0]) for sub in range(sizes[1])]


def slots_of(assign, groups, rows):
    toks = assign.shape[1]
    per_group = CLUSTERS // groups
    member = jnp.where(iota((CLUSTERS, toks), 0) == assign, 1.0, 0.0)
    member_b = member.astype(BF16)
    upto = ones_where(iota((LANES, LANES), 0) <= iota((LANES, LANES), 1))
    counts = jnp.zeros((CLUSTERS, 1), F32)
    running = []
    for first in range(0, toks, LANES):
        within = dot(member_b[:, first : first + LANES], upto)
        running.append(within + counts)
        counts = counts + within[:, LANES - 1 :]
    running = jnp.concatenate(running, axis=1)
    here, other = iota((CLUSTERS, CLUSTERS), 0), iota((CLUSTERS, CLUSTERS), 1)
    group_of = lambda index: lax.div(index, jnp.int32(per_group))
    earlier = ones_where((other < here) & (group_of(other) == group_of(here)))
    base = dot(earlier, jnp.broadcast_to(counts, (CLUSTERS, LANES)).astype(BF16))[:, :1]
    base = base + (group_of(iota((CLUSTERS, 1), 0)) * rows).astype(F32)
    slot = jnp.sum(member * (running - 1.0 + base), axis=0, keepdims=True).astype(jnp.int32)
    spread = jnp.concatenate([member_b, jnp.zeros((LANES - CLUSTERS, toks), BF16)], axis=0)
    return slot, dot_nt(jnp.ones((COUNT_ROWS, toks), BF16), spread).astype(BF16)


def project_query_kernel(sizes, groups, rows, me_ref, assign_ref, tokens_hbm, weight_hbm, cotan_hbm, *rest):
    out_refs, rest = rest[:-10], rest[-10:]
    slot_ref, tokens_ref, weight_ref, cotan_ref, query_ref, pick_ref, part_ref, sorted_ref, in_sems, out_sems = rest
    toks, width = tokens_ref.shape
    heads = weight_ref.shape[1] // HD
    fine = min(256, toks, width)

    def load(kind):
        source, target = ((cotan_hbm, cotan_ref), (weight_hbm, weight_ref), (tokens_hbm, tokens_ref))[kind]
        return [
            pltpu.make_async_copy(
                source.at[pl.ds(row, fine), :], target.at[pl.ds(row, fine), :], in_sems.at[kind, row // fine]
            )
            for row in range(0, source.shape[0], fine)
        ]

    for copy in load(0) + load(1) + load(2):
        copy.start()
    slot, tallies = slots_of(assign_ref[...], groups, rows)
    slot_ref[...] = slot
    for owner in range(sorted_ref.shape[0]):
        sorted_ref[owner, rows:, :] = tallies
    slots = pick_ref.shape[0]
    step = min(512, slots)
    for first in range(0, slots, step):
        pick_ref[first : first + step, :] = ones_where(iota((step, toks), 0) + first == slot)
    for copy in load(0):
        copy.wait()
    for first in range(0, slots, step):
        part_ref[first : first + step, :] = dot(pick_ref[first : first + step, :], cotan_ref[...])
    for copy in load(1):
        copy.wait()
    tokens = load(2)
    for index, first in enumerate(range(0, toks, fine)):
        tokens[index].wait()
        query_ref[first : first + fine, :] = dot(tokens_ref[first : first + fine, :], weight_ref[...]).astype(BF16)
    part = min(512, rows)
    low = low_half((part, LANES))
    for first in range(0, slots, part):
        group, start = first // rows, first % rows
        query = dot(pick_ref[first : first + part, :], query_ref[...])
        for pair in range(heads // 2):
            columns = slice(pair * LANES, (pair + 1) * LANES)
            q_tile, c_tile = query[:, columns], part_ref[first : first + part, columns]
            even = jnp.where(low, q_tile, swap_halves(c_tile)).astype(BF16)
            odd = jnp.where(low, swap_halves(q_tile), c_tile).astype(BF16)
            sorted_ref[group * heads + 2 * pair, start : start + part, :] = even
            sorted_ref[group * heads + 2 * pair + 1, start : start + part, :] = odd
    copies = [
        pltpu.make_async_copy(sorted_ref.at[owner_of(me_ref, ahead, sizes)], out_ref, out_sems.at[k])
        for k, (ahead, out_ref) in enumerate(zip(steps_of(sizes), out_refs))
    ]
    for copy in copies:
        copy.start()
    for copy in copies:
        copy.wait()


def project_value_kernel(groups, rows, slot_ref, tokens_ref, weight_ref, sorted_ref, turned_ref, unsort_ref, value_ref):
    toks = tokens_ref.shape[0]
    heads = weight_ref.shape[1] // HD
    step = min(512, toks)

    @pl.loop(0, toks // step)
    def _(i):
        where = pl.ds(pl.multiple_of(i * step, step), step)
        value_ref[where, :] = dot(tokens_ref[where, :], weight_ref[...]).astype(BF16)

    half = rows // 2
    part = min(256, half)
    pieces = half // part

    @pl.loop(0, groups * pieces)
    def _(i):
        group, piece = lax.div(i, jnp.int32(pieces)), lax.rem(i, jnp.int32(pieces))
        first = pl.multiple_of(piece * part, part)
        index = iota((part, toks), 0) + group * rows + first
        upper = dot(ones_where(index == slot_ref[...]), value_ref[...])
        lower = dot(ones_where(index + half == slot_ref[...]), value_ref[...])
        low = low_half((part, LANES))
        for pair in range(heads // 2):
            up = upper[:, pair * LANES : (pair + 1) * LANES]
            down = lower[:, pair * LANES : (pair + 1) * LANES]
            even = jnp.where(low, up, swap_halves(down)).astype(BF16)
            odd = jnp.where(low, swap_halves(up), down).astype(BF16)
            sorted_ref[group * heads + 2 * pair, pl.ds(first, part), :] = even
            sorted_ref[group * heads + 2 * pair + 1, pl.ds(first, part), :] = odd

    turned_ref[...] = tokens_ref[...].T
    slots = unsort_ref.shape[1]
    part = min(256, slots)
    for i in range(slots // part):
        pick = ones_where(iota((part, toks), 0) + i * part == slot_ref[...])
        unsort_ref[:, i * part : (i + 1) * part] = pick.T


def score(mixed):
    query = jnp.where(low_half(mixed.shape), mixed.astype(F32) * SCALE, 0.0).astype(BF16)
    return dot_nt(query, mixed)


def softmax_turned(scores):
    shape = scores.shape
    seen = iota(shape, 0) <= iota(shape, 1)
    scores = jnp.where(seen, scores, -jnp.inf)
    raised = jnp.exp(scores - jnp.max(scores, axis=0, keepdims=True))
    return raised * (1.0 / jnp.sum(raised, axis=0, keepdims=True))


def for_each_cluster(counts_ref, me_ref, place_ref, owners, per_group, body):
    for source in range(owners):
        place_ref[source] = 0

    def step(cluster, block):
        runs = []
        total = 0
        base = block * BLOCK_ROWS
        for source in range(owners):
            count = counts_ref[source, me_ref[3] + cluster]
            start = place_ref[source]
            runs.append((source, start, base + total))
            place_ref[source] = start + count
            total = total + count
        body(cluster, block, runs, base + total)
        return block + lax.shift_right_logical(total + (BLOCK_ROWS - 1), jnp.int32(7))

    return lax.fori_loop(0, per_group, step, jnp.int32(LEAD * UNROLL))


def gather_blocks(counts_ref, me_ref, place_ref, owners, per_group, slot_rows, wide_ref, block_ref):
    def body(cluster, block, runs, end):
        for source, start, row in runs:
            block_ref[pl.ds(row, slot_rows), :] = wide_ref[source, pl.ds(start, slot_rows), :]
        block_ref[pl.ds(end, BLOCK_ROWS), :] = jnp.zeros((BLOCK_ROWS, LANES), F32)

    blocks = for_each_cluster(counts_ref, me_ref, place_ref, owners, per_group, body)
    spare = pl.ds(pl.multiple_of(blocks * BLOCK_ROWS, BLOCK_ROWS), GROUP_ROWS)
    block_ref[spare, :] = jnp.zeros((GROUP_ROWS, LANES), F32)
    return blocks


def for_each_group(blocks, stages):
    first, second, third = stages
    groups = lax.div(blocks + (UNROLL - 1), jnp.int32(UNROLL))

    def step(i, carry):
        for slot in range(2):
            group = LEAD + 2 * i + slot
            third(group - 2, slot)
            second(group - 1, 1 - slot)
            first(group, slot)
        return carry

    lax.fori_loop(0, lax.shift_right_logical(groups + 1, jnp.int32(1)), step, 0)


def block_rows(group, ahead):
    return pl.ds(pl.multiple_of((group * UNROLL + ahead) * BLOCK_ROWS, BLOCK_ROWS), BLOCK_ROWS)


def tile_rows(ahead):
    return slice(ahead * BLOCK_ROWS, (ahead + 1) * BLOCK_ROWS)


def value_grad_kernel(sizes, per_group, slot_rows, me_ref, *refs):
    owners = sizes[0] * sizes[1]
    mixed_refs, out_refs, rest = refs[:owners], refs[owners : 2 * owners], refs[2 * owners :]
    dense_ref, counts_out_ref, counts_ref, place_ref, wide_ref, block_ref, home_ref = rest[:7]
    score_refs, probs_refs = rest[7:9], rest[9:11]
    half = out_refs[0].shape[0]
    rows = 2 * half
    for ahead, mixed_ref in zip(steps_of(sizes), mixed_refs):
        source = source_of(me_ref, ahead, sizes)
        tail = mixed_ref[rows:, :].astype(F32).astype(jnp.int32)
        counts_out_ref[pl.ds(source, 1), :] = tail[:1, :]
        wide_ref[source, :rows, :] = mixed_ref[:rows, :].astype(F32)
        wide_ref[source, rows:, :] = jnp.zeros((slot_rows, LANES), F32)
    pltpu.sync_copy(counts_out_ref, counts_ref)
    blocks = gather_blocks(counts_ref, me_ref, place_ref, owners, per_group, slot_rows, wide_ref, block_ref)

    def first(group, slot):
        for ahead in range(UNROLL):
            where = block_rows(group, ahead)
            mixed = block_ref[where, :].astype(BF16)
            dense_ref[where, :] = mixed
            score_refs[slot][tile_rows(ahead), :] = score(mixed)

    def second(group, slot):
        for ahead in range(UNROLL):
            tile = tile_rows(ahead)
            probs_refs[slot][tile, :] = softmax_turned(score_refs[slot][tile, :]).astype(BF16)

    def third(group, slot):
        for ahead in range(UNROLL):
            where = block_rows(group, ahead)
            block_ref[where, :] = dot(probs_refs[slot][tile_rows(ahead), :], dense_ref[where, :])

    for_each_group(blocks, (first, second, third))

    def scatter(cluster, block, runs, end):
        for source, start, row in runs:
            wide_ref[source, pl.ds(start, slot_rows), :] = block_ref[pl.ds(row, slot_rows), :]

    for_each_cluster(counts_ref, me_ref, place_ref, owners, per_group, scatter)
    for ahead, out_ref in zip(steps_of(sizes), out_refs):
        source = owner_of(me_ref, ahead, sizes)
        up, down = wide_ref[source, :half, :], wide_ref[source, half:rows, :]
        out_ref[...] = jnp.where(low_half((half, LANES)), swap_halves(up), down).astype(BF16)


def query_grad_kernel(
    owners, per_group, slot_rows, me_ref, counts_ref, dense_ref, value_in_ref, out_ref, place_ref, wide_ref, block_ref, *rest
):
    sums_ref, centroid_ref = rest[:2]
    score_refs, grad_probs_refs, both_refs = rest[2:4], rest[4:6], rest[6:8]
    half = value_in_ref.shape[1]
    rows = 2 * half
    for source in range(owners):
        value = value_in_ref[source].astype(F32)
        wide_ref[source, :half, :] = swap_halves(value)
        wide_ref[source, half:rows, :] = value
        wide_ref[source, rows:, :] = jnp.zeros((slot_rows, LANES), F32)
    blocks = gather_blocks(counts_ref, me_ref, place_ref, owners, per_group, slot_rows, wide_ref, block_ref)

    def first(group, slot):
        for ahead in range(UNROLL):
            where, tile = block_rows(group, ahead), tile_rows(ahead)
            mixed = dense_ref[where, :]
            value = block_ref[where, :].astype(BF16)
            cotan = jnp.where(low_half(mixed.shape), jnp.zeros_like(mixed), mixed)
            score_refs[slot][tile, :] = score(mixed)
            grad_probs_refs[slot][tile, :] = dot_nt(value, cotan)

    def second(group, slot):
        for ahead in range(UNROLL):
            tile = tile_rows(ahead)
            probs = softmax_turned(score_refs[slot][tile, :])
            grad_probs = grad_probs_refs[slot][tile, :]
            probs_half = probs.astype(BF16).astype(F32)
            row_dot = jnp.sum(probs_half * grad_probs, axis=0, keepdims=True)
            grad_scores = (probs * (grad_probs - row_dot)).astype(BF16).astype(F32)
            both_refs[slot][tile, :] = (grad_scores + grad_scores.T).astype(BF16)

    def third(group, slot):
        for ahead in range(UNROLL):
            where = block_rows(group, ahead)
            grad = dot(both_refs[slot][tile_rows(ahead), :], dense_ref[where, :]) * SCALE
            grad = grad.astype(BF16).astype(F32)
            block_ref[where, :] = grad
            sums_ref[pl.ds(group * UNROLL + ahead, 1), :] = jnp.sum(grad, axis=0, keepdims=True)

    for_each_group(blocks, (first, second, third))
    most = (owners * slot_rows + BLOCK_ROWS - 1) // BLOCK_ROWS

    def scatter(cluster, block, runs, end):
        total = jnp.zeros((1, LANES), F32)
        for ahead in range(most):
            here = block + ahead
            total = total + jnp.where(here * BLOCK_ROWS < end, sums_ref[pl.ds(here, 1), :], 0.0)
        centroid_ref[pl.ds(cluster, 1), :] = total
        for source, start, row in runs:
            wide_ref[source, pl.ds(start, slot_rows), :] = block_ref[pl.ds(row, slot_rows), :]

    for_each_cluster(counts_ref, me_ref, place_ref, owners, per_group, scatter)
    extra = out_ref.shape[1] - half
    centroid = jnp.where(
        low_half((extra, LANES)), centroid_ref[:extra, :], swap_halves(centroid_ref[extra:, :])
    ).astype(BF16)
    for source in range(owners):
        up, down = wide_ref[source, :half, :], wide_ref[source, half:rows, :]
        out_ref[source, :half, :] = jnp.where(low_half((half, LANES)), up, swap_halves(down)).astype(BF16)
        out_ref[source, half:, :] = centroid


def unfold(home_ref, out_ref, heads, start, half, finish):
    low = low_half((half, LANES))
    for group in range(home_ref.shape[0] // heads):
        first = group * 2 * half
        for pair in range(heads // 2):
            even = home_ref[group * heads + 2 * pair, start : start + half, :].astype(F32)
            odd = home_ref[group * heads + 2 * pair + 1, start : start + half, :].astype(F32)
            columns = slice(pair * LANES, (pair + 1) * LANES)
            out_ref[first : first + half, columns] = finish(jnp.where(low, even, swap_halves(odd)))
            out_ref[first + half : first + 2 * half, columns] = finish(
                jnp.where(low, swap_halves(even), odd)
            )


def to_half(x):
    return x.astype(BF16)


def bring_home(heads, home_ref, unsort_ref, sorted_ref, rows_ref):
    half = sorted_ref.shape[0] * heads // home_ref.shape[0] // 2
    unfold(home_ref, sorted_ref, heads, 0, half, to_half)
    toks = rows_ref.shape[0]
    step = min(512, toks)

    @pl.loop(0, toks // step)
    def _(i):
        where = pl.ds(pl.multiple_of(i * step, step), step)
        rows_ref[where, :] = dot(unsort_ref[where, :], sorted_ref[...]).astype(BF16)


def weight_partial(sizes, me_ref, turned_ref, rows_ref, whole_ref, sub_refs):
    width = turned_ref.shape[0]
    step = min(512, width)

    @pl.loop(0, width // step)
    def _(i):
        where = pl.ds(pl.multiple_of(i * step, step), step)
        whole_ref[where, :] = dot(turned_ref[where, :], rows_ref[...]).astype(BF16)

    piece = width // (sizes[0] * sizes[1])
    for ahead, sub_ref in enumerate(sub_refs):
        sub = lax.rem(me_ref[1] + ahead, jnp.int32(sizes[1]))
        for seq in range(sizes[0]):
            first = pl.multiple_of((seq * sizes[1] + sub) * piece, piece)
            sub_ref[seq] = whole_ref[pl.ds(first, piece), :]


def value_home_kernel(sizes, heads, me_ref, turned_ref, unsort_ref, *refs):
    part_refs, rows_ref, sub_refs = refs[: -4 - sizes[1]], refs[-4 - sizes[1]], refs[-3 - sizes[1] : -3]
    home_ref, sorted_ref, whole_ref = refs[-3:]
    for ahead, part_ref in zip(steps_of(sizes), part_refs):
        home_ref[source_of(me_ref, ahead, sizes)] = part_ref[...]
    bring_home(heads, home_ref, unsort_ref, sorted_ref, rows_ref)
    weight_partial(sizes, me_ref, turned_ref, rows_ref, whole_ref, sub_refs)


def query_home_kernel(sizes, heads, factor, me_ref, turned_ref, unsort_ref, home_ref, *refs):
    sub_refs, (rows_ref, centroid_ref, sorted_ref, whole_ref) = refs[:-4], refs[-4:]
    bring_home(heads, home_ref, unsort_ref, sorted_ref, rows_ref)
    half = sorted_ref.shape[0] * heads // (sizes[0] * sizes[1]) // 2
    unfold(home_ref, centroid_ref, heads, half, home_ref.shape[1] - half, lambda x: x * factor)
    weight_partial(sizes, me_ref, turned_ref, rows_ref, whole_ref, sub_refs)


def input_grad_kernel(first, parts, me_ref, rows_ref, value_rows_ref, w_query_ref, w_value_ref, *out_refs):
    toks = rows_ref.shape[0]
    columns = w_query_ref.shape[0] // parts
    step = min(512, toks)
    for k, out_ref in enumerate(out_refs):
        dest = lax.rem(me_ref[2] + (first + k), jnp.int32(parts))
        mine = pl.ds(pl.multiple_of(dest * columns, columns), columns)

        @pl.loop(0, toks // step)
        def _(i):
            where = pl.ds(pl.multiple_of(i * step, step), step)
            total = dot_nt(rows_ref[where, :], w_query_ref[mine, :])
            total = total + dot_nt(value_rows_ref[where, :], w_value_ref[mine, :])
            out_ref[where, :] = total.astype(BF16)


def fold_subs_kernel(me_ref, *refs):
    seqs = refs[0].shape[0]
    terms, out_refs = refs[:-seqs], refs[-seqs:]
    each = len(terms) // 2
    for ahead, out_ref in enumerate(out_refs):
        seq = lax.rem(me_ref[0] + ahead, jnp.int32(seqs))
        for which in range(2):
            total = terms[which * each][seq].astype(F32)
            for term in terms[which * each + 1 : (which + 1) * each]:
                total = total + term[seq].astype(F32)
            out_ref[which] = total.astype(BF16)


def sum_kernel(*refs):
    outs = 2 if len(refs[0].shape) == 3 else 1
    terms, out_refs = refs[:-outs], refs[-outs:]
    for which, out_ref in enumerate(out_refs):
        total = (terms[0][which] if outs == 2 else terms[0][...]).astype(F32)
        for term in terms[1:]:
            total = total + (term[which] if outs == 2 else term[...]).astype(F32)
        out_ref[...] = total.astype(out_ref.dtype)


def call(kernel, outs, inputs, smem=(0,), in_place=(), after=(), scratch=(), flops=0, vmem=24, name=None):
    def body(*refs):
        kernel(*refs[: len(inputs)], *refs[len(inputs) + len(after) :])

    def space(i):
        return pltpu.SMEM if i in smem else pl.ANY if i in in_place else pltpu.VMEM

    specs = [pl.BlockSpec(memory_space=space(i)) for i in range(len(inputs))]
    specs += [pl.BlockSpec(memory_space=pl.ANY)] * len(after)
    moved = sum(x.size * x.dtype.itemsize for x in inputs) + sum(
        x.size * x.dtype.itemsize for x in jax.tree.leaves(outs)
    )
    out_space = lambda x: pl.ANY if in_place and x.dtype == BF16 else pltpu.VMEM
    return pl.pallas_call(
        body,
        out_shape=outs,
        in_specs=specs,
        out_specs=jax.tree.map(lambda x: pl.BlockSpec(memory_space=out_space(x)), outs),
        scratch_shapes=list(scratch),
        compiler_params=pltpu.CompilerParams(vmem_limit_bytes=vmem * 2**20),
        cost_estimate=pl.CostEstimate(flops=flops, bytes_accessed=moved, transcendentals=0),
        name=name,
    )(*inputs, *after)


def exchange(parts, sizes):
    out = []
    for ahead, part in zip(steps_of(sizes), parts):
        moves = [
            (
                seq * sizes[1] + sub,
                (seq + ahead[0]) % sizes[0] * sizes[1] + (sub + ahead[1]) % sizes[1],
            )
            for seq, sub in steps_of(sizes)
        ]
        out.append(part if ahead == (0, 0) else lax.ppermute(part, OWNERS, moves))
    return out


def shift(part, axis, ahead):
    size = lax.axis_size(axis)
    return lax.ppermute(part, axis, [(i, (i + ahead) % size) for i in range(size)])


def pass_round(parts, axis):
    return [parts[0]] + [shift(parts[ahead], axis, ahead) for ahead in range(1, len(parts))]


def all_to_all(rows):
    return lax.all_to_all(rows, OWNERS, split_axis=0, concat_axis=0, tiled=True)


def on_device(tokens_in, w_query, w_value, cotangent, assignment):
    sizes = (lax.axis_size("seq"), lax.axis_size("sub"))
    owners = sizes[0] * sizes[1]
    parts = lax.axis_size("head")
    toks, width = tokens_in.shape
    width_dev = cotangent.shape[1]
    heads = width_dev // HD
    slot_rows = 2 * toks // CLUSTERS
    assert owners % heads == 0 and heads % 2 == 0
    groups = owners // heads
    per_group = CLUSTERS // groups
    rows = toks if groups == 1 else per_group * slot_rows
    half = rows // 2
    slots = groups * rows
    columns = width // parts
    capacity = (slot_rows * owners + BLOCK_ROWS - 1) // BLOCK_ROWS * BLOCK_ROWS
    extra = max(per_group // 2, 16)
    shape = jax.ShapeDtypeStruct
    seq, sub = lax.axis_index("seq"), lax.axis_index("sub")
    first = lax.div(seq * sizes[1] + sub, jnp.int32(heads)) * per_group
    me = jnp.stack([seq, sub, lax.axis_index("head"), first]).astype(jnp.int32)

    def several(count, *dims):
        return (shape(dims, BF16),) * count

    *send_mixed, slot_row = call(
        functools.partial(project_query_kernel, sizes, groups, rows),
        several(owners, rows + COUNT_ROWS, LANES) + (shape((1, toks), jnp.int32),),
        (me, assignment.reshape(1, toks), tokens_in, w_query, cotangent),
        in_place=(2, 3, 4),
        scratch=[
            pltpu.VMEM((toks, width), BF16),
            pltpu.VMEM((width, width_dev), BF16),
            pltpu.VMEM((toks, width_dev), BF16),
            pltpu.VMEM((toks, width_dev), BF16),
            pltpu.VMEM((slots, toks), BF16),
            pltpu.VMEM((slots, width_dev), F32),
            pltpu.VMEM((owners, rows + COUNT_ROWS, LANES), BF16),
            pltpu.SemaphoreType.DMA((3, max(toks, width) // min(256, toks, width))),
            pltpu.SemaphoreType.DMA((owners,)),
        ],
        flops=2 * toks * width * width_dev + 4 * slots * toks * width_dev,
        vmem=60,
        name="project_query",
    )
    got_mixed = exchange(send_mixed, sizes)
    send_value, turned, unsort = call(
        functools.partial(project_value_kernel, groups, rows),
        several(1, owners, half, LANES) + several(1, width, toks) + several(1, toks, slots),
        (slot_row, tokens_in, w_value),
        smem=(),
        scratch=[pltpu.VMEM((toks, width_dev), BF16)],
        flops=2 * toks * width * width_dev + 2 * slots * toks * width_dev,
        name="project_value",
    )
    got_value = all_to_all(send_value)
    blocks = per_group * capacity // BLOCK_ROWS
    held = blocks + (LEAD + 4) * UNROLL
    block_flops = 2 * BLOCK_ROWS * BLOCK_ROWS * LANES
    tall = pltpu.VMEM((owners, rows + slot_rows, LANES), F32)
    dense_rows = pltpu.VMEM((held * BLOCK_ROWS, LANES), F32)
    group_f32 = pltpu.VMEM((GROUP_ROWS, BLOCK_ROWS), F32)
    group_b16 = pltpu.VMEM((GROUP_ROWS, BLOCK_ROWS), BF16)
    place = pltpu.SMEM((owners,), jnp.int32)
    *back_value, dense, counts = call(
        functools.partial(value_grad_kernel, sizes, per_group, slot_rows),
        several(owners, half, LANES)
        + several(1, held * BLOCK_ROWS, LANES)
        + (shape((owners, LANES), jnp.int32),),
        (me, *got_mixed),
        scratch=[pltpu.SMEM((owners, LANES), jnp.int32), place, tall, dense_rows, tall]
        + [group_f32] * 2
        + [group_b16] * 2,
        flops=4 * blocks * block_flops,
        vmem=48,
        name="value_grad",
    )
    home_value = exchange(back_value, sizes)
    back_query = call(
        functools.partial(query_grad_kernel, owners, per_group, slot_rows),
        shape((owners, half + extra, LANES), BF16),
        (me, counts, dense, got_value),
        smem=(0, 1),
        scratch=[place, tall, dense_rows, pltpu.VMEM((held, LANES), F32), pltpu.VMEM((2 * extra, LANES), F32)]
        + [group_f32] * 4
        + [group_b16] * 2,
        flops=6 * blocks * block_flops,
        vmem=48,
        name="query_grad",
    )
    home_query = all_to_all(back_query)
    weight_flops = 2 * toks * width * width_dev
    home_flops = 2 * slots * toks * width_dev
    piece = width // owners
    sub_shapes = several(sizes[1], sizes[0], piece, width_dev)
    whole = pltpu.VMEM((width, width_dev), BF16)
    sorted_rows = pltpu.VMEM((slots, width_dev), BF16)
    value_rows, *value_weight = call(
        functools.partial(value_home_kernel, sizes, heads),
        several(1, toks, width_dev) + sub_shapes,
        (me, turned, unsort, *home_value),
        scratch=[pltpu.VMEM((owners, half, LANES), BF16), sorted_rows, whole],
        flops=weight_flops + home_flops,
        name="value_home",
    )
    *query_weight, query_rows, centroid_grad = call(
        functools.partial(query_home_kernel, sizes, heads, (CLUSTERS / (toks * owners)) ** 0.5),
        sub_shapes + several(1, toks, width_dev) + (shape((groups * 2 * extra, width_dev), F32),),
        (me, turned, unsort, home_query),
        after=[value_rows],
        scratch=[sorted_rows, whole],
        flops=weight_flops + home_flops,
        name="query_home",
    )
    partials = call(
        functools.partial(input_grad_kernel, 1, parts),
        several(parts - 1, toks, columns),
        (me, query_rows, value_rows, w_query, w_value),
        flops=weight_flops * (parts - 1) * 2 // parts,
        name="input_others",
    )
    arrived = [shift(partial, "head", k + 1) for k, partial in enumerate(partials)]
    by_seq = call(
        fold_subs_kernel,
        several(sizes[0], 2, piece, width_dev),
        (me, *pass_round(value_weight, "sub"), *pass_round(query_weight, "sub")),
        after=partials,
        name="weight_subs",
    )
    own = call(
        functools.partial(input_grad_kernel, 0, parts),
        several(1, toks, columns),
        (me, query_rows, value_rows, w_query, w_value),
        after=by_seq[:1],
        flops=weight_flops * 2 // parts,
        name="input_own",
    )
    grad_wv, grad_wq = call(
        sum_kernel,
        (shape((piece, width_dev), F32),) * 2,
        tuple(pass_round(by_seq, "seq")),
        smem=(),
        name="weight_sum",
    )
    grad_input = call(
        sum_kernel, shape((toks, columns), BF16), tuple(list(own) + arrived), smem=(), name="input_sum"
    )
    if groups > 1:
        centroid_grad = centroid_grad.reshape(groups, 2 * extra, width_dev)[:, :per_group]
        centroid_grad = centroid_grad.reshape(CLUSTERS, width_dev)
    return (grad_input, grad_wq, grad_wv, centroid_grad)


def solution(mesh):
    return jax.shard_map(
        on_device,
        mesh=mesh,
        in_specs=(
            P(("grp", "seq", "sub"), None),
            P(None, "head"),
            P(None, "head"),
            P(("grp", "seq", "sub"), "head"),
            P(("grp", "seq", "sub"), None),
        ),
        out_specs=(
            P(("grp", "seq", "sub"), "head"),
            P(("grp", "seq", "sub"), "head"),
            P(("grp", "seq", "sub"), "head"),
            P("grp", "head"),
        ),
        check_vma=False,
    )
```

```python
import functools

import jax
import jax.numpy as jnp
from jax import lax
from jax.experimental import pallas as pl
from jax.experimental.pallas import tpu as pltpu
from jax.sharding import PartitionSpec as P

HD = 64
CLUSTERS = 64
BLOCK_ROWS = 128
LANES = 128
UNROLL = 4
COUNT_ROWS = 16
SCALE = 0.5 * HD ** (-0.5)
F32 = jnp.float32
BF16 = jnp.bfloat16
OWNERS = ("seq", "sub")
GROUP_ROWS = UNROLL * BLOCK_ROWS
LEAD = 2


def iota(shape, dim):
    return lax.broadcasted_iota(jnp.int32, shape, dim)


def low_half(shape):
    return iota(shape, 1) < HD


def swap_halves(tile):
    return pltpu.roll(tile, HD, 1)


def dot(a, b):
    return jnp.dot(a, b, preferred_element_type=F32)


def dot_nt(a, b):
    return lax.dot_general(a, b, (((1,), (1,)), ((), ())), preferred_element_type=F32)


def ones_where(condition):
    return jnp.where(condition, 1.0, 0.0).astype(BF16)


def owner_of(me_ref, ahead, sizes):
    seq = lax.rem(me_ref[0] + ahead[0], jnp.int32(sizes[0]))
    sub = lax.rem(me_ref[1] + ahead[1], jnp.int32(sizes[1]))
    return seq * sizes[1] + sub


def source_of(me_ref, ahead, sizes):
    return owner_of(me_ref, ((sizes[0] - ahead[0]) % sizes[0], (sizes[1] - ahead[1]) % sizes[1]), sizes)


def steps_of(sizes):
    far = sorted(range(1, sizes[0]), key=lambda seq: -min(seq, sizes[0] - seq))
    subs = range(sizes[1])
    return [(0, 0)] + [(seq, sub) for seq in far for sub in subs] + [(0, sub) for sub in subs if sub]


def slots_of(assign, groups, rows):
    toks = assign.shape[1]
    per_group = CLUSTERS // groups
    member = jnp.where(iota((CLUSTERS, toks), 0) == assign, 1.0, 0.0)
    member_b = member.astype(BF16)
    upto = ones_where(iota((LANES, LANES), 0) <= iota((LANES, LANES), 1))
    counts = jnp.zeros((CLUSTERS, 1), F32)
    running = []
    for first in range(0, toks, LANES):
        within = dot(member_b[:, first : first + LANES], upto)
        running.append(within + counts)
        counts = counts + within[:, LANES - 1 :]
    running = jnp.concatenate(running, axis=1)
    here, other = iota((CLUSTERS, CLUSTERS), 0), iota((CLUSTERS, CLUSTERS), 1)
    group_of = lambda index: lax.div(index, jnp.int32(per_group))
    earlier = ones_where((other < here) & (group_of(other) == group_of(here)))
    base = dot(earlier, jnp.broadcast_to(counts, (CLUSTERS, LANES)).astype(BF16))[:, :1]
    base = base + (group_of(iota((CLUSTERS, 1), 0)) * rows).astype(F32)
    slot = jnp.sum(member * (running - 1.0 + base), axis=0, keepdims=True).astype(jnp.int32)
    spread = jnp.concatenate([member_b, jnp.zeros((LANES - CLUSTERS, toks), BF16)], axis=0)
    return slot, dot_nt(jnp.ones((COUNT_ROWS, toks), BF16), spread).astype(BF16)


def project_query_kernel(sizes, groups, rows, me_ref, assign_ref, tokens_hbm, weight_hbm, cotan_hbm, *rest):
    out_refs, rest = rest[:-10], rest[-10:]
    slot_ref, tokens_ref, weight_ref, cotan_ref, query_ref, pick_ref, part_ref, sorted_ref, in_sems, out_sems = rest
    toks, width = tokens_ref.shape
    heads = weight_ref.shape[1] // HD
    fine = min(256, toks, width)

    def load(kind):
        source, target = ((cotan_hbm, cotan_ref), (weight_hbm, weight_ref), (tokens_hbm, tokens_ref))[kind]
        return [
            pltpu.make_async_copy(
                source.at[pl.ds(row, fine), :], target.at[pl.ds(row, fine), :], in_sems.at[kind, row // fine]
            )
            for row in range(0, source.shape[0], fine)
        ]

    for copy in load(0) + load(1) + load(2):
        copy.start()
    slot, tallies = slots_of(assign_ref[...], groups, rows)
    slot_ref[...] = slot
    for owner in range(sorted_ref.shape[0]):
        sorted_ref[owner, rows:, :] = tallies
    slots = pick_ref.shape[0]
    step = min(512, slots)
    for first in range(0, slots, step):
        pick_ref[first : first + step, :] = ones_where(iota((step, toks), 0) + first == slot)
    for copy in load(0):
        copy.wait()
    for first in range(0, slots, step):
        part_ref[first : first + step, :] = dot(pick_ref[first : first + step, :], cotan_ref[...])
    for copy in load(1):
        copy.wait()
    tokens = load(2)
    for index, first in enumerate(range(0, toks, fine)):
        tokens[index].wait()
        query_ref[first : first + fine, :] = dot(tokens_ref[first : first + fine, :], weight_ref[...]).astype(BF16)
    part = min(512, rows)
    low = low_half((part, LANES))
    for first in range(0, slots, part):
        group, start = first // rows, first % rows
        query = dot(pick_ref[first : first + part, :], query_ref[...])
        for pair in range(heads // 2):
            columns = slice(pair * LANES, (pair + 1) * LANES)
            q_tile, c_tile = query[:, columns], part_ref[first : first + part, columns]
            even = jnp.where(low, q_tile, swap_halves(c_tile)).astype(BF16)
            odd = jnp.where(low, swap_halves(q_tile), c_tile).astype(BF16)
            sorted_ref[group * heads + 2 * pair, start : start + part, :] = even
            sorted_ref[group * heads + 2 * pair + 1, start : start + part, :] = odd
    copies = [
        pltpu.make_async_copy(sorted_ref.at[owner_of(me_ref, ahead, sizes)], out_ref, out_sems.at[k])
        for k, (ahead, out_ref) in enumerate(zip(steps_of(sizes), out_refs))
    ]
    for copy in copies:
        copy.start()
    for copy in copies:
        copy.wait()


def project_value_kernel(groups, rows, slot_ref, tokens_ref, weight_ref, sorted_ref, turned_ref, unsort_ref, value_ref):
    toks = tokens_ref.shape[0]
    heads = weight_ref.shape[1] // HD
    step = min(512, toks)

    @pl.loop(0, toks // step)
    def _(i):
        where = pl.ds(pl.multiple_of(i * step, step), step)
        value_ref[where, :] = dot(tokens_ref[where, :], weight_ref[...]).astype(BF16)

    half = rows // 2
    part = min(256, half)
    pieces = half // part

    @pl.loop(0, groups * pieces)
    def _(i):
        group, piece = lax.div(i, jnp.int32(pieces)), lax.rem(i, jnp.int32(pieces))
        first = pl.multiple_of(piece * part, part)
        index = iota((part, toks), 0) + group * rows + first
        upper = dot(ones_where(index == slot_ref[...]), value_ref[...])
        lower = dot(ones_where(index + half == slot_ref[...]), value_ref[...])
        low = low_half((part, LANES))
        for pair in range(heads // 2):
            up = upper[:, pair * LANES : (pair + 1) * LANES]
            down = lower[:, pair * LANES : (pair + 1) * LANES]
            even = jnp.where(low, up, swap_halves(down)).astype(BF16)
            odd = jnp.where(low, swap_halves(up), down).astype(BF16)
            sorted_ref[group * heads + 2 * pair, pl.ds(first, part), :] = even
            sorted_ref[group * heads + 2 * pair + 1, pl.ds(first, part), :] = odd

    turned_ref[...] = tokens_ref[...].T
    slots = unsort_ref.shape[1]
    part = min(256, slots)
    for i in range(slots // part):
        pick = ones_where(iota((part, toks), 0) + i * part == slot_ref[...])
        unsort_ref[:, i * part : (i + 1) * part] = pick.T


def score(mixed):
    query = jnp.where(low_half(mixed.shape), mixed.astype(F32) * SCALE, 0.0).astype(BF16)
    return dot_nt(query, mixed)


def softmax_turned(scores):
    shape = scores.shape
    seen = iota(shape, 0) <= iota(shape, 1)
    scores = jnp.where(seen, scores, -jnp.inf)
    raised = jnp.exp(scores - jnp.max(scores, axis=0, keepdims=True))
    return raised * (1.0 / jnp.sum(raised, axis=0, keepdims=True))


def for_each_cluster(counts_ref, me_ref, place_ref, owners, per_group, body):
    for source in range(owners):
        place_ref[source] = 0

    def step(cluster, block):
        runs = []
        total = 0
        base = block * BLOCK_ROWS
        for source in range(owners):
            count = counts_ref[source, me_ref[3] + cluster]
            start = place_ref[source]
            runs.append((source, start, base + total))
            place_ref[source] = start + count
            total = total + count
        body(cluster, block, runs, base + total)
        return block + lax.shift_right_logical(total + (BLOCK_ROWS - 1), jnp.int32(7))

    return lax.fori_loop(0, per_group, step, jnp.int32(LEAD * UNROLL))


def gather_blocks(counts_ref, me_ref, place_ref, owners, per_group, slot_rows, wide_ref, block_ref):
    def body(cluster, block, runs, end):
        for source, start, row in runs:
            block_ref[pl.ds(row, slot_rows), :] = wide_ref[source, pl.ds(start, slot_rows), :]
        block_ref[pl.ds(end, BLOCK_ROWS), :] = jnp.zeros((BLOCK_ROWS, LANES), F32)

    blocks = for_each_cluster(counts_ref, me_ref, place_ref, owners, per_group, body)
    spare = pl.ds(pl.multiple_of(blocks * BLOCK_ROWS, BLOCK_ROWS), GROUP_ROWS)
    block_ref[spare, :] = jnp.zeros((GROUP_ROWS, LANES), F32)
    return blocks


def for_each_group(blocks, stages):
    first, second, third = stages
    groups = lax.div(blocks + (UNROLL - 1), jnp.int32(UNROLL))

    def step(i, carry):
        for slot in range(2):
            group = LEAD + 2 * i + slot
            third(group - 2, slot)
            second(group - 1, 1 - slot)
            first(group, slot)
        return carry

    lax.fori_loop(0, lax.shift_right_logical(groups + 1, jnp.int32(1)), step, 0)


def block_rows(group, ahead):
    return pl.ds(pl.multiple_of((group * UNROLL + ahead) * BLOCK_ROWS, BLOCK_ROWS), BLOCK_ROWS)


def tile_rows(ahead):
    return slice(ahead * BLOCK_ROWS, (ahead + 1) * BLOCK_ROWS)


def value_grad_kernel(sizes, per_group, slot_rows, me_ref, *refs):
    owners = sizes[0] * sizes[1]
    mixed_refs, out_refs, rest = refs[:owners], refs[owners : 2 * owners], refs[2 * owners :]
    dense_ref, counts_out_ref, counts_ref, place_ref, wide_ref, block_ref, home_ref = rest[:7]
    score_refs, probs_refs = rest[7:9], rest[9:11]
    half = out_refs[0].shape[0]
    rows = 2 * half
    for ahead, mixed_ref in zip(steps_of(sizes), mixed_refs):
        source = source_of(me_ref, ahead, sizes)
        tail = mixed_ref[rows:, :].astype(F32).astype(jnp.int32)
        counts_out_ref[pl.ds(source, 1), :] = tail[:1, :]
        wide_ref[source, :rows, :] = mixed_ref[:rows, :].astype(F32)
        wide_ref[source, rows:, :] = jnp.zeros((slot_rows, LANES), F32)
    pltpu.sync_copy(counts_out_ref, counts_ref)
    blocks = gather_blocks(counts_ref, me_ref, place_ref, owners, per_group, slot_rows, wide_ref, block_ref)

    def first(group, slot):
        for ahead in range(UNROLL):
            where = block_rows(group, ahead)
            mixed = block_ref[where, :].astype(BF16)
            dense_ref[where, :] = mixed
            score_refs[slot][tile_rows(ahead), :] = score(mixed)

    def second(group, slot):
        for ahead in range(UNROLL):
            tile = tile_rows(ahead)
            probs_refs[slot][tile, :] = softmax_turned(score_refs[slot][tile, :]).astype(BF16)

    def third(group, slot):
        for ahead in range(UNROLL):
            where = block_rows(group, ahead)
            block_ref[where, :] = dot(probs_refs[slot][tile_rows(ahead), :], dense_ref[where, :])

    for_each_group(blocks, (first, second, third))

    def scatter(cluster, block, runs, end):
        for source, start, row in runs:
            wide_ref[source, pl.ds(start, slot_rows), :] = block_ref[pl.ds(row, slot_rows), :]

    for_each_cluster(counts_ref, me_ref, place_ref, owners, per_group, scatter)
    for ahead, out_ref in zip(steps_of(sizes), out_refs):
        source = owner_of(me_ref, ahead, sizes)
        up, down = wide_ref[source, :half, :], wide_ref[source, half:rows, :]
        out_ref[...] = jnp.where(low_half((half, LANES)), swap_halves(up), down).astype(BF16)


def query_grad_kernel(sizes, per_group, slot_rows, me_ref, counts_ref, dense_ref, value_in_ref, *refs):
    owners = sizes[0] * sizes[1]
    out_refs, rest = refs[:owners], refs[owners:]
    place_ref, wide_ref, block_ref, sums_ref, centroid_ref = rest[:5]
    score_refs, grad_probs_refs, both_refs = rest[5:7], rest[7:9], rest[9:11]
    half = value_in_ref.shape[1]
    rows = 2 * half
    for source in range(owners):
        value = value_in_ref[source].astype(F32)
        wide_ref[source, :half, :] = swap_halves(value)
        wide_ref[source, half:rows, :] = value
        wide_ref[source, rows:, :] = jnp.zeros((slot_rows, LANES), F32)
    blocks = gather_blocks(counts_ref, me_ref, place_ref, owners, per_group, slot_rows, wide_ref, block_ref)

    def first(group, slot):
        for ahead in range(UNROLL):
            where, tile = block_rows(group, ahead), tile_rows(ahead)
            mixed = dense_ref[where, :]
            value = block_ref[where, :].astype(BF16)
            cotan = jnp.where(low_half(mixed.shape), jnp.zeros_like(mixed), mixed)
            score_refs[slot][tile, :] = score(mixed)
            grad_probs_refs[slot][tile, :] = dot_nt(value, cotan)

    def second(group, slot):
        for ahead in range(UNROLL):
            tile = tile_rows(ahead)
            probs = softmax_turned(score_refs[slot][tile, :])
            grad_probs = grad_probs_refs[slot][tile, :]
            probs_half = probs.astype(BF16).astype(F32)
            row_dot = jnp.sum(probs_half * grad_probs, axis=0, keepdims=True)
            grad_scores = (probs * (grad_probs - row_dot)).astype(BF16).astype(F32)
            both_refs[slot][tile, :] = (grad_scores + grad_scores.T).astype(BF16)

    def third(group, slot):
        for ahead in range(UNROLL):
            where = block_rows(group, ahead)
            grad = dot(both_refs[slot][tile_rows(ahead), :], dense_ref[where, :]) * SCALE
            grad = grad.astype(BF16).astype(F32)
            block_ref[where, :] = grad
            sums_ref[pl.ds(group * UNROLL + ahead, 1), :] = jnp.sum(grad, axis=0, keepdims=True)

    for_each_group(blocks, (first, second, third))
    most = (owners * slot_rows + BLOCK_ROWS - 1) // BLOCK_ROWS

    def scatter(cluster, block, runs, end):
        total = jnp.zeros((1, LANES), F32)
        for ahead in range(most):
            here = block + ahead
            total = total + jnp.where(here * BLOCK_ROWS < end, sums_ref[pl.ds(here, 1), :], 0.0)
        centroid_ref[pl.ds(cluster, 1), :] = total
        for source, start, row in runs:
            wide_ref[source, pl.ds(start, slot_rows), :] = block_ref[pl.ds(row, slot_rows), :]

    for_each_cluster(counts_ref, me_ref, place_ref, owners, per_group, scatter)
    extra = out_refs[0].shape[0] - half
    centroid = jnp.where(
        low_half((extra, LANES)), centroid_ref[:extra, :], swap_halves(centroid_ref[extra:, :])
    ).astype(BF16)
    for ahead, out_ref in zip(steps_of(sizes), out_refs):
        source = owner_of(me_ref, ahead, sizes)
        up, down = wide_ref[source, :half, :], wide_ref[source, half:rows, :]
        out_ref[:half, :] = jnp.where(low_half((half, LANES)), up, swap_halves(down)).astype(BF16)
        out_ref[half:, :] = centroid


def unfold(home_ref, out_ref, heads, start, half, finish):
    low = low_half((half, LANES))
    for group in range(home_ref.shape[0] // heads):
        first = group * 2 * half
        for pair in range(heads // 2):
            even = home_ref[group * heads + 2 * pair, start : start + half, :].astype(F32)
            odd = home_ref[group * heads + 2 * pair + 1, start : start + half, :].astype(F32)
            columns = slice(pair * LANES, (pair + 1) * LANES)
            out_ref[first : first + half, columns] = finish(jnp.where(low, even, swap_halves(odd)))
            out_ref[first + half : first + 2 * half, columns] = finish(
                jnp.where(low, swap_halves(even), odd)
            )


def to_half(x):
    return x.astype(BF16)


def bring_home(sizes, heads, pieces, unsort_ref, home_ref, sorted_ref, rows_ref):
    for source, piece in pieces:
        home_ref[source] = piece
    half = sorted_ref.shape[0] * heads // (sizes[0] * sizes[1]) // 2
    unfold(home_ref, sorted_ref, heads, 0, half, to_half)
    toks = rows_ref.shape[0]
    step = min(512, toks)

    @pl.loop(0, toks // step)
    def _(i):
        where = pl.ds(pl.multiple_of(i * step, step), step)
        rows_ref[where, :] = dot(unsort_ref[where, :], sorted_ref[...]).astype(BF16)


def weight_partial(sizes, me_ref, turned_ref, rows_ref, whole_ref, sub_refs):
    width = turned_ref.shape[0]
    step = min(512, width)

    @pl.loop(0, width // step)
    def _(i):
        where = pl.ds(pl.multiple_of(i * step, step), step)
        whole_ref[where, :] = dot(turned_ref[where, :], rows_ref[...]).astype(BF16)

    piece = width // (sizes[0] * sizes[1])
    for ahead, sub_ref in enumerate(sub_refs):
        sub = lax.rem(me_ref[1] + ahead, jnp.int32(sizes[1]))
        for seq in range(sizes[0]):
            first = pl.multiple_of((seq * sizes[1] + sub) * piece, piece)
            sub_ref[seq] = whole_ref[pl.ds(first, piece), :]


def value_home_kernel(sizes, heads, me_ref, turned_ref, unsort_ref, *refs):
    part_refs, rows_ref, sub_refs = refs[: -4 - sizes[1]], refs[-4 - sizes[1]], refs[-3 - sizes[1] : -3]
    home_ref, sorted_ref, whole_ref = refs[-3:]
    pieces = [
        (source_of(me_ref, ahead, sizes), part_ref[...]) for ahead, part_ref in zip(steps_of(sizes), part_refs)
    ]
    bring_home(sizes, heads, pieces, unsort_ref, home_ref, sorted_ref, rows_ref)
    weight_partial(sizes, me_ref, turned_ref, rows_ref, whole_ref, sub_refs)


def input_partial(me_ref, ahead, parts, rows_ref, value_rows_ref, w_query_ref, w_value_ref, out_ref):
    toks = rows_ref.shape[0]
    columns = w_query_ref.shape[0] // parts
    step = min(512, toks)
    dest = lax.rem(me_ref[2] + ahead, jnp.int32(parts))
    mine = pl.ds(pl.multiple_of(dest * columns, columns), columns)

    @pl.loop(0, toks // step)
    def _(i):
        where = pl.ds(pl.multiple_of(i * step, step), step)
        total = dot_nt(rows_ref[where, :], w_query_ref[mine, :])
        total = total + dot_nt(value_rows_ref[where, :], w_value_ref[mine, :])
        out_ref[where, :] = total.astype(BF16)


def query_home_kernel(
    sizes, heads, factor, parts, me_ref, unsort_ref, value_rows_ref, w_query_ref, w_value_ref, *refs
):
    part_refs, out_refs, (rows_ref, centroid_ref, home_ref, sorted_ref) = (
        refs[: -3 - parts],
        refs[-3 - parts : -4],
        refs[-4:],
    )
    pieces = [
        (source_of(me_ref, ahead, sizes), part_ref[...]) for ahead, part_ref in zip(steps_of(sizes), part_refs)
    ]
    bring_home(sizes, heads, pieces, unsort_ref, home_ref, sorted_ref, rows_ref)
    half = sorted_ref.shape[0] * heads // (sizes[0] * sizes[1]) // 2
    unfold(home_ref, centroid_ref, heads, half, home_ref.shape[1] - half, lambda x: x * factor)
    for ahead, out_ref in enumerate(out_refs):
        input_partial(me_ref, ahead + 1, parts, rows_ref, value_rows_ref, w_query_ref, w_value_ref, out_ref)


def query_weight_kernel(
    sizes, parts, me_ref, turned_ref, rows_ref, value_rows_ref, w_query_ref, w_value_ref, *refs
):
    sub_refs, out_ref, whole_ref = refs[:-2], refs[-2], refs[-1]
    weight_partial(sizes, me_ref, turned_ref, rows_ref, whole_ref, sub_refs)
    input_partial(me_ref, 0, parts, rows_ref, value_rows_ref, w_query_ref, w_value_ref, out_ref)


def fold_subs_kernel(me_ref, *refs):
    seqs = refs[0].shape[0]
    terms, out_refs = refs[:-seqs], refs[-seqs:]
    for ahead, out_ref in enumerate(out_refs):
        seq = lax.rem(me_ref[0] + ahead, jnp.int32(seqs))
        total = terms[0][seq].astype(F32)
        for term in terms[1:]:
            total = total + term[seq].astype(F32)
        out_ref[...] = total.astype(BF16)


def sum_kernel(*refs):
    total = refs[0][...].astype(F32)
    for ref in refs[1:-1]:
        total = total + ref[...].astype(F32)
    refs[-1][...] = total.astype(refs[-1].dtype)


def call(kernel, outs, inputs, smem=(0,), in_place=(), after=(), scratch=(), flops=0, vmem=24, name=None):
    def body(*refs):
        kernel(*refs[: len(inputs)], *refs[len(inputs) + len(after) :])

    def space(i):
        return pltpu.SMEM if i in smem else pl.ANY if i in in_place else pltpu.VMEM

    specs = [pl.BlockSpec(memory_space=space(i)) for i in range(len(inputs))]
    specs += [pl.BlockSpec(memory_space=pl.ANY)] * len(after)
    moved = sum(x.size * x.dtype.itemsize for x in inputs) + sum(
        x.size * x.dtype.itemsize for x in jax.tree.leaves(outs)
    )
    out_space = lambda x: pl.ANY if in_place and x.dtype == BF16 else pltpu.VMEM
    return pl.pallas_call(
        body,
        out_shape=outs,
        in_specs=specs,
        out_specs=jax.tree.map(lambda x: pl.BlockSpec(memory_space=out_space(x)), outs),
        scratch_shapes=list(scratch),
        compiler_params=pltpu.CompilerParams(vmem_limit_bytes=vmem * 2**20),
        cost_estimate=pl.CostEstimate(flops=flops, bytes_accessed=moved, transcendentals=0),
        name=name,
    )(*inputs, *after)


def exchange(parts, sizes):
    out = []
    for ahead, part in zip(steps_of(sizes), parts):
        moves = [
            (
                seq * sizes[1] + sub,
                (seq + ahead[0]) % sizes[0] * sizes[1] + (sub + ahead[1]) % sizes[1],
            )
            for seq, sub in steps_of(sizes)
        ]
        out.append(part if ahead == (0, 0) else lax.ppermute(part, OWNERS, moves))
    return out


def shift(part, axis, ahead):
    size = lax.axis_size(axis)
    return lax.ppermute(part, axis, [(i, (i + ahead) % size) for i in range(size)])


def pass_round(parts, axis):
    return [parts[0]] + [shift(parts[ahead], axis, ahead) for ahead in range(1, len(parts))]


def fold_subs(me, by_sub, name, after=()):
    seqs, piece, columns = by_sub[0].shape
    return call(
        fold_subs_kernel,
        (jax.ShapeDtypeStruct((piece, columns), BF16),) * seqs,
        (me, *pass_round(by_sub, "sub")),
        after=after,
        name=name,
    )


def all_to_all(rows):
    return lax.all_to_all(rows, OWNERS, split_axis=0, concat_axis=0, tiled=True)


def add_up(terms, dtype, name):
    return call(sum_kernel, jax.ShapeDtypeStruct(terms[0].shape, dtype), tuple(terms), smem=(), name=name)


def on_device(tokens_in, w_query, w_value, cotangent, assignment):
    sizes = (lax.axis_size("seq"), lax.axis_size("sub"))
    owners = sizes[0] * sizes[1]
    parts = lax.axis_size("head")
    toks, width = tokens_in.shape
    width_dev = cotangent.shape[1]
    heads = width_dev // HD
    slot_rows = 2 * toks // CLUSTERS
    assert owners % heads == 0 and heads % 2 == 0
    groups = owners // heads
    per_group = CLUSTERS // groups
    rows = toks if groups == 1 else per_group * slot_rows
    half = rows // 2
    slots = groups * rows
    columns = width // parts
    capacity = (slot_rows * owners + BLOCK_ROWS - 1) // BLOCK_ROWS * BLOCK_ROWS
    extra = max(per_group // 2, 16)
    shape = jax.ShapeDtypeStruct
    seq, sub = lax.axis_index("seq"), lax.axis_index("sub")
    first = lax.div(seq * sizes[1] + sub, jnp.int32(heads)) * per_group
    me = jnp.stack([seq, sub, lax.axis_index("head"), first]).astype(jnp.int32)

    def several(count, *dims):
        return (shape(dims, BF16),) * count

    *send_mixed, slot_row = call(
        functools.partial(project_query_kernel, sizes, groups, rows),
        several(owners, rows + COUNT_ROWS, LANES) + (shape((1, toks), jnp.int32),),
        (me, assignment.reshape(1, toks), tokens_in, w_query, cotangent),
        in_place=(2, 3, 4),
        scratch=[
            pltpu.VMEM((toks, width), BF16),
            pltpu.VMEM((width, width_dev), BF16),
            pltpu.VMEM((toks, width_dev), BF16),
            pltpu.VMEM((toks, width_dev), BF16),
            pltpu.VMEM((slots, toks), BF16),
            pltpu.VMEM((slots, width_dev), F32),
            pltpu.VMEM((owners, rows + COUNT_ROWS, LANES), BF16),
            pltpu.SemaphoreType.DMA((3, max(toks, width) // min(256, toks, width))),
            pltpu.SemaphoreType.DMA((owners,)),
        ],
        flops=2 * toks * width * width_dev + 4 * slots * toks * width_dev,
        vmem=60,
        name="project_query",
    )
    got_mixed = exchange(send_mixed, sizes)
    send_value, turned, unsort = call(
        functools.partial(project_value_kernel, groups, rows),
        several(1, owners, half, LANES) + several(1, width, toks) + several(1, toks, slots),
        (slot_row, tokens_in, w_value),
        smem=(),
        scratch=[pltpu.VMEM((toks, width_dev), BF16)],
        flops=2 * toks * width * width_dev + 2 * slots * toks * width_dev,
        name="project_value",
    )
    send_value, _ = lax.optimization_barrier((send_value, got_mixed[1:4]))
    got_value = all_to_all(send_value)
    blocks = per_group * capacity // BLOCK_ROWS
    held = blocks + (LEAD + 4) * UNROLL
    block_flops = 2 * BLOCK_ROWS * BLOCK_ROWS * LANES
    tall = pltpu.VMEM((owners, rows + slot_rows, LANES), F32)
    dense_rows = pltpu.VMEM((held * BLOCK_ROWS, LANES), F32)
    group_f32 = pltpu.VMEM((GROUP_ROWS, BLOCK_ROWS), F32)
    group_b16 = pltpu.VMEM((GROUP_ROWS, BLOCK_ROWS), BF16)
    place = pltpu.SMEM((owners,), jnp.int32)
    *back_value, dense, counts = call(
        functools.partial(value_grad_kernel, sizes, per_group, slot_rows),
        several(owners, half, LANES)
        + several(1, held * BLOCK_ROWS, LANES)
        + (shape((owners, LANES), jnp.int32),),
        (me, *got_mixed),
        after=[unsort],
        scratch=[pltpu.SMEM((owners, LANES), jnp.int32), place, tall, dense_rows, tall]
        + [group_f32] * 2
        + [group_b16] * 2,
        flops=4 * blocks * block_flops,
        vmem=48,
        name="value_grad",
    )
    home_value = exchange(back_value, sizes)
    back_query = call(
        functools.partial(query_grad_kernel, sizes, per_group, slot_rows),
        several(owners, half + extra, LANES),
        (me, counts, dense, got_value),
        smem=(0, 1),
        scratch=[place, tall, dense_rows, pltpu.VMEM((held, LANES), F32), pltpu.VMEM((2 * extra, LANES), F32)]
        + [group_f32] * 4
        + [group_b16] * 2,
        flops=6 * blocks * block_flops,
        vmem=48,
        name="query_grad",
    )
    home_query = exchange(back_query, sizes)
    weight_flops = 2 * toks * width * width_dev
    home_flops = 2 * slots * toks * width_dev
    sub_shapes = several(sizes[1], sizes[0], width // owners, width_dev)
    whole = pltpu.VMEM((width, width_dev), BF16)
    sorted_rows = pltpu.VMEM((slots, width_dev), BF16)
    value_rows, *value_weight = call(
        functools.partial(value_home_kernel, sizes, heads),
        several(1, toks, width_dev) + sub_shapes,
        (me, turned, unsort, *home_value),
        after=back_query[:1],
        scratch=[pltpu.VMEM((owners, half, LANES), BF16), sorted_rows, whole],
        flops=weight_flops + home_flops,
        name="value_home",
    )
    value_weight = fold_subs(me, value_weight, "value_subs")
    *partials, query_rows, centroid_grad = call(
        functools.partial(query_home_kernel, sizes, heads, (CLUSTERS / (toks * owners)) ** 0.5, parts),
        several(parts - 1, toks, columns)
        + several(1, toks, width_dev)
        + (shape((groups * 2 * extra, width_dev), F32),),
        (me, unsort, value_rows, w_query, w_value, *home_query),
        after=value_weight,
        scratch=[pltpu.VMEM((owners, half + extra, LANES), BF16), sorted_rows],
        flops=weight_flops + home_flops,
        name="query_home",
    )
    arrived = [shift(partial, "head", k + 1) for k, partial in enumerate(partials)]
    value_weight, _ = lax.optimization_barrier((value_weight, home_query))
    value_weight = pass_round(value_weight, "seq")
    *query_weight, own = call(
        functools.partial(query_weight_kernel, sizes, parts),
        sub_shapes + several(1, toks, columns),
        (me, turned, query_rows, value_rows, w_query, w_value),
        scratch=[whole],
        flops=2 * weight_flops,
        name="query_weight",
    )
    query_weight = pass_round(fold_subs(me, query_weight, "query_subs"), "seq")
    grad_wv = add_up(value_weight, F32, "value_sum")
    grad_wq = add_up(query_weight, F32, "query_sum")
    grad_input = add_up([own] + arrived, BF16, "input_sum")
    if groups > 1:
        centroid_grad = centroid_grad.reshape(groups, 2 * extra, width_dev)[:, :per_group]
        centroid_grad = centroid_grad.reshape(CLUSTERS, width_dev)
    return (grad_input, grad_wq, grad_wv, centroid_grad)


def solution(mesh):
    return jax.shard_map(
        on_device,
        mesh=mesh,
        in_specs=(
            P(("grp", "seq", "sub"), None),
            P(None, "head"),
            P(None, "head"),
            P(("grp", "seq", "sub"), "head"),
            P(("grp", "seq", "sub"), None),
        ),
        out_specs=(
            P(("grp", "seq", "sub"), "head"),
            P(("grp", "seq", "sub"), "head"),
            P(("grp", "seq", "sub"), "head"),
            P("grp", "head"),
        ),
        check_vma=False,
    )
```

```python
import functools

import jax
import jax.numpy as jnp
from jax import lax
from jax.experimental import pallas as pl
from jax.experimental.pallas import tpu as pltpu
from jax.sharding import PartitionSpec as P

HD = 64
CLUSTERS = 64
BLOCK_ROWS = 128
LANES = 128
UNROLL = 4
COUNT_ROWS = 16
SCALE = 0.5 * HD ** (-0.5)
F32 = jnp.float32
BF16 = jnp.bfloat16
OWNERS = ("seq", "sub")
GROUP_ROWS = UNROLL * BLOCK_ROWS
LEAD = 2


def iota(shape, dim):
    return lax.broadcasted_iota(jnp.int32, shape, dim)


def low_half(shape):
    return iota(shape, 1) < HD


def swap_halves(tile):
    return pltpu.roll(tile, HD, 1)


def dot(a, b):
    return jnp.dot(a, b, preferred_element_type=F32)


def dot_nt(a, b):
    return lax.dot_general(a, b, (((1,), (1,)), ((), ())), preferred_element_type=F32)


def ones_where(condition):
    return jnp.where(condition, 1.0, 0.0).astype(BF16)


def owner_of(me_ref, ahead, sizes):
    seq = lax.rem(me_ref[0] + ahead[0], jnp.int32(sizes[0]))
    sub = lax.rem(me_ref[1] + ahead[1], jnp.int32(sizes[1]))
    return seq * sizes[1] + sub


def source_of(me_ref, ahead, sizes):
    return owner_of(me_ref, ((sizes[0] - ahead[0]) % sizes[0], (sizes[1] - ahead[1]) % sizes[1]), sizes)


def steps_of(sizes):
    far = sorted(range(1, sizes[0]), key=lambda seq: -min(seq, sizes[0] - seq))
    subs = range(sizes[1])
    return [(0, 0)] + [(seq, sub) for seq in far for sub in subs] + [(0, sub) for sub in subs if sub]


def hand_out(by_owner_ref, out_refs, me_ref, sizes):
    for ahead, out_ref in zip(steps_of(sizes), out_refs):
        out_ref[...] = by_owner_ref[owner_of(me_ref, ahead, sizes)]


def slots_of(assign, groups, rows):
    toks = assign.shape[1]
    per_group = CLUSTERS // groups
    member = jnp.where(iota((CLUSTERS, toks), 0) == assign, 1.0, 0.0)
    member_b = member.astype(BF16)
    upto = ones_where(iota((LANES, LANES), 0) <= iota((LANES, LANES), 1))
    counts = jnp.zeros((CLUSTERS, 1), F32)
    running = []
    for first in range(0, toks, LANES):
        within = dot(member_b[:, first : first + LANES], upto)
        running.append(within + counts)
        counts = counts + within[:, LANES - 1 :]
    running = jnp.concatenate(running, axis=1)
    here, other = iota((CLUSTERS, CLUSTERS), 0), iota((CLUSTERS, CLUSTERS), 1)
    group_of = lambda index: lax.div(index, jnp.int32(per_group))
    earlier = ones_where((other < here) & (group_of(other) == group_of(here)))
    base = dot(earlier, jnp.broadcast_to(counts, (CLUSTERS, LANES)).astype(BF16))[:, :1]
    base = base + (group_of(iota((CLUSTERS, 1), 0)) * rows).astype(F32)
    slot = jnp.sum(member * (running - 1.0 + base), axis=0, keepdims=True).astype(jnp.int32)
    spread = jnp.concatenate([member_b, jnp.zeros((LANES - CLUSTERS, toks), BF16)], axis=0)
    return slot, dot_nt(jnp.ones((COUNT_ROWS, toks), BF16), spread).astype(BF16)


def project_query_kernel(sizes, groups, rows, me_ref, assign_ref, tokens_hbm, weight_hbm, cotan_hbm, *rest):
    out_refs, rest = rest[:-10], rest[-10:]
    slot_ref, tokens_ref, weight_ref, cotan_ref, query_ref, pick_ref, part_ref, sorted_ref, in_sems, out_sems = rest
    toks, width = tokens_ref.shape
    heads = weight_ref.shape[1] // HD
    fine = min(256, toks, width)

    def load(kind):
        source, target = ((cotan_hbm, cotan_ref), (weight_hbm, weight_ref), (tokens_hbm, tokens_ref))[kind]
        return [
            pltpu.make_async_copy(
                source.at[pl.ds(row, fine), :], target.at[pl.ds(row, fine), :], in_sems.at[kind, row // fine]
            )
            for row in range(0, source.shape[0], fine)
        ]

    for copy in load(0) + load(1) + load(2):
        copy.start()
    slot, tallies = slots_of(assign_ref[...], groups, rows)
    slot_ref[...] = slot
    for owner in range(sorted_ref.shape[0]):
        sorted_ref[owner, rows:, :] = tallies
    slots = pick_ref.shape[0]
    step = min(512, slots)
    for first in range(0, slots, step):
        pick_ref[first : first + step, :] = ones_where(iota((step, toks), 0) + first == slot)
    for copy in load(0):
        copy.wait()
    for first in range(0, slots, step):
        part_ref[first : first + step, :] = dot(pick_ref[first : first + step, :], cotan_ref[...])
    for copy in load(1):
        copy.wait()
    tokens = load(2)
    for index, first in enumerate(range(0, toks, fine)):
        tokens[index].wait()
        query_ref[first : first + fine, :] = dot(tokens_ref[first : first + fine, :], weight_ref[...]).astype(BF16)
    part = min(512, rows)
    low = low_half((part, LANES))
    for first in range(0, slots, part):
        group, start = first // rows, first % rows
        query = dot(pick_ref[first : first + part, :], query_ref[...])
        for pair in range(heads // 2):
            columns = slice(pair * LANES, (pair + 1) * LANES)
            q_tile, c_tile = query[:, columns], part_ref[first : first + part, columns]
            even = jnp.where(low, q_tile, swap_halves(c_tile)).astype(BF16)
            odd = jnp.where(low, swap_halves(q_tile), c_tile).astype(BF16)
            sorted_ref[group * heads + 2 * pair, start : start + part, :] = even
            sorted_ref[group * heads + 2 * pair + 1, start : start + part, :] = odd
    copies = [
        pltpu.make_async_copy(sorted_ref.at[owner_of(me_ref, ahead, sizes)], out_ref, out_sems.at[k])
        for k, (ahead, out_ref) in enumerate(zip(steps_of(sizes), out_refs))
    ]
    for copy in copies:
        copy.start()
    for copy in copies:
        copy.wait()


def project_value_kernel(sizes, groups, rows, me_ref, slot_ref, tokens_ref, weight_ref, *rest):
    out_refs, (turned_ref, unsort_ref, value_ref, sorted_ref) = rest[:-4], rest[-4:]
    toks = tokens_ref.shape[0]
    heads = weight_ref.shape[1] // HD
    step = min(512, toks)

    @pl.loop(0, toks // step)
    def _(i):
        where = pl.ds(pl.multiple_of(i * step, step), step)
        value_ref[where, :] = dot(tokens_ref[where, :], weight_ref[...]).astype(BF16)

    half = rows // 2
    part = min(256, half)
    pieces = half // part

    @pl.loop(0, groups * pieces)
    def _(i):
        group, piece = lax.div(i, jnp.int32(pieces)), lax.rem(i, jnp.int32(pieces))
        first = pl.multiple_of(piece * part, part)
        index = iota((part, toks), 0) + group * rows + first
        upper = dot(ones_where(index == slot_ref[...]), value_ref[...])
        lower = dot(ones_where(index + half == slot_ref[...]), value_ref[...])
        low = low_half((part, LANES))
        for pair in range(heads // 2):
            up = upper[:, pair * LANES : (pair + 1) * LANES]
            down = lower[:, pair * LANES : (pair + 1) * LANES]
            even = jnp.where(low, up, swap_halves(down)).astype(BF16)
            odd = jnp.where(low, swap_halves(up), down).astype(BF16)
            sorted_ref[group * heads + 2 * pair, pl.ds(first, part), :] = even
            sorted_ref[group * heads + 2 * pair + 1, pl.ds(first, part), :] = odd

    hand_out(sorted_ref, out_refs, me_ref, sizes)
    turned_ref[...] = tokens_ref[...].T
    slots = unsort_ref.shape[1]
    part = min(256, slots)
    for i in range(slots // part):
        pick = ones_where(iota((part, toks), 0) + i * part == slot_ref[...])
        unsort_ref[:, i * part : (i + 1) * part] = pick.T


def score(mixed):
    query = jnp.where(low_half(mixed.shape), mixed.astype(F32) * SCALE, 0.0).astype(BF16)
    return dot_nt(query, mixed)


def softmax_turned(scores):
    shape = scores.shape
    seen = iota(shape, 0) <= iota(shape, 1)
    scores = jnp.where(seen, scores, -jnp.inf)
    raised = jnp.exp(scores - jnp.max(scores, axis=0, keepdims=True))
    return raised * (1.0 / jnp.sum(raised, axis=0, keepdims=True))


def for_each_cluster(counts_ref, me_ref, place_ref, owners, per_group, body):
    for source in range(owners):
        place_ref[source] = 0

    def step(cluster, block):
        runs = []
        total = 0
        base = block * BLOCK_ROWS
        for source in range(owners):
            count = counts_ref[source, me_ref[3] + cluster]
            start = place_ref[source]
            runs.append((source, start, base + total))
            place_ref[source] = start + count
            total = total + count
        body(cluster, block, runs, base + total)
        return block + lax.shift_right_logical(total + (BLOCK_ROWS - 1), jnp.int32(7))

    return lax.fori_loop(0, per_group, step, jnp.int32(LEAD * UNROLL))


def gather_blocks(counts_ref, me_ref, place_ref, owners, per_group, slot_rows, wide_ref, block_ref):
    def body(cluster, block, runs, end):
        for source, start, row in runs:
            block_ref[pl.ds(row, slot_rows), :] = wide_ref[source, pl.ds(start, slot_rows), :]
        block_ref[pl.ds(end, BLOCK_ROWS), :] = jnp.zeros((BLOCK_ROWS, LANES), F32)

    blocks = for_each_cluster(counts_ref, me_ref, place_ref, owners, per_group, body)
    spare = pl.ds(pl.multiple_of(blocks * BLOCK_ROWS, BLOCK_ROWS), GROUP_ROWS)
    block_ref[spare, :] = jnp.zeros((GROUP_ROWS, LANES), F32)
    return blocks


def for_each_group(blocks, stages):
    first, second, third = stages
    groups = lax.div(blocks + (UNROLL - 1), jnp.int32(UNROLL))

    def step(i, carry):
        for slot in range(2):
            group = LEAD + 2 * i + slot
            third(group - 2, slot)
            second(group - 1, 1 - slot)
            first(group, slot)
        return carry

    lax.fori_loop(0, lax.shift_right_logical(groups + 1, jnp.int32(1)), step, 0)


def block_rows(group, ahead):
    return pl.ds(pl.multiple_of((group * UNROLL + ahead) * BLOCK_ROWS, BLOCK_ROWS), BLOCK_ROWS)


def tile_rows(ahead):
    return slice(ahead * BLOCK_ROWS, (ahead + 1) * BLOCK_ROWS)


def value_grad_kernel(sizes, per_group, slot_rows, me_ref, *refs):
    owners = sizes[0] * sizes[1]
    mixed_refs, out_refs, rest = refs[:owners], refs[owners : 2 * owners], refs[2 * owners :]
    dense_ref, counts_out_ref, counts_ref, place_ref, wide_ref, block_ref, home_ref = rest[:7]
    score_refs, probs_refs = rest[7:9], rest[9:11]
    half = out_refs[0].shape[0]
    rows = 2 * half
    for ahead, mixed_ref in zip(steps_of(sizes), mixed_refs):
        source = source_of(me_ref, ahead, sizes)
        tail = mixed_ref[rows:, :].astype(F32).astype(jnp.int32)
        counts_out_ref[pl.ds(source, 1), :] = tail[:1, :]
        wide_ref[source, :rows, :] = mixed_ref[:rows, :].astype(F32)
        wide_ref[source, rows:, :] = jnp.zeros((slot_rows, LANES), F32)
    pltpu.sync_copy(counts_out_ref, counts_ref)
    blocks = gather_blocks(counts_ref, me_ref, place_ref, owners, per_group, slot_rows, wide_ref, block_ref)

    def first(group, slot):
        for ahead in range(UNROLL):
            where = block_rows(group, ahead)
            mixed = block_ref[where, :].astype(BF16)
            dense_ref[where, :] = mixed
            score_refs[slot][tile_rows(ahead), :] = score(mixed)

    def second(group, slot):
        for ahead in range(UNROLL):
            tile = tile_rows(ahead)
            probs_refs[slot][tile, :] = softmax_turned(score_refs[slot][tile, :]).astype(BF16)

    def third(group, slot):
        for ahead in range(UNROLL):
            where = block_rows(group, ahead)
            block_ref[where, :] = dot(probs_refs[slot][tile_rows(ahead), :], dense_ref[where, :])

    for_each_group(blocks, (first, second, third))

    def scatter(cluster, block, runs, end):
        for source, start, row in runs:
            wide_ref[source, pl.ds(start, slot_rows), :] = block_ref[pl.ds(row, slot_rows), :]

    for_each_cluster(counts_ref, me_ref, place_ref, owners, per_group, scatter)
    for ahead, out_ref in zip(steps_of(sizes), out_refs):
        source = owner_of(me_ref, ahead, sizes)
        up, down = wide_ref[source, :half, :], wide_ref[source, half:rows, :]
        out_ref[...] = jnp.where(low_half((half, LANES)), swap_halves(up), down).astype(BF16)


def query_grad_kernel(sizes, per_group, slot_rows, me_ref, counts_ref, dense_ref, *refs):
    owners = sizes[0] * sizes[1]
    value_refs, out_refs, rest = refs[:owners], refs[owners : 2 * owners], refs[2 * owners :]
    place_ref, wide_ref, block_ref, sums_ref, centroid_ref = rest[:5]
    score_refs, grad_probs_refs, both_refs = rest[5:7], rest[7:9], rest[9:11]
    half = value_refs[0].shape[0]
    rows = 2 * half
    for ahead, value_ref in zip(steps_of(sizes), value_refs):
        source = source_of(me_ref, ahead, sizes)
        value = value_ref[...].astype(F32)
        wide_ref[source, :half, :] = swap_halves(value)
        wide_ref[source, half:rows, :] = value
        wide_ref[source, rows:, :] = jnp.zeros((slot_rows, LANES), F32)
    blocks = gather_blocks(counts_ref, me_ref, place_ref, owners, per_group, slot_rows, wide_ref, block_ref)

    def first(group, slot):
        for ahead in range(UNROLL):
            where, tile = block_rows(group, ahead), tile_rows(ahead)
            mixed = dense_ref[where, :]
            value = block_ref[where, :].astype(BF16)
            cotan = jnp.where(low_half(mixed.shape), jnp.zeros_like(mixed), mixed)
            score_refs[slot][tile, :] = score(mixed)
            grad_probs_refs[slot][tile, :] = dot_nt(value, cotan)

    def second(group, slot):
        for ahead in range(UNROLL):
            tile = tile_rows(ahead)
            probs = softmax_turned(score_refs[slot][tile, :])
            grad_probs = grad_probs_refs[slot][tile, :]
            probs_half = probs.astype(BF16).astype(F32)
            row_dot = jnp.sum(probs_half * grad_probs, axis=0, keepdims=True)
            grad_scores = (probs * (grad_probs - row_dot)).astype(BF16).astype(F32)
            both_refs[slot][tile, :] = (grad_scores + grad_scores.T).astype(BF16)

    def third(group, slot):
        for ahead in range(UNROLL):
            where = block_rows(group, ahead)
            grad = dot(both_refs[slot][tile_rows(ahead), :], dense_ref[where, :]) * SCALE
            grad = grad.astype(BF16).astype(F32)
            block_ref[where, :] = grad
            sums_ref[pl.ds(group * UNROLL + ahead, 1), :] = jnp.sum(grad, axis=0, keepdims=True)

    for_each_group(blocks, (first, second, third))
    most = (owners * slot_rows + BLOCK_ROWS - 1) // BLOCK_ROWS

    def scatter(cluster, block, runs, end):
        total = jnp.zeros((1, LANES), F32)
        for ahead in range(most):
            here = block + ahead
            total = total + jnp.where(here * BLOCK_ROWS < end, sums_ref[pl.ds(here, 1), :], 0.0)
        centroid_ref[pl.ds(cluster, 1), :] = total
        for source, start, row in runs:
            wide_ref[source, pl.ds(start, slot_rows), :] = block_ref[pl.ds(row, slot_rows), :]

    for_each_cluster(counts_ref, me_ref, place_ref, owners, per_group, scatter)
    extra = out_refs[0].shape[0] - half
    centroid = jnp.where(
        low_half((extra, LANES)), centroid_ref[:extra, :], swap_halves(centroid_ref[extra:, :])
    ).astype(BF16)
    for ahead, out_ref in zip(steps_of(sizes), out_refs):
        source = owner_of(me_ref, ahead, sizes)
        up, down = wide_ref[source, :half, :], wide_ref[source, half:rows, :]
        out_ref[:half, :] = jnp.where(low_half((half, LANES)), up, swap_halves(down)).astype(BF16)
        out_ref[half:, :] = centroid


def unfold(home_ref, out_ref, heads, start, half, finish):
    low = low_half((half, LANES))
    for group in range(home_ref.shape[0] // heads):
        first = group * 2 * half
        for pair in range(heads // 2):
            even = home_ref[group * heads + 2 * pair, start : start + half, :].astype(F32)
            odd = home_ref[group * heads + 2 * pair + 1, start : start + half, :].astype(F32)
            columns = slice(pair * LANES, (pair + 1) * LANES)
            out_ref[first : first + half, columns] = finish(jnp.where(low, even, swap_halves(odd)))
            out_ref[first + half : first + 2 * half, columns] = finish(
                jnp.where(low, swap_halves(even), odd)
            )


def to_half(x):
    return x.astype(BF16)


def bring_home(sizes, heads, me_ref, part_refs, unsort_ref, home_ref, sorted_ref, rows_ref):
    for ahead, part_ref in zip(steps_of(sizes), part_refs):
        home_ref[source_of(me_ref, ahead, sizes)] = part_ref[...]
    half = sorted_ref.shape[0] * heads // (sizes[0] * sizes[1]) // 2
    unfold(home_ref, sorted_ref, heads, 0, half, to_half)
    toks = rows_ref.shape[0]
    step = min(512, toks)

    @pl.loop(0, toks // step)
    def _(i):
        where = pl.ds(pl.multiple_of(i * step, step), step)
        rows_ref[where, :] = dot(unsort_ref[where, :], sorted_ref[...]).astype(BF16)


def weight_partial(sizes, me_ref, turned_ref, rows_ref, whole_ref, sub_refs):
    width = turned_ref.shape[0]
    step = min(512, width)

    @pl.loop(0, width // step)
    def _(i):
        where = pl.ds(pl.multiple_of(i * step, step), step)
        whole_ref[where, :] = dot(turned_ref[where, :], rows_ref[...]).astype(BF16)

    piece = width // (sizes[0] * sizes[1])
    for ahead, sub_ref in enumerate(sub_refs):
        sub = lax.rem(me_ref[1] + ahead, jnp.int32(sizes[1]))
        for seq in range(sizes[0]):
            first = pl.multiple_of((seq * sizes[1] + sub) * piece, piece)
            sub_ref[seq] = whole_ref[pl.ds(first, piece), :]


def value_home_kernel(sizes, heads, me_ref, turned_ref, unsort_ref, *refs):
    part_refs, rows_ref, sub_refs = refs[: -4 - sizes[1]], refs[-4 - sizes[1]], refs[-3 - sizes[1] : -3]
    home_ref, sorted_ref, whole_ref = refs[-3:]
    bring_home(sizes, heads, me_ref, part_refs, unsort_ref, home_ref, sorted_ref, rows_ref)
    weight_partial(sizes, me_ref, turned_ref, rows_ref, whole_ref, sub_refs)


def input_partial(me_ref, ahead, parts, rows_ref, value_rows_ref, w_query_ref, w_value_ref, out_ref):
    toks = rows_ref.shape[0]
    columns = w_query_ref.shape[0] // parts
    step = min(512, toks)
    dest = lax.rem(me_ref[2] + ahead, jnp.int32(parts))
    mine = pl.ds(pl.multiple_of(dest * columns, columns), columns)

    @pl.loop(0, toks // step)
    def _(i):
        where = pl.ds(pl.multiple_of(i * step, step), step)
        total = dot_nt(rows_ref[where, :], w_query_ref[mine, :])
        total = total + dot_nt(value_rows_ref[where, :], w_value_ref[mine, :])
        out_ref[where, :] = total.astype(BF16)


def query_home_kernel(
    sizes, heads, factor, parts, me_ref, unsort_ref, value_rows_ref, w_query_ref, w_value_ref, *refs
):
    part_refs, out_refs, (rows_ref, centroid_ref, home_ref, sorted_ref) = (
        refs[: -3 - parts],
        refs[-3 - parts : -4],
        refs[-4:],
    )
    bring_home(sizes, heads, me_ref, part_refs, unsort_ref, home_ref, sorted_ref, rows_ref)
    half = sorted_ref.shape[0] * heads // (sizes[0] * sizes[1]) // 2
    unfold(home_ref, centroid_ref, heads, half, home_ref.shape[1] - half, lambda x: x * factor)
    for ahead, out_ref in enumerate(out_refs):
        input_partial(me_ref, ahead + 1, parts, rows_ref, value_rows_ref, w_query_ref, w_value_ref, out_ref)


def query_weight_kernel(sizes, me_ref, turned_ref, rows_ref, *refs):
    weight_partial(sizes, me_ref, turned_ref, rows_ref, refs[-1], refs[:-1])


def input_own_kernel(parts, me_ref, *refs):
    input_partial(me_ref, 0, parts, *refs)


def fold_subs_kernel(me_ref, *refs):
    seqs = refs[0].shape[0]
    terms, out_refs = refs[:-seqs], refs[-seqs:]
    for ahead, out_ref in enumerate(out_refs):
        seq = lax.rem(me_ref[0] + ahead, jnp.int32(seqs))
        total = terms[0][seq].astype(F32)
        for term in terms[1:]:
            total = total + term[seq].astype(F32)
        out_ref[...] = total.astype(BF16)


def sum_kernel(*refs):
    total = refs[0][...].astype(F32)
    for ref in refs[1:-1]:
        total = total + ref[...].astype(F32)
    refs[-1][...] = total.astype(refs[-1].dtype)


def call(kernel, outs, inputs, smem=(0,), in_place=(), after=(), scratch=(), flops=0, vmem=24, name=None):
    def body(*refs):
        kernel(*refs[: len(inputs)], *refs[len(inputs) + len(after) :])

    def space(i):
        return pltpu.SMEM if i in smem else pl.ANY if i in in_place else pltpu.VMEM

    specs = [pl.BlockSpec(memory_space=space(i)) for i in range(len(inputs))]
    specs += [pl.BlockSpec(memory_space=pl.ANY)] * len(after)
    moved = sum(x.size * x.dtype.itemsize for x in inputs) + sum(
        x.size * x.dtype.itemsize for x in jax.tree.leaves(outs)
    )
    out_space = lambda x: pl.ANY if in_place and x.dtype == BF16 else pltpu.VMEM
    return pl.pallas_call(
        body,
        out_shape=outs,
        in_specs=specs,
        out_specs=jax.tree.map(lambda x: pl.BlockSpec(memory_space=out_space(x)), outs),
        scratch_shapes=list(scratch),
        compiler_params=pltpu.CompilerParams(vmem_limit_bytes=vmem * 2**20),
        cost_estimate=pl.CostEstimate(flops=flops, bytes_accessed=moved, transcendentals=0),
        name=name,
    )(*inputs, *after)


def exchange(parts, sizes):
    out = []
    for ahead, part in zip(steps_of(sizes), parts):
        moves = [
            (
                seq * sizes[1] + sub,
                (seq + ahead[0]) % sizes[0] * sizes[1] + (sub + ahead[1]) % sizes[1],
            )
            for seq, sub in steps_of(sizes)
        ]
        out.append(part if ahead == (0, 0) else lax.ppermute(part, OWNERS, moves))
    return out


def shift(part, axis, ahead):
    size = lax.axis_size(axis)
    return lax.ppermute(part, axis, [(i, (i + ahead) % size) for i in range(size)])


def pass_round(parts, axis):
    return [parts[0]] + [shift(parts[ahead], axis, ahead) for ahead in range(1, len(parts))]


def fold_subs(me, by_sub, name):
    seqs, piece, columns = by_sub[0].shape
    return call(
        fold_subs_kernel,
        (jax.ShapeDtypeStruct((piece, columns), BF16),) * seqs,
        (me, *pass_round(by_sub, "sub")),
        name=name,
    )


def add_up(terms, dtype, name):
    return call(sum_kernel, jax.ShapeDtypeStruct(terms[0].shape, dtype), tuple(terms), smem=(), name=name)


def on_device(tokens_in, w_query, w_value, cotangent, assignment):
    sizes = (lax.axis_size("seq"), lax.axis_size("sub"))
    owners = sizes[0] * sizes[1]
    parts = lax.axis_size("head")
    toks, width = tokens_in.shape
    width_dev = cotangent.shape[1]
    heads = width_dev // HD
    slot_rows = 2 * toks // CLUSTERS
    assert owners % heads == 0 and heads % 2 == 0
    groups = owners // heads
    per_group = CLUSTERS // groups
    rows = toks if groups == 1 else per_group * slot_rows
    half = rows // 2
    slots = groups * rows
    columns = width // parts
    capacity = (slot_rows * owners + BLOCK_ROWS - 1) // BLOCK_ROWS * BLOCK_ROWS
    extra = max(per_group // 2, 16)
    shape = jax.ShapeDtypeStruct
    seq, sub = lax.axis_index("seq"), lax.axis_index("sub")
    first = lax.div(seq * sizes[1] + sub, jnp.int32(heads)) * per_group
    me = jnp.stack([seq, sub, lax.axis_index("head"), first]).astype(jnp.int32)

    def several(count, *dims):
        return (shape(dims, BF16),) * count

    *send_mixed, slot_row = call(
        functools.partial(project_query_kernel, sizes, groups, rows),
        several(owners, rows + COUNT_ROWS, LANES) + (shape((1, toks), jnp.int32),),
        (me, assignment.reshape(1, toks), tokens_in, w_query, cotangent),
        in_place=(2, 3, 4),
        scratch=[
            pltpu.VMEM((toks, width), BF16),
            pltpu.VMEM((width, width_dev), BF16),
            pltpu.VMEM((toks, width_dev), BF16),
            pltpu.VMEM((toks, width_dev), BF16),
            pltpu.VMEM((slots, toks), BF16),
            pltpu.VMEM((slots, width_dev), F32),
            pltpu.VMEM((owners, rows + COUNT_ROWS, LANES), BF16),
            pltpu.SemaphoreType.DMA((3, max(toks, width) // min(256, toks, width))),
            pltpu.SemaphoreType.DMA((owners,)),
        ],
        flops=2 * toks * width * width_dev + 4 * slots * toks * width_dev,
        vmem=60,
        name="project_query",
    )
    got_mixed = exchange(send_mixed, sizes)
    *send_value, turned, unsort = call(
        functools.partial(project_value_kernel, sizes, groups, rows),
        several(owners, half, LANES) + several(1, width, toks) + several(1, toks, slots),
        (me, slot_row, tokens_in, w_value),
        scratch=[pltpu.VMEM((toks, width_dev), BF16), pltpu.VMEM((owners, half, LANES), BF16)],
        flops=2 * toks * width * width_dev + 2 * slots * toks * width_dev,
        name="project_value",
    )
    got_value = exchange(send_value, sizes)
    blocks = per_group * capacity // BLOCK_ROWS
    held = blocks + (LEAD + 4) * UNROLL
    block_flops = 2 * BLOCK_ROWS * BLOCK_ROWS * LANES
    tall = pltpu.VMEM((owners, rows + slot_rows, LANES), F32)
    dense_rows = pltpu.VMEM((held * BLOCK_ROWS, LANES), F32)
    group_f32 = pltpu.VMEM((GROUP_ROWS, BLOCK_ROWS), F32)
    group_b16 = pltpu.VMEM((GROUP_ROWS, BLOCK_ROWS), BF16)
    place = pltpu.SMEM((owners,), jnp.int32)
    *back_value, dense, counts = call(
        functools.partial(value_grad_kernel, sizes, per_group, slot_rows),
        several(owners, half, LANES)
        + several(1, held * BLOCK_ROWS, LANES)
        + (shape((owners, LANES), jnp.int32),),
        (me, *got_mixed),
        scratch=[pltpu.SMEM((owners, LANES), jnp.int32), place, tall, dense_rows, tall]
        + [group_f32] * 2
        + [group_b16] * 2,
        flops=4 * blocks * block_flops,
        vmem=48,
        name="value_grad",
    )
    home_value = exchange(back_value, sizes)
    back_query = call(
        functools.partial(query_grad_kernel, sizes, per_group, slot_rows),
        several(owners, half + extra, LANES),
        (me, counts, dense, *got_value),
        smem=(0, 1),
        scratch=[place, tall, dense_rows, pltpu.VMEM((held, LANES), F32), pltpu.VMEM((2 * extra, LANES), F32)]
        + [group_f32] * 4
        + [group_b16] * 2,
        flops=6 * blocks * block_flops,
        vmem=48,
        name="query_grad",
    )
    home_query = exchange(back_query, sizes)
    weight_flops = 2 * toks * width * width_dev
    home_flops = 2 * slots * toks * width_dev
    sub_shapes = several(sizes[1], sizes[0], width // owners, width_dev)
    whole = pltpu.VMEM((width, width_dev), BF16)
    sorted_rows = pltpu.VMEM((slots, width_dev), BF16)
    value_rows, *value_weight = call(
        functools.partial(value_home_kernel, sizes, heads),
        several(1, toks, width_dev) + sub_shapes,
        (me, turned, unsort, *home_value),
        scratch=[pltpu.VMEM((owners, half, LANES), BF16), sorted_rows, whole],
        flops=weight_flops + home_flops,
        name="value_home",
    )
    value_weight = fold_subs(me, value_weight, "value_subs")
    *partials, query_rows, centroid_grad = call(
        functools.partial(query_home_kernel, sizes, heads, (CLUSTERS / (toks * owners)) ** 0.5, parts),
        several(parts - 1, toks, columns)
        + several(1, toks, width_dev)
        + (shape((groups * 2 * extra, width_dev), F32),),
        (me, unsort, value_rows, w_query, w_value, *home_query),
        scratch=[pltpu.VMEM((owners, half + extra, LANES), BF16), sorted_rows],
        flops=weight_flops + home_flops,
        name="query_home",
    )
    arrived = [shift(partial, "head", k + 1) for k, partial in enumerate(partials)]
    value_weight, _ = lax.optimization_barrier((value_weight, home_query))
    value_weight = pass_round(value_weight, "seq")
    query_weight = call(
        functools.partial(query_weight_kernel, sizes),
        sub_shapes,
        (me, turned, query_rows),
        scratch=[whole],
        flops=weight_flops,
        name="query_weight",
    )
    query_weight = fold_subs(me, query_weight, "query_subs")
    own = call(
        functools.partial(input_own_kernel, parts),
        shape((toks, columns), BF16),
        (me, query_rows, value_rows, w_query, w_value),
        after=query_weight[:1],
        flops=weight_flops * 2 // parts,
        name="input_own",
    )
    query_weight = pass_round(query_weight, "seq")
    grad_wv = add_up(value_weight, F32, "value_sum")
    grad_wq = add_up(query_weight, F32, "query_sum")
    grad_input = add_up([own] + arrived, BF16, "input_sum")
    if groups > 1:
        centroid_grad = centroid_grad.reshape(groups, 2 * extra, width_dev)[:, :per_group]
        centroid_grad = centroid_grad.reshape(CLUSTERS, width_dev)
    return (grad_input, grad_wq, grad_wv, centroid_grad)


def solution(mesh):
    return jax.shard_map(
        on_device,
        mesh=mesh,
        in_specs=(
            P(("grp", "seq", "sub"), None),
            P(None, "head"),
            P(None, "head"),
            P(("grp", "seq", "sub"), "head"),
            P(("grp", "seq", "sub"), None),
        ),
        out_specs=(
            P(("grp", "seq", "sub"), "head"),
            P(("grp", "seq", "sub"), "head"),
            P(("grp", "seq", "sub"), "head"),
            P("grp", "head"),
        ),
        check_vma=False,
    )
```

```python
import functools

import jax
import jax.numpy as jnp
from jax import lax
from jax.experimental import pallas as pl
from jax.experimental.pallas import tpu as pltpu
from jax.sharding import PartitionSpec as P

HD = 64
CLUSTERS = 64
BLOCK_ROWS = 128
LANES = 128
UNROLL = 4
COUNT_ROWS = 16
SCALE = 0.5 * HD ** (-0.5)
F32 = jnp.float32
BF16 = jnp.bfloat16
OWNERS = ("seq", "sub")
GROUP_ROWS = UNROLL * BLOCK_ROWS
LEAD = 2


def iota(shape, dim):
    return lax.broadcasted_iota(jnp.int32, shape, dim)


def low_half(shape):
    return iota(shape, 1) < HD


def swap_halves(tile):
    return pltpu.roll(tile, HD, 1)


def dot(a, b):
    return jnp.dot(a, b, preferred_element_type=F32)


def dot_nt(a, b):
    return lax.dot_general(a, b, (((1,), (1,)), ((), ())), preferred_element_type=F32)


def ones_where(condition):
    return jnp.where(condition, 1.0, 0.0).astype(BF16)


def owner_of(me_ref, ahead, sizes):
    seq = lax.rem(me_ref[0] + ahead[0], jnp.int32(sizes[0]))
    sub = lax.rem(me_ref[1] + ahead[1], jnp.int32(sizes[1]))
    return seq * sizes[1] + sub


def source_of(me_ref, ahead, sizes):
    return owner_of(me_ref, ((sizes[0] - ahead[0]) % sizes[0], (sizes[1] - ahead[1]) % sizes[1]), sizes)


def steps_of(sizes):
    far = sorted(range(1, sizes[0]), key=lambda seq: -min(seq, sizes[0] - seq))
    subs = range(sizes[1])
    return [(0, 0)] + [(seq, sub) for seq in far for sub in subs] + [(0, sub) for sub in subs if sub]


def hand_out(by_owner_ref, out_refs, me_ref, sizes):
    for ahead, out_ref in zip(steps_of(sizes), out_refs):
        out_ref[...] = by_owner_ref[owner_of(me_ref, ahead, sizes)]


def slots_of(assign, groups, rows):
    toks = assign.shape[1]
    per_group = CLUSTERS // groups
    member = jnp.where(iota((CLUSTERS, toks), 0) == assign, 1.0, 0.0)
    member_b = member.astype(BF16)
    upto = ones_where(iota((LANES, LANES), 0) <= iota((LANES, LANES), 1))
    counts = jnp.zeros((CLUSTERS, 1), F32)
    running = []
    for first in range(0, toks, LANES):
        within = dot(member_b[:, first : first + LANES], upto)
        running.append(within + counts)
        counts = counts + within[:, LANES - 1 :]
    running = jnp.concatenate(running, axis=1)
    here, other = iota((CLUSTERS, CLUSTERS), 0), iota((CLUSTERS, CLUSTERS), 1)
    group_of = lambda index: lax.div(index, jnp.int32(per_group))
    earlier = ones_where((other < here) & (group_of(other) == group_of(here)))
    base = dot(earlier, jnp.broadcast_to(counts, (CLUSTERS, LANES)).astype(BF16))[:, :1]
    base = base + (group_of(iota((CLUSTERS, 1), 0)) * rows).astype(F32)
    slot = jnp.sum(member * (running - 1.0 + base), axis=0, keepdims=True).astype(jnp.int32)
    spread = jnp.concatenate([member_b, jnp.zeros((LANES - CLUSTERS, toks), BF16)], axis=0)
    return slot, dot_nt(jnp.ones((COUNT_ROWS, toks), BF16), spread).astype(BF16)


def beside(query, cotan):
    low = low_half(query.shape)
    even = jnp.where(low, query, swap_halves(cotan)).astype(BF16)
    return even, jnp.where(low, swap_halves(query), cotan).astype(BF16)


def load_rows(source, target, sems, fine):
    return [
        pltpu.make_async_copy(source.at[pl.ds(row, fine), :], target.at[pl.ds(row, fine), :], sems.at[row // fine])
        for row in range(0, target.shape[0], fine)
    ]


def project_far_kernel(sizes, groups, rows, heads, assign_ref, tokens_hbm, weight_hbm, cotan_hbm, *refs):
    out_refs, refs = refs[: sizes[1]], refs[sizes[1] :]
    slot_ref, tokens_ref, weight_ref, cotan_ref, mixed_ref, sems = refs
    toks = tokens_ref.shape[0]
    fine = min(256, toks)
    me = (lax.axis_index("seq"), lax.axis_index("sub"))
    owner = owner_of(me, steps_of(sizes)[1], sizes) - me[1]
    group, head = lax.div(owner, jnp.int32(heads)), lax.rem(owner, jnp.int32(heads))
    columns = pl.ds(pl.multiple_of(head * HD, LANES), sizes[1] * HD)
    loads = [
        load_rows(source, target, sems.at[kind], fine)
        for kind, (source, target) in enumerate(
            ((weight_hbm.at[:, columns], weight_ref), (tokens_hbm, tokens_ref), (cotan_hbm.at[:, columns], cotan_ref))
        )
    ]
    for load in loads:
        for copy in load:
            copy.start()
    slot, tallies = slots_of(assign_ref[...], groups, rows)
    slot_ref[...] = slot
    pick = ones_where(iota((rows, toks), 0) + group * rows == slot)
    for copy in loads[0] + loads[2]:
        copy.wait()
    step = min(512, toks)
    for first in range(0, toks, step):
        for copy in loads[1][first // fine : (first + step) // fine]:
            copy.wait()
        where = slice(first, first + step)
        query, cotan = dot(tokens_ref[where, :], weight_ref[...]), cotan_ref[where, :].astype(F32)
        for pair in range(sizes[1] // 2):
            pair_columns = slice(pair * LANES, (pair + 1) * LANES)
            even, odd = beside(query[:, pair_columns], cotan[:, pair_columns])
            mixed_ref[where, 2 * pair * LANES : (2 * pair + 1) * LANES] = even
            mixed_ref[where, (2 * pair + 1) * LANES : (2 * pair + 2) * LANES] = odd
    in_order = dot(pick, mixed_ref[...]).astype(BF16)
    for ahead, out_ref in enumerate(out_refs):
        sub = lax.rem(me[1] + ahead, jnp.int32(sizes[1]))
        for other in range(sizes[1]):

            @pl.when(sub == other)
            def _():
                out_ref[:rows, :] = in_order[:, other * LANES : (other + 1) * LANES]

        out_ref[rows:, :] = tallies


def project_query_kernel(sizes, groups, rows, me_ref, slot_ref, assign_ref, tokens_ref, weight_ref, cotan_ref, *rest):
    out_refs, (mixed_ref, sorted_ref) = rest[:-2], rest[-2:]
    toks = tokens_ref.shape[0]
    heads = weight_ref.shape[1] // HD
    step = min(512, toks)
    for first in range(0, toks, step):
        where = slice(first, first + step)
        query, cotan = dot(tokens_ref[where, :], weight_ref[...]), cotan_ref[where, :].astype(F32)
        for pair in range(heads // 2):
            columns = slice(pair * LANES, (pair + 1) * LANES)
            even, odd = beside(query[:, columns], cotan[:, columns])
            mixed_ref[where, 2 * pair * LANES : (2 * pair + 1) * LANES] = even
            mixed_ref[where, (2 * pair + 1) * LANES : (2 * pair + 2) * LANES] = odd
    part = min(512, rows)
    pieces = rows // part

    @pl.loop(0, groups * pieces)
    def _(i):
        group, piece = lax.div(i, jnp.int32(pieces)), lax.rem(i, jnp.int32(pieces))
        first = pl.multiple_of(piece * part, part)
        pick = ones_where(iota((part, toks), 0) + i * part == slot_ref[...])
        sorted_rows = dot(pick, mixed_ref[...]).astype(BF16)
        for head in range(heads):
            sorted_ref[group * heads + head, pl.ds(first, part), :] = sorted_rows[
                :, head * LANES : (head + 1) * LANES
            ]

    member = jnp.where(iota((LANES, toks), 0) == assign_ref[...], 1.0, 0.0).astype(BF16)
    tallies = dot_nt(jnp.ones((COUNT_ROWS, toks), BF16), member).astype(BF16)
    for owner in range(sorted_ref.shape[0]):
        sorted_ref[owner, rows:, :] = tallies
    steps = steps_of(sizes)
    for ahead, out_ref in zip(steps[:1] + steps[1 + sizes[1] :], out_refs):
        out_ref[...] = sorted_ref[owner_of(me_ref, ahead, sizes)]


def project_value_kernel(sizes, groups, rows, me_ref, slot_ref, tokens_ref, weight_ref, *rest):
    out_refs, (turned_ref, unsort_ref, value_ref, sorted_ref) = rest[:-4], rest[-4:]
    toks = tokens_ref.shape[0]
    heads = weight_ref.shape[1] // HD
    step = min(512, toks)

    @pl.loop(0, toks // step)
    def _(i):
        where = pl.ds(pl.multiple_of(i * step, step), step)
        value_ref[where, :] = dot(tokens_ref[where, :], weight_ref[...]).astype(BF16)

    half = rows // 2
    part = min(256, half)
    pieces = half // part

    @pl.loop(0, groups * pieces)
    def _(i):
        group, piece = lax.div(i, jnp.int32(pieces)), lax.rem(i, jnp.int32(pieces))
        first = pl.multiple_of(piece * part, part)
        index = iota((part, toks), 0) + group * rows + first
        upper = dot(ones_where(index == slot_ref[...]), value_ref[...])
        lower = dot(ones_where(index + half == slot_ref[...]), value_ref[...])
        low = low_half((part, LANES))
        for pair in range(heads // 2):
            up = upper[:, pair * LANES : (pair + 1) * LANES]
            down = lower[:, pair * LANES : (pair + 1) * LANES]
            even = jnp.where(low, up, swap_halves(down)).astype(BF16)
            odd = jnp.where(low, swap_halves(up), down).astype(BF16)
            sorted_ref[group * heads + 2 * pair, pl.ds(first, part), :] = even
            sorted_ref[group * heads + 2 * pair + 1, pl.ds(first, part), :] = odd

    hand_out(sorted_ref, out_refs, me_ref, sizes)
    turned_ref[...] = tokens_ref[...].T
    slots = unsort_ref.shape[1]
    part = min(256, slots)
    for i in range(slots // part):
        pick = ones_where(iota((part, toks), 0) + i * part == slot_ref[...])
        unsort_ref[:, i * part : (i + 1) * part] = pick.T


def score(mixed):
    query = jnp.where(low_half(mixed.shape), mixed.astype(F32) * SCALE, 0.0).astype(BF16)
    return dot_nt(query, mixed)


def softmax_turned(scores):
    shape = scores.shape
    seen = iota(shape, 0) <= iota(shape, 1)
    scores = jnp.where(seen, scores, -jnp.inf)
    raised = jnp.exp(scores - jnp.max(scores, axis=0, keepdims=True))
    return raised * (1.0 / jnp.sum(raised, axis=0, keepdims=True))


def for_each_cluster(counts_ref, me_ref, place_ref, owners, per_group, body):
    for source in range(owners):
        place_ref[source] = 0

    def step(cluster, block):
        runs = []
        total = 0
        base = block * BLOCK_ROWS
        for source in range(owners):
            count = counts_ref[source, me_ref[3] + cluster]
            start = place_ref[source]
            runs.append((source, start, base + total))
            place_ref[source] = start + count
            total = total + count
        body(cluster, block, runs, base + total)
        return block + lax.shift_right_logical(total + (BLOCK_ROWS - 1), jnp.int32(7))

    return lax.fori_loop(0, per_group, step, jnp.int32(LEAD * UNROLL))


def gather_blocks(counts_ref, me_ref, place_ref, owners, per_group, slot_rows, wide_ref, block_ref):
    def body(cluster, block, runs, end):
        for source, start, row in runs:
            block_ref[pl.ds(row, slot_rows), :] = wide_ref[source, pl.ds(start, slot_rows), :]
        block_ref[pl.ds(end, BLOCK_ROWS), :] = jnp.zeros((BLOCK_ROWS, LANES), F32)

    blocks = for_each_cluster(counts_ref, me_ref, place_ref, owners, per_group, body)
    spare = pl.ds(pl.multiple_of(blocks * BLOCK_ROWS, BLOCK_ROWS), GROUP_ROWS)
    block_ref[spare, :] = jnp.zeros((GROUP_ROWS, LANES), F32)
    return blocks


def for_each_group(blocks, stages):
    first, second, third = stages
    groups = lax.div(blocks + (UNROLL - 1), jnp.int32(UNROLL))

    def step(i, carry):
        for slot in range(2):
            group = LEAD + 2 * i + slot
            third(group - 2, slot)
            second(group - 1, 1 - slot)
            first(group, slot)
        return carry

    lax.fori_loop(0, lax.shift_right_logical(groups + 1, jnp.int32(1)), step, 0)


def block_rows(group, ahead):
    return pl.ds(pl.multiple_of((group * UNROLL + ahead) * BLOCK_ROWS, BLOCK_ROWS), BLOCK_ROWS)


def tile_rows(ahead):
    return slice(ahead * BLOCK_ROWS, (ahead + 1) * BLOCK_ROWS)


def value_grad_kernel(sizes, per_group, slot_rows, me_ref, *refs):
    owners = sizes[0] * sizes[1]
    mixed_refs, out_refs, rest = refs[:owners], refs[owners : 2 * owners], refs[2 * owners :]
    dense_ref, counts_out_ref, counts_ref, place_ref, wide_ref, block_ref, home_ref = rest[:7]
    score_refs, probs_refs = rest[7:9], rest[9:11]
    half = out_refs[0].shape[0]
    rows = 2 * half
    for ahead, mixed_ref in zip(steps_of(sizes), mixed_refs):
        source = source_of(me_ref, ahead, sizes)
        tail = mixed_ref[rows:, :].astype(F32).astype(jnp.int32)
        counts_out_ref[pl.ds(source, 1), :] = tail[:1, :]
        wide_ref[source, :rows, :] = mixed_ref[:rows, :].astype(F32)
        wide_ref[source, rows:, :] = jnp.zeros((slot_rows, LANES), F32)
    pltpu.sync_copy(counts_out_ref, counts_ref)
    blocks = gather_blocks(counts_ref, me_ref, place_ref, owners, per_group, slot_rows, wide_ref, block_ref)

    def first(group, slot):
        for ahead in range(UNROLL):
            where = block_rows(group, ahead)
            mixed = block_ref[where, :].astype(BF16)
            dense_ref[where, :] = mixed
            score_refs[slot][tile_rows(ahead), :] = score(mixed)

    def second(group, slot):
        for ahead in range(UNROLL):
            tile = tile_rows(ahead)
            probs_refs[slot][tile, :] = softmax_turned(score_refs[slot][tile, :]).astype(BF16)

    def third(group, slot):
        for ahead in range(UNROLL):
            where = block_rows(group, ahead)
            block_ref[where, :] = dot(probs_refs[slot][tile_rows(ahead), :], dense_ref[where, :])

    for_each_group(blocks, (first, second, third))

    def scatter(cluster, block, runs, end):
        for source, start, row in runs:
            wide_ref[source, pl.ds(start, slot_rows), :] = block_ref[pl.ds(row, slot_rows), :]

    for_each_cluster(counts_ref, me_ref, place_ref, owners, per_group, scatter)
    for ahead, out_ref in zip(steps_of(sizes), out_refs):
        source = owner_of(me_ref, ahead, sizes)
        up, down = wide_ref[source, :half, :], wide_ref[source, half:rows, :]
        out_ref[...] = jnp.where(low_half((half, LANES)), swap_halves(up), down).astype(BF16)


def query_grad_kernel(sizes, per_group, slot_rows, me_ref, counts_ref, dense_ref, *refs):
    owners = sizes[0] * sizes[1]
    value_refs, out_refs, rest = refs[:owners], refs[owners : 2 * owners], refs[2 * owners :]
    place_ref, wide_ref, block_ref, sums_ref, centroid_ref = rest[:5]
    score_refs, grad_probs_refs, both_refs = rest[5:7], rest[7:9], rest[9:11]
    half = value_refs[0].shape[0]
    rows = 2 * half
    for ahead, value_ref in zip(steps_of(sizes), value_refs):
        source = source_of(me_ref, ahead, sizes)
        value = value_ref[...].astype(F32)
        wide_ref[source, :half, :] = swap_halves(value)
        wide_ref[source, half:rows, :] = value
        wide_ref[source, rows:, :] = jnp.zeros((slot_rows, LANES), F32)
    blocks = gather_blocks(counts_ref, me_ref, place_ref, owners, per_group, slot_rows, wide_ref, block_ref)

    def first(group, slot):
        for ahead in range(UNROLL):
            where, tile = block_rows(group, ahead), tile_rows(ahead)
            mixed = dense_ref[where, :]
            value = block_ref[where, :].astype(BF16)
            cotan = jnp.where(low_half(mixed.shape), jnp.zeros_like(mixed), mixed)
            score_refs[slot][tile, :] = score(mixed)
            grad_probs_refs[slot][tile, :] = dot_nt(value, cotan)

    def second(group, slot):
        for ahead in range(UNROLL):
            tile = tile_rows(ahead)
            probs = softmax_turned(score_refs[slot][tile, :])
            grad_probs = grad_probs_refs[slot][tile, :]
            probs_half = probs.astype(BF16).astype(F32)
            row_dot = jnp.sum(probs_half * grad_probs, axis=0, keepdims=True)
            grad_scores = (probs * (grad_probs - row_dot)).astype(BF16).astype(F32)
            both_refs[slot][tile, :] = (grad_scores + grad_scores.T).astype(BF16)

    def third(group, slot):
        for ahead in range(UNROLL):
            where = block_rows(group, ahead)
            grad = dot(both_refs[slot][tile_rows(ahead), :], dense_ref[where, :]) * SCALE
            grad = grad.astype(BF16).astype(F32)
            block_ref[where, :] = grad
            sums_ref[pl.ds(group * UNROLL + ahead, 1), :] = jnp.sum(grad, axis=0, keepdims=True)

    for_each_group(blocks, (first, second, third))
    most = (owners * slot_rows + BLOCK_ROWS - 1) // BLOCK_ROWS

    def scatter(cluster, block, runs, end):
        total = jnp.zeros((1, LANES), F32)
        for ahead in range(most):
            here = block + ahead
            total = total + jnp.where(here * BLOCK_ROWS < end, sums_ref[pl.ds(here, 1), :], 0.0)
        centroid_ref[pl.ds(cluster, 1), :] = total
        for source, start, row in runs:
            wide_ref[source, pl.ds(start, slot_rows), :] = block_ref[pl.ds(row, slot_rows), :]

    for_each_cluster(counts_ref, me_ref, place_ref, owners, per_group, scatter)
    extra = out_refs[0].shape[0] - half
    centroid = jnp.where(
        low_half((extra, LANES)), centroid_ref[:extra, :], swap_halves(centroid_ref[extra:, :])
    ).astype(BF16)
    for ahead, out_ref in zip(steps_of(sizes), out_refs):
        source = owner_of(me_ref, ahead, sizes)
        up, down = wide_ref[source, :half, :], wide_ref[source, half:rows, :]
        out_ref[:half, :] = jnp.where(low_half((half, LANES)), up, swap_halves(down)).astype(BF16)
        out_ref[half:, :] = centroid


def unfold(home_ref, out_ref, heads, start, half, finish):
    low = low_half((half, LANES))
    for group in range(home_ref.shape[0] // heads):
        first = group * 2 * half
        for pair in range(heads // 2):
            even = home_ref[group * heads + 2 * pair, start : start + half, :].astype(F32)
            odd = home_ref[group * heads + 2 * pair + 1, start : start + half, :].astype(F32)
            columns = slice(pair * LANES, (pair + 1) * LANES)
            out_ref[first : first + half, columns] = finish(jnp.where(low, even, swap_halves(odd)))
            out_ref[first + half : first + 2 * half, columns] = finish(
                jnp.where(low, swap_halves(even), odd)
            )


def to_half(x):
    return x.astype(BF16)


def bring_home(sizes, heads, me_ref, part_refs, unsort_ref, home_ref, sorted_ref, rows_ref):
    for ahead, part_ref in zip(steps_of(sizes), part_refs):
        home_ref[source_of(me_ref, ahead, sizes)] = part_ref[...]
    half = sorted_ref.shape[0] * heads // (sizes[0] * sizes[1]) // 2
    unfold(home_ref, sorted_ref, heads, 0, half, to_half)
    toks = rows_ref.shape[0]
    step = min(512, toks)

    @pl.loop(0, toks // step)
    def _(i):
        where = pl.ds(pl.multiple_of(i * step, step), step)
        rows_ref[where, :] = dot(unsort_ref[where, :], sorted_ref[...]).astype(BF16)


def weight_partial(sizes, me_ref, turned_ref, rows_ref, whole_ref, sub_refs):
    width = turned_ref.shape[0]
    step = min(512, width)

    @pl.loop(0, width // step)
    def _(i):
        where = pl.ds(pl.multiple_of(i * step, step), step)
        whole_ref[where, :] = dot(turned_ref[where, :], rows_ref[...]).astype(BF16)

    piece = width // (sizes[0] * sizes[1])
    for ahead, sub_ref in enumerate(sub_refs):
        sub = lax.rem(me_ref[1] + ahead, jnp.int32(sizes[1]))
        for seq in range(sizes[0]):
            first = pl.multiple_of((seq * sizes[1] + sub) * piece, piece)
            sub_ref[seq] = whole_ref[pl.ds(first, piece), :]


def value_home_kernel(sizes, heads, me_ref, turned_ref, unsort_ref, *refs):
    part_refs, rows_ref, sub_refs = refs[: -4 - sizes[1]], refs[-4 - sizes[1]], refs[-3 - sizes[1] : -3]
    home_ref, sorted_ref, whole_ref = refs[-3:]
    bring_home(sizes, heads, me_ref, part_refs, unsort_ref, home_ref, sorted_ref, rows_ref)
    weight_partial(sizes, me_ref, turned_ref, rows_ref, whole_ref, sub_refs)


def input_partial(me_ref, ahead, parts, rows_ref, value_rows_ref, w_query_ref, w_value_ref, out_ref):
    toks = rows_ref.shape[0]
    columns = w_query_ref.shape[0] // parts
    step = min(512, toks)
    dest = lax.rem(me_ref[2] + ahead, jnp.int32(parts))
    mine = pl.ds(pl.multiple_of(dest * columns, columns), columns)

    @pl.loop(0, toks // step)
    def _(i):
        where = pl.ds(pl.multiple_of(i * step, step), step)
        total = dot_nt(rows_ref[where, :], w_query_ref[mine, :])
        total = total + dot_nt(value_rows_ref[where, :], w_value_ref[mine, :])
        out_ref[where, :] = total.astype(BF16)


def query_home_kernel(
    sizes, heads, factor, parts, me_ref, unsort_ref, value_rows_ref, w_query_ref, w_value_ref, *refs
):
    part_refs, out_refs, (rows_ref, centroid_ref, home_ref, sorted_ref) = (
        refs[: -3 - parts],
        refs[-3 - parts : -4],
        refs[-4:],
    )
    bring_home(sizes, heads, me_ref, part_refs, unsort_ref, home_ref, sorted_ref, rows_ref)
    half = sorted_ref.shape[0] * heads // (sizes[0] * sizes[1]) // 2
    unfold(home_ref, centroid_ref, heads, half, home_ref.shape[1] - half, lambda x: x * factor)
    for ahead, out_ref in enumerate(out_refs):
        input_partial(me_ref, ahead + 1, parts, rows_ref, value_rows_ref, w_query_ref, w_value_ref, out_ref)


def query_weight_kernel(sizes, me_ref, turned_ref, rows_ref, *refs):
    weight_partial(sizes, me_ref, turned_ref, rows_ref, refs[-1], refs[:-1])


def input_own_kernel(parts, me_ref, *refs):
    input_partial(me_ref, 0, parts, *refs)


def fold_subs_kernel(me_ref, *refs):
    seqs = refs[0].shape[0]
    terms, out_refs = refs[:-seqs], refs[-seqs:]
    for ahead, out_ref in enumerate(out_refs):
        seq = lax.rem(me_ref[0] + ahead, jnp.int32(seqs))
        total = terms[0][seq].astype(F32)
        for term in terms[1:]:
            total = total + term[seq].astype(F32)
        out_ref[...] = total.astype(BF16)


def sum_kernel(*refs):
    total = refs[0][...].astype(F32)
    for ref in refs[1:-1]:
        total = total + ref[...].astype(F32)
    refs[-1][...] = total.astype(refs[-1].dtype)


def call(kernel, outs, inputs, smem=(0,), in_place=(), after=(), scratch=(), flops=0, vmem=24, name=None):
    def body(*refs):
        kernel(*refs[: len(inputs)], *refs[len(inputs) + len(after) :])

    def space(i):
        return pltpu.SMEM if i in smem else pl.ANY if i in in_place else pltpu.VMEM

    specs = [pl.BlockSpec(memory_space=space(i)) for i in range(len(inputs))]
    specs += [pl.BlockSpec(memory_space=pl.ANY)] * len(after)
    moved = sum(x.size * x.dtype.itemsize for x in inputs) + sum(
        x.size * x.dtype.itemsize for x in jax.tree.leaves(outs)
    )
    return pl.pallas_call(
        body,
        out_shape=outs,
        in_specs=specs,
        out_specs=jax.tree.map(lambda _: pl.BlockSpec(memory_space=pltpu.VMEM), outs),
        scratch_shapes=list(scratch),
        compiler_params=pltpu.CompilerParams(vmem_limit_bytes=vmem * 2**20),
        cost_estimate=pl.CostEstimate(flops=flops, bytes_accessed=moved, transcendentals=0),
        name=name,
    )(*inputs, *after)


def exchange(parts, sizes):
    out = []
    for ahead, part in zip(steps_of(sizes), parts):
        moves = [
            (
                seq * sizes[1] + sub,
                (seq + ahead[0]) % sizes[0] * sizes[1] + (sub + ahead[1]) % sizes[1],
            )
            for seq, sub in steps_of(sizes)
        ]
        out.append(part if ahead == (0, 0) else lax.ppermute(part, OWNERS, moves))
    return out


def shift(part, axis, ahead):
    size = lax.axis_size(axis)
    return lax.ppermute(part, axis, [(i, (i + ahead) % size) for i in range(size)])


def pass_round(parts, axis):
    return [parts[0]] + [shift(parts[ahead], axis, ahead) for ahead in range(1, len(parts))]


def fold_subs(me, by_sub, name):
    seqs, piece, columns = by_sub[0].shape
    return call(
        fold_subs_kernel,
        (jax.ShapeDtypeStruct((piece, columns), BF16),) * seqs,
        (me, *pass_round(by_sub, "sub")),
        name=name,
    )


def add_up(terms, dtype, name):
    return call(sum_kernel, jax.ShapeDtypeStruct(terms[0].shape, dtype), tuple(terms), smem=(), name=name)


def on_device(tokens_in, w_query, w_value, cotangent, assignment):
    sizes = (lax.axis_size("seq"), lax.axis_size("sub"))
    owners = sizes[0] * sizes[1]
    parts = lax.axis_size("head")
    toks, width = tokens_in.shape
    width_dev = cotangent.shape[1]
    heads = width_dev // HD
    slot_rows = 2 * toks // CLUSTERS
    assert owners % heads == 0 and heads % 2 == 0
    groups = owners // heads
    per_group = CLUSTERS // groups
    rows = toks if groups == 1 else per_group * slot_rows
    half = rows // 2
    slots = groups * rows
    columns = width // parts
    capacity = (slot_rows * owners + BLOCK_ROWS - 1) // BLOCK_ROWS * BLOCK_ROWS
    extra = max(per_group // 2, 16)
    shape = jax.ShapeDtypeStruct
    seq, sub = lax.axis_index("seq"), lax.axis_index("sub")
    first = lax.div(seq * sizes[1] + sub, jnp.int32(heads)) * per_group
    me = jnp.stack([seq, sub, lax.axis_index("head"), first]).astype(jnp.int32)

    def several(count, *dims):
        return (shape(dims, BF16),) * count

    assign_row = assignment.reshape(1, toks)
    *far_mixed, slot_row = call(
        functools.partial(project_far_kernel, sizes, groups, rows, heads),
        several(sizes[1], rows + COUNT_ROWS, LANES) + (shape((1, toks), jnp.int32),),
        (assign_row, tokens_in, w_query, cotangent),
        smem=(),
        in_place=(1, 2, 3),
        scratch=[
            pltpu.VMEM((toks, width), BF16),
            pltpu.VMEM((width, sizes[1] * HD), BF16),
            pltpu.VMEM((toks, sizes[1] * HD), BF16),
            pltpu.VMEM((toks, sizes[1] * LANES), BF16),
            pltpu.SemaphoreType.DMA((3, max(toks, width) // min(256, toks))),
        ],
        flops=2 * toks * width * sizes[1] * HD + 2 * rows * toks * sizes[1] * LANES,
        vmem=60,
        name="project_far",
    )
    own_mixed, *near_mixed = call(
        functools.partial(project_query_kernel, sizes, groups, rows),
        several(owners - sizes[1], rows + COUNT_ROWS, LANES),
        (me, slot_row, assign_row, tokens_in, w_query, cotangent),
        scratch=[pltpu.VMEM((toks, 2 * width_dev), BF16), pltpu.VMEM((owners, rows + COUNT_ROWS, LANES), BF16)],
        flops=2 * toks * width * width_dev + 4 * slots * toks * width_dev,
        name="project_query",
    )
    send_mixed = [own_mixed, *far_mixed, *near_mixed]
    got_mixed = exchange(send_mixed, sizes)
    *send_value, turned, unsort = call(
        functools.partial(project_value_kernel, sizes, groups, rows),
        several(owners, half, LANES) + several(1, width, toks) + several(1, toks, slots),
        (me, slot_row, tokens_in, w_value),
        after=near_mixed[:1],
        scratch=[pltpu.VMEM((toks, width_dev), BF16), pltpu.VMEM((owners, half, LANES), BF16)],
        flops=2 * toks * width * width_dev + 2 * slots * toks * width_dev,
        name="project_value",
    )
    got_value = exchange(send_value, sizes)
    blocks = per_group * capacity // BLOCK_ROWS
    held = blocks + (LEAD + 4) * UNROLL
    block_flops = 2 * BLOCK_ROWS * BLOCK_ROWS * LANES
    tall = pltpu.VMEM((owners, rows + slot_rows, LANES), F32)
    dense_rows = pltpu.VMEM((held * BLOCK_ROWS, LANES), F32)
    group_f32 = pltpu.VMEM((GROUP_ROWS, BLOCK_ROWS), F32)
    group_b16 = pltpu.VMEM((GROUP_ROWS, BLOCK_ROWS), BF16)
    place = pltpu.SMEM((owners,), jnp.int32)
    *back_value, dense, counts = call(
        functools.partial(value_grad_kernel, sizes, per_group, slot_rows),
        several(owners, half, LANES)
        + several(1, held * BLOCK_ROWS, LANES)
        + (shape((owners, LANES), jnp.int32),),
        (me, *got_mixed),
        scratch=[pltpu.SMEM((owners, LANES), jnp.int32), place, tall, dense_rows, tall]
        + [group_f32] * 2
        + [group_b16] * 2,
        flops=4 * blocks * block_flops,
        vmem=48,
        name="value_grad",
    )
    home_value = exchange(back_value, sizes)
    back_query = call(
        functools.partial(query_grad_kernel, sizes, per_group, slot_rows),
        several(owners, half + extra, LANES),
        (me, counts, dense, *got_value),
        smem=(0, 1),
        scratch=[place, tall, dense_rows, pltpu.VMEM((held, LANES), F32), pltpu.VMEM((2 * extra, LANES), F32)]
        + [group_f32] * 4
        + [group_b16] * 2,
        flops=6 * blocks * block_flops,
        vmem=48,
        name="query_grad",
    )
    home_query = exchange(back_query, sizes)
    weight_flops = 2 * toks * width * width_dev
    home_flops = 2 * slots * toks * width_dev
    sub_shapes = several(sizes[1], sizes[0], width // owners, width_dev)
    whole = pltpu.VMEM((width, width_dev), BF16)
    sorted_rows = pltpu.VMEM((slots, width_dev), BF16)
    value_rows, *value_weight = call(
        functools.partial(value_home_kernel, sizes, heads),
        several(1, toks, width_dev) + sub_shapes,
        (me, turned, unsort, *home_value),
        scratch=[pltpu.VMEM((owners, half, LANES), BF16), sorted_rows, whole],
        flops=weight_flops + home_flops,
        name="value_home",
    )
    value_weight = fold_subs(me, value_weight, "value_subs")
    *partials, query_rows, centroid_grad = call(
        functools.partial(query_home_kernel, sizes, heads, (CLUSTERS / (toks * owners)) ** 0.5, parts),
        several(parts - 1, toks, columns)
        + several(1, toks, width_dev)
        + (shape((groups * 2 * extra, width_dev), F32),),
        (me, unsort, value_rows, w_query, w_value, *home_query),
        scratch=[pltpu.VMEM((owners, half + extra, LANES), BF16), sorted_rows],
        flops=weight_flops + home_flops,
        name="query_home",
    )
    arrived = [shift(partial, "head", k + 1) for k, partial in enumerate(partials)]
    value_weight, _ = lax.optimization_barrier((value_weight, home_query))
    value_weight = pass_round(value_weight, "seq")
    query_weight = call(
        functools.partial(query_weight_kernel, sizes),
        sub_shapes,
        (me, turned, query_rows),
        scratch=[whole],
        flops=weight_flops,
        name="query_weight",
    )
    query_weight = fold_subs(me, query_weight, "query_subs")
    own = call(
        functools.partial(input_own_kernel, parts),
        shape((toks, columns), BF16),
        (me, query_rows, value_rows, w_query, w_value),
        after=query_weight[:1],
        flops=weight_flops * 2 // parts,
        name="input_own",
    )
    query_weight = pass_round(query_weight, "seq")
    grad_wv = add_up(value_weight, F32, "value_sum")
    grad_wq = add_up(query_weight, F32, "query_sum")
    grad_input = add_up([own] + arrived, BF16, "input_sum")
    if groups > 1:
        centroid_grad = centroid_grad.reshape(groups, 2 * extra, width_dev)[:, :per_group]
        centroid_grad = centroid_grad.reshape(CLUSTERS, width_dev)
    return (grad_input, grad_wq, grad_wv, centroid_grad)


def solution(mesh):
    return jax.shard_map(
        on_device,
        mesh=mesh,
        in_specs=(
            P(("grp", "seq", "sub"), None),
            P(None, "head"),
            P(None, "head"),
            P(("grp", "seq", "sub"), "head"),
            P(("grp", "seq", "sub"), None),
        ),
        out_specs=(
            P(("grp", "seq", "sub"), "head"),
            P(("grp", "seq", "sub"), "head"),
            P(("grp", "seq", "sub"), "head"),
            P("grp", "head"),
        ),
        check_vma=False,
    )
```

```python
import functools

import jax
import jax.numpy as jnp
from jax import lax
from jax.experimental import pallas as pl
from jax.experimental.pallas import tpu as pltpu
from jax.sharding import PartitionSpec as P

HD = 64
CLUSTERS = 64
BLOCK_ROWS = 128
LANES = 128
UNROLL = 4
COUNT_ROWS = 16
SCALE = 0.5 * HD ** (-0.5)
F32 = jnp.float32
BF16 = jnp.bfloat16
OWNERS = ("seq", "sub")
GROUP_ROWS = UNROLL * BLOCK_ROWS
LEAD = 2


def iota(shape, dim):
    return lax.broadcasted_iota(jnp.int32, shape, dim)


def low_half(shape):
    return iota(shape, 1) < HD


def swap_halves(tile):
    return pltpu.roll(tile, HD, 1)


def dot(a, b):
    return jnp.dot(a, b, preferred_element_type=F32)


def dot_nt(a, b):
    return lax.dot_general(a, b, (((1,), (1,)), ((), ())), preferred_element_type=F32)


def ones_where(condition):
    return jnp.where(condition, 1.0, 0.0).astype(BF16)


def owner_of(me_ref, ahead, sizes):
    seq = lax.rem(me_ref[0] + ahead[0], jnp.int32(sizes[0]))
    sub = lax.rem(me_ref[1] + ahead[1], jnp.int32(sizes[1]))
    return seq * sizes[1] + sub


def source_of(me_ref, ahead, sizes):
    return owner_of(me_ref, ((sizes[0] - ahead[0]) % sizes[0], (sizes[1] - ahead[1]) % sizes[1]), sizes)


def steps_of(sizes):
    far = sorted(range(1, sizes[0]), key=lambda seq: -min(seq, sizes[0] - seq))
    subs = range(sizes[1])
    return [(0, 0)] + [(seq, sub) for seq in far for sub in subs] + [(0, sub) for sub in subs if sub]


def hand_out(by_owner_ref, out_refs, me_ref, sizes):
    for ahead, out_ref in zip(steps_of(sizes), out_refs):
        out_ref[...] = by_owner_ref[owner_of(me_ref, ahead, sizes)]


def slots_of(assign, groups, rows):
    toks = assign.shape[1]
    per_group = CLUSTERS // groups
    member = jnp.where(iota((CLUSTERS, toks), 0) == assign, 1.0, 0.0)
    member_b = member.astype(BF16)
    upto = ones_where(iota((LANES, LANES), 0) <= iota((LANES, LANES), 1))
    counts = jnp.zeros((CLUSTERS, 1), F32)
    running = []
    for first in range(0, toks, LANES):
        within = dot(member_b[:, first : first + LANES], upto)
        running.append(within + counts)
        counts = counts + within[:, LANES - 1 :]
    running = jnp.concatenate(running, axis=1)
    here, other = iota((CLUSTERS, CLUSTERS), 0), iota((CLUSTERS, CLUSTERS), 1)
    group_of = lambda index: lax.div(index, jnp.int32(per_group))
    earlier = ones_where((other < here) & (group_of(other) == group_of(here)))
    base = dot(earlier, jnp.broadcast_to(counts, (CLUSTERS, LANES)).astype(BF16))[:, :1]
    base = base + (group_of(iota((CLUSTERS, 1), 0)) * rows).astype(F32)
    slot = jnp.sum(member * (running - 1.0 + base), axis=0, keepdims=True).astype(jnp.int32)
    spread = jnp.concatenate([member_b, jnp.zeros((LANES - CLUSTERS, toks), BF16)], axis=0)
    return slot, dot_nt(jnp.ones((COUNT_ROWS, toks), BF16), spread).astype(BF16)


def beside(query, cotan):
    low = low_half(query.shape)
    even = jnp.where(low, query, swap_halves(cotan)).astype(BF16)
    return even, jnp.where(low, swap_halves(query), cotan).astype(BF16)


def load_rows(source, target, sems, fine):
    return [
        pltpu.make_async_copy(source.at[pl.ds(row, fine), :], target.at[pl.ds(row, fine), :], sems.at[row // fine])
        for row in range(0, target.shape[0], fine)
    ]


def project_far_kernel(sizes, groups, rows, heads, assign_ref, tokens_hbm, weight_hbm, cotan_hbm, *refs):
    out_refs, refs = refs[: sizes[1]], refs[sizes[1] :]
    slot_ref, tokens_ref, weight_ref, cotan_ref, mixed_ref, sems = refs
    toks = tokens_ref.shape[0]
    fine = min(256, toks)
    me = (lax.axis_index("seq"), lax.axis_index("sub"))
    owner = owner_of(me, steps_of(sizes)[1], sizes) - me[1]
    group, head = lax.div(owner, jnp.int32(heads)), lax.rem(owner, jnp.int32(heads))
    columns = pl.ds(pl.multiple_of(head * HD, LANES), sizes[1] * HD)
    loads = [
        load_rows(source, target, sems.at[kind], fine)
        for kind, (source, target) in enumerate(
            ((weight_hbm.at[:, columns], weight_ref), (tokens_hbm, tokens_ref), (cotan_hbm.at[:, columns], cotan_ref))
        )
    ]
    for load in loads:
        for copy in load:
            copy.start()
    slot, tallies = slots_of(assign_ref[...], groups, rows)
    slot_ref[...] = slot
    pick = ones_where(iota((rows, toks), 0) + group * rows == slot)
    for copy in loads[0] + loads[2]:
        copy.wait()
    step = min(512, toks)
    for first in range(0, toks, step):
        for copy in loads[1][first // fine : (first + step) // fine]:
            copy.wait()
        where = slice(first, first + step)
        query, cotan = dot(tokens_ref[where, :], weight_ref[...]), cotan_ref[where, :].astype(F32)
        for pair in range(sizes[1] // 2):
            pair_columns = slice(pair * LANES, (pair + 1) * LANES)
            even, odd = beside(query[:, pair_columns], cotan[:, pair_columns])
            mixed_ref[where, 2 * pair * LANES : (2 * pair + 1) * LANES] = even
            mixed_ref[where, (2 * pair + 1) * LANES : (2 * pair + 2) * LANES] = odd
    in_order = dot(pick, mixed_ref[...]).astype(BF16)
    for ahead, out_ref in enumerate(out_refs):
        sub = lax.rem(me[1] + ahead, jnp.int32(sizes[1]))
        for other in range(sizes[1]):

            @pl.when(sub == other)
            def _():
                out_ref[:rows, :] = in_order[:, other * LANES : (other + 1) * LANES]

        out_ref[rows:, :] = tallies


def project_query_kernel(sizes, groups, rows, me_ref, slot_ref, assign_ref, tokens_ref, weight_ref, cotan_ref, *rest):
    out_refs, (mixed_ref, sorted_ref) = rest[:-2], rest[-2:]
    toks = tokens_ref.shape[0]
    heads = weight_ref.shape[1] // HD
    step = min(512, toks)
    for first in range(0, toks, step):
        where = slice(first, first + step)
        query, cotan = dot(tokens_ref[where, :], weight_ref[...]), cotan_ref[where, :].astype(F32)
        for pair in range(heads // 2):
            columns = slice(pair * LANES, (pair + 1) * LANES)
            even, odd = beside(query[:, columns], cotan[:, columns])
            mixed_ref[where, 2 * pair * LANES : (2 * pair + 1) * LANES] = even
            mixed_ref[where, (2 * pair + 1) * LANES : (2 * pair + 2) * LANES] = odd
    part = min(512, rows)
    pieces = rows // part

    @pl.loop(0, groups * pieces)
    def _(i):
        group, piece = lax.div(i, jnp.int32(pieces)), lax.rem(i, jnp.int32(pieces))
        first = pl.multiple_of(piece * part, part)
        pick = ones_where(iota((part, toks), 0) + i * part == slot_ref[...])
        sorted_rows = dot(pick, mixed_ref[...]).astype(BF16)
        for head in range(heads):
            sorted_ref[group * heads + head, pl.ds(first, part), :] = sorted_rows[
                :, head * LANES : (head + 1) * LANES
            ]

    member = jnp.where(iota((LANES, toks), 0) == assign_ref[...], 1.0, 0.0).astype(BF16)
    tallies = dot_nt(jnp.ones((COUNT_ROWS, toks), BF16), member).astype(BF16)
    for owner in range(sorted_ref.shape[0]):
        sorted_ref[owner, rows:, :] = tallies
    steps = steps_of(sizes)
    for ahead, out_ref in zip(steps[:1] + steps[1 + sizes[1] :], out_refs):
        out_ref[...] = sorted_ref[owner_of(me_ref, ahead, sizes)]


def project_value_kernel(sizes, groups, rows, me_ref, slot_ref, tokens_ref, weight_ref, *rest):
    out_refs, (turned_ref, unsort_ref, value_ref, sorted_ref) = rest[:-4], rest[-4:]
    toks = tokens_ref.shape[0]
    heads = weight_ref.shape[1] // HD
    step = min(512, toks)

    @pl.loop(0, toks // step)
    def _(i):
        where = pl.ds(pl.multiple_of(i * step, step), step)
        value_ref[where, :] = dot(tokens_ref[where, :], weight_ref[...]).astype(BF16)

    half = rows // 2
    part = min(256, half)
    pieces = half // part

    @pl.loop(0, groups * pieces)
    def _(i):
        group, piece = lax.div(i, jnp.int32(pieces)), lax.rem(i, jnp.int32(pieces))
        first = pl.multiple_of(piece * part, part)
        index = iota((part, toks), 0) + group * rows + first
        upper = dot(ones_where(index == slot_ref[...]), value_ref[...])
        lower = dot(ones_where(index + half == slot_ref[...]), value_ref[...])
        low = low_half((part, LANES))
        for pair in range(heads // 2):
            up = upper[:, pair * LANES : (pair + 1) * LANES]
            down = lower[:, pair * LANES : (pair + 1) * LANES]
            even = jnp.where(low, up, swap_halves(down)).astype(BF16)
            odd = jnp.where(low, swap_halves(up), down).astype(BF16)
            sorted_ref[group * heads + 2 * pair, pl.ds(first, part), :] = even
            sorted_ref[group * heads + 2 * pair + 1, pl.ds(first, part), :] = odd

    hand_out(sorted_ref, out_refs, me_ref, sizes)
    turned_ref[...] = tokens_ref[...].T
    slots = unsort_ref.shape[1]
    part = min(256, slots)
    for i in range(slots // part):
        pick = ones_where(iota((part, toks), 0) + i * part == slot_ref[...])
        unsort_ref[:, i * part : (i + 1) * part] = pick.T


def score(mixed):
    query = jnp.where(low_half(mixed.shape), mixed.astype(F32) * SCALE, 0.0).astype(BF16)
    return dot_nt(query, mixed)


def softmax_turned(scores):
    shape = scores.shape
    seen = iota(shape, 0) <= iota(shape, 1)
    scores = jnp.where(seen, scores, -jnp.inf)
    raised = jnp.exp(scores - jnp.max(scores, axis=0, keepdims=True))
    return raised * (1.0 / jnp.sum(raised, axis=0, keepdims=True))


def for_each_cluster(counts_ref, me_ref, place_ref, owners, per_group, body):
    for source in range(owners):
        place_ref[source] = 0

    def step(cluster, block):
        runs = []
        total = 0
        base = block * BLOCK_ROWS
        for source in range(owners):
            count = counts_ref[source, me_ref[3] + cluster]
            start = place_ref[source]
            runs.append((source, start, base + total))
            place_ref[source] = start + count
            total = total + count
        body(cluster, block, runs, base + total)
        return block + lax.shift_right_logical(total + (BLOCK_ROWS - 1), jnp.int32(7))

    return lax.fori_loop(0, per_group, step, jnp.int32(LEAD * UNROLL))


def gather_blocks(counts_ref, me_ref, place_ref, owners, per_group, slot_rows, wide_ref, block_ref):
    def body(cluster, block, runs, end):
        for source, start, row in runs:
            block_ref[pl.ds(row, slot_rows), :] = wide_ref[source, pl.ds(start, slot_rows), :]
        block_ref[pl.ds(end, BLOCK_ROWS), :] = jnp.zeros((BLOCK_ROWS, LANES), F32)

    blocks = for_each_cluster(counts_ref, me_ref, place_ref, owners, per_group, body)
    spare = pl.ds(pl.multiple_of(blocks * BLOCK_ROWS, BLOCK_ROWS), GROUP_ROWS)
    block_ref[spare, :] = jnp.zeros((GROUP_ROWS, LANES), F32)
    return blocks


def for_each_group(blocks, stages):
    first, second, third = stages
    groups = lax.div(blocks + (UNROLL - 1), jnp.int32(UNROLL))

    def step(i, carry):
        for slot in range(2):
            group = LEAD + 2 * i + slot
            third(group - 2, slot)
            second(group - 1, 1 - slot)
            first(group, slot)
        return carry

    lax.fori_loop(0, lax.shift_right_logical(groups + 1, jnp.int32(1)), step, 0)


def block_rows(group, ahead):
    return pl.ds(pl.multiple_of((group * UNROLL + ahead) * BLOCK_ROWS, BLOCK_ROWS), BLOCK_ROWS)


def tile_rows(ahead):
    return slice(ahead * BLOCK_ROWS, (ahead + 1) * BLOCK_ROWS)


def value_grad_kernel(sizes, per_group, slot_rows, me_ref, *refs):
    owners = sizes[0] * sizes[1]
    mixed_refs, out_refs, rest = refs[:owners], refs[owners : 2 * owners], refs[2 * owners :]
    dense_ref, counts_out_ref, counts_ref, place_ref, wide_ref, block_ref, home_ref = rest[:7]
    score_refs, probs_refs = rest[7:9], rest[9:11]
    half = out_refs[0].shape[0]
    rows = 2 * half
    for ahead, mixed_ref in zip(steps_of(sizes), mixed_refs):
        source = source_of(me_ref, ahead, sizes)
        tail = mixed_ref[rows:, :].astype(F32).astype(jnp.int32)
        counts_out_ref[pl.ds(source, 1), :] = tail[:1, :]
        wide_ref[source, :rows, :] = mixed_ref[:rows, :].astype(F32)
        wide_ref[source, rows:, :] = jnp.zeros((slot_rows, LANES), F32)
    pltpu.sync_copy(counts_out_ref, counts_ref)
    blocks = gather_blocks(counts_ref, me_ref, place_ref, owners, per_group, slot_rows, wide_ref, block_ref)

    def first(group, slot):
        for ahead in range(UNROLL):
            where = block_rows(group, ahead)
            mixed = block_ref[where, :].astype(BF16)
            dense_ref[where, :] = mixed
            score_refs[slot][tile_rows(ahead), :] = score(mixed)

    def second(group, slot):
        for ahead in range(UNROLL):
            tile = tile_rows(ahead)
            probs_refs[slot][tile, :] = softmax_turned(score_refs[slot][tile, :]).astype(BF16)

    def third(group, slot):
        for ahead in range(UNROLL):
            where = block_rows(group, ahead)
            block_ref[where, :] = dot(probs_refs[slot][tile_rows(ahead), :], dense_ref[where, :])

    for_each_group(blocks, (first, second, third))

    def scatter(cluster, block, runs, end):
        for source, start, row in runs:
            wide_ref[source, pl.ds(start, slot_rows), :] = block_ref[pl.ds(row, slot_rows), :]

    for_each_cluster(counts_ref, me_ref, place_ref, owners, per_group, scatter)
    for ahead, out_ref in zip(steps_of(sizes), out_refs):
        source = owner_of(me_ref, ahead, sizes)
        up, down = wide_ref[source, :half, :], wide_ref[source, half:rows, :]
        out_ref[...] = jnp.where(low_half((half, LANES)), swap_halves(up), down).astype(BF16)


def query_grad_kernel(sizes, per_group, slot_rows, me_ref, counts_ref, dense_ref, *refs):
    owners = sizes[0] * sizes[1]
    value_refs, out_refs, rest = refs[:owners], refs[owners : 2 * owners], refs[2 * owners :]
    place_ref, wide_ref, block_ref, sums_ref, centroid_ref = rest[:5]
    score_refs, grad_probs_refs, both_refs = rest[5:7], rest[7:9], rest[9:11]
    half = value_refs[0].shape[0]
    rows = 2 * half
    for ahead, value_ref in zip(steps_of(sizes), value_refs):
        source = source_of(me_ref, ahead, sizes)
        value = value_ref[...].astype(F32)
        wide_ref[source, :half, :] = swap_halves(value)
        wide_ref[source, half:rows, :] = value
        wide_ref[source, rows:, :] = jnp.zeros((slot_rows, LANES), F32)
    blocks = gather_blocks(counts_ref, me_ref, place_ref, owners, per_group, slot_rows, wide_ref, block_ref)

    def first(group, slot):
        for ahead in range(UNROLL):
            where, tile = block_rows(group, ahead), tile_rows(ahead)
            mixed = dense_ref[where, :]
            value = block_ref[where, :].astype(BF16)
            cotan = jnp.where(low_half(mixed.shape), jnp.zeros_like(mixed), mixed)
            score_refs[slot][tile, :] = score(mixed)
            grad_probs_refs[slot][tile, :] = dot_nt(value, cotan)

    def second(group, slot):
        for ahead in range(UNROLL):
            tile = tile_rows(ahead)
            probs = softmax_turned(score_refs[slot][tile, :])
            grad_probs = grad_probs_refs[slot][tile, :]
            probs_half = probs.astype(BF16).astype(F32)
            row_dot = jnp.sum(probs_half * grad_probs, axis=0, keepdims=True)
            grad_scores = (probs * (grad_probs - row_dot)).astype(BF16).astype(F32)
            both_refs[slot][tile, :] = (grad_scores + grad_scores.T).astype(BF16)

    def third(group, slot):
        for ahead in range(UNROLL):
            where = block_rows(group, ahead)
            grad = dot(both_refs[slot][tile_rows(ahead), :], dense_ref[where, :]) * SCALE
            grad = grad.astype(BF16).astype(F32)
            block_ref[where, :] = grad
            sums_ref[pl.ds(group * UNROLL + ahead, 1), :] = jnp.sum(grad, axis=0, keepdims=True)

    for_each_group(blocks, (first, second, third))
    most = (owners * slot_rows + BLOCK_ROWS - 1) // BLOCK_ROWS

    def scatter(cluster, block, runs, end):
        total = jnp.zeros((1, LANES), F32)
        for ahead in range(most):
            here = block + ahead
            total = total + jnp.where(here * BLOCK_ROWS < end, sums_ref[pl.ds(here, 1), :], 0.0)
        centroid_ref[pl.ds(cluster, 1), :] = total
        for source, start, row in runs:
            wide_ref[source, pl.ds(start, slot_rows), :] = block_ref[pl.ds(row, slot_rows), :]

    for_each_cluster(counts_ref, me_ref, place_ref, owners, per_group, scatter)
    extra = out_refs[0].shape[0] - half
    centroid = jnp.where(
        low_half((extra, LANES)), centroid_ref[:extra, :], swap_halves(centroid_ref[extra:, :])
    ).astype(BF16)
    for ahead, out_ref in zip(steps_of(sizes), out_refs):
        source = owner_of(me_ref, ahead, sizes)
        up, down = wide_ref[source, :half, :], wide_ref[source, half:rows, :]
        out_ref[:half, :] = jnp.where(low_half((half, LANES)), up, swap_halves(down)).astype(BF16)
        out_ref[half:, :] = centroid


def unfold(home_ref, out_ref, heads, start, half, finish):
    low = low_half((half, LANES))
    for group in range(home_ref.shape[0] // heads):
        first = group * 2 * half
        for pair in range(heads // 2):
            even = home_ref[group * heads + 2 * pair, start : start + half, :].astype(F32)
            odd = home_ref[group * heads + 2 * pair + 1, start : start + half, :].astype(F32)
            columns = slice(pair * LANES, (pair + 1) * LANES)
            out_ref[first : first + half, columns] = finish(jnp.where(low, even, swap_halves(odd)))
            out_ref[first + half : first + 2 * half, columns] = finish(
                jnp.where(low, swap_halves(even), odd)
            )


def to_half(x):
    return x.astype(BF16)


def bring_home(sizes, heads, me_ref, part_refs, unsort_ref, home_ref, sorted_ref, rows_ref):
    for ahead, part_ref in zip(steps_of(sizes), part_refs):
        home_ref[source_of(me_ref, ahead, sizes)] = part_ref[...]
    half = sorted_ref.shape[0] * heads // (sizes[0] * sizes[1]) // 2
    unfold(home_ref, sorted_ref, heads, 0, half, to_half)
    toks = rows_ref.shape[0]
    step = min(512, toks)

    @pl.loop(0, toks // step)
    def _(i):
        where = pl.ds(pl.multiple_of(i * step, step), step)
        rows_ref[where, :] = dot(unsort_ref[where, :], sorted_ref[...]).astype(BF16)


def weight_partial(sizes, me_ref, turned_ref, rows_ref, whole_ref, sub_refs):
    width = turned_ref.shape[0]
    step = min(512, width)

    @pl.loop(0, width // step)
    def _(i):
        where = pl.ds(pl.multiple_of(i * step, step), step)
        whole_ref[where, :] = dot(turned_ref[where, :], rows_ref[...]).astype(BF16)

    piece = width // (sizes[0] * sizes[1])
    for ahead, sub_ref in enumerate(sub_refs):
        sub = lax.rem(me_ref[1] + ahead, jnp.int32(sizes[1]))
        for seq in range(sizes[0]):
            first = pl.multiple_of((seq * sizes[1] + sub) * piece, piece)
            sub_ref[seq] = whole_ref[pl.ds(first, piece), :]


def value_home_kernel(sizes, heads, me_ref, turned_ref, unsort_ref, *refs):
    part_refs, rows_ref, sub_refs = refs[: -4 - sizes[1]], refs[-4 - sizes[1]], refs[-3 - sizes[1] : -3]
    home_ref, sorted_ref, whole_ref = refs[-3:]
    bring_home(sizes, heads, me_ref, part_refs, unsort_ref, home_ref, sorted_ref, rows_ref)
    weight_partial(sizes, me_ref, turned_ref, rows_ref, whole_ref, sub_refs)


def input_partial(me_ref, ahead, parts, rows_ref, value_rows_ref, w_query_ref, w_value_ref, out_ref):
    toks = rows_ref.shape[0]
    columns = w_query_ref.shape[0] // parts
    step = min(512, toks)
    dest = lax.rem(me_ref[2] + ahead, jnp.int32(parts))
    mine = pl.ds(pl.multiple_of(dest * columns, columns), columns)

    @pl.loop(0, toks // step)
    def _(i):
        where = pl.ds(pl.multiple_of(i * step, step), step)
        total = dot_nt(rows_ref[where, :], w_query_ref[mine, :])
        total = total + dot_nt(value_rows_ref[where, :], w_value_ref[mine, :])
        out_ref[where, :] = total.astype(BF16)


def query_home_kernel(
    sizes, heads, factor, parts, me_ref, unsort_ref, value_rows_ref, w_query_ref, w_value_ref, *refs
):
    part_refs, out_refs, (rows_ref, centroid_ref, home_ref, sorted_ref) = (
        refs[: -3 - parts],
        refs[-3 - parts : -4],
        refs[-4:],
    )
    bring_home(sizes, heads, me_ref, part_refs, unsort_ref, home_ref, sorted_ref, rows_ref)
    half = sorted_ref.shape[0] * heads // (sizes[0] * sizes[1]) // 2
    unfold(home_ref, centroid_ref, heads, half, home_ref.shape[1] - half, lambda x: x * factor)
    for ahead, out_ref in enumerate(out_refs):
        input_partial(me_ref, ahead + 1, parts, rows_ref, value_rows_ref, w_query_ref, w_value_ref, out_ref)


def query_weight_kernel(sizes, me_ref, turned_ref, rows_ref, *refs):
    weight_partial(sizes, me_ref, turned_ref, rows_ref, refs[-1], refs[:-1])


def input_own_kernel(parts, me_ref, *refs):
    input_partial(me_ref, 0, parts, *refs)


def fold_subs_kernel(me_ref, *refs):
    seqs = refs[0].shape[0]
    terms, out_refs = refs[:-seqs], refs[-seqs:]
    for ahead, out_ref in enumerate(out_refs):
        seq = lax.rem(me_ref[0] + ahead, jnp.int32(seqs))
        total = terms[0][seq].astype(F32)
        for term in terms[1:]:
            total = total + term[seq].astype(F32)
        out_ref[...] = total.astype(BF16)


def sum_kernel(*refs):
    total = refs[0][...].astype(F32)
    for ref in refs[1:-1]:
        total = total + ref[...].astype(F32)
    refs[-1][...] = total.astype(refs[-1].dtype)


def call(kernel, outs, inputs, smem=(0,), in_place=(), after=(), scratch=(), flops=0, vmem=24, name=None):
    def body(*refs):
        kernel(*refs[: len(inputs)], *refs[len(inputs) + len(after) :])

    def space(i):
        return pltpu.SMEM if i in smem else pl.ANY if i in in_place else pltpu.VMEM

    specs = [pl.BlockSpec(memory_space=space(i)) for i in range(len(inputs))]
    specs += [pl.BlockSpec(memory_space=pl.ANY)] * len(after)
    moved = sum(x.size * x.dtype.itemsize for x in inputs) + sum(
        x.size * x.dtype.itemsize for x in jax.tree.leaves(outs)
    )
    return pl.pallas_call(
        body,
        out_shape=outs,
        in_specs=specs,
        out_specs=jax.tree.map(lambda _: pl.BlockSpec(memory_space=pltpu.VMEM), outs),
        scratch_shapes=list(scratch),
        compiler_params=pltpu.CompilerParams(vmem_limit_bytes=vmem * 2**20),
        cost_estimate=pl.CostEstimate(flops=flops, bytes_accessed=moved, transcendentals=0),
        name=name,
    )(*inputs, *after)


def exchange(parts, sizes):
    out = []
    for ahead, part in zip(steps_of(sizes), parts):
        moves = [
            (
                seq * sizes[1] + sub,
                (seq + ahead[0]) % sizes[0] * sizes[1] + (sub + ahead[1]) % sizes[1],
            )
            for seq, sub in steps_of(sizes)
        ]
        out.append(part if ahead == (0, 0) else lax.ppermute(part, OWNERS, moves))
    return out


def shift(part, axis, ahead):
    size = lax.axis_size(axis)
    return lax.ppermute(part, axis, [(i, (i + ahead) % size) for i in range(size)])


def pass_round(parts, axis):
    return [parts[0]] + [shift(parts[ahead], axis, ahead) for ahead in range(1, len(parts))]


def fold_subs(me, by_sub, name):
    seqs, piece, columns = by_sub[0].shape
    return call(
        fold_subs_kernel,
        (jax.ShapeDtypeStruct((piece, columns), BF16),) * seqs,
        (me, *pass_round(by_sub, "sub")),
        name=name,
    )


def add_up(terms, dtype, name):
    return call(sum_kernel, jax.ShapeDtypeStruct(terms[0].shape, dtype), tuple(terms), smem=(), name=name)


def on_device(tokens_in, w_query, w_value, cotangent, assignment):
    sizes = (lax.axis_size("seq"), lax.axis_size("sub"))
    owners = sizes[0] * sizes[1]
    parts = lax.axis_size("head")
    toks, width = tokens_in.shape
    width_dev = cotangent.shape[1]
    heads = width_dev // HD
    slot_rows = 2 * toks // CLUSTERS
    assert owners % heads == 0 and heads % 2 == 0
    groups = owners // heads
    per_group = CLUSTERS // groups
    rows = toks if groups == 1 else per_group * slot_rows
    half = rows // 2
    slots = groups * rows
    columns = width // parts
    capacity = (slot_rows * owners + BLOCK_ROWS - 1) // BLOCK_ROWS * BLOCK_ROWS
    extra = max(per_group // 2, 16)
    shape = jax.ShapeDtypeStruct
    seq, sub = lax.axis_index("seq"), lax.axis_index("sub")
    first = lax.div(seq * sizes[1] + sub, jnp.int32(heads)) * per_group
    me = jnp.stack([seq, sub, lax.axis_index("head"), first]).astype(jnp.int32)

    def several(count, *dims):
        return (shape(dims, BF16),) * count

    assign_row = assignment.reshape(1, toks)
    *far_mixed, slot_row = call(
        functools.partial(project_far_kernel, sizes, groups, rows, heads),
        several(sizes[1], rows + COUNT_ROWS, LANES) + (shape((1, toks), jnp.int32),),
        (assign_row, tokens_in, w_query, cotangent),
        smem=(),
        in_place=(1, 2, 3),
        scratch=[
            pltpu.VMEM((toks, width), BF16),
            pltpu.VMEM((width, sizes[1] * HD), BF16),
            pltpu.VMEM((toks, sizes[1] * HD), BF16),
            pltpu.VMEM((toks, sizes[1] * LANES), BF16),
            pltpu.SemaphoreType.DMA((3, max(toks, width) // min(256, toks))),
        ],
        flops=2 * toks * width * sizes[1] * HD + 2 * rows * toks * sizes[1] * LANES,
        vmem=60,
        name="project_far",
    )
    own_mixed, *near_mixed = call(
        functools.partial(project_query_kernel, sizes, groups, rows),
        several(owners - sizes[1], rows + COUNT_ROWS, LANES),
        (me, slot_row, assign_row, tokens_in, w_query, cotangent),
        scratch=[pltpu.VMEM((toks, 2 * width_dev), BF16), pltpu.VMEM((owners, rows + COUNT_ROWS, LANES), BF16)],
        flops=2 * toks * width * width_dev + 4 * slots * toks * width_dev,
        name="project_query",
    )
    send_mixed = [own_mixed, *far_mixed, *near_mixed]
    got_mixed = exchange(send_mixed, sizes)
    *send_value, turned, unsort = call(
        functools.partial(project_value_kernel, sizes, groups, rows),
        several(owners, half, LANES) + several(1, width, toks) + several(1, toks, slots),
        (me, slot_row, tokens_in, w_value),
        after=near_mixed[:1],
        scratch=[pltpu.VMEM((toks, width_dev), BF16), pltpu.VMEM((owners, half, LANES), BF16)],
        flops=2 * toks * width * width_dev + 2 * slots * toks * width_dev,
        name="project_value",
    )
    behind = [got_mixed[min(k + 2, owners - 1)] for k in range(owners)]
    send_value = [lax.optimization_barrier(pair)[0] for pair in zip(send_value, behind)]
    got_value = exchange(send_value, sizes)
    blocks = per_group * capacity // BLOCK_ROWS
    held = blocks + (LEAD + 4) * UNROLL
    block_flops = 2 * BLOCK_ROWS * BLOCK_ROWS * LANES
    tall = pltpu.VMEM((owners, rows + slot_rows, LANES), F32)
    dense_rows = pltpu.VMEM((held * BLOCK_ROWS, LANES), F32)
    group_f32 = pltpu.VMEM((GROUP_ROWS, BLOCK_ROWS), F32)
    group_b16 = pltpu.VMEM((GROUP_ROWS, BLOCK_ROWS), BF16)
    place = pltpu.SMEM((owners,), jnp.int32)
    *back_value, dense, counts = call(
        functools.partial(value_grad_kernel, sizes, per_group, slot_rows),
        several(owners, half, LANES)
        + several(1, held * BLOCK_ROWS, LANES)
        + (shape((owners, LANES), jnp.int32),),
        (me, *got_mixed),
        after=[unsort],
        scratch=[pltpu.SMEM((owners, LANES), jnp.int32), place, tall, dense_rows, tall]
        + [group_f32] * 2
        + [group_b16] * 2,
        flops=4 * blocks * block_flops,
        vmem=48,
        name="value_grad",
    )
    home_value = exchange(back_value, sizes)
    back_query = call(
        functools.partial(query_grad_kernel, sizes, per_group, slot_rows),
        several(owners, half + extra, LANES),
        (me, counts, dense, *got_value),
        smem=(0, 1),
        scratch=[place, tall, dense_rows, pltpu.VMEM((held, LANES), F32), pltpu.VMEM((2 * extra, LANES), F32)]
        + [group_f32] * 4
        + [group_b16] * 2,
        flops=6 * blocks * block_flops,
        vmem=48,
        name="query_grad",
    )
    home_query = exchange(back_query, sizes)
    weight_flops = 2 * toks * width * width_dev
    home_flops = 2 * slots * toks * width_dev
    sub_shapes = several(sizes[1], sizes[0], width // owners, width_dev)
    whole = pltpu.VMEM((width, width_dev), BF16)
    sorted_rows = pltpu.VMEM((slots, width_dev), BF16)
    value_rows, *value_weight = call(
        functools.partial(value_home_kernel, sizes, heads),
        several(1, toks, width_dev) + sub_shapes,
        (me, turned, unsort, *home_value),
        scratch=[pltpu.VMEM((owners, half, LANES), BF16), sorted_rows, whole],
        flops=weight_flops + home_flops,
        name="value_home",
    )
    value_weight = fold_subs(me, value_weight, "value_subs")
    *partials, query_rows, centroid_grad = call(
        functools.partial(query_home_kernel, sizes, heads, (CLUSTERS / (toks * owners)) ** 0.5, parts),
        several(parts - 1, toks, columns)
        + several(1, toks, width_dev)
        + (shape((groups * 2 * extra, width_dev), F32),),
        (me, unsort, value_rows, w_query, w_value, *home_query),
        scratch=[pltpu.VMEM((owners, half + extra, LANES), BF16), sorted_rows],
        flops=weight_flops + home_flops,
        name="query_home",
    )
    arrived = [shift(partial, "head", k + 1) for k, partial in enumerate(partials)]
    value_weight, _ = lax.optimization_barrier((value_weight, home_query))
    value_weight = pass_round(value_weight, "seq")
    query_weight = call(
        functools.partial(query_weight_kernel, sizes),
        sub_shapes,
        (me, turned, query_rows),
        scratch=[whole],
        flops=weight_flops,
        name="query_weight",
    )
    query_weight = fold_subs(me, query_weight, "query_subs")
    own = call(
        functools.partial(input_own_kernel, parts),
        shape((toks, columns), BF16),
        (me, query_rows, value_rows, w_query, w_value),
        after=query_weight[:1],
        flops=weight_flops * 2 // parts,
        name="input_own",
    )
    query_weight = pass_round(query_weight, "seq")
    grad_wv = add_up(value_weight, F32, "value_sum")
    grad_wq = add_up(query_weight, F32, "query_sum")
    grad_input = add_up([own] + arrived, BF16, "input_sum")
    if groups > 1:
        centroid_grad = centroid_grad.reshape(groups, 2 * extra, width_dev)[:, :per_group]
        centroid_grad = centroid_grad.reshape(CLUSTERS, width_dev)
    return (grad_input, grad_wq, grad_wv, centroid_grad)


def solution(mesh):
    return jax.shard_map(
        on_device,
        mesh=mesh,
        in_specs=(
            P(("grp", "seq", "sub"), None),
            P(None, "head"),
            P(None, "head"),
            P(("grp", "seq", "sub"), "head"),
            P(("grp", "seq", "sub"), None),
        ),
        out_specs=(
            P(("grp", "seq", "sub"), "head"),
            P(("grp", "seq", "sub"), "head"),
            P(("grp", "seq", "sub"), "head"),
            P("grp", "head"),
        ),
        check_vma=False,
    )
```

```python
import functools

import jax
import jax.numpy as jnp
from jax import lax
from jax.experimental import pallas as pl
from jax.experimental.pallas import tpu as pltpu
from jax.sharding import PartitionSpec as P

HD = 64
CLUSTERS = 64
BLOCK_ROWS = 128
LANES = 128
UNROLL = 4
COUNT_ROWS = 16
SCALE = 0.5 * HD ** (-0.5)
F32 = jnp.float32
BF16 = jnp.bfloat16
OWNERS = ("seq", "sub")
GROUP_ROWS = UNROLL * BLOCK_ROWS
LEAD = 2


def iota(shape, dim):
    return lax.broadcasted_iota(jnp.int32, shape, dim)


def low_half(shape):
    return iota(shape, 1) < HD


def swap_halves(tile):
    return pltpu.roll(tile, HD, 1)


def dot(a, b):
    return jnp.dot(a, b, preferred_element_type=F32)


def dot_nt(a, b):
    return lax.dot_general(a, b, (((1,), (1,)), ((), ())), preferred_element_type=F32)


def ones_where(condition):
    return jnp.where(condition, 1.0, 0.0).astype(BF16)


def owner_of(me_ref, ahead, sizes):
    seq = lax.rem(me_ref[0] + ahead[0], jnp.int32(sizes[0]))
    sub = lax.rem(me_ref[1] + ahead[1], jnp.int32(sizes[1]))
    return seq * sizes[1] + sub


def source_of(me_ref, ahead, sizes):
    return owner_of(me_ref, ((sizes[0] - ahead[0]) % sizes[0], (sizes[1] - ahead[1]) % sizes[1]), sizes)


def steps_of(sizes):
    far = sorted(range(1, sizes[0]), key=lambda seq: -min(seq, sizes[0] - seq))
    subs = range(sizes[1])
    return [(0, 0)] + [(seq, sub) for seq in far for sub in subs] + [(0, sub) for sub in subs if sub]


def hand_out(by_owner_ref, out_refs, me_ref, sizes):
    for ahead, out_ref in zip(steps_of(sizes), out_refs):
        out_ref[...] = by_owner_ref[owner_of(me_ref, ahead, sizes)]


def slots_of(assign, groups, rows):
    toks = assign.shape[1]
    per_group = CLUSTERS // groups
    member = jnp.where(iota((CLUSTERS, toks), 0) == assign, 1.0, 0.0)
    member_b = member.astype(BF16)
    upto = ones_where(iota((LANES, LANES), 0) <= iota((LANES, LANES), 1))
    counts = jnp.zeros((CLUSTERS, 1), F32)
    running = []
    for first in range(0, toks, LANES):
        within = dot(member_b[:, first : first + LANES], upto)
        running.append(within + counts)
        counts = counts + within[:, LANES - 1 :]
    running = jnp.concatenate(running, axis=1)
    here, other = iota((CLUSTERS, CLUSTERS), 0), iota((CLUSTERS, CLUSTERS), 1)
    group_of = lambda index: lax.div(index, jnp.int32(per_group))
    earlier = ones_where((other < here) & (group_of(other) == group_of(here)))
    base = dot(earlier, jnp.broadcast_to(counts, (CLUSTERS, LANES)).astype(BF16))[:, :1]
    base = base + (group_of(iota((CLUSTERS, 1), 0)) * rows).astype(F32)
    slot = jnp.sum(member * (running - 1.0 + base), axis=0, keepdims=True).astype(jnp.int32)
    spread = jnp.concatenate([member_b, jnp.zeros((LANES - CLUSTERS, toks), BF16)], axis=0)
    return slot, dot_nt(jnp.ones((COUNT_ROWS, toks), BF16), spread).astype(BF16)


def beside(query, cotan):
    low = low_half(query.shape)
    even = jnp.where(low, query, swap_halves(cotan)).astype(BF16)
    return even, jnp.where(low, swap_halves(query), cotan).astype(BF16)


def load_rows(source, target, sems, fine):
    return [
        pltpu.make_async_copy(source.at[pl.ds(row, fine), :], target.at[pl.ds(row, fine), :], sems.at[row // fine])
        for row in range(0, target.shape[0], fine)
    ]


def project_far_kernel(sizes, groups, rows, heads, assign_ref, tokens_hbm, weight_hbm, cotan_hbm, *refs):
    out_refs, refs = refs[: sizes[1]], refs[sizes[1] :]
    slot_ref, tokens_ref, weight_ref, cotan_ref, mixed_ref, sems = refs
    toks = tokens_ref.shape[0]
    fine = min(256, toks)
    me = (lax.axis_index("seq"), lax.axis_index("sub"))
    owner = owner_of(me, steps_of(sizes)[1], sizes) - me[1]
    group, head = lax.div(owner, jnp.int32(heads)), lax.rem(owner, jnp.int32(heads))
    columns = pl.ds(pl.multiple_of(head * HD, LANES), sizes[1] * HD)
    loads = [
        load_rows(source, target, sems.at[kind], fine)
        for kind, (source, target) in enumerate(
            ((weight_hbm.at[:, columns], weight_ref), (tokens_hbm, tokens_ref), (cotan_hbm.at[:, columns], cotan_ref))
        )
    ]
    for load in loads:
        for copy in load:
            copy.start()
    slot, tallies = slots_of(assign_ref[...], groups, rows)
    slot_ref[...] = slot
    pick = ones_where(iota((rows, toks), 0) + group * rows == slot)
    for copy in loads[0] + loads[2]:
        copy.wait()
    step = min(512, toks)
    for first in range(0, toks, step):
        for copy in loads[1][first // fine : (first + step) // fine]:
            copy.wait()
        where = slice(first, first + step)
        query, cotan = dot(tokens_ref[where, :], weight_ref[...]), cotan_ref[where, :].astype(F32)
        for pair in range(sizes[1] // 2):
            pair_columns = slice(pair * LANES, (pair + 1) * LANES)
            even, odd = beside(query[:, pair_columns], cotan[:, pair_columns])
            mixed_ref[where, 2 * pair * LANES : (2 * pair + 1) * LANES] = even
            mixed_ref[where, (2 * pair + 1) * LANES : (2 * pair + 2) * LANES] = odd
    in_order = dot(pick, mixed_ref[...]).astype(BF16)
    for ahead, out_ref in enumerate(out_refs):
        sub = lax.rem(me[1] + ahead, jnp.int32(sizes[1]))
        for other in range(sizes[1]):

            @pl.when(sub == other)
            def _():
                out_ref[:rows, :] = in_order[:, other * LANES : (other + 1) * LANES]

        out_ref[rows:, :] = tallies


def project_query_kernel(sizes, groups, rows, me_ref, slot_ref, assign_ref, tokens_ref, weight_ref, cotan_ref, *rest):
    out_refs, (mixed_ref, sorted_ref) = rest[:-2], rest[-2:]
    toks = tokens_ref.shape[0]
    heads = weight_ref.shape[1] // HD
    step = min(512, toks)
    for first in range(0, toks, step):
        where = slice(first, first + step)
        query, cotan = dot(tokens_ref[where, :], weight_ref[...]), cotan_ref[where, :].astype(F32)
        for pair in range(heads // 2):
            columns = slice(pair * LANES, (pair + 1) * LANES)
            even, odd = beside(query[:, columns], cotan[:, columns])
            mixed_ref[where, 2 * pair * LANES : (2 * pair + 1) * LANES] = even
            mixed_ref[where, (2 * pair + 1) * LANES : (2 * pair + 2) * LANES] = odd
    part = min(512, rows)
    pieces = rows // part

    @pl.loop(0, groups * pieces)
    def _(i):
        group, piece = lax.div(i, jnp.int32(pieces)), lax.rem(i, jnp.int32(pieces))
        first = pl.multiple_of(piece * part, part)
        pick = ones_where(iota((part, toks), 0) + i * part == slot_ref[...])
        sorted_rows = dot(pick, mixed_ref[...]).astype(BF16)
        for head in range(heads):
            sorted_ref[group * heads + head, pl.ds(first, part), :] = sorted_rows[
                :, head * LANES : (head + 1) * LANES
            ]

    member = jnp.where(iota((LANES, toks), 0) == assign_ref[...], 1.0, 0.0).astype(BF16)
    tallies = dot_nt(jnp.ones((COUNT_ROWS, toks), BF16), member).astype(BF16)
    for owner in range(sorted_ref.shape[0]):
        sorted_ref[owner, rows:, :] = tallies
    steps = steps_of(sizes)
    for ahead, out_ref in zip(steps[:1] + steps[1 + sizes[1] :], out_refs):
        out_ref[...] = sorted_ref[owner_of(me_ref, ahead, sizes)]


def project_value_kernel(sizes, groups, rows, me_ref, slot_ref, tokens_ref, weight_ref, *rest):
    out_refs, (turned_ref, unsort_ref, value_ref, sorted_ref) = rest[:-4], rest[-4:]
    toks = tokens_ref.shape[0]
    heads = weight_ref.shape[1] // HD
    step = min(512, toks)

    @pl.loop(0, toks // step)
    def _(i):
        where = pl.ds(pl.multiple_of(i * step, step), step)
        value_ref[where, :] = dot(tokens_ref[where, :], weight_ref[...]).astype(BF16)

    half = rows // 2
    part = min(256, half)
    pieces = half // part

    @pl.loop(0, groups * pieces)
    def _(i):
        group, piece = lax.div(i, jnp.int32(pieces)), lax.rem(i, jnp.int32(pieces))
        first = pl.multiple_of(piece * part, part)
        index = iota((part, toks), 0) + group * rows + first
        upper = dot(ones_where(index == slot_ref[...]), value_ref[...])
        lower = dot(ones_where(index + half == slot_ref[...]), value_ref[...])
        low = low_half((part, LANES))
        for pair in range(heads // 2):
            up = upper[:, pair * LANES : (pair + 1) * LANES]
            down = lower[:, pair * LANES : (pair + 1) * LANES]
            even = jnp.where(low, up, swap_halves(down)).astype(BF16)
            odd = jnp.where(low, swap_halves(up), down).astype(BF16)
            sorted_ref[group * heads + 2 * pair, pl.ds(first, part), :] = even
            sorted_ref[group * heads + 2 * pair + 1, pl.ds(first, part), :] = odd

    hand_out(sorted_ref, out_refs, me_ref, sizes)
    turned = tokens_ref[...].T
    slots = unsort_ref.shape[1]
    part = min(256, slots)
    for i in range(slots // part):
        pick = ones_where(iota((part, toks), 0) + i * part == slot_ref[...])
        unsort_ref[:, i * part : (i + 1) * part] = pick.T
        turned_ref[:, i * part : (i + 1) * part] = dot_nt(turned, pick).astype(BF16)


def score(mixed):
    query = jnp.where(low_half(mixed.shape), mixed.astype(F32) * SCALE, 0.0).astype(BF16)
    return dot_nt(query, mixed)


def softmax_turned(scores):
    shape = scores.shape
    seen = iota(shape, 0) <= iota(shape, 1)
    scores = jnp.where(seen, scores, -jnp.inf)
    raised = jnp.exp(scores - jnp.max(scores, axis=0, keepdims=True))
    return raised * (1.0 / jnp.sum(raised, axis=0, keepdims=True))


def for_each_cluster(counts_ref, me_ref, place_ref, owners, per_group, body):
    for source in range(owners):
        place_ref[source] = 0

    def step(cluster, block):
        runs = []
        total = 0
        base = block * BLOCK_ROWS
        for source in range(owners):
            count = counts_ref[source, me_ref[3] + cluster]
            start = place_ref[source]
            runs.append((source, start, base + total))
            place_ref[source] = start + count
            total = total + count
        body(cluster, block, runs, base + total)
        return block + lax.shift_right_logical(total + (BLOCK_ROWS - 1), jnp.int32(7))

    return lax.fori_loop(0, per_group, step, jnp.int32(LEAD * UNROLL))


def gather_blocks(counts_ref, me_ref, place_ref, owners, per_group, slot_rows, wide_ref, block_ref):
    def body(cluster, block, runs, end):
        for source, start, row in runs:
            block_ref[pl.ds(row, slot_rows), :] = wide_ref[source, pl.ds(start, slot_rows), :]
        block_ref[pl.ds(end, BLOCK_ROWS), :] = jnp.zeros((BLOCK_ROWS, LANES), F32)

    blocks = for_each_cluster(counts_ref, me_ref, place_ref, owners, per_group, body)
    spare = pl.ds(pl.multiple_of(blocks * BLOCK_ROWS, BLOCK_ROWS), GROUP_ROWS)
    block_ref[spare, :] = jnp.zeros((GROUP_ROWS, LANES), F32)
    return blocks


def for_each_group(blocks, stages):
    first, second, third = stages
    groups = lax.div(blocks + (UNROLL - 1), jnp.int32(UNROLL))

    def step(i, carry):
        for slot in range(2):
            group = LEAD + 2 * i + slot
            third(group - 2, slot)
            second(group - 1, 1 - slot)
            first(group, slot)
        return carry

    lax.fori_loop(0, lax.shift_right_logical(groups + 1, jnp.int32(1)), step, 0)


def block_rows(group, ahead):
    return pl.ds(pl.multiple_of((group * UNROLL + ahead) * BLOCK_ROWS, BLOCK_ROWS), BLOCK_ROWS)


def tile_rows(ahead):
    return slice(ahead * BLOCK_ROWS, (ahead + 1) * BLOCK_ROWS)


def value_grad_kernel(sizes, per_group, slot_rows, me_ref, *refs):
    owners = sizes[0] * sizes[1]
    mixed_refs, out_refs, rest = refs[:owners], refs[owners : 2 * owners], refs[2 * owners :]
    dense_ref, counts_out_ref, counts_ref, place_ref, wide_ref, block_ref, home_ref = rest[:7]
    score_refs, probs_refs = rest[7:9], rest[9:11]
    half = out_refs[0].shape[0]
    rows = 2 * half
    for ahead, mixed_ref in zip(steps_of(sizes), mixed_refs):
        source = source_of(me_ref, ahead, sizes)
        tail = mixed_ref[rows:, :].astype(F32).astype(jnp.int32)
        counts_out_ref[pl.ds(source, 1), :] = tail[:1, :]
        wide_ref[source, :rows, :] = mixed_ref[:rows, :].astype(F32)
        wide_ref[source, rows:, :] = jnp.zeros((slot_rows, LANES), F32)
    pltpu.sync_copy(counts_out_ref, counts_ref)
    blocks = gather_blocks(counts_ref, me_ref, place_ref, owners, per_group, slot_rows, wide_ref, block_ref)

    def first(group, slot):
        for ahead in range(UNROLL):
            where = block_rows(group, ahead)
            mixed = block_ref[where, :].astype(BF16)
            dense_ref[where, :] = mixed
            score_refs[slot][tile_rows(ahead), :] = score(mixed)

    def second(group, slot):
        for ahead in range(UNROLL):
            tile = tile_rows(ahead)
            probs_refs[slot][tile, :] = softmax_turned(score_refs[slot][tile, :]).astype(BF16)

    def third(group, slot):
        for ahead in range(UNROLL):
            where = block_rows(group, ahead)
            block_ref[where, :] = dot(probs_refs[slot][tile_rows(ahead), :], dense_ref[where, :])

    for_each_group(blocks, (first, second, third))

    def scatter(cluster, block, runs, end):
        for source, start, row in runs:
            wide_ref[source, pl.ds(start, slot_rows), :] = block_ref[pl.ds(row, slot_rows), :]

    for_each_cluster(counts_ref, me_ref, place_ref, owners, per_group, scatter)
    for ahead, out_ref in zip(steps_of(sizes), out_refs):
        source = owner_of(me_ref, ahead, sizes)
        up, down = wide_ref[source, :half, :], wide_ref[source, half:rows, :]
        out_ref[...] = jnp.where(low_half((half, LANES)), swap_halves(up), down).astype(BF16)


def query_grad_kernel(sizes, per_group, slot_rows, me_ref, counts_ref, dense_ref, *refs):
    owners = sizes[0] * sizes[1]
    value_refs, out_refs, rest = refs[:owners], refs[owners : 2 * owners], refs[2 * owners :]
    place_ref, wide_ref, block_ref, sums_ref, centroid_ref = rest[:5]
    score_refs, grad_probs_refs, both_refs = rest[5:7], rest[7:9], rest[9:11]
    half = value_refs[0].shape[0]
    rows = 2 * half
    for ahead, value_ref in zip(steps_of(sizes), value_refs):
        source = source_of(me_ref, ahead, sizes)
        value = value_ref[...].astype(F32)
        wide_ref[source, :half, :] = swap_halves(value)
        wide_ref[source, half:rows, :] = value
        wide_ref[source, rows:, :] = jnp.zeros((slot_rows, LANES), F32)
    blocks = gather_blocks(counts_ref, me_ref, place_ref, owners, per_group, slot_rows, wide_ref, block_ref)

    def first(group, slot):
        for ahead in range(UNROLL):
            where, tile = block_rows(group, ahead), tile_rows(ahead)
            mixed = dense_ref[where, :]
            value = block_ref[where, :].astype(BF16)
            cotan = jnp.where(low_half(mixed.shape), jnp.zeros_like(mixed), mixed)
            score_refs[slot][tile, :] = score(mixed)
            grad_probs_refs[slot][tile, :] = dot_nt(value, cotan)

    def second(group, slot):
        for ahead in range(UNROLL):
            tile = tile_rows(ahead)
            probs = softmax_turned(score_refs[slot][tile, :])
            grad_probs = grad_probs_refs[slot][tile, :]
            probs_half = probs.astype(BF16).astype(F32)
            row_dot = jnp.sum(probs_half * grad_probs, axis=0, keepdims=True)
            grad_scores = (probs * (grad_probs - row_dot)).astype(BF16).astype(F32)
            both_refs[slot][tile, :] = (grad_scores + grad_scores.T).astype(BF16)

    def third(group, slot):
        for ahead in range(UNROLL):
            where = block_rows(group, ahead)
            grad = dot(both_refs[slot][tile_rows(ahead), :], dense_ref[where, :]) * SCALE
            grad = grad.astype(BF16).astype(F32)
            block_ref[where, :] = grad
            sums_ref[pl.ds(group * UNROLL + ahead, 1), :] = jnp.sum(grad, axis=0, keepdims=True)

    for_each_group(blocks, (first, second, third))
    most = (owners * slot_rows + BLOCK_ROWS - 1) // BLOCK_ROWS

    def scatter(cluster, block, runs, end):
        total = jnp.zeros((1, LANES), F32)
        for ahead in range(most):
            here = block + ahead
            total = total + jnp.where(here * BLOCK_ROWS < end, sums_ref[pl.ds(here, 1), :], 0.0)
        centroid_ref[pl.ds(cluster, 1), :] = total
        for source, start, row in runs:
            wide_ref[source, pl.ds(start, slot_rows), :] = block_ref[pl.ds(row, slot_rows), :]

    for_each_cluster(counts_ref, me_ref, place_ref, owners, per_group, scatter)
    extra = out_refs[0].shape[0] - half
    centroid = jnp.where(
        low_half((extra, LANES)), centroid_ref[:extra, :], swap_halves(centroid_ref[extra:, :])
    ).astype(BF16)
    for ahead, out_ref in zip(steps_of(sizes), out_refs):
        source = owner_of(me_ref, ahead, sizes)
        up, down = wide_ref[source, :half, :], wide_ref[source, half:rows, :]
        out_ref[:half, :] = jnp.where(low_half((half, LANES)), up, swap_halves(down)).astype(BF16)
        out_ref[half:, :] = centroid


def unfold(home_ref, out_ref, heads, start, half, finish):
    low = low_half((half, LANES))
    for group in range(home_ref.shape[0] // heads):
        first = group * 2 * half
        for pair in range(heads // 2):
            even = home_ref[group * heads + 2 * pair, start : start + half, :].astype(F32)
            odd = home_ref[group * heads + 2 * pair + 1, start : start + half, :].astype(F32)
            columns = slice(pair * LANES, (pair + 1) * LANES)
            out_ref[first : first + half, columns] = finish(jnp.where(low, even, swap_halves(odd)))
            out_ref[first + half : first + 2 * half, columns] = finish(
                jnp.where(low, swap_halves(even), odd)
            )


def to_half(x):
    return x.astype(BF16)


def bring_home(sizes, heads, me_ref, part_refs, home_ref, rows_ref):
    for ahead, part_ref in zip(steps_of(sizes), part_refs):
        home_ref[source_of(me_ref, ahead, sizes)] = part_ref[...]
    unfold(home_ref, rows_ref, heads, 0, rows_ref.shape[0] * heads // home_ref.shape[0] // 2, to_half)


def weight_partial(sizes, me_ref, turned_ref, rows_ref, whole_ref, sub_refs):
    width = turned_ref.shape[0]
    step = min(512, width)

    @pl.loop(0, width // step)
    def _(i):
        where = pl.ds(pl.multiple_of(i * step, step), step)
        whole_ref[where, :] = dot(turned_ref[where, :], rows_ref[...]).astype(BF16)

    piece = width // (sizes[0] * sizes[1])
    for ahead, sub_ref in enumerate(sub_refs):
        sub = lax.rem(me_ref[1] + ahead, jnp.int32(sizes[1]))
        for seq in range(sizes[0]):
            first = pl.multiple_of((seq * sizes[1] + sub) * piece, piece)
            sub_ref[seq] = whole_ref[pl.ds(first, piece), :]


def input_columns(me_ref, ahead, parts, width):
    columns = width // parts
    dest = lax.rem(me_ref[2] + ahead, jnp.int32(parts))
    return pl.ds(pl.multiple_of(dest * columns, columns), columns)


def value_home_kernel(sizes, heads, parts, me_ref, turned_ref, weight_ref, *refs):
    part_refs, refs = refs[: sizes[0] * sizes[1]], refs[sizes[0] * sizes[1] :]
    rows_ref, term_refs, refs = refs[0], refs[1:parts], refs[parts:]
    sub_refs, (home_ref, whole_ref) = refs[: sizes[1]], refs[sizes[1] :]
    bring_home(sizes, heads, me_ref, part_refs, home_ref, rows_ref)
    for k, term_ref in enumerate(term_refs):
        mine = input_columns(me_ref, k + 1, parts, weight_ref.shape[0])
        term_ref[...] = dot_nt(rows_ref[...], weight_ref[mine, :])
    weight_partial(sizes, me_ref, turned_ref, rows_ref, whole_ref, sub_refs)


def query_home_kernel(sizes, heads, factor, parts, me_ref, weight_ref, *refs):
    term_refs, refs = refs[: parts - 1], refs[parts - 1 :]
    part_refs, refs = refs[: sizes[0] * sizes[1]], refs[sizes[0] * sizes[1] :]
    out_refs, (rows_ref, centroid_ref, home_ref) = refs[: parts - 1], refs[parts - 1 :]
    bring_home(sizes, heads, me_ref, part_refs, home_ref, rows_ref)
    for k, (term_ref, out_ref) in enumerate(zip(term_refs, out_refs)):
        mine = input_columns(me_ref, k + 1, parts, weight_ref.shape[0])
        out_ref[...] = (dot_nt(rows_ref[...], weight_ref[mine, :]) + term_ref[...]).astype(BF16)
    half = rows_ref.shape[0] * heads // home_ref.shape[0] // 2
    unfold(home_ref, centroid_ref, heads, half, home_ref.shape[1] - half, lambda x: x * factor)


def query_weight_kernel(sizes, me_ref, turned_ref, rows_ref, *refs):
    weight_partial(sizes, me_ref, turned_ref, rows_ref, refs[-1], refs[:-1])


def input_own_kernel(parts, me_ref, rows_ref, value_rows_ref, w_query_ref, w_value_ref, out_ref):
    mine = input_columns(me_ref, 0, parts, w_query_ref.shape[0])
    total = dot_nt(rows_ref[...], w_query_ref[mine, :]) + dot_nt(value_rows_ref[...], w_value_ref[mine, :])
    out_ref[...] = total.astype(BF16)


def fold_subs_kernel(me_ref, *refs):
    seqs = refs[0].shape[0]
    terms, out_refs = refs[:-seqs], refs[-seqs:]
    for ahead, out_ref in enumerate(out_refs):
        seq = lax.rem(me_ref[0] + ahead, jnp.int32(seqs))
        total = terms[0][seq].astype(F32)
        for term in terms[1:]:
            total = total + term[seq].astype(F32)
        out_ref[...] = total.astype(BF16)


def sum_kernel(*refs):
    total = refs[0][...].astype(F32)
    for ref in refs[1:-1]:
        total = total + ref[...].astype(F32)
    refs[-1][...] = total.astype(refs[-1].dtype)


def input_sum_kernel(unsort_ref, *refs):
    part_refs, out_ref, total_ref = refs[:-2], refs[-2], refs[-1]
    total = part_refs[0][...].astype(F32)
    for part_ref in part_refs[1:]:
        total = total + part_ref[...].astype(F32)
    total_ref[...] = total.astype(BF16)
    out_ref[...] = dot(unsort_ref[...], total_ref[...]).astype(BF16)


def call(kernel, outs, inputs, smem=(0,), in_place=(), after=(), scratch=(), flops=0, vmem=24, name=None):
    def body(*refs):
        kernel(*refs[: len(inputs)], *refs[len(inputs) + len(after) :])

    def space(i):
        return pltpu.SMEM if i in smem else pl.ANY if i in in_place else pltpu.VMEM

    specs = [pl.BlockSpec(memory_space=space(i)) for i in range(len(inputs))]
    specs += [pl.BlockSpec(memory_space=pl.ANY)] * len(after)
    moved = sum(x.size * x.dtype.itemsize for x in inputs) + sum(
        x.size * x.dtype.itemsize for x in jax.tree.leaves(outs)
    )
    return pl.pallas_call(
        body,
        out_shape=outs,
        in_specs=specs,
        out_specs=jax.tree.map(lambda _: pl.BlockSpec(memory_space=pltpu.VMEM), outs),
        scratch_shapes=list(scratch),
        compiler_params=pltpu.CompilerParams(vmem_limit_bytes=vmem * 2**20),
        cost_estimate=pl.CostEstimate(flops=flops, bytes_accessed=moved, transcendentals=0),
        name=name,
    )(*inputs, *after)


def exchange(parts, sizes):
    out = []
    for ahead, part in zip(steps_of(sizes), parts):
        moves = [
            (
                seq * sizes[1] + sub,
                (seq + ahead[0]) % sizes[0] * sizes[1] + (sub + ahead[1]) % sizes[1],
            )
            for seq, sub in steps_of(sizes)
        ]
        out.append(part if ahead == (0, 0) else lax.ppermute(part, OWNERS, moves))
    return out


def shift(part, axis, ahead):
    size = lax.axis_size(axis)
    return lax.ppermute(part, axis, [(i, (i + ahead) % size) for i in range(size)])


def pass_round(parts, axis):
    return [parts[0]] + [shift(parts[ahead], axis, ahead) for ahead in range(1, len(parts))]


def fold_subs(me, by_sub, name):
    seqs, piece, columns = by_sub[0].shape
    return call(
        fold_subs_kernel,
        (jax.ShapeDtypeStruct((piece, columns), BF16),) * seqs,
        (me, *pass_round(by_sub, "sub")),
        name=name,
    )


def add_up(terms, dtype, name):
    return call(sum_kernel, jax.ShapeDtypeStruct(terms[0].shape, dtype), tuple(terms), smem=(), name=name)


def on_device(tokens_in, w_query, w_value, cotangent, assignment):
    sizes = (lax.axis_size("seq"), lax.axis_size("sub"))
    owners = sizes[0] * sizes[1]
    parts = lax.axis_size("head")
    toks, width = tokens_in.shape
    width_dev = cotangent.shape[1]
    heads = width_dev // HD
    slot_rows = 2 * toks // CLUSTERS
    assert owners % heads == 0 and heads % 2 == 0
    groups = owners // heads
    per_group = CLUSTERS // groups
    rows = toks if groups == 1 else per_group * slot_rows
    half = rows // 2
    slots = groups * rows
    columns = width // parts
    capacity = (slot_rows * owners + BLOCK_ROWS - 1) // BLOCK_ROWS * BLOCK_ROWS
    extra = max(per_group // 2, 16)
    shape = jax.ShapeDtypeStruct
    seq, sub = lax.axis_index("seq"), lax.axis_index("sub")
    first = lax.div(seq * sizes[1] + sub, jnp.int32(heads)) * per_group
    me = jnp.stack([seq, sub, lax.axis_index("head"), first]).astype(jnp.int32)

    def several(count, *dims):
        return (shape(dims, BF16),) * count

    assign_row = assignment.reshape(1, toks)
    *far_mixed, slot_row = call(
        functools.partial(project_far_kernel, sizes, groups, rows, heads),
        several(sizes[1], rows + COUNT_ROWS, LANES) + (shape((1, toks), jnp.int32),),
        (assign_row, tokens_in, w_query, cotangent),
        smem=(),
        in_place=(1, 2, 3),
        scratch=[
            pltpu.VMEM((toks, width), BF16),
            pltpu.VMEM((width, sizes[1] * HD), BF16),
            pltpu.VMEM((toks, sizes[1] * HD), BF16),
            pltpu.VMEM((toks, sizes[1] * LANES), BF16),
            pltpu.SemaphoreType.DMA((3, max(toks, width) // min(256, toks))),
        ],
        flops=2 * toks * width * sizes[1] * HD + 2 * rows * toks * sizes[1] * LANES,
        vmem=60,
        name="project_far",
    )
    own_mixed, *near_mixed = call(
        functools.partial(project_query_kernel, sizes, groups, rows),
        several(owners - sizes[1], rows + COUNT_ROWS, LANES),
        (me, slot_row, assign_row, tokens_in, w_query, cotangent),
        scratch=[pltpu.VMEM((toks, 2 * width_dev), BF16), pltpu.VMEM((owners, rows + COUNT_ROWS, LANES), BF16)],
        flops=2 * toks * width * width_dev + 4 * slots * toks * width_dev,
        name="project_query",
    )
    send_mixed = [own_mixed, *far_mixed, *near_mixed]
    got_mixed = exchange(send_mixed, sizes)
    *send_value, turned, unsort = call(
        functools.partial(project_value_kernel, sizes, groups, rows),
        several(owners, half, LANES) + several(1, width, slots) + several(1, toks, slots),
        (me, slot_row, tokens_in, w_value),
        after=near_mixed[:1],
        scratch=[pltpu.VMEM((toks, width_dev), BF16), pltpu.VMEM((owners, half, LANES), BF16)],
        flops=2 * toks * width * width_dev + 2 * slots * toks * width_dev,
        name="project_value",
    )
    behind = [got_mixed[owners - k if k else 0] for k in range(owners)]
    send_value = [lax.optimization_barrier(pair)[0] for pair in zip(send_value, behind)]
    got_value = exchange(send_value, sizes)
    blocks = per_group * capacity // BLOCK_ROWS
    held = blocks + (LEAD + 4) * UNROLL
    block_flops = 2 * BLOCK_ROWS * BLOCK_ROWS * LANES
    tall = pltpu.VMEM((owners, rows + slot_rows, LANES), F32)
    dense_rows = pltpu.VMEM((held * BLOCK_ROWS, LANES), F32)
    group_f32 = pltpu.VMEM((GROUP_ROWS, BLOCK_ROWS), F32)
    group_b16 = pltpu.VMEM((GROUP_ROWS, BLOCK_ROWS), BF16)
    place = pltpu.SMEM((owners,), jnp.int32)
    *back_value, dense, counts = call(
        functools.partial(value_grad_kernel, sizes, per_group, slot_rows),
        several(owners, half, LANES)
        + several(1, held * BLOCK_ROWS, LANES)
        + (shape((owners, LANES), jnp.int32),),
        (me, *got_mixed),
        after=[unsort],
        scratch=[pltpu.SMEM((owners, LANES), jnp.int32), place, tall, dense_rows, tall]
        + [group_f32] * 2
        + [group_b16] * 2,
        flops=4 * blocks * block_flops,
        vmem=48,
        name="value_grad",
    )
    home_value = exchange(back_value, sizes)
    back_query = call(
        functools.partial(query_grad_kernel, sizes, per_group, slot_rows),
        several(owners, half + extra, LANES),
        (me, counts, dense, *got_value),
        smem=(0, 1),
        scratch=[place, tall, dense_rows, pltpu.VMEM((held, LANES), F32), pltpu.VMEM((2 * extra, LANES), F32)]
        + [group_f32] * 4
        + [group_b16] * 2,
        flops=6 * blocks * block_flops,
        vmem=48,
        name="query_grad",
    )
    home_query = exchange(back_query, sizes)
    weight_flops = 2 * slots * width * width_dev
    home_flops = weight_flops // parts * (parts - 1)
    sub_shapes = several(sizes[1], sizes[0], width // owners, width_dev)
    whole = pltpu.VMEM((width, width_dev), BF16)
    value_rows, *refs = call(
        functools.partial(value_home_kernel, sizes, heads, parts),
        several(1, slots, width_dev) + (shape((slots, columns), F32),) * (parts - 1) + sub_shapes,
        (me, turned, w_value, *home_value),
        scratch=[pltpu.VMEM((owners, half, LANES), BF16), whole],
        flops=weight_flops + home_flops,
        name="value_home",
    )
    value_terms, value_weight = refs[: parts - 1], refs[parts - 1 :]
    value_weight = fold_subs(me, value_weight, "value_subs")
    *partials, query_rows, centroid_grad = call(
        functools.partial(query_home_kernel, sizes, heads, (CLUSTERS / (toks * owners)) ** 0.5, parts),
        several(parts - 1, slots, columns)
        + several(1, slots, width_dev)
        + (shape((groups * 2 * extra, width_dev), F32),),
        (me, w_query, *value_terms, *home_query),
        scratch=[pltpu.VMEM((owners, half + extra, LANES), BF16)],
        flops=home_flops,
        name="query_home",
    )
    arrived = [shift(partial, "head", k + 1) for k, partial in enumerate(partials)]
    value_weight, _ = lax.optimization_barrier((value_weight, home_query))
    value_weight = pass_round(value_weight, "seq")
    query_weight = call(
        functools.partial(query_weight_kernel, sizes),
        sub_shapes,
        (me, turned, query_rows),
        scratch=[whole],
        flops=weight_flops,
        name="query_weight",
    )
    query_weight = fold_subs(me, query_weight, "query_subs")
    own = call(
        functools.partial(input_own_kernel, parts),
        shape((slots, columns), BF16),
        (me, query_rows, value_rows, w_query, w_value),
        after=query_weight[:1],
        flops=weight_flops * 2 // parts,
        name="input_own",
    )
    query_weight = pass_round(query_weight, "seq")
    grad_wv = add_up(value_weight, F32, "value_sum")
    grad_wq = add_up(query_weight, F32, "query_sum")
    grad_input = call(
        input_sum_kernel,
        shape((toks, columns), BF16),
        (unsort, own, *arrived),
        smem=(),
        scratch=[pltpu.VMEM((slots, columns), BF16)],
        flops=2 * toks * slots * columns,
        name="input_sum",
    )
    if groups > 1:
        centroid_grad = centroid_grad.reshape(groups, 2 * extra, width_dev)[:, :per_group]
        centroid_grad = centroid_grad.reshape(CLUSTERS, width_dev)
    return (grad_input, grad_wq, grad_wv, centroid_grad)


def solution(mesh):
    return jax.shard_map(
        on_device,
        mesh=mesh,
        in_specs=(
            P(("grp", "seq", "sub"), None),
            P(None, "head"),
            P(None, "head"),
            P(("grp", "seq", "sub"), "head"),
            P(("grp", "seq", "sub"), None),
        ),
        out_specs=(
            P(("grp", "seq", "sub"), "head"),
            P(("grp", "seq", "sub"), "head"),
            P(("grp", "seq", "sub"), "head"),
            P("grp", "head"),
        ),
        check_vma=False,
    )
```

```python
import functools

import jax
import jax.numpy as jnp
from jax import lax
from jax.experimental import pallas as pl
from jax.experimental.pallas import tpu as pltpu
from jax.sharding import PartitionSpec as P

HD = 64
CLUSTERS = 64
BLOCK_ROWS = 128
LANES = 128
UNROLL = 4
COUNT_ROWS = 16
SCALE = 0.5 * HD ** (-0.5)
F32 = jnp.float32
BF16 = jnp.bfloat16
OWNERS = ("seq", "sub")
GROUP_ROWS = UNROLL * BLOCK_ROWS
LEAD = 2


def iota(shape, dim):
    return lax.broadcasted_iota(jnp.int32, shape, dim)


def low_half(shape):
    return iota(shape, 1) < HD


def swap_halves(tile):
    return pltpu.roll(tile, HD, 1)


def dot(a, b):
    return jnp.dot(a, b, preferred_element_type=F32)


def dot_nt(a, b):
    return lax.dot_general(a, b, (((1,), (1,)), ((), ())), preferred_element_type=F32)


def ones_where(condition):
    return jnp.where(condition, 1.0, 0.0).astype(BF16)


def owner_of(me_ref, ahead, sizes):
    seq = lax.rem(me_ref[0] + ahead[0], jnp.int32(sizes[0]))
    sub = lax.rem(me_ref[1] + ahead[1], jnp.int32(sizes[1]))
    return seq * sizes[1] + sub


def source_of(me_ref, ahead, sizes):
    return owner_of(me_ref, ((sizes[0] - ahead[0]) % sizes[0], (sizes[1] - ahead[1]) % sizes[1]), sizes)


def steps_of(sizes):
    far = sorted(range(1, sizes[0]), key=lambda seq: -min(seq, sizes[0] - seq))
    subs = range(sizes[1])
    return [(0, 0)] + [(seq, sub) for seq in far for sub in subs] + [(0, sub) for sub in subs if sub]


def hand_out(by_owner_ref, out_refs, me_ref, sizes):
    for ahead, out_ref in zip(steps_of(sizes), out_refs):
        out_ref[...] = by_owner_ref[owner_of(me_ref, ahead, sizes)]


def slots_of(assign, groups, rows):
    toks = assign.shape[1]
    per_group = CLUSTERS // groups
    member = jnp.where(iota((CLUSTERS, toks), 0) == assign, 1.0, 0.0)
    member_b = member.astype(BF16)
    upto = ones_where(iota((LANES, LANES), 0) <= iota((LANES, LANES), 1))
    counts = jnp.zeros((CLUSTERS, 1), F32)
    running = []
    for first in range(0, toks, LANES):
        within = dot(member_b[:, first : first + LANES], upto)
        running.append(within + counts)
        counts = counts + within[:, LANES - 1 :]
    running = jnp.concatenate(running, axis=1)
    here, other = iota((CLUSTERS, CLUSTERS), 0), iota((CLUSTERS, CLUSTERS), 1)
    group_of = lambda index: lax.div(index, jnp.int32(per_group))
    earlier = ones_where((other < here) & (group_of(other) == group_of(here)))
    base = dot(earlier, jnp.broadcast_to(counts, (CLUSTERS, LANES)).astype(BF16))[:, :1]
    base = base + (group_of(iota((CLUSTERS, 1), 0)) * rows).astype(F32)
    slot = jnp.sum(member * (running - 1.0 + base), axis=0, keepdims=True).astype(jnp.int32)
    spread = jnp.concatenate([member_b, jnp.zeros((LANES - CLUSTERS, toks), BF16)], axis=0)
    return slot, dot_nt(jnp.ones((COUNT_ROWS, toks), BF16), spread).astype(BF16)


def beside(query, cotan):
    low = low_half(query.shape)
    even = jnp.where(low, query, swap_halves(cotan)).astype(BF16)
    return even, jnp.where(low, swap_halves(query), cotan).astype(BF16)


def load_rows(source, target, sems, fine):
    return [
        pltpu.make_async_copy(source.at[pl.ds(row, fine), :], target.at[pl.ds(row, fine), :], sems.at[row // fine])
        for row in range(0, target.shape[0], fine)
    ]


def project_far_kernel(sizes, groups, rows, heads, assign_ref, tokens_hbm, weight_hbm, cotan_hbm, *refs):
    out_refs, refs = refs[: sizes[1]], refs[sizes[1] :]
    slot_ref, tokens_ref, weight_ref, cotan_ref, mixed_ref, sems = refs
    toks = tokens_ref.shape[0]
    fine = min(256, toks)
    me = (lax.axis_index("seq"), lax.axis_index("sub"))
    owner = owner_of(me, steps_of(sizes)[1], sizes) - me[1]
    group, head = lax.div(owner, jnp.int32(heads)), lax.rem(owner, jnp.int32(heads))
    columns = pl.ds(pl.multiple_of(head * HD, LANES), sizes[1] * HD)
    loads = [
        load_rows(source, target, sems.at[kind], fine)
        for kind, (source, target) in enumerate(
            ((weight_hbm.at[:, columns], weight_ref), (tokens_hbm, tokens_ref), (cotan_hbm.at[:, columns], cotan_ref))
        )
    ]
    for load in loads:
        for copy in load:
            copy.start()
    slot, tallies = slots_of(assign_ref[...], groups, rows)
    slot_ref[...] = slot
    pick = ones_where(iota((rows, toks), 0) + group * rows == slot)
    for copy in loads[0] + loads[2]:
        copy.wait()
    step = min(512, toks)
    for first in range(0, toks, step):
        for copy in loads[1][first // fine : (first + step) // fine]:
            copy.wait()
        where = slice(first, first + step)
        query, cotan = dot(tokens_ref[where, :], weight_ref[...]), cotan_ref[where, :].astype(F32)
        for pair in range(sizes[1] // 2):
            pair_columns = slice(pair * LANES, (pair + 1) * LANES)
            even, odd = beside(query[:, pair_columns], cotan[:, pair_columns])
            mixed_ref[where, 2 * pair * LANES : (2 * pair + 1) * LANES] = even
            mixed_ref[where, (2 * pair + 1) * LANES : (2 * pair + 2) * LANES] = odd
    in_order = dot(pick, mixed_ref[...]).astype(BF16)
    for ahead, out_ref in enumerate(out_refs):
        sub = lax.rem(me[1] + ahead, jnp.int32(sizes[1]))
        for other in range(sizes[1]):

            @pl.when(sub == other)
            def _():
                out_ref[:rows, :] = in_order[:, other * LANES : (other + 1) * LANES]

        out_ref[rows:, :] = tallies


def project_query_kernel(sizes, groups, rows, me_ref, slot_ref, assign_ref, tokens_ref, weight_ref, cotan_ref, *rest):
    out_refs, (mixed_ref, sorted_ref) = rest[:-2], rest[-2:]
    toks = tokens_ref.shape[0]
    heads = weight_ref.shape[1] // HD
    step = min(512, toks)
    for first in range(0, toks, step):
        where = slice(first, first + step)
        query, cotan = dot(tokens_ref[where, :], weight_ref[...]), cotan_ref[where, :].astype(F32)
        for pair in range(heads // 2):
            columns = slice(pair * LANES, (pair + 1) * LANES)
            even, odd = beside(query[:, columns], cotan[:, columns])
            mixed_ref[where, 2 * pair * LANES : (2 * pair + 1) * LANES] = even
            mixed_ref[where, (2 * pair + 1) * LANES : (2 * pair + 2) * LANES] = odd
    part = min(512, rows)
    pieces = rows // part

    @pl.loop(0, groups * pieces)
    def _(i):
        group, piece = lax.div(i, jnp.int32(pieces)), lax.rem(i, jnp.int32(pieces))
        first = pl.multiple_of(piece * part, part)
        pick = ones_where(iota((part, toks), 0) + i * part == slot_ref[...])
        sorted_rows = dot(pick, mixed_ref[...]).astype(BF16)
        for head in range(heads):
            sorted_ref[group * heads + head, pl.ds(first, part), :] = sorted_rows[
                :, head * LANES : (head + 1) * LANES
            ]

    member = jnp.where(iota((LANES, toks), 0) == assign_ref[...], 1.0, 0.0).astype(BF16)
    tallies = dot_nt(jnp.ones((COUNT_ROWS, toks), BF16), member).astype(BF16)
    for owner in range(sorted_ref.shape[0]):
        sorted_ref[owner, rows:, :] = tallies
    steps = steps_of(sizes)
    for ahead, out_ref in zip(steps[:1] + steps[1 + sizes[1] :], out_refs):
        out_ref[...] = sorted_ref[owner_of(me_ref, ahead, sizes)]


def project_value_kernel(sizes, groups, rows, me_ref, slot_ref, tokens_ref, weight_ref, *rest):
    out_refs, (turned_ref, unsort_ref, value_ref, sorted_ref) = rest[:-4], rest[-4:]
    toks = tokens_ref.shape[0]
    heads = weight_ref.shape[1] // HD
    step = min(512, toks)

    @pl.loop(0, toks // step)
    def _(i):
        where = pl.ds(pl.multiple_of(i * step, step), step)
        value_ref[where, :] = dot(tokens_ref[where, :], weight_ref[...]).astype(BF16)

    half = rows // 2
    part = min(256, half)
    pieces = half // part

    @pl.loop(0, groups * pieces)
    def _(i):
        group, piece = lax.div(i, jnp.int32(pieces)), lax.rem(i, jnp.int32(pieces))
        first = pl.multiple_of(piece * part, part)
        index = iota((part, toks), 0) + group * rows + first
        upper = dot(ones_where(index == slot_ref[...]), value_ref[...])
        lower = dot(ones_where(index + half == slot_ref[...]), value_ref[...])
        low = low_half((part, LANES))
        for pair in range(heads // 2):
            up = upper[:, pair * LANES : (pair + 1) * LANES]
            down = lower[:, pair * LANES : (pair + 1) * LANES]
            even = jnp.where(low, up, swap_halves(down)).astype(BF16)
            odd = jnp.where(low, swap_halves(up), down).astype(BF16)
            sorted_ref[group * heads + 2 * pair, pl.ds(first, part), :] = even
            sorted_ref[group * heads + 2 * pair + 1, pl.ds(first, part), :] = odd

    hand_out(sorted_ref, out_refs, me_ref, sizes)
    turned = tokens_ref[...].T
    slots = unsort_ref.shape[1]
    part = min(256, slots)
    for i in range(slots // part):
        pick = ones_where(iota((part, toks), 0) + i * part == slot_ref[...])
        unsort_ref[:, i * part : (i + 1) * part] = pick.T
        turned_ref[:, i * part : (i + 1) * part] = dot_nt(turned, pick).astype(BF16)


def score(mixed):
    query = jnp.where(low_half(mixed.shape), mixed.astype(F32) * SCALE, 0.0).astype(BF16)
    return dot_nt(query, mixed)


def softmax_turned(scores):
    shape = scores.shape
    seen = iota(shape, 0) <= iota(shape, 1)
    scores = jnp.where(seen, scores, -jnp.inf)
    raised = jnp.exp(scores - jnp.max(scores, axis=0, keepdims=True))
    return raised * (1.0 / jnp.sum(raised, axis=0, keepdims=True))


def for_each_cluster(counts_ref, me_ref, place_ref, owners, per_group, body):
    for source in range(owners):
        place_ref[source] = 0

    def step(cluster, block):
        runs = []
        total = 0
        base = block * BLOCK_ROWS
        for source in range(owners):
            count = counts_ref[source, me_ref[3] + cluster]
            start = place_ref[source]
            runs.append((source, start, base + total))
            place_ref[source] = start + count
            total = total + count
        body(cluster, block, runs, base + total)
        return block + lax.shift_right_logical(total + (BLOCK_ROWS - 1), jnp.int32(7))

    return lax.fori_loop(0, per_group, step, jnp.int32(LEAD * UNROLL))


def gather_blocks(counts_ref, me_ref, place_ref, owners, per_group, slot_rows, wide_ref, block_ref):
    def body(cluster, block, runs, end):
        for source, start, row in runs:
            block_ref[pl.ds(row, slot_rows), :] = wide_ref[source, pl.ds(start, slot_rows), :]
        block_ref[pl.ds(end, BLOCK_ROWS), :] = jnp.zeros((BLOCK_ROWS, LANES), F32)

    blocks = for_each_cluster(counts_ref, me_ref, place_ref, owners, per_group, body)
    spare = pl.ds(pl.multiple_of(blocks * BLOCK_ROWS, BLOCK_ROWS), GROUP_ROWS)
    block_ref[spare, :] = jnp.zeros((GROUP_ROWS, LANES), F32)
    return blocks


def for_each_group(blocks, stages):
    first, second, third = stages
    groups = lax.div(blocks + (UNROLL - 1), jnp.int32(UNROLL))

    def step(i, carry):
        for slot in range(2):
            group = LEAD + 2 * i + slot
            third(group - 2, slot)
            second(group - 1, 1 - slot)
            first(group, slot)
        return carry

    lax.fori_loop(0, lax.shift_right_logical(groups + 1, jnp.int32(1)), step, 0)


def block_rows(group, ahead):
    return pl.ds(pl.multiple_of((group * UNROLL + ahead) * BLOCK_ROWS, BLOCK_ROWS), BLOCK_ROWS)


def tile_rows(ahead):
    return slice(ahead * BLOCK_ROWS, (ahead + 1) * BLOCK_ROWS)


def value_grad_kernel(sizes, per_group, slot_rows, me_ref, *refs):
    owners = sizes[0] * sizes[1]
    mixed_refs, out_refs, rest = refs[:owners], refs[owners : 2 * owners], refs[2 * owners :]
    dense_ref, counts_out_ref, counts_ref, place_ref, wide_ref, block_ref, home_ref = rest[:7]
    score_refs, probs_refs = rest[7:9], rest[9:11]
    half = out_refs[0].shape[0]
    rows = 2 * half
    for ahead, mixed_ref in zip(steps_of(sizes), mixed_refs):
        source = source_of(me_ref, ahead, sizes)
        tail = mixed_ref[rows:, :].astype(F32).astype(jnp.int32)
        counts_out_ref[pl.ds(source, 1), :] = tail[:1, :]
        wide_ref[source, :rows, :] = mixed_ref[:rows, :].astype(F32)
        wide_ref[source, rows:, :] = jnp.zeros((slot_rows, LANES), F32)
    pltpu.sync_copy(counts_out_ref, counts_ref)
    blocks = gather_blocks(counts_ref, me_ref, place_ref, owners, per_group, slot_rows, wide_ref, block_ref)

    def first(group, slot):
        for ahead in range(UNROLL):
            where = block_rows(group, ahead)
            mixed = block_ref[where, :].astype(BF16)
            dense_ref[where, :] = mixed
            score_refs[slot][tile_rows(ahead), :] = score(mixed)

    def second(group, slot):
        for ahead in range(UNROLL):
            tile = tile_rows(ahead)
            probs_refs[slot][tile, :] = softmax_turned(score_refs[slot][tile, :]).astype(BF16)

    def third(group, slot):
        for ahead in range(UNROLL):
            where = block_rows(group, ahead)
            block_ref[where, :] = dot(probs_refs[slot][tile_rows(ahead), :], dense_ref[where, :])

    for_each_group(blocks, (first, second, third))

    def scatter(cluster, block, runs, end):
        for source, start, row in runs:
            wide_ref[source, pl.ds(start, slot_rows), :] = block_ref[pl.ds(row, slot_rows), :]

    for_each_cluster(counts_ref, me_ref, place_ref, owners, per_group, scatter)
    for ahead, out_ref in zip(steps_of(sizes), out_refs):
        source = owner_of(me_ref, ahead, sizes)
        up, down = wide_ref[source, :half, :], wide_ref[source, half:rows, :]
        out_ref[...] = jnp.where(low_half((half, LANES)), swap_halves(up), down).astype(BF16)


def query_grad_kernel(sizes, per_group, slot_rows, me_ref, counts_ref, dense_ref, *refs):
    owners = sizes[0] * sizes[1]
    value_refs, out_refs, rest = refs[:owners], refs[owners : 2 * owners], refs[2 * owners :]
    place_ref, wide_ref, block_ref, sums_ref, centroid_ref = rest[:5]
    score_refs, grad_probs_refs, both_refs = rest[5:7], rest[7:9], rest[9:11]
    half = value_refs[0].shape[0]
    rows = 2 * half
    for ahead, value_ref in zip(steps_of(sizes), value_refs):
        source = source_of(me_ref, ahead, sizes)
        value = value_ref[...].astype(F32)
        wide_ref[source, :half, :] = swap_halves(value)
        wide_ref[source, half:rows, :] = value
        wide_ref[source, rows:, :] = jnp.zeros((slot_rows, LANES), F32)
    blocks = gather_blocks(counts_ref, me_ref, place_ref, owners, per_group, slot_rows, wide_ref, block_ref)

    def first(group, slot):
        for ahead in range(UNROLL):
            where, tile = block_rows(group, ahead), tile_rows(ahead)
            mixed = dense_ref[where, :]
            value = block_ref[where, :].astype(BF16)
            cotan = jnp.where(low_half(mixed.shape), jnp.zeros_like(mixed), mixed)
            score_refs[slot][tile, :] = score(mixed)
            grad_probs_refs[slot][tile, :] = dot_nt(value, cotan)

    def second(group, slot):
        for ahead in range(UNROLL):
            tile = tile_rows(ahead)
            probs = softmax_turned(score_refs[slot][tile, :])
            grad_probs = grad_probs_refs[slot][tile, :]
            probs_half = probs.astype(BF16).astype(F32)
            row_dot = jnp.sum(probs_half * grad_probs, axis=0, keepdims=True)
            grad_scores = (probs * (grad_probs - row_dot)).astype(BF16).astype(F32)
            both_refs[slot][tile, :] = (grad_scores + grad_scores.T).astype(BF16)

    def third(group, slot):
        for ahead in range(UNROLL):
            where = block_rows(group, ahead)
            grad = dot(both_refs[slot][tile_rows(ahead), :], dense_ref[where, :]) * SCALE
            grad = grad.astype(BF16).astype(F32)
            block_ref[where, :] = grad
            sums_ref[pl.ds(group * UNROLL + ahead, 1), :] = jnp.sum(grad, axis=0, keepdims=True)

    for_each_group(blocks, (first, second, third))
    most = (owners * slot_rows + BLOCK_ROWS - 1) // BLOCK_ROWS

    def scatter(cluster, block, runs, end):
        total = jnp.zeros((1, LANES), F32)
        for ahead in range(most):
            here = block + ahead
            total = total + jnp.where(here * BLOCK_ROWS < end, sums_ref[pl.ds(here, 1), :], 0.0)
        centroid_ref[pl.ds(cluster, 1), :] = total
        for source, start, row in runs:
            wide_ref[source, pl.ds(start, slot_rows), :] = block_ref[pl.ds(row, slot_rows), :]

    for_each_cluster(counts_ref, me_ref, place_ref, owners, per_group, scatter)
    extra = out_refs[0].shape[0] - half
    centroid = jnp.where(
        low_half((extra, LANES)), centroid_ref[:extra, :], swap_halves(centroid_ref[extra:, :])
    ).astype(BF16)
    for ahead, out_ref in zip(steps_of(sizes), out_refs):
        source = owner_of(me_ref, ahead, sizes)
        up, down = wide_ref[source, :half, :], wide_ref[source, half:rows, :]
        out_ref[:half, :] = jnp.where(low_half((half, LANES)), up, swap_halves(down)).astype(BF16)
        out_ref[half:, :] = centroid


def unfold(home_ref, out_ref, heads, start, half, finish):
    low = low_half((half, LANES))
    for group in range(home_ref.shape[0] // heads):
        first = group * 2 * half
        for pair in range(heads // 2):
            even = home_ref[group * heads + 2 * pair, start : start + half, :].astype(F32)
            odd = home_ref[group * heads + 2 * pair + 1, start : start + half, :].astype(F32)
            columns = slice(pair * LANES, (pair + 1) * LANES)
            out_ref[first : first + half, columns] = finish(jnp.where(low, even, swap_halves(odd)))
            out_ref[first + half : first + 2 * half, columns] = finish(
                jnp.where(low, swap_halves(even), odd)
            )


def to_half(x):
    return x.astype(BF16)


def bring_home(sizes, heads, me_ref, part_refs, home_ref, rows_ref):
    for ahead, part_ref in zip(steps_of(sizes), part_refs):
        home_ref[source_of(me_ref, ahead, sizes)] = part_ref[...]
    unfold(home_ref, rows_ref, heads, 0, rows_ref.shape[0] * heads // home_ref.shape[0] // 2, to_half)


def weight_partial(sizes, me_ref, turned_ref, rows_ref, sub_refs):
    piece = turned_ref.shape[0] // (sizes[0] * sizes[1])
    for ahead, sub_ref in enumerate(sub_refs):
        sub = lax.rem(me_ref[1] + ahead, jnp.int32(sizes[1]))
        first = [pl.multiple_of((seq * sizes[1] + sub) * piece, piece) for seq in range(sizes[0])]
        turned = jnp.concatenate([turned_ref[pl.ds(row, piece), :] for row in first], axis=0)
        partial = dot(turned, rows_ref[...]).astype(BF16)
        for seq in range(sizes[0]):
            sub_ref[seq] = partial[seq * piece : (seq + 1) * piece, :]


def input_columns(me_ref, ahead, parts, width):
    columns = width // parts
    dest = lax.rem(me_ref[2] + ahead, jnp.int32(parts))
    return pl.ds(pl.multiple_of(dest * columns, columns), columns)


def value_home_kernel(sizes, heads, parts, me_ref, turned_ref, weight_ref, *refs):
    part_refs, refs = refs[: sizes[0] * sizes[1]], refs[sizes[0] * sizes[1] :]
    rows_ref, term_refs, refs = refs[0], refs[1:parts], refs[parts:]
    sub_refs, home_ref = refs[: sizes[1]], refs[sizes[1]]
    bring_home(sizes, heads, me_ref, part_refs, home_ref, rows_ref)
    for k, term_ref in enumerate(term_refs):
        mine = input_columns(me_ref, k + 1, parts, weight_ref.shape[0])
        term_ref[...] = dot_nt(rows_ref[...], weight_ref[mine, :])
    weight_partial(sizes, me_ref, turned_ref, rows_ref, sub_refs)


def query_home_kernel(sizes, heads, factor, parts, me_ref, weight_ref, *refs):
    term_refs, refs = refs[: parts - 1], refs[parts - 1 :]
    part_refs, refs = refs[: sizes[0] * sizes[1]], refs[sizes[0] * sizes[1] :]
    out_refs, (rows_ref, centroid_ref, home_ref) = refs[: parts - 1], refs[parts - 1 :]
    bring_home(sizes, heads, me_ref, part_refs, home_ref, rows_ref)
    for k, (term_ref, out_ref) in enumerate(zip(term_refs, out_refs)):
        mine = input_columns(me_ref, k + 1, parts, weight_ref.shape[0])
        out_ref[...] = (dot_nt(rows_ref[...], weight_ref[mine, :]) + term_ref[...]).astype(BF16)
    half = rows_ref.shape[0] * heads // home_ref.shape[0] // 2
    unfold(home_ref, centroid_ref, heads, half, home_ref.shape[1] - half, lambda x: x * factor)


def query_weight_kernel(sizes, me_ref, turned_ref, rows_ref, *sub_refs):
    weight_partial(sizes, me_ref, turned_ref, rows_ref, sub_refs)


def input_own_kernel(parts, me_ref, rows_ref, value_rows_ref, w_query_ref, w_value_ref, out_ref):
    mine = input_columns(me_ref, 0, parts, w_query_ref.shape[0])
    total = dot_nt(rows_ref[...], w_query_ref[mine, :]) + dot_nt(value_rows_ref[...], w_value_ref[mine, :])
    out_ref[...] = total.astype(BF16)


def fold_subs_kernel(me_ref, *refs):
    seqs = refs[0].shape[0]
    terms, out_refs = refs[:-seqs], refs[-seqs:]
    for ahead, out_ref in enumerate(out_refs):
        seq = lax.rem(me_ref[0] + ahead, jnp.int32(seqs))
        total = terms[0][seq].astype(F32)
        for term in terms[1:]:
            total = total + term[seq].astype(F32)
        out_ref[...] = total.astype(BF16)


def sum_kernel(*refs):
    total = refs[0][...].astype(F32)
    for ref in refs[1:-1]:
        total = total + ref[...].astype(F32)
    refs[-1][...] = total.astype(refs[-1].dtype)


def input_sum_kernel(unsort_ref, *refs):
    part_refs, out_ref, total_ref = refs[:-2], refs[-2], refs[-1]
    total = part_refs[0][...].astype(F32)
    for part_ref in part_refs[1:]:
        total = total + part_ref[...].astype(F32)
    total_ref[...] = total.astype(BF16)
    out_ref[...] = dot(unsort_ref[...], total_ref[...]).astype(BF16)


def call(kernel, outs, inputs, smem=(0,), in_place=(), after=(), scratch=(), flops=0, vmem=24, name=None):
    def body(*refs):
        kernel(*refs[: len(inputs)], *refs[len(inputs) + len(after) :])

    def space(i):
        return pltpu.SMEM if i in smem else pl.ANY if i in in_place else pltpu.VMEM

    specs = [pl.BlockSpec(memory_space=space(i)) for i in range(len(inputs))]
    specs += [pl.BlockSpec(memory_space=pl.ANY)] * len(after)
    moved = sum(x.size * x.dtype.itemsize for x in inputs) + sum(
        x.size * x.dtype.itemsize for x in jax.tree.leaves(outs)
    )
    return pl.pallas_call(
        body,
        out_shape=outs,
        in_specs=specs,
        out_specs=jax.tree.map(lambda _: pl.BlockSpec(memory_space=pltpu.VMEM), outs),
        scratch_shapes=list(scratch),
        compiler_params=pltpu.CompilerParams(vmem_limit_bytes=vmem * 2**20),
        cost_estimate=pl.CostEstimate(flops=flops, bytes_accessed=moved, transcendentals=0),
        name=name,
    )(*inputs, *after)


def exchange(parts, sizes):
    out = []
    for ahead, part in zip(steps_of(sizes), parts):
        moves = [
            (
                seq * sizes[1] + sub,
                (seq + ahead[0]) % sizes[0] * sizes[1] + (sub + ahead[1]) % sizes[1],
            )
            for seq, sub in steps_of(sizes)
        ]
        out.append(part if ahead == (0, 0) else lax.ppermute(part, OWNERS, moves))
    return out


def shift(part, axis, ahead):
    size = lax.axis_size(axis)
    return lax.ppermute(part, axis, [(i, (i + ahead) % size) for i in range(size)])


def pass_round(parts, axis):
    return [parts[0]] + [shift(parts[ahead], axis, ahead) for ahead in range(1, len(parts))]


def fold_subs(me, by_sub, name):
    seqs, piece, columns = by_sub[0].shape
    return call(
        fold_subs_kernel,
        (jax.ShapeDtypeStruct((piece, columns), BF16),) * seqs,
        (me, *pass_round(by_sub, "sub")),
        name=name,
    )


def add_up(terms, dtype, name, after=()):
    out = jax.ShapeDtypeStruct(terms[0].shape, dtype)
    return call(sum_kernel, out, tuple(terms), smem=(), after=after, name=name)


def on_device(tokens_in, w_query, w_value, cotangent, assignment):
    sizes = (lax.axis_size("seq"), lax.axis_size("sub"))
    owners = sizes[0] * sizes[1]
    parts = lax.axis_size("head")
    toks, width = tokens_in.shape
    width_dev = cotangent.shape[1]
    heads = width_dev // HD
    slot_rows = 2 * toks // CLUSTERS
    assert owners % heads == 0 and heads % 2 == 0
    groups = owners // heads
    per_group = CLUSTERS // groups
    rows = toks if groups == 1 else per_group * slot_rows
    half = rows // 2
    slots = groups * rows
    columns = width // parts
    capacity = (slot_rows * owners + BLOCK_ROWS - 1) // BLOCK_ROWS * BLOCK_ROWS
    extra = max(per_group // 2, 16)
    shape = jax.ShapeDtypeStruct
    seq, sub = lax.axis_index("seq"), lax.axis_index("sub")
    first = lax.div(seq * sizes[1] + sub, jnp.int32(heads)) * per_group
    me = jnp.stack([seq, sub, lax.axis_index("head"), first]).astype(jnp.int32)

    def several(count, *dims):
        return (shape(dims, BF16),) * count

    assign_row = assignment.reshape(1, toks)
    *far_mixed, slot_row = call(
        functools.partial(project_far_kernel, sizes, groups, rows, heads),
        several(sizes[1], rows + COUNT_ROWS, LANES) + (shape((1, toks), jnp.int32),),
        (assign_row, tokens_in, w_query, cotangent),
        smem=(),
        in_place=(1, 2, 3),
        scratch=[
            pltpu.VMEM((toks, width), BF16),
            pltpu.VMEM((width, sizes[1] * HD), BF16),
            pltpu.VMEM((toks, sizes[1] * HD), BF16),
            pltpu.VMEM((toks, sizes[1] * LANES), BF16),
            pltpu.SemaphoreType.DMA((3, max(toks, width) // min(256, toks))),
        ],
        flops=2 * toks * width * sizes[1] * HD + 2 * rows * toks * sizes[1] * LANES,
        vmem=60,
        name="project_far",
    )
    own_mixed, *near_mixed = call(
        functools.partial(project_query_kernel, sizes, groups, rows),
        several(owners - sizes[1], rows + COUNT_ROWS, LANES),
        (me, slot_row, assign_row, tokens_in, w_query, cotangent),
        scratch=[pltpu.VMEM((toks, 2 * width_dev), BF16), pltpu.VMEM((owners, rows + COUNT_ROWS, LANES), BF16)],
        flops=2 * toks * width * width_dev + 4 * slots * toks * width_dev,
        name="project_query",
    )
    send_mixed = [own_mixed, *far_mixed, *near_mixed]
    got_mixed = exchange(send_mixed, sizes)
    *send_value, turned, unsort = call(
        functools.partial(project_value_kernel, sizes, groups, rows),
        several(owners, half, LANES) + several(1, width, slots) + several(1, toks, slots),
        (me, slot_row, tokens_in, w_value),
        after=near_mixed[:1],
        scratch=[pltpu.VMEM((toks, width_dev), BF16), pltpu.VMEM((owners, half, LANES), BF16)],
        flops=2 * toks * width * width_dev + 2 * slots * toks * width_dev,
        name="project_value",
    )
    behind = [0, *range(3, owners), 2, 1][:owners]
    send_value = [lax.optimization_barrier((part, got_mixed[k]))[0] for part, k in zip(send_value, behind)]
    got_value = exchange(send_value, sizes)
    blocks = per_group * capacity // BLOCK_ROWS
    held = blocks + (LEAD + 4) * UNROLL
    block_flops = 2 * BLOCK_ROWS * BLOCK_ROWS * LANES
    tall = pltpu.VMEM((owners, rows + slot_rows, LANES), F32)
    dense_rows = pltpu.VMEM((held * BLOCK_ROWS, LANES), F32)
    group_f32 = pltpu.VMEM((GROUP_ROWS, BLOCK_ROWS), F32)
    group_b16 = pltpu.VMEM((GROUP_ROWS, BLOCK_ROWS), BF16)
    place = pltpu.SMEM((owners,), jnp.int32)
    *back_value, dense, counts = call(
        functools.partial(value_grad_kernel, sizes, per_group, slot_rows),
        several(owners, half, LANES)
        + several(1, held * BLOCK_ROWS, LANES)
        + (shape((owners, LANES), jnp.int32),),
        (me, *got_mixed),
        after=[unsort],
        scratch=[pltpu.SMEM((owners, LANES), jnp.int32), place, tall, dense_rows, tall]
        + [group_f32] * 2
        + [group_b16] * 2,
        flops=4 * blocks * block_flops,
        vmem=48,
        name="value_grad",
    )
    home_value = exchange(back_value, sizes)
    back_query = call(
        functools.partial(query_grad_kernel, sizes, per_group, slot_rows),
        several(owners, half + extra, LANES),
        (me, counts, dense, *got_value),
        smem=(0, 1),
        scratch=[place, tall, dense_rows, pltpu.VMEM((held, LANES), F32), pltpu.VMEM((2 * extra, LANES), F32)]
        + [group_f32] * 4
        + [group_b16] * 2,
        flops=6 * blocks * block_flops,
        vmem=48,
        name="query_grad",
    )
    home_query = exchange(back_query, sizes)
    weight_flops = 2 * slots * width * width_dev
    home_flops = weight_flops // parts * (parts - 1)
    sub_shapes = several(sizes[1], sizes[0], width // owners, width_dev)
    value_rows, *refs = call(
        functools.partial(value_home_kernel, sizes, heads, parts),
        several(1, slots, width_dev) + (shape((slots, columns), F32),) * (parts - 1) + sub_shapes,
        (me, turned, w_value, *home_value),
        scratch=[pltpu.VMEM((owners, half, LANES), BF16)],
        flops=weight_flops + home_flops,
        name="value_home",
    )
    value_terms, value_weight = refs[: parts - 1], refs[parts - 1 :]
    value_weight = fold_subs(me, value_weight, "value_subs")
    *partials, query_rows, centroid_grad = call(
        functools.partial(query_home_kernel, sizes, heads, (CLUSTERS / (toks * owners)) ** 0.5, parts),
        several(parts - 1, slots, columns)
        + several(1, slots, width_dev)
        + (shape((groups * 2 * extra, width_dev), F32),),
        (me, w_query, *value_terms, *home_query),
        scratch=[pltpu.VMEM((owners, half + extra, LANES), BF16)],
        flops=home_flops,
        name="query_home",
    )
    arrived = [shift(partial, "head", k + 1) for k, partial in enumerate(partials)]
    value_weight, _ = lax.optimization_barrier((value_weight, home_query))
    value_weight = pass_round(value_weight, "seq")
    query_weight = call(
        functools.partial(query_weight_kernel, sizes),
        sub_shapes,
        (me, turned, query_rows),
        flops=weight_flops,
        name="query_weight",
    )
    query_weight = fold_subs(me, query_weight, "query_subs")
    own = call(
        functools.partial(input_own_kernel, parts),
        shape((slots, columns), BF16),
        (me, query_rows, value_rows, w_query, w_value),
        after=query_weight[:1],
        flops=weight_flops * 2 // parts,
        name="input_own",
    )
    query_weight = pass_round(query_weight, "seq")
    grad_wv = add_up(value_weight, F32, "value_sum", [own])
    grad_input = call(
        input_sum_kernel,
        shape((toks, columns), BF16),
        (unsort, own, *arrived),
        smem=(),
        scratch=[pltpu.VMEM((slots, columns), BF16)],
        flops=2 * toks * slots * columns,
        name="input_sum",
    )
    grad_wq = add_up(query_weight, F32, "query_sum", [grad_input])
    if groups > 1:
        centroid_grad = centroid_grad.reshape(groups, 2 * extra, width_dev)[:, :per_group]
        centroid_grad = centroid_grad.reshape(CLUSTERS, width_dev)
    return (grad_input, grad_wq, grad_wv, centroid_grad)


def solution(mesh):
    return jax.shard_map(
        on_device,
        mesh=mesh,
        in_specs=(
            P(("grp", "seq", "sub"), None),
            P(None, "head"),
            P(None, "head"),
            P(("grp", "seq", "sub"), "head"),
            P(("grp", "seq", "sub"), None),
        ),
        out_specs=(
            P(("grp", "seq", "sub"), "head"),
            P(("grp", "seq", "sub"), "head"),
            P(("grp", "seq", "sub"), "head"),
            P("grp", "head"),
        ),
        check_vma=False,
    )
```

```python
import functools

import jax
import jax.numpy as jnp
from jax import lax
from jax.experimental import pallas as pl
from jax.experimental.pallas import tpu as pltpu
from jax.sharding import PartitionSpec as P

HD = 64
CLUSTERS = 64
BLOCK_ROWS = 128
LANES = 128
UNROLL = 4
COUNT_ROWS = 16
SCALE = 0.5 * HD ** (-0.5)
F32 = jnp.float32
BF16 = jnp.bfloat16
OWNERS = ("seq", "sub")
GROUP_ROWS = UNROLL * BLOCK_ROWS
LEAD = 2


def iota(shape, dim):
    return lax.broadcasted_iota(jnp.int32, shape, dim)


def low_half(shape):
    return iota(shape, 1) < HD


def swap_halves(tile):
    return pltpu.roll(tile, HD, 1)


def dot(a, b):
    return jnp.dot(a, b, preferred_element_type=F32)


def dot_nt(a, b):
    return lax.dot_general(a, b, (((1,), (1,)), ((), ())), preferred_element_type=F32)


def ones_where(condition):
    return jnp.where(condition, 1.0, 0.0).astype(BF16)


def owner_of(me_ref, ahead, sizes):
    seq = lax.rem(me_ref[0] + ahead[0], jnp.int32(sizes[0]))
    sub = lax.rem(me_ref[1] + ahead[1], jnp.int32(sizes[1]))
    return seq * sizes[1] + sub


def source_of(me_ref, ahead, sizes):
    return owner_of(me_ref, ((sizes[0] - ahead[0]) % sizes[0], (sizes[1] - ahead[1]) % sizes[1]), sizes)


def steps_of(sizes):
    far = sorted(range(1, sizes[0]), key=lambda seq: -min(seq, sizes[0] - seq))
    subs = range(sizes[1])
    return [(0, 0)] + [(seq, sub) for seq in far for sub in subs] + [(0, sub) for sub in subs if sub]


def hand_out(by_owner_ref, out_refs, me_ref, sizes):
    for ahead, out_ref in zip(steps_of(sizes), out_refs):
        out_ref[...] = by_owner_ref[owner_of(me_ref, ahead, sizes)]


def slots_of(assign, groups, rows):
    toks = assign.shape[1]
    per_group = CLUSTERS // groups
    member = jnp.where(iota((CLUSTERS, toks), 0) == assign, 1.0, 0.0)
    member_b = member.astype(BF16)
    upto = ones_where(iota((LANES, LANES), 0) <= iota((LANES, LANES), 1))
    counts = jnp.zeros((CLUSTERS, 1), F32)
    running = []
    for first in range(0, toks, LANES):
        within = dot(member_b[:, first : first + LANES], upto)
        running.append(within + counts)
        counts = counts + within[:, LANES - 1 :]
    running = jnp.concatenate(running, axis=1)
    here, other = iota((CLUSTERS, CLUSTERS), 0), iota((CLUSTERS, CLUSTERS), 1)
    group_of = lambda index: lax.div(index, jnp.int32(per_group))
    earlier = ones_where((other < here) & (group_of(other) == group_of(here)))
    base = dot(earlier, jnp.broadcast_to(counts, (CLUSTERS, LANES)).astype(BF16))[:, :1]
    base = base + (group_of(iota((CLUSTERS, 1), 0)) * rows).astype(F32)
    slot = jnp.sum(member * (running - 1.0 + base), axis=0, keepdims=True).astype(jnp.int32)
    spread = jnp.concatenate([member_b, jnp.zeros((LANES - CLUSTERS, toks), BF16)], axis=0)
    return slot, dot_nt(jnp.ones((COUNT_ROWS, toks), BF16), spread).astype(BF16)


def beside(query, cotan):
    low = low_half(query.shape)
    even = jnp.where(low, query, swap_halves(cotan)).astype(BF16)
    return even, jnp.where(low, swap_halves(query), cotan).astype(BF16)


def load_rows(source, target, sems, fine):
    return [
        pltpu.make_async_copy(source.at[pl.ds(row, fine), :], target.at[pl.ds(row, fine), :], sems.at[row // fine])
        for row in range(0, target.shape[0], fine)
    ]


def project_far_kernel(sizes, groups, rows, heads, assign_ref, tokens_hbm, weight_hbm, cotan_hbm, *refs):
    out_refs, refs = refs[: sizes[1]], refs[sizes[1] :]
    slot_ref, tokens_ref, weight_ref, cotan_ref, mixed_ref, sems = refs
    toks = tokens_ref.shape[0]
    fine = min(256, toks)
    me = (lax.axis_index("seq"), lax.axis_index("sub"))
    owner = owner_of(me, steps_of(sizes)[1], sizes) - me[1]
    group, head = lax.div(owner, jnp.int32(heads)), lax.rem(owner, jnp.int32(heads))
    columns = pl.ds(pl.multiple_of(head * HD, LANES), sizes[1] * HD)
    loads = [
        load_rows(source, target, sems.at[kind], fine)
        for kind, (source, target) in enumerate(
            ((weight_hbm.at[:, columns], weight_ref), (tokens_hbm, tokens_ref), (cotan_hbm.at[:, columns], cotan_ref))
        )
    ]
    for load in loads:
        for copy in load:
            copy.start()
    slot, tallies = slots_of(assign_ref[...], groups, rows)
    slot_ref[...] = slot
    pick = ones_where(iota((rows, toks), 0) + group * rows == slot)
    for copy in loads[0] + loads[2]:
        copy.wait()
    step = min(512, toks)
    for first in range(0, toks, step):
        for copy in loads[1][first // fine : (first + step) // fine]:
            copy.wait()
        where = slice(first, first + step)
        query, cotan = dot(tokens_ref[where, :], weight_ref[...]), cotan_ref[where, :].astype(F32)
        for pair in range(sizes[1] // 2):
            pair_columns = slice(pair * LANES, (pair + 1) * LANES)
            even, odd = beside(query[:, pair_columns], cotan[:, pair_columns])
            mixed_ref[where, 2 * pair * LANES : (2 * pair + 1) * LANES] = even
            mixed_ref[where, (2 * pair + 1) * LANES : (2 * pair + 2) * LANES] = odd
    in_order = dot(pick, mixed_ref[...]).astype(BF16)
    for ahead, out_ref in enumerate(out_refs):
        sub = lax.rem(me[1] + ahead, jnp.int32(sizes[1]))
        for other in range(sizes[1]):

            @pl.when(sub == other)
            def _():
                out_ref[:rows, :] = in_order[:, other * LANES : (other + 1) * LANES]

        out_ref[rows:, :] = tallies


def project_query_kernel(sizes, groups, rows, me_ref, slot_ref, assign_ref, tokens_ref, weight_ref, cotan_ref, *rest):
    out_refs, (mixed_ref, sorted_ref) = rest[:-2], rest[-2:]
    toks = tokens_ref.shape[0]
    heads = weight_ref.shape[1] // HD
    step = min(512, toks)
    for first in range(0, toks, step):
        where = slice(first, first + step)
        query, cotan = dot(tokens_ref[where, :], weight_ref[...]), cotan_ref[where, :].astype(F32)
        for pair in range(heads // 2):
            columns = slice(pair * LANES, (pair + 1) * LANES)
            even, odd = beside(query[:, columns], cotan[:, columns])
            mixed_ref[where, 2 * pair * LANES : (2 * pair + 1) * LANES] = even
            mixed_ref[where, (2 * pair + 1) * LANES : (2 * pair + 2) * LANES] = odd
    part = min(512, rows)
    pieces = rows // part

    @pl.loop(0, groups * pieces)
    def _(i):
        group, piece = lax.div(i, jnp.int32(pieces)), lax.rem(i, jnp.int32(pieces))
        first = pl.multiple_of(piece * part, part)
        pick = ones_where(iota((part, toks), 0) + i * part == slot_ref[...])
        sorted_rows = dot(pick, mixed_ref[...]).astype(BF16)
        for head in range(heads):
            sorted_ref[group * heads + head, pl.ds(first, part), :] = sorted_rows[
                :, head * LANES : (head + 1) * LANES
            ]

    member = jnp.where(iota((LANES, toks), 0) == assign_ref[...], 1.0, 0.0).astype(BF16)
    tallies = dot_nt(jnp.ones((COUNT_ROWS, toks), BF16), member).astype(BF16)
    for owner in range(sorted_ref.shape[0]):
        sorted_ref[owner, rows:, :] = tallies
    steps = steps_of(sizes)
    for ahead, out_ref in zip(steps[:1] + steps[1 + sizes[1] :], out_refs):
        out_ref[...] = sorted_ref[owner_of(me_ref, ahead, sizes)]


def project_value_kernel(sizes, groups, rows, me_ref, slot_ref, tokens_ref, weight_ref, *rest):
    out_refs, (turned_ref, unsort_ref, value_ref, sorted_ref) = rest[:-4], rest[-4:]
    toks = tokens_ref.shape[0]
    heads = weight_ref.shape[1] // HD
    step = min(512, toks)

    @pl.loop(0, toks // step)
    def _(i):
        where = pl.ds(pl.multiple_of(i * step, step), step)
        value_ref[where, :] = dot(tokens_ref[where, :], weight_ref[...]).astype(BF16)

    half = rows // 2
    part = min(256, half)
    pieces = half // part

    @pl.loop(0, groups * pieces)
    def _(i):
        group, piece = lax.div(i, jnp.int32(pieces)), lax.rem(i, jnp.int32(pieces))
        first = pl.multiple_of(piece * part, part)
        index = iota((part, toks), 0) + group * rows + first
        upper = dot(ones_where(index == slot_ref[...]), value_ref[...])
        lower = dot(ones_where(index + half == slot_ref[...]), value_ref[...])
        low = low_half((part, LANES))
        for pair in range(heads // 2):
            up = upper[:, pair * LANES : (pair + 1) * LANES]
            down = lower[:, pair * LANES : (pair + 1) * LANES]
            even = jnp.where(low, up, swap_halves(down)).astype(BF16)
            odd = jnp.where(low, swap_halves(up), down).astype(BF16)
            sorted_ref[group * heads + 2 * pair, pl.ds(first, part), :] = even
            sorted_ref[group * heads + 2 * pair + 1, pl.ds(first, part), :] = odd

    hand_out(sorted_ref, out_refs, me_ref, sizes)
    turned = tokens_ref[...].T
    slots = unsort_ref.shape[1]
    part = min(256, slots)
    for i in range(slots // part):
        pick = ones_where(iota((part, toks), 0) + i * part == slot_ref[...])
        unsort_ref[:, i * part : (i + 1) * part] = pick.T
        turned_ref[:, i * part : (i + 1) * part] = dot_nt(turned, pick).astype(BF16)


def score(mixed):
    query = jnp.where(low_half(mixed.shape), mixed.astype(F32) * SCALE, 0.0).astype(BF16)
    return dot_nt(query, mixed)


def softmax_turned(scores):
    shape = scores.shape
    seen = iota(shape, 0) <= iota(shape, 1)
    scores = jnp.where(seen, scores, -jnp.inf)
    raised = jnp.exp(scores - jnp.max(scores, axis=0, keepdims=True))
    return raised * (1.0 / jnp.sum(raised, axis=0, keepdims=True))


def for_each_cluster(counts_ref, me_ref, place_ref, owners, per_group, body):
    for source in range(owners):
        place_ref[source] = 0

    def step(cluster, block):
        runs = []
        total = 0
        base = block * BLOCK_ROWS
        for source in range(owners):
            count = counts_ref[source, me_ref[3] + cluster]
            start = place_ref[source]
            runs.append((source, start, base + total))
            place_ref[source] = start + count
            total = total + count
        body(cluster, block, runs, base + total)
        return block + lax.shift_right_logical(total + (BLOCK_ROWS - 1), jnp.int32(7))

    return lax.fori_loop(0, per_group, step, jnp.int32(LEAD * UNROLL))


def gather_blocks(counts_ref, me_ref, place_ref, owners, per_group, slot_rows, wide_ref, block_ref):
    def body(cluster, block, runs, end):
        for source, start, row in runs:
            block_ref[pl.ds(row, slot_rows), :] = wide_ref[source, pl.ds(start, slot_rows), :]
        block_ref[pl.ds(end, BLOCK_ROWS), :] = jnp.zeros((BLOCK_ROWS, LANES), F32)

    blocks = for_each_cluster(counts_ref, me_ref, place_ref, owners, per_group, body)
    spare = pl.ds(pl.multiple_of(blocks * BLOCK_ROWS, BLOCK_ROWS), GROUP_ROWS)
    block_ref[spare, :] = jnp.zeros((GROUP_ROWS, LANES), F32)
    return blocks


def for_each_group(blocks, stages):
    first, second, third = stages
    groups = lax.div(blocks + (UNROLL - 1), jnp.int32(UNROLL))

    def step(i, carry):
        for slot in range(2):
            group = LEAD + 2 * i + slot
            third(group - 2, slot)
            second(group - 1, 1 - slot)
            first(group, slot)
        return carry

    lax.fori_loop(0, lax.shift_right_logical(groups + 1, jnp.int32(1)), step, 0)


def block_rows(group, ahead):
    return pl.ds(pl.multiple_of((group * UNROLL + ahead) * BLOCK_ROWS, BLOCK_ROWS), BLOCK_ROWS)


def tile_rows(ahead):
    return slice(ahead * BLOCK_ROWS, (ahead + 1) * BLOCK_ROWS)


def value_grad_kernel(sizes, per_group, slot_rows, me_ref, *refs):
    owners = sizes[0] * sizes[1]
    mixed_refs, out_refs, rest = refs[:owners], refs[owners : 2 * owners], refs[2 * owners :]
    dense_ref, counts_out_ref, counts_ref, place_ref, wide_ref, block_ref, home_ref = rest[:7]
    score_refs, probs_refs = rest[7:9], rest[9:11]
    half = out_refs[0].shape[0]
    rows = 2 * half
    for ahead, mixed_ref in zip(steps_of(sizes), mixed_refs):
        source = source_of(me_ref, ahead, sizes)
        tail = mixed_ref[rows:, :].astype(F32).astype(jnp.int32)
        counts_out_ref[pl.ds(source, 1), :] = tail[:1, :]
        wide_ref[source, :rows, :] = mixed_ref[:rows, :].astype(F32)
        wide_ref[source, rows:, :] = jnp.zeros((slot_rows, LANES), F32)
    pltpu.sync_copy(counts_out_ref, counts_ref)
    blocks = gather_blocks(counts_ref, me_ref, place_ref, owners, per_group, slot_rows, wide_ref, block_ref)

    def first(group, slot):
        for ahead in range(UNROLL):
            where = block_rows(group, ahead)
            mixed = block_ref[where, :].astype(BF16)
            dense_ref[where, :] = mixed
            score_refs[slot][tile_rows(ahead), :] = score(mixed)

    def second(group, slot):
        for ahead in range(UNROLL):
            tile = tile_rows(ahead)
            probs_refs[slot][tile, :] = softmax_turned(score_refs[slot][tile, :]).astype(BF16)

    def third(group, slot):
        for ahead in range(UNROLL):
            where = block_rows(group, ahead)
            block_ref[where, :] = dot(probs_refs[slot][tile_rows(ahead), :], dense_ref[where, :])

    for_each_group(blocks, (first, second, third))

    def scatter(cluster, block, runs, end):
        for source, start, row in runs:
            wide_ref[source, pl.ds(start, slot_rows), :] = block_ref[pl.ds(row, slot_rows), :]

    for_each_cluster(counts_ref, me_ref, place_ref, owners, per_group, scatter)
    for ahead, out_ref in zip(steps_of(sizes), out_refs):
        source = owner_of(me_ref, ahead, sizes)
        up, down = wide_ref[source, :half, :], wide_ref[source, half:rows, :]
        out_ref[...] = jnp.where(low_half((half, LANES)), swap_halves(up), down).astype(BF16)


def query_grad_kernel(sizes, per_group, slot_rows, me_ref, counts_ref, dense_ref, *refs):
    owners = sizes[0] * sizes[1]
    value_refs, out_refs, rest = refs[:owners], refs[owners : 2 * owners], refs[2 * owners :]
    place_ref, wide_ref, block_ref, sums_ref, centroid_ref = rest[:5]
    score_refs, grad_probs_refs, both_refs = rest[5:7], rest[7:9], rest[9:11]
    half = value_refs[0].shape[0]
    rows = 2 * half
    for ahead, value_ref in zip(steps_of(sizes), value_refs):
        source = source_of(me_ref, ahead, sizes)
        value = value_ref[...].astype(F32)
        wide_ref[source, :half, :] = swap_halves(value)
        wide_ref[source, half:rows, :] = value
        wide_ref[source, rows:, :] = jnp.zeros((slot_rows, LANES), F32)
    blocks = gather_blocks(counts_ref, me_ref, place_ref, owners, per_group, slot_rows, wide_ref, block_ref)

    def first(group, slot):
        for ahead in range(UNROLL):
            where, tile = block_rows(group, ahead), tile_rows(ahead)
            mixed = dense_ref[where, :]
            value = block_ref[where, :].astype(BF16)
            cotan = jnp.where(low_half(mixed.shape), jnp.zeros_like(mixed), mixed)
            score_refs[slot][tile, :] = score(mixed)
            grad_probs_refs[slot][tile, :] = dot_nt(value, cotan)

    def second(group, slot):
        for ahead in range(UNROLL):
            tile = tile_rows(ahead)
            probs = softmax_turned(score_refs[slot][tile, :])
            grad_probs = grad_probs_refs[slot][tile, :]
            probs_half = probs.astype(BF16).astype(F32)
            row_dot = jnp.sum(probs_half * grad_probs, axis=0, keepdims=True)
            grad_scores = (probs * (grad_probs - row_dot)).astype(BF16).astype(F32)
            both_refs[slot][tile, :] = (grad_scores + grad_scores.T).astype(BF16)

    def third(group, slot):
        for ahead in range(UNROLL):
            where = block_rows(group, ahead)
            grad = dot(both_refs[slot][tile_rows(ahead), :], dense_ref[where, :]) * SCALE
            grad = grad.astype(BF16).astype(F32)
            block_ref[where, :] = grad
            sums_ref[pl.ds(group * UNROLL + ahead, 1), :] = jnp.sum(grad, axis=0, keepdims=True)

    for_each_group(blocks, (first, second, third))
    most = (owners * slot_rows + BLOCK_ROWS - 1) // BLOCK_ROWS

    def scatter(cluster, block, runs, end):
        total = jnp.zeros((1, LANES), F32)
        for ahead in range(most):
            here = block + ahead
            total = total + jnp.where(here * BLOCK_ROWS < end, sums_ref[pl.ds(here, 1), :], 0.0)
        centroid_ref[pl.ds(cluster, 1), :] = total
        for source, start, row in runs:
            wide_ref[source, pl.ds(start, slot_rows), :] = block_ref[pl.ds(row, slot_rows), :]

    for_each_cluster(counts_ref, me_ref, place_ref, owners, per_group, scatter)
    extra = out_refs[0].shape[0] - half
    centroid = jnp.where(
        low_half((extra, LANES)), centroid_ref[:extra, :], swap_halves(centroid_ref[extra:, :])
    ).astype(BF16)
    for ahead, out_ref in zip(steps_of(sizes), out_refs):
        source = owner_of(me_ref, ahead, sizes)
        up, down = wide_ref[source, :half, :], wide_ref[source, half:rows, :]
        out_ref[:half, :] = jnp.where(low_half((half, LANES)), up, swap_halves(down)).astype(BF16)
        out_ref[half:, :] = centroid


def unfold(home_ref, out_ref, heads, start, half, finish):
    low = low_half((half, LANES))
    for group in range(home_ref.shape[0] // heads):
        first = group * 2 * half
        for pair in range(heads // 2):
            even = home_ref[group * heads + 2 * pair, start : start + half, :].astype(F32)
            odd = home_ref[group * heads + 2 * pair + 1, start : start + half, :].astype(F32)
            columns = slice(pair * LANES, (pair + 1) * LANES)
            out_ref[first : first + half, columns] = finish(jnp.where(low, even, swap_halves(odd)))
            out_ref[first + half : first + 2 * half, columns] = finish(
                jnp.where(low, swap_halves(even), odd)
            )


def to_half(x):
    return x.astype(BF16)


def bring_home(sizes, heads, me_ref, part_refs, home_ref, rows_ref):
    for ahead, part_ref in zip(steps_of(sizes), part_refs):
        home_ref[source_of(me_ref, ahead, sizes)] = part_ref[...]
    unfold(home_ref, rows_ref, heads, 0, rows_ref.shape[0] * heads // home_ref.shape[0] // 2, to_half)


def weight_partial(sizes, me_ref, turned_ref, rows_ref, sub_refs):
    piece = turned_ref.shape[0] // (sizes[0] * sizes[1])
    for ahead, sub_ref in enumerate(sub_refs):
        sub = lax.rem(me_ref[1] + ahead, jnp.int32(sizes[1]))
        first = [pl.multiple_of((seq * sizes[1] + sub) * piece, piece) for seq in range(sizes[0])]
        turned = jnp.concatenate([turned_ref[pl.ds(row, piece), :] for row in first], axis=0)
        partial = dot(turned, rows_ref[...]).astype(BF16)
        for seq in range(sizes[0]):
            sub_ref[seq] = partial[seq * piece : (seq + 1) * piece, :]


def input_columns(me_ref, ahead, parts, width):
    columns = width // parts
    dest = lax.rem(me_ref[2] + ahead, jnp.int32(parts))
    return pl.ds(pl.multiple_of(dest * columns, columns), columns)


def value_home_kernel(sizes, heads, parts, me_ref, turned_ref, weight_ref, *refs):
    part_refs, refs = refs[: sizes[0] * sizes[1]], refs[sizes[0] * sizes[1] :]
    rows_ref, term_refs, refs = refs[0], refs[1:parts], refs[parts:]
    sub_refs, home_ref = refs[: sizes[1]], refs[sizes[1]]
    bring_home(sizes, heads, me_ref, part_refs, home_ref, rows_ref)
    for k, term_ref in enumerate(term_refs):
        mine = input_columns(me_ref, k + 1, parts, weight_ref.shape[0])
        term_ref[...] = dot_nt(rows_ref[...], weight_ref[mine, :])
    weight_partial(sizes, me_ref, turned_ref, rows_ref, sub_refs)


def query_home_kernel(sizes, heads, factor, parts, me_ref, weight_ref, *refs):
    term_refs, refs = refs[: parts - 1], refs[parts - 1 :]
    part_refs, refs = refs[: sizes[0] * sizes[1]], refs[sizes[0] * sizes[1] :]
    out_refs, (rows_ref, centroid_ref, home_ref) = refs[: parts - 1], refs[parts - 1 :]
    bring_home(sizes, heads, me_ref, part_refs, home_ref, rows_ref)
    for k, (term_ref, out_ref) in enumerate(zip(term_refs, out_refs)):
        mine = input_columns(me_ref, k + 1, parts, weight_ref.shape[0])
        out_ref[...] = (dot_nt(rows_ref[...], weight_ref[mine, :]) + term_ref[...]).astype(BF16)
    half = rows_ref.shape[0] * heads // home_ref.shape[0] // 2
    unfold(home_ref, centroid_ref, heads, half, home_ref.shape[1] - half, lambda x: x * factor)


def query_weight_kernel(sizes, me_ref, turned_ref, rows_ref, *sub_refs):
    weight_partial(sizes, me_ref, turned_ref, rows_ref, sub_refs)


def input_own_kernel(parts, me_ref, rows_ref, value_rows_ref, w_query_ref, w_value_ref, out_ref):
    mine = input_columns(me_ref, 0, parts, w_query_ref.shape[0])
    total = dot_nt(rows_ref[...], w_query_ref[mine, :]) + dot_nt(value_rows_ref[...], w_value_ref[mine, :])
    out_ref[...] = total.astype(BF16)


def fold_subs_kernel(me_ref, *refs):
    seqs = refs[0].shape[0]
    terms, out_refs = refs[:-seqs], refs[-seqs:]
    for ahead, out_ref in enumerate(out_refs):
        seq = lax.rem(me_ref[0] + ahead, jnp.int32(seqs))
        total = terms[0][seq].astype(F32)
        for term in terms[1:]:
            total = total + term[seq].astype(F32)
        out_ref[...] = total.astype(BF16)


def sum_kernel(*refs):
    total = refs[0][...].astype(F32)
    for ref in refs[1:-1]:
        total = total + ref[...].astype(F32)
    refs[-1][...] = total.astype(refs[-1].dtype)


def input_sum_kernel(unsort_ref, *refs):
    part_refs, out_ref, total_ref = refs[:-2], refs[-2], refs[-1]
    total = part_refs[0][...].astype(F32)
    for part_ref in part_refs[1:]:
        total = total + part_ref[...].astype(F32)
    total_ref[...] = total.astype(BF16)
    out_ref[...] = dot(unsort_ref[...], total_ref[...]).astype(BF16)


def call(kernel, outs, inputs, smem=(0,), in_place=(), after=(), scratch=(), flops=0, vmem=24, name=None):
    def body(*refs):
        kernel(*refs[: len(inputs)], *refs[len(inputs) + len(after) :])

    def space(i):
        return pltpu.SMEM if i in smem else pl.ANY if i in in_place else pltpu.VMEM

    specs = [pl.BlockSpec(memory_space=space(i)) for i in range(len(inputs))]
    specs += [pl.BlockSpec(memory_space=pl.ANY)] * len(after)
    moved = sum(x.size * x.dtype.itemsize for x in inputs) + sum(
        x.size * x.dtype.itemsize for x in jax.tree.leaves(outs)
    )
    return pl.pallas_call(
        body,
        out_shape=outs,
        in_specs=specs,
        out_specs=jax.tree.map(lambda _: pl.BlockSpec(memory_space=pltpu.VMEM), outs),
        scratch_shapes=list(scratch),
        compiler_params=pltpu.CompilerParams(vmem_limit_bytes=vmem * 2**20),
        cost_estimate=pl.CostEstimate(flops=flops, bytes_accessed=moved, transcendentals=0),
        name=name,
    )(*inputs, *after)


def exchange(parts, sizes):
    out = []
    for ahead, part in zip(steps_of(sizes), parts):
        moves = [
            (
                seq * sizes[1] + sub,
                (seq + ahead[0]) % sizes[0] * sizes[1] + (sub + ahead[1]) % sizes[1],
            )
            for seq, sub in steps_of(sizes)
        ]
        out.append(part if ahead == (0, 0) else lax.ppermute(part, OWNERS, moves))
    return out


def shift(part, axis, ahead):
    size = lax.axis_size(axis)
    return lax.ppermute(part, axis, [(i, (i + ahead) % size) for i in range(size)])


def pass_round(parts, axis):
    return [parts[0]] + [shift(parts[ahead], axis, ahead) for ahead in range(1, len(parts))]


def fold_subs(me, by_sub, name):
    seqs, piece, columns = by_sub[0].shape
    return call(
        fold_subs_kernel,
        (jax.ShapeDtypeStruct((piece, columns), BF16),) * seqs,
        (me, *pass_round(by_sub, "sub")),
        name=name,
    )


def add_up(terms, dtype, name, after=()):
    out = jax.ShapeDtypeStruct(terms[0].shape, dtype)
    return call(sum_kernel, out, tuple(terms), smem=(), after=after, vmem=60, name=name)


def on_device(tokens_in, w_query, w_value, cotangent, assignment):
    sizes = (lax.axis_size("seq"), lax.axis_size("sub"))
    owners = sizes[0] * sizes[1]
    parts = lax.axis_size("head")
    toks, width = tokens_in.shape
    width_dev = cotangent.shape[1]
    heads = width_dev // HD
    slot_rows = 2 * toks // CLUSTERS
    assert owners % heads == 0 and heads % 2 == 0
    groups = owners // heads
    per_group = CLUSTERS // groups
    rows = toks if groups == 1 else per_group * slot_rows
    half = rows // 2
    slots = groups * rows
    columns = width // parts
    capacity = (slot_rows * owners + BLOCK_ROWS - 1) // BLOCK_ROWS * BLOCK_ROWS
    extra = max(per_group // 2, 16)
    shape = jax.ShapeDtypeStruct
    seq, sub = lax.axis_index("seq"), lax.axis_index("sub")
    first = lax.div(seq * sizes[1] + sub, jnp.int32(heads)) * per_group
    me = jnp.stack([seq, sub, lax.axis_index("head"), first]).astype(jnp.int32)

    def several(count, *dims):
        return (shape(dims, BF16),) * count

    assign_row = assignment.reshape(1, toks)
    *far_mixed, slot_row = call(
        functools.partial(project_far_kernel, sizes, groups, rows, heads),
        several(sizes[1], rows + COUNT_ROWS, LANES) + (shape((1, toks), jnp.int32),),
        (assign_row, tokens_in, w_query, cotangent),
        smem=(),
        in_place=(1, 2, 3),
        scratch=[
            pltpu.VMEM((toks, width), BF16),
            pltpu.VMEM((width, sizes[1] * HD), BF16),
            pltpu.VMEM((toks, sizes[1] * HD), BF16),
            pltpu.VMEM((toks, sizes[1] * LANES), BF16),
            pltpu.SemaphoreType.DMA((3, max(toks, width) // min(256, toks))),
        ],
        flops=2 * toks * width * sizes[1] * HD + 2 * rows * toks * sizes[1] * LANES,
        vmem=60,
        name="project_far",
    )
    own_mixed, *near_mixed = call(
        functools.partial(project_query_kernel, sizes, groups, rows),
        several(owners - sizes[1], rows + COUNT_ROWS, LANES),
        (me, slot_row, assign_row, tokens_in, w_query, cotangent),
        scratch=[pltpu.VMEM((toks, 2 * width_dev), BF16), pltpu.VMEM((owners, rows + COUNT_ROWS, LANES), BF16)],
        flops=2 * toks * width * width_dev + 4 * slots * toks * width_dev,
        name="project_query",
    )
    send_mixed = [own_mixed, *far_mixed, *near_mixed]
    got_mixed = exchange(send_mixed, sizes)
    *send_value, turned, unsort = call(
        functools.partial(project_value_kernel, sizes, groups, rows),
        several(owners, half, LANES) + several(1, width, slots) + several(1, toks, slots),
        (me, slot_row, tokens_in, w_value),
        after=near_mixed[:1],
        scratch=[pltpu.VMEM((toks, width_dev), BF16), pltpu.VMEM((owners, half, LANES), BF16)],
        flops=2 * toks * width * width_dev + 2 * slots * toks * width_dev,
        name="project_value",
    )
    behind = [0, *range(3, owners), 2, 1][:owners]
    send_value = [lax.optimization_barrier((part, got_mixed[k]))[0] for part, k in zip(send_value, behind)]
    got_value = exchange(send_value, sizes)
    blocks = per_group * capacity // BLOCK_ROWS
    held = blocks + (LEAD + 4) * UNROLL
    block_flops = 2 * BLOCK_ROWS * BLOCK_ROWS * LANES
    tall = pltpu.VMEM((owners, rows + slot_rows, LANES), F32)
    dense_rows = pltpu.VMEM((held * BLOCK_ROWS, LANES), F32)
    group_f32 = pltpu.VMEM((GROUP_ROWS, BLOCK_ROWS), F32)
    group_b16 = pltpu.VMEM((GROUP_ROWS, BLOCK_ROWS), BF16)
    place = pltpu.SMEM((owners,), jnp.int32)
    *back_value, dense, counts = call(
        functools.partial(value_grad_kernel, sizes, per_group, slot_rows),
        several(owners, half, LANES)
        + several(1, held * BLOCK_ROWS, LANES)
        + (shape((owners, LANES), jnp.int32),),
        (me, *got_mixed),
        after=[unsort],
        scratch=[pltpu.SMEM((owners, LANES), jnp.int32), place, tall, dense_rows, tall]
        + [group_f32] * 2
        + [group_b16] * 2,
        flops=4 * blocks * block_flops,
        vmem=48,
        name="value_grad",
    )
    home_value = exchange(back_value, sizes)
    back_query = call(
        functools.partial(query_grad_kernel, sizes, per_group, slot_rows),
        several(owners, half + extra, LANES),
        (me, counts, dense, *got_value),
        smem=(0, 1),
        scratch=[place, tall, dense_rows, pltpu.VMEM((held, LANES), F32), pltpu.VMEM((2 * extra, LANES), F32)]
        + [group_f32] * 4
        + [group_b16] * 2,
        flops=6 * blocks * block_flops,
        vmem=48,
        name="query_grad",
    )
    home_query = exchange(back_query, sizes)
    weight_flops = 2 * slots * width * width_dev
    home_flops = weight_flops // parts * (parts - 1)
    sub_shapes = several(sizes[1], sizes[0], width // owners, width_dev)
    value_rows, *refs = call(
        functools.partial(value_home_kernel, sizes, heads, parts),
        several(1, slots, width_dev) + (shape((slots, columns), F32),) * (parts - 1) + sub_shapes,
        (me, turned, w_value, *home_value),
        scratch=[pltpu.VMEM((owners, half, LANES), BF16)],
        flops=weight_flops + home_flops,
        name="value_home",
    )
    value_terms, value_weight = refs[: parts - 1], refs[parts - 1 :]
    value_weight = fold_subs(me, value_weight, "value_subs")
    *partials, query_rows, centroid_grad = call(
        functools.partial(query_home_kernel, sizes, heads, (CLUSTERS / (toks * owners)) ** 0.5, parts),
        several(parts - 1, slots, columns)
        + several(1, slots, width_dev)
        + (shape((groups * 2 * extra, width_dev), F32),),
        (me, w_query, *value_terms, *home_query),
        scratch=[pltpu.VMEM((owners, half + extra, LANES), BF16)],
        flops=home_flops,
        name="query_home",
    )
    arrived = [shift(partial, "head", k + 1) for k, partial in enumerate(partials)]
    value_weight, _ = lax.optimization_barrier((value_weight, home_query))
    value_weight = pass_round(value_weight, "seq")
    query_weight = call(
        functools.partial(query_weight_kernel, sizes),
        sub_shapes,
        (me, turned, query_rows),
        flops=weight_flops,
        name="query_weight",
    )
    query_weight = fold_subs(me, query_weight, "query_subs")
    own = call(
        functools.partial(input_own_kernel, parts),
        shape((slots, columns), BF16),
        (me, query_rows, value_rows, w_query, w_value),
        after=query_weight[:1],
        flops=weight_flops * 2 // parts,
        name="input_own",
    )
    query_weight = pass_round(query_weight, "seq")
    grad_wv = add_up(value_weight, F32, "value_sum", [own])
    grad_input = call(
        input_sum_kernel,
        shape((toks, columns), BF16),
        (unsort, own, *arrived),
        smem=(),
        scratch=[pltpu.VMEM((slots, columns), BF16)],
        flops=2 * toks * slots * columns,
        name="input_sum",
    )
    grad_wq = add_up(query_weight, F32, "query_sum", [grad_input])
    if groups > 1:
        centroid_grad = centroid_grad.reshape(groups, 2 * extra, width_dev)[:, :per_group]
        centroid_grad = centroid_grad.reshape(CLUSTERS, width_dev)
    return (grad_input, grad_wq, grad_wv, centroid_grad)


def solution(mesh):
    return jax.shard_map(
        on_device,
        mesh=mesh,
        in_specs=(
            P(("grp", "seq", "sub"), None),
            P(None, "head"),
            P(None, "head"),
            P(("grp", "seq", "sub"), "head"),
            P(("grp", "seq", "sub"), None),
        ),
        out_specs=(
            P(("grp", "seq", "sub"), "head"),
            P(("grp", "seq", "sub"), "head"),
            P(("grp", "seq", "sub"), "head"),
            P("grp", "head"),
        ),
        check_vma=False,
    )
```

```python
import functools

import jax
import jax.numpy as jnp
from jax import lax
from jax.experimental import pallas as pl
from jax.experimental.pallas import tpu as pltpu
from jax.sharding import PartitionSpec as P

HD = 64
CLUSTERS = 64
BLOCK_ROWS = 128
LANES = 128
UNROLL = 4
COUNT_ROWS = 16
SCALE = 0.5 * HD ** (-0.5)
F32 = jnp.float32
BF16 = jnp.bfloat16
OWNERS = ("seq", "sub")
GROUP_ROWS = UNROLL * BLOCK_ROWS
LEAD = 2


def iota(shape, dim):
    return lax.broadcasted_iota(jnp.int32, shape, dim)


def low_half(shape):
    return iota(shape, 1) < HD


def swap_halves(tile):
    return pltpu.roll(tile, HD, 1)


def dot(a, b):
    return jnp.dot(a, b, preferred_element_type=F32)


def dot_nt(a, b):
    return lax.dot_general(a, b, (((1,), (1,)), ((), ())), preferred_element_type=F32)


def ones_where(condition):
    return jnp.where(condition, 1.0, 0.0).astype(BF16)


def owner_of(me_ref, ahead, sizes):
    seq = lax.rem(me_ref[0] + ahead[0], jnp.int32(sizes[0]))
    sub = lax.rem(me_ref[1] + ahead[1], jnp.int32(sizes[1]))
    return seq * sizes[1] + sub


def source_of(me_ref, ahead, sizes):
    return owner_of(me_ref, ((sizes[0] - ahead[0]) % sizes[0], (sizes[1] - ahead[1]) % sizes[1]), sizes)


def steps_of(sizes):
    far = sorted(range(1, sizes[0]), key=lambda seq: -min(seq, sizes[0] - seq))
    subs = range(sizes[1])
    return [(0, 0)] + [(seq, sub) for seq in far for sub in subs] + [(0, sub) for sub in subs if sub]


def hand_out(by_owner_ref, out_refs, me_ref, sizes):
    for ahead, out_ref in zip(steps_of(sizes), out_refs):
        out_ref[...] = by_owner_ref[owner_of(me_ref, ahead, sizes)]


def slots_of(assign, groups, rows):
    toks = assign.shape[1]
    per_group = CLUSTERS // groups
    member = jnp.where(iota((CLUSTERS, toks), 0) == assign, 1.0, 0.0)
    member_b = member.astype(BF16)
    upto = ones_where(iota((LANES, LANES), 0) <= iota((LANES, LANES), 1))
    counts = jnp.zeros((CLUSTERS, 1), F32)
    running = []
    for first in range(0, toks, LANES):
        within = dot(member_b[:, first : first + LANES], upto)
        running.append(within + counts)
        counts = counts + within[:, LANES - 1 :]
    running = jnp.concatenate(running, axis=1)
    here, other = iota((CLUSTERS, CLUSTERS), 0), iota((CLUSTERS, CLUSTERS), 1)
    group_of = lambda index: lax.div(index, jnp.int32(per_group))
    earlier = ones_where((other < here) & (group_of(other) == group_of(here)))
    base = dot(earlier, jnp.broadcast_to(counts, (CLUSTERS, LANES)).astype(BF16))[:, :1]
    base = base + (group_of(iota((CLUSTERS, 1), 0)) * rows).astype(F32)
    slot = jnp.sum(member * (running - 1.0 + base), axis=0, keepdims=True).astype(jnp.int32)
    spread = jnp.concatenate([member_b, jnp.zeros((LANES - CLUSTERS, toks), BF16)], axis=0)
    return slot, dot_nt(jnp.ones((COUNT_ROWS, toks), BF16), spread).astype(BF16)


def beside(query, cotan):
    low = low_half(query.shape)
    even = jnp.where(low, query, swap_halves(cotan)).astype(BF16)
    return even, jnp.where(low, swap_halves(query), cotan).astype(BF16)


def load_rows(source, target, sems, fine):
    return [
        pltpu.make_async_copy(source.at[pl.ds(row, fine), :], target.at[pl.ds(row, fine), :], sems.at[row // fine])
        for row in range(0, target.shape[0], fine)
    ]


def project_far_kernel(sizes, groups, rows, heads, assign_ref, tokens_hbm, weight_hbm, cotan_hbm, *refs):
    out_refs, refs = refs[: sizes[1]], refs[sizes[1] :]
    slot_ref, tokens_ref, weight_ref, cotan_ref, mixed_ref, sems = refs
    toks = tokens_ref.shape[0]
    fine = min(256, toks)
    me = (lax.axis_index("seq"), lax.axis_index("sub"))
    owner = owner_of(me, steps_of(sizes)[1], sizes) - me[1]
    group, head = lax.div(owner, jnp.int32(heads)), lax.rem(owner, jnp.int32(heads))
    columns = pl.ds(pl.multiple_of(head * HD, LANES), sizes[1] * HD)
    loads = [
        load_rows(source, target, sems.at[kind], fine)
        for kind, (source, target) in enumerate(
            ((weight_hbm.at[:, columns], weight_ref), (tokens_hbm, tokens_ref), (cotan_hbm.at[:, columns], cotan_ref))
        )
    ]
    for load in loads:
        for copy in load:
            copy.start()
    slot, tallies = slots_of(assign_ref[...], groups, rows)
    slot_ref[...] = slot
    pick = ones_where(iota((rows, toks), 0) + group * rows == slot)
    for copy in loads[0] + loads[2]:
        copy.wait()
    step = min(512, toks)
    for first in range(0, toks, step):
        for copy in loads[1][first // fine : (first + step) // fine]:
            copy.wait()
        where = slice(first, first + step)
        query, cotan = dot(tokens_ref[where, :], weight_ref[...]), cotan_ref[where, :].astype(F32)
        for pair in range(sizes[1] // 2):
            pair_columns = slice(pair * LANES, (pair + 1) * LANES)
            even, odd = beside(query[:, pair_columns], cotan[:, pair_columns])
            mixed_ref[where, 2 * pair * LANES : (2 * pair + 1) * LANES] = even
            mixed_ref[where, (2 * pair + 1) * LANES : (2 * pair + 2) * LANES] = odd
    in_order = dot(pick, mixed_ref[...]).astype(BF16)
    for ahead, out_ref in enumerate(out_refs):
        sub = lax.rem(me[1] + ahead, jnp.int32(sizes[1]))
        for other in range(sizes[1]):

            @pl.when(sub == other)
            def _():
                out_ref[:rows, :] = in_order[:, other * LANES : (other + 1) * LANES]

        out_ref[rows:, :] = tallies


def project_query_kernel(sizes, groups, rows, me_ref, slot_ref, assign_ref, tokens_ref, weight_ref, cotan_ref, *rest):
    out_refs, (mixed_ref, sorted_ref) = rest[:-2], rest[-2:]
    toks = tokens_ref.shape[0]
    heads = weight_ref.shape[1] // HD
    step = min(512, toks)
    for first in range(0, toks, step):
        where = slice(first, first + step)
        query, cotan = dot(tokens_ref[where, :], weight_ref[...]), cotan_ref[where, :].astype(F32)
        for pair in range(heads // 2):
            columns = slice(pair * LANES, (pair + 1) * LANES)
            even, odd = beside(query[:, columns], cotan[:, columns])
            mixed_ref[where, 2 * pair * LANES : (2 * pair + 1) * LANES] = even
            mixed_ref[where, (2 * pair + 1) * LANES : (2 * pair + 2) * LANES] = odd
    part = min(512, rows)
    pieces = rows // part

    @pl.loop(0, groups * pieces)
    def _(i):
        group, piece = lax.div(i, jnp.int32(pieces)), lax.rem(i, jnp.int32(pieces))
        first = pl.multiple_of(piece * part, part)
        pick = ones_where(iota((part, toks), 0) + i * part == slot_ref[...])
        sorted_rows = dot(pick, mixed_ref[...]).astype(BF16)
        for head in range(heads):
            sorted_ref[group * heads + head, pl.ds(first, part), :] = sorted_rows[
                :, head * LANES : (head + 1) * LANES
            ]

    member = jnp.where(iota((LANES, toks), 0) == assign_ref[...], 1.0, 0.0).astype(BF16)
    tallies = dot_nt(jnp.ones((COUNT_ROWS, toks), BF16), member).astype(BF16)
    for owner in range(sorted_ref.shape[0]):
        sorted_ref[owner, rows:, :] = tallies
    steps = steps_of(sizes)
    for ahead, out_ref in zip(steps[:1] + steps[1 + sizes[1] :], out_refs):
        out_ref[...] = sorted_ref[owner_of(me_ref, ahead, sizes)]


def project_value_kernel(sizes, groups, rows, me_ref, slot_ref, tokens_ref, weight_ref, *rest):
    out_refs, (turned_ref, unsort_ref, value_ref, sorted_ref) = rest[:-4], rest[-4:]
    toks = tokens_ref.shape[0]
    heads = weight_ref.shape[1] // HD
    step = min(512, toks)

    @pl.loop(0, toks // step)
    def _(i):
        where = pl.ds(pl.multiple_of(i * step, step), step)
        value_ref[where, :] = dot(tokens_ref[where, :], weight_ref[...]).astype(BF16)

    half = rows // 2
    part = min(256, half)
    pieces = half // part

    @pl.loop(0, groups * pieces)
    def _(i):
        group, piece = lax.div(i, jnp.int32(pieces)), lax.rem(i, jnp.int32(pieces))
        first = pl.multiple_of(piece * part, part)
        index = iota((part, toks), 0) + group * rows + first
        upper = dot(ones_where(index == slot_ref[...]), value_ref[...])
        lower = dot(ones_where(index + half == slot_ref[...]), value_ref[...])
        low = low_half((part, LANES))
        for pair in range(heads // 2):
            up = upper[:, pair * LANES : (pair + 1) * LANES]
            down = lower[:, pair * LANES : (pair + 1) * LANES]
            even = jnp.where(low, up, swap_halves(down)).astype(BF16)
            odd = jnp.where(low, swap_halves(up), down).astype(BF16)
            sorted_ref[group * heads + 2 * pair, pl.ds(first, part), :] = even
            sorted_ref[group * heads + 2 * pair + 1, pl.ds(first, part), :] = odd

    hand_out(sorted_ref, out_refs, me_ref, sizes)
    turned = tokens_ref[...].T
    slots = unsort_ref.shape[1]
    part = min(256, slots)
    for i in range(slots // part):
        pick = ones_where(iota((part, toks), 0) + i * part == slot_ref[...])
        unsort_ref[:, i * part : (i + 1) * part] = pick.T
        turned_ref[:, i * part : (i + 1) * part] = dot_nt(turned, pick).astype(BF16)


def score(mixed):
    query = jnp.where(low_half(mixed.shape), mixed.astype(F32) * SCALE, 0.0).astype(BF16)
    return dot_nt(query, mixed)


def softmax_turned(scores):
    shape = scores.shape
    seen = iota(shape, 0) <= iota(shape, 1)
    scores = jnp.where(seen, scores, -jnp.inf)
    raised = jnp.exp(scores - jnp.max(scores, axis=0, keepdims=True))
    return raised * (1.0 / jnp.sum(raised, axis=0, keepdims=True))


def for_each_cluster(counts_ref, me_ref, place_ref, owners, per_group, body):
    for source in range(owners):
        place_ref[source] = 0

    def step(cluster, block):
        runs = []
        total = 0
        base = block * BLOCK_ROWS
        for source in range(owners):
            count = counts_ref[source, me_ref[3] + cluster]
            start = place_ref[source]
            runs.append((source, start, base + total))
            place_ref[source] = start + count
            total = total + count
        body(cluster, block, runs, base + total)
        return block + lax.shift_right_logical(total + (BLOCK_ROWS - 1), jnp.int32(7))

    return lax.fori_loop(0, per_group, step, jnp.int32(LEAD * UNROLL))


def gather_blocks(counts_ref, me_ref, place_ref, owners, per_group, slot_rows, wide_ref, block_ref):
    def body(cluster, block, runs, end):
        for source, start, row in runs:
            block_ref[pl.ds(row, slot_rows), :] = wide_ref[source, pl.ds(start, slot_rows), :]
        block_ref[pl.ds(end, BLOCK_ROWS), :] = jnp.zeros((BLOCK_ROWS, LANES), F32)

    blocks = for_each_cluster(counts_ref, me_ref, place_ref, owners, per_group, body)
    spare = pl.ds(pl.multiple_of(blocks * BLOCK_ROWS, BLOCK_ROWS), GROUP_ROWS)
    block_ref[spare, :] = jnp.zeros((GROUP_ROWS, LANES), F32)
    return blocks


def for_each_group(blocks, stages):
    first, second, third = stages
    groups = lax.div(blocks + (UNROLL - 1), jnp.int32(UNROLL))

    def step(i, carry):
        for slot in range(2):
            group = LEAD + 2 * i + slot
            third(group - 2, slot)
            second(group - 1, 1 - slot)
            first(group, slot)
        return carry

    lax.fori_loop(0, lax.shift_right_logical(groups + 1, jnp.int32(1)), step, 0)


def block_rows(group, ahead):
    return pl.ds(pl.multiple_of((group * UNROLL + ahead) * BLOCK_ROWS, BLOCK_ROWS), BLOCK_ROWS)


def tile_rows(ahead):
    return slice(ahead * BLOCK_ROWS, (ahead + 1) * BLOCK_ROWS)


def value_grad_kernel(sizes, per_group, slot_rows, me_ref, *refs):
    owners = sizes[0] * sizes[1]
    mixed_refs, out_refs, rest = refs[:owners], refs[owners : 2 * owners], refs[2 * owners :]
    dense_ref, counts_out_ref, counts_ref, place_ref, wide_ref, block_ref, home_ref = rest[:7]
    score_refs, probs_refs = rest[7:9], rest[9:11]
    half = out_refs[0].shape[0]
    rows = 2 * half
    for ahead, mixed_ref in zip(steps_of(sizes), mixed_refs):
        source = source_of(me_ref, ahead, sizes)
        tail = mixed_ref[rows:, :].astype(F32).astype(jnp.int32)
        counts_out_ref[pl.ds(source, 1), :] = tail[:1, :]
        wide_ref[source, :rows, :] = mixed_ref[:rows, :].astype(F32)
        wide_ref[source, rows:, :] = jnp.zeros((slot_rows, LANES), F32)
    pltpu.sync_copy(counts_out_ref, counts_ref)
    blocks = gather_blocks(counts_ref, me_ref, place_ref, owners, per_group, slot_rows, wide_ref, block_ref)

    def first(group, slot):
        for ahead in range(UNROLL):
            where = block_rows(group, ahead)
            mixed = block_ref[where, :].astype(BF16)
            dense_ref[where, :] = mixed
            score_refs[slot][tile_rows(ahead), :] = score(mixed)

    def second(group, slot):
        for ahead in range(UNROLL):
            tile = tile_rows(ahead)
            probs_refs[slot][tile, :] = softmax_turned(score_refs[slot][tile, :]).astype(BF16)

    def third(group, slot):
        for ahead in range(UNROLL):
            where = block_rows(group, ahead)
            block_ref[where, :] = dot(probs_refs[slot][tile_rows(ahead), :], dense_ref[where, :])

    for_each_group(blocks, (first, second, third))

    def scatter(cluster, block, runs, end):
        for source, start, row in runs:
            wide_ref[source, pl.ds(start, slot_rows), :] = block_ref[pl.ds(row, slot_rows), :]

    for_each_cluster(counts_ref, me_ref, place_ref, owners, per_group, scatter)
    for ahead, out_ref in zip(steps_of(sizes), out_refs):
        source = owner_of(me_ref, ahead, sizes)
        up, down = wide_ref[source, :half, :], wide_ref[source, half:rows, :]
        out_ref[...] = jnp.where(low_half((half, LANES)), swap_halves(up), down).astype(BF16)


def query_grad_kernel(sizes, per_group, slot_rows, me_ref, counts_ref, dense_ref, *refs):
    owners = sizes[0] * sizes[1]
    value_refs, out_refs, rest = refs[:owners], refs[owners : 2 * owners], refs[2 * owners :]
    place_ref, wide_ref, block_ref, sums_ref, centroid_ref = rest[:5]
    score_refs, grad_probs_refs, both_refs = rest[5:7], rest[7:9], rest[9:11]
    half = value_refs[0].shape[0]
    rows = 2 * half
    for ahead, value_ref in zip(steps_of(sizes), value_refs):
        source = source_of(me_ref, ahead, sizes)
        value = value_ref[...].astype(F32)
        wide_ref[source, :half, :] = swap_halves(value)
        wide_ref[source, half:rows, :] = value
        wide_ref[source, rows:, :] = jnp.zeros((slot_rows, LANES), F32)
    blocks = gather_blocks(counts_ref, me_ref, place_ref, owners, per_group, slot_rows, wide_ref, block_ref)

    def first(group, slot):
        for ahead in range(UNROLL):
            where, tile = block_rows(group, ahead), tile_rows(ahead)
            mixed = dense_ref[where, :]
            value = block_ref[where, :].astype(BF16)
            cotan = jnp.where(low_half(mixed.shape), jnp.zeros_like(mixed), mixed)
            score_refs[slot][tile, :] = score(mixed)
            grad_probs_refs[slot][tile, :] = dot_nt(value, cotan)

    def second(group, slot):
        for ahead in range(UNROLL):
            tile = tile_rows(ahead)
            probs = softmax_turned(score_refs[slot][tile, :])
            grad_probs = grad_probs_refs[slot][tile, :]
            probs_half = probs.astype(BF16).astype(F32)
            row_dot = jnp.sum(probs_half * grad_probs, axis=0, keepdims=True)
            grad_scores = (probs * (grad_probs - row_dot)).astype(BF16).astype(F32)
            both_refs[slot][tile, :] = (grad_scores + grad_scores.T).astype(BF16)

    def third(group, slot):
        for ahead in range(UNROLL):
            where = block_rows(group, ahead)
            grad = dot(both_refs[slot][tile_rows(ahead), :], dense_ref[where, :]) * SCALE
            grad = grad.astype(BF16).astype(F32)
            block_ref[where, :] = grad
            sums_ref[pl.ds(group * UNROLL + ahead, 1), :] = jnp.sum(grad, axis=0, keepdims=True)

    for_each_group(blocks, (first, second, third))
    most = (owners * slot_rows + BLOCK_ROWS - 1) // BLOCK_ROWS

    def scatter(cluster, block, runs, end):
        total = jnp.zeros((1, LANES), F32)
        for ahead in range(most):
            here = block + ahead
            total = total + jnp.where(here * BLOCK_ROWS < end, sums_ref[pl.ds(here, 1), :], 0.0)
        centroid_ref[pl.ds(cluster, 1), :] = total
        for source, start, row in runs:
            wide_ref[source, pl.ds(start, slot_rows), :] = block_ref[pl.ds(row, slot_rows), :]

    for_each_cluster(counts_ref, me_ref, place_ref, owners, per_group, scatter)
    extra = out_refs[0].shape[0] - half
    centroid = jnp.where(
        low_half((extra, LANES)), centroid_ref[:extra, :], swap_halves(centroid_ref[extra:, :])
    ).astype(BF16)
    for ahead, out_ref in zip(steps_of(sizes), out_refs):
        source = owner_of(me_ref, ahead, sizes)
        up, down = wide_ref[source, :half, :], wide_ref[source, half:rows, :]
        out_ref[:half, :] = jnp.where(low_half((half, LANES)), up, swap_halves(down)).astype(BF16)
        out_ref[half:, :] = centroid


def unfold(home_ref, out_ref, heads, start, half, finish):
    low = low_half((half, LANES))
    for group in range(home_ref.shape[0] // heads):
        first = group * 2 * half
        for pair in range(heads // 2):
            even = home_ref[group * heads + 2 * pair, start : start + half, :].astype(F32)
            odd = home_ref[group * heads + 2 * pair + 1, start : start + half, :].astype(F32)
            columns = slice(pair * LANES, (pair + 1) * LANES)
            out_ref[first : first + half, columns] = finish(jnp.where(low, even, swap_halves(odd)))
            out_ref[first + half : first + 2 * half, columns] = finish(
                jnp.where(low, swap_halves(even), odd)
            )


def to_half(x):
    return x.astype(BF16)


def bring_home(sizes, heads, me_ref, part_refs, home_ref, rows_ref):
    for ahead, part_ref in zip(steps_of(sizes), part_refs):
        home_ref[source_of(me_ref, ahead, sizes)] = part_ref[...]
    unfold(home_ref, rows_ref, heads, 0, rows_ref.shape[0] * heads // home_ref.shape[0] // 2, to_half)


def weight_partial(sizes, me_ref, turned_ref, rows_ref, sub_refs):
    piece = turned_ref.shape[0] // (sizes[0] * sizes[1])
    for ahead, sub_ref in enumerate(sub_refs):
        sub = lax.rem(me_ref[1] + ahead, jnp.int32(sizes[1]))
        first = [pl.multiple_of((seq * sizes[1] + sub) * piece, piece) for seq in range(sizes[0])]
        turned = jnp.concatenate([turned_ref[pl.ds(row, piece), :] for row in first], axis=0)
        partial = dot(turned, rows_ref[...]).astype(BF16)
        for seq in range(sizes[0]):
            sub_ref[seq] = partial[seq * piece : (seq + 1) * piece, :]


def input_columns(me_ref, ahead, parts, width):
    columns = width // parts
    dest = lax.rem(me_ref[2] + ahead, jnp.int32(parts))
    return pl.ds(pl.multiple_of(dest * columns, columns), columns)


def value_home_kernel(sizes, heads, parts, me_ref, turned_ref, weight_ref, *refs):
    part_refs, refs = refs[: sizes[0] * sizes[1]], refs[sizes[0] * sizes[1] :]
    rows_ref, term_refs, refs = refs[0], refs[1:parts], refs[parts:]
    sub_refs, home_ref = refs[: sizes[1]], refs[sizes[1]]
    bring_home(sizes, heads, me_ref, part_refs, home_ref, rows_ref)
    for k, term_ref in enumerate(term_refs):
        mine = input_columns(me_ref, k + 1, parts, weight_ref.shape[0])
        term_ref[...] = dot_nt(rows_ref[...], weight_ref[mine, :])
    weight_partial(sizes, me_ref, turned_ref, rows_ref, sub_refs)


def query_home_kernel(sizes, heads, factor, parts, me_ref, weight_ref, *refs):
    term_refs, refs = refs[: parts - 1], refs[parts - 1 :]
    part_refs, refs = refs[: sizes[0] * sizes[1]], refs[sizes[0] * sizes[1] :]
    out_refs, (rows_ref, centroid_ref, home_ref) = refs[: parts - 1], refs[parts - 1 :]
    bring_home(sizes, heads, me_ref, part_refs, home_ref, rows_ref)
    for k, (term_ref, out_ref) in enumerate(zip(term_refs, out_refs)):
        mine = input_columns(me_ref, k + 1, parts, weight_ref.shape[0])
        out_ref[...] = (dot_nt(rows_ref[...], weight_ref[mine, :]) + term_ref[...]).astype(BF16)
    half = rows_ref.shape[0] * heads // home_ref.shape[0] // 2
    unfold(home_ref, centroid_ref, heads, half, home_ref.shape[1] - half, lambda x: x * factor)


def query_weight_kernel(sizes, me_ref, turned_ref, rows_ref, *sub_refs):
    weight_partial(sizes, me_ref, turned_ref, rows_ref, sub_refs)


def input_own_kernel(parts, me_ref, rows_ref, value_rows_ref, w_query_ref, w_value_ref, out_ref):
    mine = input_columns(me_ref, 0, parts, w_query_ref.shape[0])
    total = dot_nt(rows_ref[...], w_query_ref[mine, :]) + dot_nt(value_rows_ref[...], w_value_ref[mine, :])
    out_ref[...] = total.astype(BF16)


def fold_subs_kernel(me_ref, *refs):
    seqs = refs[0].shape[0]
    terms, out_refs = refs[:-seqs], refs[-seqs:]
    for ahead, out_ref in enumerate(out_refs):
        seq = lax.rem(me_ref[0] + ahead, jnp.int32(seqs))
        total = terms[0][seq].astype(F32)
        for term in terms[1:]:
            total = total + term[seq].astype(F32)
        out_ref[...] = total.astype(BF16)


def sum_kernel(*refs):
    total = refs[0][...].astype(F32)
    for ref in refs[1:-1]:
        total = total + ref[...].astype(F32)
    refs[-1][...] = total.astype(refs[-1].dtype)


def input_sum_kernel(unsort_ref, weight_ref, *refs):
    part_refs, out_ref, weight_out_ref, total_ref = refs[:-3], refs[-3], refs[-2], refs[-1]
    total = part_refs[0][...].astype(F32)
    for part_ref in part_refs[1:]:
        total = total + part_ref[...].astype(F32)
    total_ref[...] = total.astype(BF16)
    out_ref[...] = dot(unsort_ref[...], total_ref[...]).astype(BF16)
    weight_out_ref[...] = weight_ref[...]


def call(kernel, outs, inputs, smem=(0,), in_place=(), after=(), scratch=(), flops=0, vmem=24, name=None):
    def body(*refs):
        kernel(*refs[: len(inputs)], *refs[len(inputs) + len(after) :])

    def space(i):
        return pltpu.SMEM if i in smem else pl.ANY if i in in_place else pltpu.VMEM

    specs = [pl.BlockSpec(memory_space=space(i)) for i in range(len(inputs))]
    specs += [pl.BlockSpec(memory_space=pl.ANY)] * len(after)
    moved = sum(x.size * x.dtype.itemsize for x in inputs) + sum(
        x.size * x.dtype.itemsize for x in jax.tree.leaves(outs)
    )
    return pl.pallas_call(
        body,
        out_shape=outs,
        in_specs=specs,
        out_specs=jax.tree.map(lambda _: pl.BlockSpec(memory_space=pltpu.VMEM), outs),
        scratch_shapes=list(scratch),
        compiler_params=pltpu.CompilerParams(vmem_limit_bytes=vmem * 2**20),
        cost_estimate=pl.CostEstimate(flops=flops, bytes_accessed=moved, transcendentals=0),
        name=name,
    )(*inputs, *after)


def exchange(parts, sizes):
    out = []
    for ahead, part in zip(steps_of(sizes), parts):
        moves = [
            (
                seq * sizes[1] + sub,
                (seq + ahead[0]) % sizes[0] * sizes[1] + (sub + ahead[1]) % sizes[1],
            )
            for seq, sub in steps_of(sizes)
        ]
        out.append(part if ahead == (0, 0) else lax.ppermute(part, OWNERS, moves))
    return out


def shift(part, axis, ahead):
    size = lax.axis_size(axis)
    return lax.ppermute(part, axis, [(i, (i + ahead) % size) for i in range(size)])


def pass_round(parts, axis):
    return [parts[0]] + [shift(parts[ahead], axis, ahead) for ahead in range(1, len(parts))]


def fold_subs(me, by_sub, name):
    seqs, piece, columns = by_sub[0].shape
    return call(
        fold_subs_kernel,
        (jax.ShapeDtypeStruct((piece, columns), BF16),) * seqs,
        (me, *pass_round(by_sub, "sub")),
        name=name,
    )


def add_up(terms, dtype, name, after=()):
    out = jax.ShapeDtypeStruct(terms[0].shape, dtype)
    return call(sum_kernel, out, tuple(terms), smem=(), after=after, name=name)


def on_device(tokens_in, w_query, w_value, cotangent, assignment):
    sizes = (lax.axis_size("seq"), lax.axis_size("sub"))
    owners = sizes[0] * sizes[1]
    parts = lax.axis_size("head")
    toks, width = tokens_in.shape
    width_dev = cotangent.shape[1]
    heads = width_dev // HD
    slot_rows = 2 * toks // CLUSTERS
    assert owners % heads == 0 and heads % 2 == 0
    groups = owners // heads
    per_group = CLUSTERS // groups
    rows = toks if groups == 1 else per_group * slot_rows
    half = rows // 2
    slots = groups * rows
    columns = width // parts
    capacity = (slot_rows * owners + BLOCK_ROWS - 1) // BLOCK_ROWS * BLOCK_ROWS
    extra = max(per_group // 2, 16)
    shape = jax.ShapeDtypeStruct
    seq, sub = lax.axis_index("seq"), lax.axis_index("sub")
    first = lax.div(seq * sizes[1] + sub, jnp.int32(heads)) * per_group
    me = jnp.stack([seq, sub, lax.axis_index("head"), first]).astype(jnp.int32)

    def several(count, *dims):
        return (shape(dims, BF16),) * count

    assign_row = assignment.reshape(1, toks)
    *far_mixed, slot_row = call(
        functools.partial(project_far_kernel, sizes, groups, rows, heads),
        several(sizes[1], rows + COUNT_ROWS, LANES) + (shape((1, toks), jnp.int32),),
        (assign_row, tokens_in, w_query, cotangent),
        smem=(),
        in_place=(1, 2, 3),
        scratch=[
            pltpu.VMEM((toks, width), BF16),
            pltpu.VMEM((width, sizes[1] * HD), BF16),
            pltpu.VMEM((toks, sizes[1] * HD), BF16),
            pltpu.VMEM((toks, sizes[1] * LANES), BF16),
            pltpu.SemaphoreType.DMA((3, max(toks, width) // min(256, toks))),
        ],
        flops=2 * toks * width * sizes[1] * HD + 2 * rows * toks * sizes[1] * LANES,
        vmem=60,
        name="project_far",
    )
    own_mixed, *near_mixed = call(
        functools.partial(project_query_kernel, sizes, groups, rows),
        several(owners - sizes[1], rows + COUNT_ROWS, LANES),
        (me, slot_row, assign_row, tokens_in, w_query, cotangent),
        scratch=[pltpu.VMEM((toks, 2 * width_dev), BF16), pltpu.VMEM((owners, rows + COUNT_ROWS, LANES), BF16)],
        flops=2 * toks * width * width_dev + 4 * slots * toks * width_dev,
        name="project_query",
    )
    send_mixed = [own_mixed, *far_mixed, *near_mixed]
    got_mixed = exchange(send_mixed, sizes)
    *send_value, turned, unsort = call(
        functools.partial(project_value_kernel, sizes, groups, rows),
        several(owners, half, LANES) + several(1, width, slots) + several(1, toks, slots),
        (me, slot_row, tokens_in, w_value),
        after=near_mixed[:1],
        scratch=[pltpu.VMEM((toks, width_dev), BF16), pltpu.VMEM((owners, half, LANES), BF16)],
        flops=2 * toks * width * width_dev + 2 * slots * toks * width_dev,
        name="project_value",
    )
    behind = [0, *range(3, owners), 2, 1][:owners]
    send_value = [lax.optimization_barrier((part, got_mixed[k]))[0] for part, k in zip(send_value, behind)]
    got_value = exchange(send_value, sizes)
    blocks = per_group * capacity // BLOCK_ROWS
    held = blocks + (LEAD + 4) * UNROLL
    block_flops = 2 * BLOCK_ROWS * BLOCK_ROWS * LANES
    tall = pltpu.VMEM((owners, rows + slot_rows, LANES), F32)
    dense_rows = pltpu.VMEM((held * BLOCK_ROWS, LANES), F32)
    group_f32 = pltpu.VMEM((GROUP_ROWS, BLOCK_ROWS), F32)
    group_b16 = pltpu.VMEM((GROUP_ROWS, BLOCK_ROWS), BF16)
    place = pltpu.SMEM((owners,), jnp.int32)
    *back_value, dense, counts = call(
        functools.partial(value_grad_kernel, sizes, per_group, slot_rows),
        several(owners, half, LANES)
        + several(1, held * BLOCK_ROWS, LANES)
        + (shape((owners, LANES), jnp.int32),),
        (me, *got_mixed),
        after=[unsort],
        scratch=[pltpu.SMEM((owners, LANES), jnp.int32), place, tall, dense_rows, tall]
        + [group_f32] * 2
        + [group_b16] * 2,
        flops=4 * blocks * block_flops,
        vmem=48,
        name="value_grad",
    )
    home_value = exchange(back_value, sizes)
    back_query = call(
        functools.partial(query_grad_kernel, sizes, per_group, slot_rows),
        several(owners, half + extra, LANES),
        (me, counts, dense, *got_value),
        smem=(0, 1),
        scratch=[place, tall, dense_rows, pltpu.VMEM((held, LANES), F32), pltpu.VMEM((2 * extra, LANES), F32)]
        + [group_f32] * 4
        + [group_b16] * 2,
        flops=6 * blocks * block_flops,
        vmem=48,
        name="query_grad",
    )
    home_query = exchange(back_query, sizes)
    weight_flops = 2 * slots * width * width_dev
    home_flops = weight_flops // parts * (parts - 1)
    piece = width // owners
    sub_shapes = several(sizes[1], sizes[0], piece, width_dev)
    value_rows, *refs = call(
        functools.partial(value_home_kernel, sizes, heads, parts),
        several(1, slots, width_dev) + (shape((slots, columns), F32),) * (parts - 1) + sub_shapes,
        (me, turned, w_value, *home_value),
        scratch=[pltpu.VMEM((owners, half, LANES), BF16)],
        flops=weight_flops + home_flops,
        name="value_home",
    )
    value_terms, value_weight = refs[: parts - 1], refs[parts - 1 :]
    value_weight = fold_subs(me, value_weight, "value_subs")
    *partials, query_rows, centroid_grad = call(
        functools.partial(query_home_kernel, sizes, heads, (CLUSTERS / (toks * owners)) ** 0.5, parts),
        several(parts - 1, slots, columns)
        + several(1, slots, width_dev)
        + (shape((groups * 2 * extra, width_dev), F32),),
        (me, w_query, *value_terms, *home_query),
        scratch=[pltpu.VMEM((owners, half + extra, LANES), BF16)],
        flops=home_flops,
        name="query_home",
    )
    arrived = [shift(partial, "head", k + 1) for k, partial in enumerate(partials)]
    value_weight, _ = lax.optimization_barrier((value_weight, home_query))
    value_weight = pass_round(value_weight, "seq")
    query_weight = call(
        functools.partial(query_weight_kernel, sizes),
        sub_shapes,
        (me, turned, query_rows),
        flops=weight_flops,
        name="query_weight",
    )
    query_weight = fold_subs(me, query_weight, "query_subs")
    own = call(
        functools.partial(input_own_kernel, parts),
        shape((slots, columns), BF16),
        (me, query_rows, value_rows, w_query, w_value),
        after=query_weight[:1],
        flops=weight_flops * 2 // parts,
        name="input_own",
    )
    query_weight = pass_round(query_weight, "seq")
    grad_wv = add_up(value_weight, F32, "value_sum", [own])
    grad_input, own_weight = call(
        input_sum_kernel,
        several(1, toks, columns) + several(1, piece, width_dev),
        (unsort, query_weight[0], own, *arrived),
        smem=(),
        scratch=[pltpu.VMEM((slots, columns), BF16)],
        flops=2 * toks * slots * columns,
        name="input_sum",
    )
    grad_wq = add_up([own_weight, *query_weight[1:]], F32, "query_sum")
    if groups > 1:
        centroid_grad = centroid_grad.reshape(groups, 2 * extra, width_dev)[:, :per_group]
        centroid_grad = centroid_grad.reshape(CLUSTERS, width_dev)
    return (grad_input, grad_wq, grad_wv, centroid_grad)


def solution(mesh):
    return jax.shard_map(
        on_device,
        mesh=mesh,
        in_specs=(
            P(("grp", "seq", "sub"), None),
            P(None, "head"),
            P(None, "head"),
            P(("grp", "seq", "sub"), "head"),
            P(("grp", "seq", "sub"), None),
        ),
        out_specs=(
            P(("grp", "seq", "sub"), "head"),
            P(("grp", "seq", "sub"), "head"),
            P(("grp", "seq", "sub"), "head"),
            P("grp", "head"),
        ),
        check_vma=False,
    )
```

```python
import functools

import jax
import jax.numpy as jnp
from jax import lax
from jax.experimental import pallas as pl
from jax.experimental.pallas import tpu as pltpu
from jax.sharding import PartitionSpec as P

HD = 64
CLUSTERS = 64
BLOCK_ROWS = 128
LANES = 128
UNROLL = 4
COUNT_ROWS = 16
SCALE = 0.5 * HD ** (-0.5)
F32 = jnp.float32
BF16 = jnp.bfloat16
OWNERS = ("seq", "sub")
GROUP_ROWS = UNROLL * BLOCK_ROWS
LEAD = 2


def iota(shape, dim):
    return lax.broadcasted_iota(jnp.int32, shape, dim)


def low_half(shape):
    return iota(shape, 1) < HD


def swap_halves(tile):
    return pltpu.roll(tile, HD, 1)


def dot(a, b):
    return jnp.dot(a, b, preferred_element_type=F32)


def dot_nt(a, b):
    return lax.dot_general(a, b, (((1,), (1,)), ((), ())), preferred_element_type=F32)


def ones_where(condition):
    return jnp.where(condition, 1.0, 0.0).astype(BF16)


def owner_of(me_ref, ahead, sizes):
    seq = lax.rem(me_ref[0] + ahead[0], jnp.int32(sizes[0]))
    sub = lax.rem(me_ref[1] + ahead[1], jnp.int32(sizes[1]))
    return seq * sizes[1] + sub


def source_of(me_ref, ahead, sizes):
    return owner_of(me_ref, ((sizes[0] - ahead[0]) % sizes[0], (sizes[1] - ahead[1]) % sizes[1]), sizes)


def steps_of(sizes):
    far = sorted(range(1, sizes[0]), key=lambda seq: -min(seq, sizes[0] - seq))
    subs = range(sizes[1])
    return [(0, 0)] + [(seq, sub) for seq in far for sub in subs] + [(0, sub) for sub in subs if sub]


def hand_out(by_owner_ref, out_refs, me_ref, sizes):
    for ahead, out_ref in zip(steps_of(sizes), out_refs):
        out_ref[...] = by_owner_ref[owner_of(me_ref, ahead, sizes)]


def slots_of(assign, groups, rows):
    toks = assign.shape[1]
    per_group = CLUSTERS // groups
    member = jnp.where(iota((CLUSTERS, toks), 0) == assign, 1.0, 0.0)
    member_b = member.astype(BF16)
    upto = ones_where(iota((LANES, LANES), 0) <= iota((LANES, LANES), 1))
    counts = jnp.zeros((CLUSTERS, 1), F32)
    running = []
    for first in range(0, toks, LANES):
        within = dot(member_b[:, first : first + LANES], upto)
        running.append(within + counts)
        counts = counts + within[:, LANES - 1 :]
    running = jnp.concatenate(running, axis=1)
    here, other = iota((CLUSTERS, CLUSTERS), 0), iota((CLUSTERS, CLUSTERS), 1)
    group_of = lambda index: lax.div(index, jnp.int32(per_group))
    earlier = ones_where((other < here) & (group_of(other) == group_of(here)))
    base = dot(earlier, jnp.broadcast_to(counts, (CLUSTERS, LANES)).astype(BF16))[:, :1]
    base = base + (group_of(iota((CLUSTERS, 1), 0)) * rows).astype(F32)
    slot = jnp.sum(member * (running - 1.0 + base), axis=0, keepdims=True).astype(jnp.int32)
    spread = jnp.concatenate([member_b, jnp.zeros((LANES - CLUSTERS, toks), BF16)], axis=0)
    return slot, dot_nt(jnp.ones((COUNT_ROWS, toks), BF16), spread).astype(BF16)


def beside(query, cotan):
    low = low_half(query.shape)
    even = jnp.where(low, query, swap_halves(cotan)).astype(BF16)
    return even, jnp.where(low, swap_halves(query), cotan).astype(BF16)


def load_rows(source, target, sems, fine):
    return [
        pltpu.make_async_copy(source.at[pl.ds(row, fine), :], target.at[pl.ds(row, fine), :], sems.at[row // fine])
        for row in range(0, target.shape[0], fine)
    ]


def project_far_kernel(sizes, groups, rows, heads, assign_ref, tokens_hbm, weight_hbm, cotan_hbm, *refs):
    out_refs, refs = refs[: sizes[1]], refs[sizes[1] :]
    slot_ref, tokens_ref, weight_ref, cotan_ref, mixed_ref, sems = refs
    toks = tokens_ref.shape[0]
    fine = min(256, toks)
    me = (lax.axis_index("seq"), lax.axis_index("sub"))
    owner = owner_of(me, steps_of(sizes)[1], sizes) - me[1]
    group, head = lax.div(owner, jnp.int32(heads)), lax.rem(owner, jnp.int32(heads))
    columns = pl.ds(pl.multiple_of(head * HD, LANES), sizes[1] * HD)
    loads = [
        load_rows(source, target, sems.at[kind], fine)
        for kind, (source, target) in enumerate(
            ((weight_hbm.at[:, columns], weight_ref), (tokens_hbm, tokens_ref), (cotan_hbm.at[:, columns], cotan_ref))
        )
    ]
    for load in loads:
        for copy in load:
            copy.start()
    slot, tallies = slots_of(assign_ref[...], groups, rows)
    slot_ref[...] = slot
    pick = ones_where(iota((rows, toks), 0) + group * rows == slot)
    for copy in loads[0] + loads[2]:
        copy.wait()
    step = min(512, toks)
    for first in range(0, toks, step):
        for copy in loads[1][first // fine : (first + step) // fine]:
            copy.wait()
        where = slice(first, first + step)
        query, cotan = dot(tokens_ref[where, :], weight_ref[...]), cotan_ref[where, :].astype(F32)
        for pair in range(sizes[1] // 2):
            pair_columns = slice(pair * LANES, (pair + 1) * LANES)
            even, odd = beside(query[:, pair_columns], cotan[:, pair_columns])
            mixed_ref[where, 2 * pair * LANES : (2 * pair + 1) * LANES] = even
            mixed_ref[where, (2 * pair + 1) * LANES : (2 * pair + 2) * LANES] = odd
    in_order = dot(pick, mixed_ref[...]).astype(BF16)
    for ahead, out_ref in enumerate(out_refs):
        sub = lax.rem(me[1] + ahead, jnp.int32(sizes[1]))
        for other in range(sizes[1]):

            @pl.when(sub == other)
            def _():
                out_ref[:rows, :] = in_order[:, other * LANES : (other + 1) * LANES]

        out_ref[rows:, :] = tallies


def project_query_kernel(sizes, groups, rows, me_ref, slot_ref, assign_ref, tokens_ref, weight_ref, cotan_ref, *rest):
    out_refs, (mixed_ref, sorted_ref) = rest[:-2], rest[-2:]
    toks = tokens_ref.shape[0]
    heads = weight_ref.shape[1] // HD
    step = min(512, toks)
    for first in range(0, toks, step):
        where = slice(first, first + step)
        query, cotan = dot(tokens_ref[where, :], weight_ref[...]), cotan_ref[where, :].astype(F32)
        for pair in range(heads // 2):
            columns = slice(pair * LANES, (pair + 1) * LANES)
            even, odd = beside(query[:, columns], cotan[:, columns])
            mixed_ref[where, 2 * pair * LANES : (2 * pair + 1) * LANES] = even
            mixed_ref[where, (2 * pair + 1) * LANES : (2 * pair + 2) * LANES] = odd
    part = min(512, rows)
    pieces = rows // part

    @pl.loop(0, groups * pieces)
    def _(i):
        group, piece = lax.div(i, jnp.int32(pieces)), lax.rem(i, jnp.int32(pieces))
        first = pl.multiple_of(piece * part, part)
        pick = ones_where(iota((part, toks), 0) + i * part == slot_ref[...])
        sorted_rows = dot(pick, mixed_ref[...]).astype(BF16)
        for head in range(heads):
            sorted_ref[group * heads + head, pl.ds(first, part), :] = sorted_rows[
                :, head * LANES : (head + 1) * LANES
            ]

    member = jnp.where(iota((LANES, toks), 0) == assign_ref[...], 1.0, 0.0).astype(BF16)
    tallies = dot_nt(jnp.ones((COUNT_ROWS, toks), BF16), member).astype(BF16)
    for owner in range(sorted_ref.shape[0]):
        sorted_ref[owner, rows:, :] = tallies
    steps = steps_of(sizes)
    for ahead, out_ref in zip(steps[:1] + steps[1 + sizes[1] :], out_refs):
        out_ref[...] = sorted_ref[owner_of(me_ref, ahead, sizes)]


def project_value_kernel(sizes, groups, rows, me_ref, slot_ref, tokens_ref, weight_ref, *rest):
    out_refs, (turned_ref, unsort_ref, value_ref, sorted_ref) = rest[:-4], rest[-4:]
    toks = tokens_ref.shape[0]
    heads = weight_ref.shape[1] // HD
    step = min(512, toks)

    @pl.loop(0, toks // step)
    def _(i):
        where = pl.ds(pl.multiple_of(i * step, step), step)
        value_ref[where, :] = dot(tokens_ref[where, :], weight_ref[...]).astype(BF16)

    half = rows // 2
    part = min(256, half)
    pieces = half // part

    @pl.loop(0, groups * pieces)
    def _(i):
        group, piece = lax.div(i, jnp.int32(pieces)), lax.rem(i, jnp.int32(pieces))
        first = pl.multiple_of(piece * part, part)
        index = iota((part, toks), 0) + group * rows + first
        upper = dot(ones_where(index == slot_ref[...]), value_ref[...])
        lower = dot(ones_where(index + half == slot_ref[...]), value_ref[...])
        low = low_half((part, LANES))
        for pair in range(heads // 2):
            up = upper[:, pair * LANES : (pair + 1) * LANES]
            down = lower[:, pair * LANES : (pair + 1) * LANES]
            even = jnp.where(low, up, swap_halves(down)).astype(BF16)
            odd = jnp.where(low, swap_halves(up), down).astype(BF16)
            sorted_ref[group * heads + 2 * pair, pl.ds(first, part), :] = even
            sorted_ref[group * heads + 2 * pair + 1, pl.ds(first, part), :] = odd

    hand_out(sorted_ref, out_refs, me_ref, sizes)
    turned = tokens_ref[...].T
    slots = unsort_ref.shape[1]
    part = min(256, slots)
    for i in range(slots // part):
        pick = ones_where(iota((part, toks), 0) + i * part == slot_ref[...])
        unsort_ref[:, i * part : (i + 1) * part] = pick.T
        turned_ref[:, i * part : (i + 1) * part] = dot_nt(turned, pick).astype(BF16)


def score(mixed):
    query = jnp.where(low_half(mixed.shape), mixed.astype(F32) * SCALE, 0.0).astype(BF16)
    return dot_nt(query, mixed)


def softmax_turned(scores):
    shape = scores.shape
    seen = iota(shape, 0) <= iota(shape, 1)
    scores = jnp.where(seen, scores, -jnp.inf)
    raised = jnp.exp(scores - jnp.max(scores, axis=0, keepdims=True))
    return raised * (1.0 / jnp.sum(raised, axis=0, keepdims=True))


def for_each_cluster(counts_ref, me_ref, place_ref, owners, per_group, body):
    for source in range(owners):
        place_ref[source] = 0

    def step(cluster, block):
        runs = []
        total = 0
        base = block * BLOCK_ROWS
        for source in range(owners):
            count = counts_ref[source, me_ref[3] + cluster]
            start = place_ref[source]
            runs.append((source, start, base + total))
            place_ref[source] = start + count
            total = total + count
        body(cluster, block, runs, base + total)
        return block + lax.shift_right_logical(total + (BLOCK_ROWS - 1), jnp.int32(7))

    return lax.fori_loop(0, per_group, step, jnp.int32(LEAD * UNROLL))


def gather_blocks(counts_ref, me_ref, place_ref, owners, per_group, slot_rows, wide_ref, block_ref):
    def body(cluster, block, runs, end):
        for source, start, row in runs:
            block_ref[pl.ds(row, slot_rows), :] = wide_ref[source, pl.ds(start, slot_rows), :]
        block_ref[pl.ds(end, BLOCK_ROWS), :] = jnp.zeros((BLOCK_ROWS, LANES), F32)

    blocks = for_each_cluster(counts_ref, me_ref, place_ref, owners, per_group, body)
    spare = pl.ds(pl.multiple_of(blocks * BLOCK_ROWS, BLOCK_ROWS), GROUP_ROWS)
    block_ref[spare, :] = jnp.zeros((GROUP_ROWS, LANES), F32)
    return blocks


def for_each_group(blocks, stages):
    first, second, third = stages
    groups = lax.div(blocks + (UNROLL - 1), jnp.int32(UNROLL))

    def step(i, carry):
        for slot in range(2):
            group = LEAD + 2 * i + slot
            third(group - 2, slot)
            second(group - 1, 1 - slot)
            first(group, slot)
        return carry

    lax.fori_loop(0, lax.shift_right_logical(groups + 1, jnp.int32(1)), step, 0)


def block_rows(group, ahead):
    return pl.ds(pl.multiple_of((group * UNROLL + ahead) * BLOCK_ROWS, BLOCK_ROWS), BLOCK_ROWS)


def tile_rows(ahead):
    return slice(ahead * BLOCK_ROWS, (ahead + 1) * BLOCK_ROWS)


def value_grad_kernel(sizes, per_group, slot_rows, me_ref, *refs):
    owners = sizes[0] * sizes[1]
    mixed_refs, out_refs, rest = refs[:owners], refs[owners : 2 * owners], refs[2 * owners :]
    dense_ref, counts_out_ref, counts_ref, place_ref, wide_ref, block_ref, home_ref = rest[:7]
    score_refs, probs_refs = rest[7:9], rest[9:11]
    half = out_refs[0].shape[0]
    rows = 2 * half
    for ahead, mixed_ref in zip(steps_of(sizes), mixed_refs):
        source = source_of(me_ref, ahead, sizes)
        tail = mixed_ref[rows:, :].astype(F32).astype(jnp.int32)
        counts_out_ref[pl.ds(source, 1), :] = tail[:1, :]
        wide_ref[source, :rows, :] = mixed_ref[:rows, :].astype(F32)
        wide_ref[source, rows:, :] = jnp.zeros((slot_rows, LANES), F32)
    pltpu.sync_copy(counts_out_ref, counts_ref)
    blocks = gather_blocks(counts_ref, me_ref, place_ref, owners, per_group, slot_rows, wide_ref, block_ref)

    def first(group, slot):
        for ahead in range(UNROLL):
            where = block_rows(group, ahead)
            mixed = block_ref[where, :].astype(BF16)
            dense_ref[where, :] = mixed
            score_refs[slot][tile_rows(ahead), :] = score(mixed)

    def second(group, slot):
        for ahead in range(UNROLL):
            tile = tile_rows(ahead)
            probs_refs[slot][tile, :] = softmax_turned(score_refs[slot][tile, :]).astype(BF16)

    def third(group, slot):
        for ahead in range(UNROLL):
            where = block_rows(group, ahead)
            block_ref[where, :] = dot(probs_refs[slot][tile_rows(ahead), :], dense_ref[where, :])

    for_each_group(blocks, (first, second, third))

    def scatter(cluster, block, runs, end):
        for source, start, row in runs:
            wide_ref[source, pl.ds(start, slot_rows), :] = block_ref[pl.ds(row, slot_rows), :]

    for_each_cluster(counts_ref, me_ref, place_ref, owners, per_group, scatter)
    for ahead, out_ref in zip(steps_of(sizes), out_refs):
        source = owner_of(me_ref, ahead, sizes)
        up, down = wide_ref[source, :half, :], wide_ref[source, half:rows, :]
        out_ref[...] = jnp.where(low_half((half, LANES)), swap_halves(up), down).astype(BF16)


def query_grad_kernel(sizes, per_group, slot_rows, me_ref, counts_ref, dense_ref, *refs):
    owners = sizes[0] * sizes[1]
    value_refs, out_refs, rest = refs[:owners], refs[owners : 2 * owners], refs[2 * owners :]
    place_ref, wide_ref, block_ref, sums_ref, centroid_ref = rest[:5]
    score_refs, grad_probs_refs, both_refs = rest[5:7], rest[7:9], rest[9:11]
    half = value_refs[0].shape[0]
    rows = 2 * half
    for ahead, value_ref in zip(steps_of(sizes), value_refs):
        source = source_of(me_ref, ahead, sizes)
        value = value_ref[...].astype(F32)
        wide_ref[source, :half, :] = swap_halves(value)
        wide_ref[source, half:rows, :] = value
        wide_ref[source, rows:, :] = jnp.zeros((slot_rows, LANES), F32)
    blocks = gather_blocks(counts_ref, me_ref, place_ref, owners, per_group, slot_rows, wide_ref, block_ref)

    def first(group, slot):
        for ahead in range(UNROLL):
            where, tile = block_rows(group, ahead), tile_rows(ahead)
            mixed = dense_ref[where, :]
            value = block_ref[where, :].astype(BF16)
            cotan = jnp.where(low_half(mixed.shape), jnp.zeros_like(mixed), mixed)
            score_refs[slot][tile, :] = score(mixed)
            grad_probs_refs[slot][tile, :] = dot_nt(value, cotan)

    def second(group, slot):
        for ahead in range(UNROLL):
            tile = tile_rows(ahead)
            probs = softmax_turned(score_refs[slot][tile, :])
            grad_probs = grad_probs_refs[slot][tile, :]
            probs_half = probs.astype(BF16).astype(F32)
            row_dot = jnp.sum(probs_half * grad_probs, axis=0, keepdims=True)
            grad_scores = (probs * (grad_probs - row_dot)).astype(BF16).astype(F32)
            both_refs[slot][tile, :] = (grad_scores + grad_scores.T).astype(BF16)

    def third(group, slot):
        for ahead in range(UNROLL):
            where = block_rows(group, ahead)
            grad = dot(both_refs[slot][tile_rows(ahead), :], dense_ref[where, :]) * SCALE
            grad = grad.astype(BF16).astype(F32)
            block_ref[where, :] = grad
            sums_ref[pl.ds(group * UNROLL + ahead, 1), :] = jnp.sum(grad, axis=0, keepdims=True)

    for_each_group(blocks, (first, second, third))
    most = (owners * slot_rows + BLOCK_ROWS - 1) // BLOCK_ROWS

    def scatter(cluster, block, runs, end):
        total = jnp.zeros((1, LANES), F32)
        for ahead in range(most):
            here = block + ahead
            total = total + jnp.where(here * BLOCK_ROWS < end, sums_ref[pl.ds(here, 1), :], 0.0)
        centroid_ref[pl.ds(cluster, 1), :] = total
        for source, start, row in runs:
            wide_ref[source, pl.ds(start, slot_rows), :] = block_ref[pl.ds(row, slot_rows), :]

    for_each_cluster(counts_ref, me_ref, place_ref, owners, per_group, scatter)
    extra = out_refs[0].shape[0] - half
    centroid = jnp.where(
        low_half((extra, LANES)), centroid_ref[:extra, :], swap_halves(centroid_ref[extra:, :])
    ).astype(BF16)
    for ahead, out_ref in zip(steps_of(sizes), out_refs):
        source = owner_of(me_ref, ahead, sizes)
        up, down = wide_ref[source, :half, :], wide_ref[source, half:rows, :]
        out_ref[:half, :] = jnp.where(low_half((half, LANES)), up, swap_halves(down)).astype(BF16)
        out_ref[half:, :] = centroid


def unfold(home_ref, out_ref, heads, start, half, finish):
    low = low_half((half, LANES))
    for group in range(home_ref.shape[0] // heads):
        first = group * 2 * half
        for pair in range(heads // 2):
            even = home_ref[group * heads + 2 * pair, start : start + half, :].astype(F32)
            odd = home_ref[group * heads + 2 * pair + 1, start : start + half, :].astype(F32)
            columns = slice(pair * LANES, (pair + 1) * LANES)
            out_ref[first : first + half, columns] = finish(jnp.where(low, even, swap_halves(odd)))
            out_ref[first + half : first + 2 * half, columns] = finish(
                jnp.where(low, swap_halves(even), odd)
            )


def to_half(x):
    return x.astype(BF16)


def bring_home(sizes, heads, me_ref, part_refs, home_ref, rows_ref):
    for ahead, part_ref in zip(steps_of(sizes), part_refs):
        home_ref[source_of(me_ref, ahead, sizes)] = part_ref[...]
    unfold(home_ref, rows_ref, heads, 0, rows_ref.shape[0] * heads // home_ref.shape[0] // 2, to_half)


def weight_partial(sizes, me_ref, turned_ref, rows_ref, sub_refs):
    piece = turned_ref.shape[0] // (sizes[0] * sizes[1])
    for ahead, sub_ref in enumerate(sub_refs):
        sub = lax.rem(me_ref[1] + ahead, jnp.int32(sizes[1]))
        first = [pl.multiple_of((seq * sizes[1] + sub) * piece, piece) for seq in range(sizes[0])]
        turned = jnp.concatenate([turned_ref[pl.ds(row, piece), :] for row in first], axis=0)
        partial = dot(turned, rows_ref[...]).astype(BF16)
        for seq in range(sizes[0]):
            sub_ref[seq] = partial[seq * piece : (seq + 1) * piece, :]


def input_columns(me_ref, ahead, parts, width):
    columns = width // parts
    dest = lax.rem(me_ref[2] + ahead, jnp.int32(parts))
    return pl.ds(pl.multiple_of(dest * columns, columns), columns)


def value_home_kernel(sizes, heads, parts, me_ref, turned_ref, weight_ref, *refs):
    part_refs, refs = refs[: sizes[0] * sizes[1]], refs[sizes[0] * sizes[1] :]
    rows_ref, term_refs, refs = refs[0], refs[1:parts], refs[parts:]
    sub_refs, home_ref = refs[: sizes[1]], refs[sizes[1]]
    bring_home(sizes, heads, me_ref, part_refs, home_ref, rows_ref)
    for k, term_ref in enumerate(term_refs):
        mine = input_columns(me_ref, k + 1, parts, weight_ref.shape[0])
        term_ref[...] = dot_nt(rows_ref[...], weight_ref[mine, :])
    weight_partial(sizes, me_ref, turned_ref, rows_ref, sub_refs)


def query_home_kernel(sizes, heads, factor, parts, me_ref, weight_ref, *refs):
    term_refs, refs = refs[: parts - 1], refs[parts - 1 :]
    part_refs, refs = refs[: sizes[0] * sizes[1]], refs[sizes[0] * sizes[1] :]
    out_refs, (rows_ref, centroid_ref, home_ref) = refs[: parts - 1], refs[parts - 1 :]
    bring_home(sizes, heads, me_ref, part_refs, home_ref, rows_ref)
    for k, (term_ref, out_ref) in enumerate(zip(term_refs, out_refs)):
        mine = input_columns(me_ref, k + 1, parts, weight_ref.shape[0])
        out_ref[...] = (dot_nt(rows_ref[...], weight_ref[mine, :]) + term_ref[...]).astype(BF16)
    half = rows_ref.shape[0] * heads // home_ref.shape[0] // 2
    unfold(home_ref, centroid_ref, heads, half, home_ref.shape[1] - half, lambda x: x * factor)


def query_weight_kernel(sizes, me_ref, turned_ref, rows_ref, *sub_refs):
    weight_partial(sizes, me_ref, turned_ref, rows_ref, sub_refs)


def input_own_kernel(parts, me_ref, rows_ref, value_rows_ref, w_query_ref, w_value_ref, out_ref):
    mine = input_columns(me_ref, 0, parts, w_query_ref.shape[0])
    total = dot_nt(rows_ref[...], w_query_ref[mine, :]) + dot_nt(value_rows_ref[...], w_value_ref[mine, :])
    out_ref[...] = total.astype(BF16)


def fold_subs_kernel(me_ref, *refs):
    seqs = refs[0].shape[0]
    terms, out_refs = refs[:-seqs], refs[-seqs:]
    for ahead, out_ref in enumerate(out_refs):
        seq = lax.rem(me_ref[0] + ahead, jnp.int32(seqs))
        total = terms[0][seq].astype(F32)
        for term in terms[1:]:
            total = total + term[seq].astype(F32)
        out_ref[...] = total.astype(BF16)


def sum_kernel(*refs):
    total = refs[0][...].astype(F32)
    for ref in refs[1:-1]:
        total = total + ref[...].astype(F32)
    refs[-1][...] = total.astype(refs[-1].dtype)


def input_sum_kernel(unsort_ref, weight_ref, *refs):
    part_refs, out_ref, weight_out_ref, total_ref = refs[:-3], refs[-3], refs[-2], refs[-1]
    total = part_refs[0][...].astype(F32)
    for part_ref in part_refs[1:]:
        total = total + part_ref[...].astype(F32)
    total_ref[...] = total.astype(BF16)
    out_ref[...] = dot(unsort_ref[...], total_ref[...]).astype(BF16)
    weight_out_ref[...] = weight_ref[...]


def call(kernel, outs, inputs, smem=(0,), in_place=(), after=(), scratch=(), flops=0, vmem=24, name=None):
    def body(*refs):
        kernel(*refs[: len(inputs)], *refs[len(inputs) + len(after) :])

    def space(i):
        return pltpu.SMEM if i in smem else pl.ANY if i in in_place else pltpu.VMEM

    specs = [pl.BlockSpec(memory_space=space(i)) for i in range(len(inputs))]
    specs += [pl.BlockSpec(memory_space=pl.ANY)] * len(after)
    moved = sum(x.size * x.dtype.itemsize for x in inputs) + sum(
        x.size * x.dtype.itemsize for x in jax.tree.leaves(outs)
    )
    return pl.pallas_call(
        body,
        out_shape=outs,
        in_specs=specs,
        out_specs=jax.tree.map(lambda _: pl.BlockSpec(memory_space=pltpu.VMEM), outs),
        scratch_shapes=list(scratch),
        compiler_params=pltpu.CompilerParams(vmem_limit_bytes=vmem * 2**20),
        cost_estimate=pl.CostEstimate(flops=flops, bytes_accessed=moved, transcendentals=0),
        name=name,
    )(*inputs, *after)


def exchange(parts, sizes):
    out = []
    for ahead, part in zip(steps_of(sizes), parts):
        moves = [
            (
                seq * sizes[1] + sub,
                (seq + ahead[0]) % sizes[0] * sizes[1] + (sub + ahead[1]) % sizes[1],
            )
            for seq, sub in steps_of(sizes)
        ]
        out.append(part if ahead == (0, 0) else lax.ppermute(part, OWNERS, moves))
    return out


def shift(part, axis, ahead):
    size = lax.axis_size(axis)
    return lax.ppermute(part, axis, [(i, (i + ahead) % size) for i in range(size)])


def pass_round(parts, axis):
    return [parts[0]] + [shift(parts[ahead], axis, ahead) for ahead in range(1, len(parts))]


def fold_subs(me, by_sub, name):
    seqs, piece, columns = by_sub[0].shape
    return call(
        fold_subs_kernel,
        (jax.ShapeDtypeStruct((piece, columns), BF16),) * seqs,
        (me, *pass_round(by_sub, "sub")),
        name=name,
    )


def add_up(terms, dtype, name, after=()):
    out = jax.ShapeDtypeStruct(terms[0].shape, dtype)
    return call(sum_kernel, out, tuple(terms), smem=(), after=after, name=name)


def on_device(tokens_in, w_query, w_value, cotangent, assignment):
    sizes = (lax.axis_size("seq"), lax.axis_size("sub"))
    owners = sizes[0] * sizes[1]
    parts = lax.axis_size("head")
    toks, width = tokens_in.shape
    width_dev = cotangent.shape[1]
    heads = width_dev // HD
    slot_rows = 2 * toks // CLUSTERS
    assert owners % heads == 0 and heads % 2 == 0
    groups = owners // heads
    per_group = CLUSTERS // groups
    rows = toks if groups == 1 else per_group * slot_rows
    half = rows // 2
    slots = groups * rows
    columns = width // parts
    capacity = (slot_rows * owners + BLOCK_ROWS - 1) // BLOCK_ROWS * BLOCK_ROWS
    extra = max(per_group // 2, 16)
    shape = jax.ShapeDtypeStruct
    seq, sub = lax.axis_index("seq"), lax.axis_index("sub")
    first = lax.div(seq * sizes[1] + sub, jnp.int32(heads)) * per_group
    me = jnp.stack([seq, sub, lax.axis_index("head"), first]).astype(jnp.int32)

    def several(count, *dims):
        return (shape(dims, BF16),) * count

    assign_row = assignment.reshape(1, toks)
    *far_mixed, slot_row = call(
        functools.partial(project_far_kernel, sizes, groups, rows, heads),
        several(sizes[1], rows + COUNT_ROWS, LANES) + (shape((1, toks), jnp.int32),),
        (assign_row, tokens_in, w_query, cotangent),
        smem=(),
        in_place=(1, 2, 3),
        scratch=[
            pltpu.VMEM((toks, width), BF16),
            pltpu.VMEM((width, sizes[1] * HD), BF16),
            pltpu.VMEM((toks, sizes[1] * HD), BF16),
            pltpu.VMEM((toks, sizes[1] * LANES), BF16),
            pltpu.SemaphoreType.DMA((3, max(toks, width) // min(256, toks))),
        ],
        flops=2 * toks * width * sizes[1] * HD + 2 * rows * toks * sizes[1] * LANES,
        vmem=60,
        name="project_far",
    )
    own_mixed, *near_mixed = call(
        functools.partial(project_query_kernel, sizes, groups, rows),
        several(owners - sizes[1], rows + COUNT_ROWS, LANES),
        (me, slot_row, assign_row, tokens_in, w_query, cotangent),
        scratch=[pltpu.VMEM((toks, 2 * width_dev), BF16), pltpu.VMEM((owners, rows + COUNT_ROWS, LANES), BF16)],
        flops=2 * toks * width * width_dev + 4 * slots * toks * width_dev,
        name="project_query",
    )
    send_mixed = [own_mixed, *far_mixed, *near_mixed]
    got_mixed = exchange(send_mixed, sizes)
    *send_value, turned, unsort = call(
        functools.partial(project_value_kernel, sizes, groups, rows),
        several(owners, half, LANES) + several(1, width, slots) + several(1, toks, slots),
        (me, slot_row, tokens_in, w_value),
        after=near_mixed[:1],
        scratch=[pltpu.VMEM((toks, width_dev), BF16), pltpu.VMEM((owners, half, LANES), BF16)],
        flops=2 * toks * width * width_dev + 2 * slots * toks * width_dev,
        name="project_value",
    )
    behind = [0, *range(3, owners), 2, 1][:owners]
    send_value = [lax.optimization_barrier((part, got_mixed[k]))[0] for part, k in zip(send_value, behind)]
    got_value = exchange(send_value, sizes)
    blocks = per_group * capacity // BLOCK_ROWS
    held = blocks + (LEAD + 4) * UNROLL
    block_flops = 2 * BLOCK_ROWS * BLOCK_ROWS * LANES
    tall = pltpu.VMEM((owners, rows + slot_rows, LANES), F32)
    dense_rows = pltpu.VMEM((held * BLOCK_ROWS, LANES), F32)
    group_f32 = pltpu.VMEM((GROUP_ROWS, BLOCK_ROWS), F32)
    group_b16 = pltpu.VMEM((GROUP_ROWS, BLOCK_ROWS), BF16)
    place = pltpu.SMEM((owners,), jnp.int32)
    *back_value, dense, counts = call(
        functools.partial(value_grad_kernel, sizes, per_group, slot_rows),
        several(owners, half, LANES)
        + several(1, held * BLOCK_ROWS, LANES)
        + (shape((owners, LANES), jnp.int32),),
        (me, *got_mixed),
        after=[unsort],
        scratch=[pltpu.SMEM((owners, LANES), jnp.int32), place, tall, dense_rows, tall]
        + [group_f32] * 2
        + [group_b16] * 2,
        flops=4 * blocks * block_flops,
        vmem=48,
        name="value_grad",
    )
    back_value, _ = lax.optimization_barrier((back_value, got_value[1:]))
    home_value = exchange(back_value, sizes)
    back_query = call(
        functools.partial(query_grad_kernel, sizes, per_group, slot_rows),
        several(owners, half + extra, LANES),
        (me, counts, dense, *got_value),
        smem=(0, 1),
        scratch=[place, tall, dense_rows, pltpu.VMEM((held, LANES), F32), pltpu.VMEM((2 * extra, LANES), F32)]
        + [group_f32] * 4
        + [group_b16] * 2,
        flops=6 * blocks * block_flops,
        vmem=48,
        name="query_grad",
    )
    home_query = exchange(back_query, sizes)
    weight_flops = 2 * slots * width * width_dev
    home_flops = weight_flops // parts * (parts - 1)
    piece = width // owners
    sub_shapes = several(sizes[1], sizes[0], piece, width_dev)
    value_rows, *refs = call(
        functools.partial(value_home_kernel, sizes, heads, parts),
        several(1, slots, width_dev) + (shape((slots, columns), F32),) * (parts - 1) + sub_shapes,
        (me, turned, w_value, *home_value),
        scratch=[pltpu.VMEM((owners, half, LANES), BF16)],
        flops=weight_flops + home_flops,
        name="value_home",
    )
    value_terms, value_weight = refs[: parts - 1], refs[parts - 1 :]
    value_weight = fold_subs(me, value_weight, "value_subs")
    *partials, query_rows, centroid_grad = call(
        functools.partial(query_home_kernel, sizes, heads, (CLUSTERS / (toks * owners)) ** 0.5, parts),
        several(parts - 1, slots, columns)
        + several(1, slots, width_dev)
        + (shape((groups * 2 * extra, width_dev), F32),),
        (me, w_query, *value_terms, *home_query),
        scratch=[pltpu.VMEM((owners, half + extra, LANES), BF16)],
        flops=home_flops,
        name="query_home",
    )
    arrived = [shift(partial, "head", k + 1) for k, partial in enumerate(partials)]
    value_weight, _ = lax.optimization_barrier((value_weight, home_query))
    value_weight = pass_round(value_weight, "seq")
    query_weight = call(
        functools.partial(query_weight_kernel, sizes),
        sub_shapes,
        (me, turned, query_rows),
        flops=weight_flops,
        name="query_weight",
    )
    query_weight = fold_subs(me, query_weight, "query_subs")
    own = call(
        functools.partial(input_own_kernel, parts),
        shape((slots, columns), BF16),
        (me, query_rows, value_rows, w_query, w_value),
        after=query_weight[:1],
        flops=weight_flops * 2 // parts,
        name="input_own",
    )
    query_weight = pass_round(query_weight, "seq")
    grad_wv = add_up(value_weight, F32, "value_sum", [own])
    grad_input, own_weight = call(
        input_sum_kernel,
        several(1, toks, columns) + several(1, piece, width_dev),
        (unsort, query_weight[0], own, *arrived),
        smem=(),
        scratch=[pltpu.VMEM((slots, columns), BF16)],
        flops=2 * toks * slots * columns,
        name="input_sum",
    )
    grad_wq = add_up([own_weight, *query_weight[1:]], F32, "query_sum")
    if groups > 1:
        centroid_grad = centroid_grad.reshape(groups, 2 * extra, width_dev)[:, :per_group]
        centroid_grad = centroid_grad.reshape(CLUSTERS, width_dev)
    return (grad_input, grad_wq, grad_wv, centroid_grad)


def solution(mesh):
    return jax.shard_map(
        on_device,
        mesh=mesh,
        in_specs=(
            P(("grp", "seq", "sub"), None),
            P(None, "head"),
            P(None, "head"),
            P(("grp", "seq", "sub"), "head"),
            P(("grp", "seq", "sub"), None),
        ),
        out_specs=(
            P(("grp", "seq", "sub"), "head"),
            P(("grp", "seq", "sub"), "head"),
            P(("grp", "seq", "sub"), "head"),
            P("grp", "head"),
        ),
        check_vma=False,
    )
```

```python
import functools

import jax
import jax.numpy as jnp
from jax import lax
from jax.experimental import pallas as pl
from jax.experimental.pallas import tpu as pltpu
from jax.sharding import PartitionSpec as P

HD = 64
CLUSTERS = 64
BLOCK_ROWS = 128
LANES = 128
UNROLL = 4
COUNT_ROWS = 16
SCALE = 0.5 * HD ** (-0.5)
F32 = jnp.float32
BF16 = jnp.bfloat16
OWNERS = ("seq", "sub")
GROUP_ROWS = UNROLL * BLOCK_ROWS
LEAD = 2


def iota(shape, dim):
    return lax.broadcasted_iota(jnp.int32, shape, dim)


def low_half(shape):
    return iota(shape, 1) < HD


def swap_halves(tile):
    return pltpu.roll(tile, HD, 1)


def dot(a, b):
    return jnp.dot(a, b, preferred_element_type=F32)


def dot_nt(a, b):
    return lax.dot_general(a, b, (((1,), (1,)), ((), ())), preferred_element_type=F32)


def ones_where(condition):
    return jnp.where(condition, 1.0, 0.0).astype(BF16)


def owner_of(me_ref, ahead, sizes):
    seq = lax.rem(me_ref[0] + ahead[0], jnp.int32(sizes[0]))
    sub = lax.rem(me_ref[1] + ahead[1], jnp.int32(sizes[1]))
    return seq * sizes[1] + sub


def source_of(me_ref, ahead, sizes):
    return owner_of(me_ref, ((sizes[0] - ahead[0]) % sizes[0], (sizes[1] - ahead[1]) % sizes[1]), sizes)


def steps_of(sizes):
    far = sorted(range(1, sizes[0]), key=lambda seq: -min(seq, sizes[0] - seq))
    subs = range(sizes[1])
    return [(0, 0)] + [(seq, sub) for seq in far for sub in subs] + [(0, sub) for sub in subs if sub]


def hand_out(by_owner_ref, out_refs, me_ref, sizes):
    for ahead, out_ref in zip(steps_of(sizes), out_refs):
        out_ref[...] = by_owner_ref[owner_of(me_ref, ahead, sizes)]


def slots_of(assign, groups, rows):
    toks = assign.shape[1]
    per_group = CLUSTERS // groups
    member = jnp.where(iota((CLUSTERS, toks), 0) == assign, 1.0, 0.0)
    member_b = member.astype(BF16)
    upto = ones_where(iota((LANES, LANES), 0) <= iota((LANES, LANES), 1))
    counts = jnp.zeros((CLUSTERS, 1), F32)
    running = []
    for first in range(0, toks, LANES):
        within = dot(member_b[:, first : first + LANES], upto)
        running.append(within + counts)
        counts = counts + within[:, LANES - 1 :]
    running = jnp.concatenate(running, axis=1)
    here, other = iota((CLUSTERS, CLUSTERS), 0), iota((CLUSTERS, CLUSTERS), 1)
    group_of = lambda index: lax.div(index, jnp.int32(per_group))
    earlier = ones_where((other < here) & (group_of(other) == group_of(here)))
    base = dot(earlier, jnp.broadcast_to(counts, (CLUSTERS, LANES)).astype(BF16))[:, :1]
    base = base + (group_of(iota((CLUSTERS, 1), 0)) * rows).astype(F32)
    slot = jnp.sum(member * (running - 1.0 + base), axis=0, keepdims=True).astype(jnp.int32)
    spread = jnp.concatenate([member_b, jnp.zeros((LANES - CLUSTERS, toks), BF16)], axis=0)
    return slot, dot_nt(jnp.ones((COUNT_ROWS, toks), BF16), spread).astype(BF16)


def arrivals(sizes, me_ref, refs):
    seqs, subs = sizes
    for ahead in steps_of(sizes):
        if ahead[1] == 0:
            piece = refs[ahead[0]][me_ref[1]]
        else:
            piece = refs[seqs + ahead[1] - 1][ahead[0]]
        yield source_of(me_ref, ahead, sizes), piece


def swap_kernel(sizes, me_ref, *refs):
    for k, out_ref in enumerate(refs[sizes[0] :]):
        sub = lax.rem(me_ref[1] + (k + 1), jnp.int32(sizes[1]))
        for seq in range(sizes[0]):
            out_ref[seq] = refs[seq][sub]


def beside(query, cotan):
    low = low_half(query.shape)
    even = jnp.where(low, query, swap_halves(cotan)).astype(BF16)
    return even, jnp.where(low, swap_halves(query), cotan).astype(BF16)


def load_rows(source, target, sems, fine):
    return [
        pltpu.make_async_copy(source.at[pl.ds(row, fine), :], target.at[pl.ds(row, fine), :], sems.at[row // fine])
        for row in range(0, target.shape[0], fine)
    ]


def project_far_kernel(sizes, groups, rows, heads, assign_ref, tokens_hbm, weight_hbm, cotan_hbm, *refs):
    out_refs, refs = refs[: sizes[1]], refs[sizes[1] :]
    slot_ref, tokens_ref, weight_ref, cotan_ref, mixed_ref, sems = refs
    toks = tokens_ref.shape[0]
    fine = min(256, toks)
    me = (lax.axis_index("seq"), lax.axis_index("sub"))
    owner = owner_of(me, steps_of(sizes)[1], sizes) - me[1]
    group, head = lax.div(owner, jnp.int32(heads)), lax.rem(owner, jnp.int32(heads))
    columns = pl.ds(pl.multiple_of(head * HD, LANES), sizes[1] * HD)
    loads = [
        load_rows(source, target, sems.at[kind], fine)
        for kind, (source, target) in enumerate(
            ((weight_hbm.at[:, columns], weight_ref), (tokens_hbm, tokens_ref), (cotan_hbm.at[:, columns], cotan_ref))
        )
    ]
    for load in loads:
        for copy in load:
            copy.start()
    slot, tallies = slots_of(assign_ref[...], groups, rows)
    slot_ref[...] = slot
    pick = ones_where(iota((rows, toks), 0) + group * rows == slot)
    for copy in loads[0] + loads[2]:
        copy.wait()
    step = min(512, toks)
    for first in range(0, toks, step):
        for copy in loads[1][first // fine : (first + step) // fine]:
            copy.wait()
        where = slice(first, first + step)
        query, cotan = dot(tokens_ref[where, :], weight_ref[...]), cotan_ref[where, :].astype(F32)
        for pair in range(sizes[1] // 2):
            pair_columns = slice(pair * LANES, (pair + 1) * LANES)
            even, odd = beside(query[:, pair_columns], cotan[:, pair_columns])
            mixed_ref[where, 2 * pair * LANES : (2 * pair + 1) * LANES] = even
            mixed_ref[where, (2 * pair + 1) * LANES : (2 * pair + 2) * LANES] = odd
    in_order = dot(pick, mixed_ref[...]).astype(BF16)
    for ahead, out_ref in enumerate(out_refs):
        sub = lax.rem(me[1] + ahead, jnp.int32(sizes[1]))
        for other in range(sizes[1]):

            @pl.when(sub == other)
            def _():
                out_ref[:rows, :] = in_order[:, other * LANES : (other + 1) * LANES]

        out_ref[rows:, :] = tallies


def project_query_kernel(sizes, groups, rows, me_ref, slot_ref, assign_ref, tokens_ref, weight_ref, cotan_ref, *rest):
    out_refs, (mixed_ref, sorted_ref) = rest[:-2], rest[-2:]
    toks = tokens_ref.shape[0]
    heads = weight_ref.shape[1] // HD
    step = min(512, toks)
    for first in range(0, toks, step):
        where = slice(first, first + step)
        query, cotan = dot(tokens_ref[where, :], weight_ref[...]), cotan_ref[where, :].astype(F32)
        for pair in range(heads // 2):
            columns = slice(pair * LANES, (pair + 1) * LANES)
            even, odd = beside(query[:, columns], cotan[:, columns])
            mixed_ref[where, 2 * pair * LANES : (2 * pair + 1) * LANES] = even
            mixed_ref[where, (2 * pair + 1) * LANES : (2 * pair + 2) * LANES] = odd
    part = min(512, rows)
    pieces = rows // part

    @pl.loop(0, groups * pieces)
    def _(i):
        group, piece = lax.div(i, jnp.int32(pieces)), lax.rem(i, jnp.int32(pieces))
        first = pl.multiple_of(piece * part, part)
        pick = ones_where(iota((part, toks), 0) + i * part == slot_ref[...])
        sorted_rows = dot(pick, mixed_ref[...]).astype(BF16)
        for head in range(heads):
            sorted_ref[group * heads + head, pl.ds(first, part), :] = sorted_rows[
                :, head * LANES : (head + 1) * LANES
            ]

    member = jnp.where(iota((LANES, toks), 0) == assign_ref[...], 1.0, 0.0).astype(BF16)
    tallies = dot_nt(jnp.ones((COUNT_ROWS, toks), BF16), member).astype(BF16)
    for owner in range(sorted_ref.shape[0]):
        sorted_ref[owner, rows:, :] = tallies
    steps = steps_of(sizes)
    for ahead, out_ref in zip(steps[:1] + steps[1 + sizes[1] :], out_refs):
        out_ref[...] = sorted_ref[owner_of(me_ref, ahead, sizes)]


def project_value_kernel(sizes, groups, rows, me_ref, slot_ref, tokens_ref, weight_ref, *rest):
    out_refs, (turned_ref, unsort_ref, value_ref, sorted_ref) = rest[:-4], rest[-4:]
    toks = tokens_ref.shape[0]
    heads = weight_ref.shape[1] // HD
    step = min(512, toks)

    @pl.loop(0, toks // step)
    def _(i):
        where = pl.ds(pl.multiple_of(i * step, step), step)
        value_ref[where, :] = dot(tokens_ref[where, :], weight_ref[...]).astype(BF16)

    half = rows // 2
    part = min(256, half)
    pieces = half // part

    @pl.loop(0, groups * pieces)
    def _(i):
        group, piece = lax.div(i, jnp.int32(pieces)), lax.rem(i, jnp.int32(pieces))
        first = pl.multiple_of(piece * part, part)
        index = iota((part, toks), 0) + group * rows + first
        upper = dot(ones_where(index == slot_ref[...]), value_ref[...])
        lower = dot(ones_where(index + half == slot_ref[...]), value_ref[...])
        low = low_half((part, LANES))
        for pair in range(heads // 2):
            up = upper[:, pair * LANES : (pair + 1) * LANES]
            down = lower[:, pair * LANES : (pair + 1) * LANES]
            even = jnp.where(low, up, swap_halves(down)).astype(BF16)
            odd = jnp.where(low, swap_halves(up), down).astype(BF16)
            sorted_ref[group * heads + 2 * pair, pl.ds(first, part), :] = even
            sorted_ref[group * heads + 2 * pair + 1, pl.ds(first, part), :] = odd

    hand_out(sorted_ref, out_refs, me_ref, sizes)
    turned = tokens_ref[...].T
    slots = unsort_ref.shape[1]
    part = min(256, slots)
    for i in range(slots // part):
        pick = ones_where(iota((part, toks), 0) + i * part == slot_ref[...])
        unsort_ref[:, i * part : (i + 1) * part] = pick.T
        turned_ref[:, i * part : (i + 1) * part] = dot_nt(turned, pick).astype(BF16)


def score(mixed):
    query = jnp.where(low_half(mixed.shape), mixed.astype(F32) * SCALE, 0.0).astype(BF16)
    return dot_nt(query, mixed)


def softmax_turned(scores):
    shape = scores.shape
    seen = iota(shape, 0) <= iota(shape, 1)
    scores = jnp.where(seen, scores, -jnp.inf)
    raised = jnp.exp(scores - jnp.max(scores, axis=0, keepdims=True))
    return raised * (1.0 / jnp.sum(raised, axis=0, keepdims=True))


def for_each_cluster(counts_ref, me_ref, place_ref, owners, per_group, body):
    for source in range(owners):
        place_ref[source] = 0

    def step(cluster, block):
        runs = []
        total = 0
        base = block * BLOCK_ROWS
        for source in range(owners):
            count = counts_ref[source, me_ref[3] + cluster]
            start = place_ref[source]
            runs.append((source, start, base + total))
            place_ref[source] = start + count
            total = total + count
        body(cluster, block, runs, base + total)
        return block + lax.shift_right_logical(total + (BLOCK_ROWS - 1), jnp.int32(7))

    return lax.fori_loop(0, per_group, step, jnp.int32(LEAD * UNROLL))


def gather_blocks(counts_ref, me_ref, place_ref, owners, per_group, slot_rows, wide_ref, block_ref):
    def body(cluster, block, runs, end):
        for source, start, row in runs:
            block_ref[pl.ds(row, slot_rows), :] = wide_ref[source, pl.ds(start, slot_rows), :]
        block_ref[pl.ds(end, BLOCK_ROWS), :] = jnp.zeros((BLOCK_ROWS, LANES), F32)

    blocks = for_each_cluster(counts_ref, me_ref, place_ref, owners, per_group, body)
    spare = pl.ds(pl.multiple_of(blocks * BLOCK_ROWS, BLOCK_ROWS), GROUP_ROWS)
    block_ref[spare, :] = jnp.zeros((GROUP_ROWS, LANES), F32)
    return blocks


def for_each_group(blocks, stages):
    first, second, third = stages
    groups = lax.div(blocks + (UNROLL - 1), jnp.int32(UNROLL))

    def step(i, carry):
        for slot in range(2):
            group = LEAD + 2 * i + slot
            third(group - 2, slot)
            second(group - 1, 1 - slot)
            first(group, slot)
        return carry

    lax.fori_loop(0, lax.shift_right_logical(groups + 1, jnp.int32(1)), step, 0)


def block_rows(group, ahead):
    return pl.ds(pl.multiple_of((group * UNROLL + ahead) * BLOCK_ROWS, BLOCK_ROWS), BLOCK_ROWS)


def tile_rows(ahead):
    return slice(ahead * BLOCK_ROWS, (ahead + 1) * BLOCK_ROWS)


def value_grad_kernel(sizes, per_group, slot_rows, me_ref, *refs):
    owners = sizes[0] * sizes[1]
    mixed_refs, out_refs, rest = refs[:owners], refs[owners : owners + sizes[0]], refs[owners + sizes[0] :]
    dense_ref, counts_out_ref, counts_ref, place_ref, wide_ref, block_ref, home_ref = rest[:7]
    score_refs, probs_refs = rest[7:9], rest[9:11]
    half = out_refs[0].shape[1]
    rows = 2 * half
    for ahead, mixed_ref in zip(steps_of(sizes), mixed_refs):
        source = source_of(me_ref, ahead, sizes)
        tail = mixed_ref[rows:, :].astype(F32).astype(jnp.int32)
        counts_out_ref[pl.ds(source, 1), :] = tail[:1, :]
        wide_ref[source, :rows, :] = mixed_ref[:rows, :].astype(F32)
        wide_ref[source, rows:, :] = jnp.zeros((slot_rows, LANES), F32)
    pltpu.sync_copy(counts_out_ref, counts_ref)
    blocks = gather_blocks(counts_ref, me_ref, place_ref, owners, per_group, slot_rows, wide_ref, block_ref)

    def first(group, slot):
        for ahead in range(UNROLL):
            where = block_rows(group, ahead)
            mixed = block_ref[where, :].astype(BF16)
            dense_ref[where, :] = mixed
            score_refs[slot][tile_rows(ahead), :] = score(mixed)

    def second(group, slot):
        for ahead in range(UNROLL):
            tile = tile_rows(ahead)
            probs_refs[slot][tile, :] = softmax_turned(score_refs[slot][tile, :]).astype(BF16)

    def third(group, slot):
        for ahead in range(UNROLL):
            where = block_rows(group, ahead)
            block_ref[where, :] = dot(probs_refs[slot][tile_rows(ahead), :], dense_ref[where, :])

    for_each_group(blocks, (first, second, third))

    def scatter(cluster, block, runs, end):
        for source, start, row in runs:
            wide_ref[source, pl.ds(start, slot_rows), :] = block_ref[pl.ds(row, slot_rows), :]

    for_each_cluster(counts_ref, me_ref, place_ref, owners, per_group, scatter)
    for ahead, out_ref in enumerate(out_refs):
        for sub in range(sizes[1]):
            source = owner_of(me_ref, (ahead, 0), sizes) - me_ref[1] + sub
            up, down = wide_ref[source, :half, :], wide_ref[source, half:rows, :]
            out_ref[sub] = jnp.where(low_half((half, LANES)), swap_halves(up), down).astype(BF16)


def query_grad_kernel(sizes, per_group, slot_rows, me_ref, counts_ref, dense_ref, *refs):
    owners = sizes[0] * sizes[1]
    value_refs, out_refs, rest = refs[:owners], refs[owners : 2 * owners], refs[2 * owners :]
    place_ref, wide_ref, block_ref, sums_ref, centroid_ref = rest[:5]
    score_refs, grad_probs_refs, both_refs = rest[5:7], rest[7:9], rest[9:11]
    half = value_refs[0].shape[0]
    rows = 2 * half
    for ahead, value_ref in zip(steps_of(sizes), value_refs):
        source = source_of(me_ref, ahead, sizes)
        value = value_ref[...].astype(F32)
        wide_ref[source, :half, :] = swap_halves(value)
        wide_ref[source, half:rows, :] = value
        wide_ref[source, rows:, :] = jnp.zeros((slot_rows, LANES), F32)
    blocks = gather_blocks(counts_ref, me_ref, place_ref, owners, per_group, slot_rows, wide_ref, block_ref)

    def first(group, slot):
        for ahead in range(UNROLL):
            where, tile = block_rows(group, ahead), tile_rows(ahead)
            mixed = dense_ref[where, :]
            value = block_ref[where, :].astype(BF16)
            cotan = jnp.where(low_half(mixed.shape), jnp.zeros_like(mixed), mixed)
            score_refs[slot][tile, :] = score(mixed)
            grad_probs_refs[slot][tile, :] = dot_nt(value, cotan)

    def second(group, slot):
        for ahead in range(UNROLL):
            tile = tile_rows(ahead)
            probs = softmax_turned(score_refs[slot][tile, :])
            grad_probs = grad_probs_refs[slot][tile, :]
            probs_half = probs.astype(BF16).astype(F32)
            row_dot = jnp.sum(probs_half * grad_probs, axis=0, keepdims=True)
            grad_scores = (probs * (grad_probs - row_dot)).astype(BF16).astype(F32)
            both_refs[slot][tile, :] = (grad_scores + grad_scores.T).astype(BF16)

    def third(group, slot):
        for ahead in range(UNROLL):
            where = block_rows(group, ahead)
            grad = dot(both_refs[slot][tile_rows(ahead), :], dense_ref[where, :]) * SCALE
            grad = grad.astype(BF16).astype(F32)
            block_ref[where, :] = grad
            sums_ref[pl.ds(group * UNROLL + ahead, 1), :] = jnp.sum(grad, axis=0, keepdims=True)

    for_each_group(blocks, (first, second, third))
    most = (owners * slot_rows + BLOCK_ROWS - 1) // BLOCK_ROWS

    def scatter(cluster, block, runs, end):
        total = jnp.zeros((1, LANES), F32)
        for ahead in range(most):
            here = block + ahead
            total = total + jnp.where(here * BLOCK_ROWS < end, sums_ref[pl.ds(here, 1), :], 0.0)
        centroid_ref[pl.ds(cluster, 1), :] = total
        for source, start, row in runs:
            wide_ref[source, pl.ds(start, slot_rows), :] = block_ref[pl.ds(row, slot_rows), :]

    for_each_cluster(counts_ref, me_ref, place_ref, owners, per_group, scatter)
    extra = out_refs[0].shape[0] - half
    centroid = jnp.where(
        low_half((extra, LANES)), centroid_ref[:extra, :], swap_halves(centroid_ref[extra:, :])
    ).astype(BF16)
    for ahead, out_ref in zip(steps_of(sizes), out_refs):
        source = owner_of(me_ref, ahead, sizes)
        up, down = wide_ref[source, :half, :], wide_ref[source, half:rows, :]
        out_ref[:half, :] = jnp.where(low_half((half, LANES)), up, swap_halves(down)).astype(BF16)
        out_ref[half:, :] = centroid


def unfold(home_ref, out_ref, heads, start, half, finish):
    low = low_half((half, LANES))
    for group in range(home_ref.shape[0] // heads):
        first = group * 2 * half
        for pair in range(heads // 2):
            even = home_ref[group * heads + 2 * pair, start : start + half, :].astype(F32)
            odd = home_ref[group * heads + 2 * pair + 1, start : start + half, :].astype(F32)
            columns = slice(pair * LANES, (pair + 1) * LANES)
            out_ref[first : first + half, columns] = finish(jnp.where(low, even, swap_halves(odd)))
            out_ref[first + half : first + 2 * half, columns] = finish(
                jnp.where(low, swap_halves(even), odd)
            )


def to_half(x):
    return x.astype(BF16)


def bring_home(sizes, heads, pieces, home_ref, rows_ref):
    for source, piece in pieces:
        home_ref[source] = piece
    unfold(home_ref, rows_ref, heads, 0, rows_ref.shape[0] * heads // home_ref.shape[0] // 2, to_half)


def weight_partial(sizes, me_ref, turned_ref, rows_ref, sub_refs):
    piece = turned_ref.shape[0] // (sizes[0] * sizes[1])
    for ahead, sub_ref in enumerate(sub_refs):
        sub = lax.rem(me_ref[1] + ahead, jnp.int32(sizes[1]))
        first = [pl.multiple_of((seq * sizes[1] + sub) * piece, piece) for seq in range(sizes[0])]
        turned = jnp.concatenate([turned_ref[pl.ds(row, piece), :] for row in first], axis=0)
        partial = dot(turned, rows_ref[...]).astype(BF16)
        for seq in range(sizes[0]):
            sub_ref[seq] = partial[seq * piece : (seq + 1) * piece, :]


def input_columns(me_ref, ahead, parts, width):
    columns = width // parts
    dest = lax.rem(me_ref[2] + ahead, jnp.int32(parts))
    return pl.ds(pl.multiple_of(dest * columns, columns), columns)


def value_home_kernel(sizes, heads, parts, me_ref, turned_ref, weight_ref, *refs):
    came = sizes[0] + sizes[1] - 1
    part_refs, refs = refs[:came], refs[came:]
    rows_ref, term_refs, refs = refs[0], refs[1:parts], refs[parts:]
    sub_refs, home_ref = refs[: sizes[1]], refs[sizes[1]]
    bring_home(sizes, heads, arrivals(sizes, me_ref, part_refs), home_ref, rows_ref)
    for k, term_ref in enumerate(term_refs):
        mine = input_columns(me_ref, k + 1, parts, weight_ref.shape[0])
        term_ref[...] = dot_nt(rows_ref[...], weight_ref[mine, :])
    weight_partial(sizes, me_ref, turned_ref, rows_ref, sub_refs)


def query_home_kernel(sizes, heads, factor, parts, me_ref, weight_ref, *refs):
    term_refs, refs = refs[: parts - 1], refs[parts - 1 :]
    part_refs, refs = refs[: sizes[0] * sizes[1]], refs[sizes[0] * sizes[1] :]
    out_refs, (rows_ref, centroid_ref, home_ref) = refs[: parts - 1], refs[parts - 1 :]
    pieces = [
        (source_of(me_ref, ahead, sizes), part_ref[...]) for ahead, part_ref in zip(steps_of(sizes), part_refs)
    ]
    bring_home(sizes, heads, pieces, home_ref, rows_ref)
    for k, (term_ref, out_ref) in enumerate(zip(term_refs, out_refs)):
        mine = input_columns(me_ref, k + 1, parts, weight_ref.shape[0])
        out_ref[...] = (dot_nt(rows_ref[...], weight_ref[mine, :]) + term_ref[...]).astype(BF16)
    half = rows_ref.shape[0] * heads // home_ref.shape[0] // 2
    unfold(home_ref, centroid_ref, heads, half, home_ref.shape[1] - half, lambda x: x * factor)


def query_weight_kernel(sizes, me_ref, turned_ref, rows_ref, *sub_refs):
    weight_partial(sizes, me_ref, turned_ref, rows_ref, sub_refs)


def input_own_kernel(parts, me_ref, rows_ref, value_rows_ref, w_query_ref, w_value_ref, out_ref):
    mine = input_columns(me_ref, 0, parts, w_query_ref.shape[0])
    total = dot_nt(rows_ref[...], w_query_ref[mine, :]) + dot_nt(value_rows_ref[...], w_value_ref[mine, :])
    out_ref[...] = total.astype(BF16)


def fold_subs_kernel(me_ref, *refs):
    seqs = refs[0].shape[0]
    terms, out_refs = refs[:-seqs], refs[-seqs:]
    for ahead, out_ref in enumerate(out_refs):
        seq = lax.rem(me_ref[0] + ahead, jnp.int32(seqs))
        total = terms[0][seq].astype(F32)
        for term in terms[1:]:
            total = total + term[seq].astype(F32)
        out_ref[...] = total.astype(BF16)


def sum_kernel(*refs):
    total = refs[0][...].astype(F32)
    for ref in refs[1:-1]:
        total = total + ref[...].astype(F32)
    refs[-1][...] = total.astype(refs[-1].dtype)


def input_sum_kernel(unsort_ref, weight_ref, *refs):
    part_refs, out_ref, weight_out_ref, total_ref = refs[:-3], refs[-3], refs[-2], refs[-1]
    total = part_refs[0][...].astype(F32)
    for part_ref in part_refs[1:]:
        total = total + part_ref[...].astype(F32)
    total_ref[...] = total.astype(BF16)
    out_ref[...] = dot(unsort_ref[...], total_ref[...]).astype(BF16)
    weight_out_ref[...] = weight_ref[...]


def call(kernel, outs, inputs, smem=(0,), in_place=(), after=(), scratch=(), flops=0, vmem=24, name=None):
    def body(*refs):
        kernel(*refs[: len(inputs)], *refs[len(inputs) + len(after) :])

    def space(i):
        return pltpu.SMEM if i in smem else pl.ANY if i in in_place else pltpu.VMEM

    specs = [pl.BlockSpec(memory_space=space(i)) for i in range(len(inputs))]
    specs += [pl.BlockSpec(memory_space=pl.ANY)] * len(after)
    moved = sum(x.size * x.dtype.itemsize for x in inputs) + sum(
        x.size * x.dtype.itemsize for x in jax.tree.leaves(outs)
    )
    return pl.pallas_call(
        body,
        out_shape=outs,
        in_specs=specs,
        out_specs=jax.tree.map(lambda _: pl.BlockSpec(memory_space=pltpu.VMEM), outs),
        scratch_shapes=list(scratch),
        compiler_params=pltpu.CompilerParams(vmem_limit_bytes=vmem * 2**20),
        cost_estimate=pl.CostEstimate(flops=flops, bytes_accessed=moved, transcendentals=0),
        name=name,
    )(*inputs, *after)


def exchange(parts, sizes):
    out = []
    for ahead, part in zip(steps_of(sizes), parts):
        moves = [
            (
                seq * sizes[1] + sub,
                (seq + ahead[0]) % sizes[0] * sizes[1] + (sub + ahead[1]) % sizes[1],
            )
            for seq, sub in steps_of(sizes)
        ]
        out.append(part if ahead == (0, 0) else lax.ppermute(part, OWNERS, moves))
    return out


def shift(part, axis, ahead):
    size = lax.axis_size(axis)
    return lax.ppermute(part, axis, [(i, (i + ahead) % size) for i in range(size)])


def pass_round(parts, axis):
    return [parts[0]] + [shift(parts[ahead], axis, ahead) for ahead in range(1, len(parts))]


def exchange_by_chip(me, parts, sizes, name, after=()):
    came = pass_round(parts, "seq")
    swapped = call(
        functools.partial(swap_kernel, sizes),
        (jax.ShapeDtypeStruct((sizes[0], *parts[0].shape[1:]), BF16),) * (sizes[1] - 1),
        (me, *came),
        after=after,
        name=name,
    )
    return came + [shift(part, "sub", k + 1) for k, part in enumerate(swapped)]


def fold_subs(me, by_sub, name):
    seqs, piece, columns = by_sub[0].shape
    return call(
        fold_subs_kernel,
        (jax.ShapeDtypeStruct((piece, columns), BF16),) * seqs,
        (me, *pass_round(by_sub, "sub")),
        name=name,
    )


def add_up(terms, dtype, name, after=()):
    out = jax.ShapeDtypeStruct(terms[0].shape, dtype)
    return call(sum_kernel, out, tuple(terms), smem=(), after=after, name=name)


def on_device(tokens_in, w_query, w_value, cotangent, assignment):
    sizes = (lax.axis_size("seq"), lax.axis_size("sub"))
    owners = sizes[0] * sizes[1]
    parts = lax.axis_size("head")
    toks, width = tokens_in.shape
    width_dev = cotangent.shape[1]
    heads = width_dev // HD
    slot_rows = 2 * toks // CLUSTERS
    assert owners % heads == 0 and heads % 2 == 0
    groups = owners // heads
    per_group = CLUSTERS // groups
    rows = toks if groups == 1 else per_group * slot_rows
    half = rows // 2
    slots = groups * rows
    columns = width // parts
    capacity = (slot_rows * owners + BLOCK_ROWS - 1) // BLOCK_ROWS * BLOCK_ROWS
    extra = max(per_group // 2, 16)
    shape = jax.ShapeDtypeStruct
    seq, sub = lax.axis_index("seq"), lax.axis_index("sub")
    first = lax.div(seq * sizes[1] + sub, jnp.int32(heads)) * per_group
    me = jnp.stack([seq, sub, lax.axis_index("head"), first]).astype(jnp.int32)

    def several(count, *dims):
        return (shape(dims, BF16),) * count

    assign_row = assignment.reshape(1, toks)
    *far_mixed, slot_row = call(
        functools.partial(project_far_kernel, sizes, groups, rows, heads),
        several(sizes[1], rows + COUNT_ROWS, LANES) + (shape((1, toks), jnp.int32),),
        (assign_row, tokens_in, w_query, cotangent),
        smem=(),
        in_place=(1, 2, 3),
        scratch=[
            pltpu.VMEM((toks, width), BF16),
            pltpu.VMEM((width, sizes[1] * HD), BF16),
            pltpu.VMEM((toks, sizes[1] * HD), BF16),
            pltpu.VMEM((toks, sizes[1] * LANES), BF16),
            pltpu.SemaphoreType.DMA((3, max(toks, width) // min(256, toks))),
        ],
        flops=2 * toks * width * sizes[1] * HD + 2 * rows * toks * sizes[1] * LANES,
        vmem=60,
        name="project_far",
    )
    own_mixed, *near_mixed = call(
        functools.partial(project_query_kernel, sizes, groups, rows),
        several(owners - sizes[1], rows + COUNT_ROWS, LANES),
        (me, slot_row, assign_row, tokens_in, w_query, cotangent),
        scratch=[pltpu.VMEM((toks, 2 * width_dev), BF16), pltpu.VMEM((owners, rows + COUNT_ROWS, LANES), BF16)],
        flops=2 * toks * width * width_dev + 4 * slots * toks * width_dev,
        name="project_query",
    )
    send_mixed = [own_mixed, *far_mixed, *near_mixed]
    got_mixed = exchange(send_mixed, sizes)
    *send_value, turned, unsort = call(
        functools.partial(project_value_kernel, sizes, groups, rows),
        several(owners, half, LANES) + several(1, width, slots) + several(1, toks, slots),
        (me, slot_row, tokens_in, w_value),
        after=near_mixed[:1],
        scratch=[pltpu.VMEM((toks, width_dev), BF16), pltpu.VMEM((owners, half, LANES), BF16)],
        flops=2 * toks * width * width_dev + 2 * slots * toks * width_dev,
        name="project_value",
    )
    behind = [0, *range(3, owners), 2, 1][:owners]
    send_value = [lax.optimization_barrier((part, got_mixed[k]))[0] for part, k in zip(send_value, behind)]
    got_value = exchange(send_value, sizes)
    blocks = per_group * capacity // BLOCK_ROWS
    held = blocks + (LEAD + 4) * UNROLL
    block_flops = 2 * BLOCK_ROWS * BLOCK_ROWS * LANES
    tall = pltpu.VMEM((owners, rows + slot_rows, LANES), F32)
    dense_rows = pltpu.VMEM((held * BLOCK_ROWS, LANES), F32)
    group_f32 = pltpu.VMEM((GROUP_ROWS, BLOCK_ROWS), F32)
    group_b16 = pltpu.VMEM((GROUP_ROWS, BLOCK_ROWS), BF16)
    place = pltpu.SMEM((owners,), jnp.int32)
    *back_value, dense, counts = call(
        functools.partial(value_grad_kernel, sizes, per_group, slot_rows),
        several(sizes[0], sizes[1], half, LANES)
        + several(1, held * BLOCK_ROWS, LANES)
        + (shape((owners, LANES), jnp.int32),),
        (me, *got_mixed),
        after=[unsort],
        scratch=[pltpu.SMEM((owners, LANES), jnp.int32), place, tall, dense_rows, tall]
        + [group_f32] * 2
        + [group_b16] * 2,
        flops=4 * blocks * block_flops,
        vmem=48,
        name="value_grad",
    )
    back_value, _ = lax.optimization_barrier((back_value, got_value[1:]))
    back_query = call(
        functools.partial(query_grad_kernel, sizes, per_group, slot_rows),
        several(owners, half + extra, LANES),
        (me, counts, dense, *got_value),
        smem=(0, 1),
        scratch=[place, tall, dense_rows, pltpu.VMEM((held, LANES), F32), pltpu.VMEM((2 * extra, LANES), F32)]
        + [group_f32] * 4
        + [group_b16] * 2,
        flops=6 * blocks * block_flops,
        vmem=48,
        name="query_grad",
    )
    home_query = exchange(back_query, sizes)
    home_value = exchange_by_chip(me, back_value, sizes, "swap", home_query[1:3])
    weight_flops = 2 * slots * width * width_dev
    home_flops = weight_flops // parts * (parts - 1)
    piece = width // owners
    sub_shapes = several(sizes[1], sizes[0], piece, width_dev)
    value_rows, *refs = call(
        functools.partial(value_home_kernel, sizes, heads, parts),
        several(1, slots, width_dev) + (shape((slots, columns), F32),) * (parts - 1) + sub_shapes,
        (me, turned, w_value, *home_value),
        scratch=[pltpu.VMEM((owners, half, LANES), BF16)],
        flops=weight_flops + home_flops,
        name="value_home",
    )
    value_terms, value_weight = refs[: parts - 1], refs[parts - 1 :]
    value_weight = fold_subs(me, value_weight, "value_subs")
    *partials, query_rows, centroid_grad = call(
        functools.partial(query_home_kernel, sizes, heads, (CLUSTERS / (toks * owners)) ** 0.5, parts),
        several(parts - 1, slots, columns)
        + several(1, slots, width_dev)
        + (shape((groups * 2 * extra, width_dev), F32),),
        (me, w_query, *value_terms, *home_query),
        scratch=[pltpu.VMEM((owners, half + extra, LANES), BF16)],
        flops=home_flops,
        name="query_home",
    )
    arrived = [shift(partial, "head", k + 1) for k, partial in enumerate(partials)]
    value_weight, _ = lax.optimization_barrier((value_weight, home_query))
    value_weight = pass_round(value_weight, "seq")
    query_weight = call(
        functools.partial(query_weight_kernel, sizes),
        sub_shapes,
        (me, turned, query_rows),
        flops=weight_flops,
        name="query_weight",
    )
    query_weight = fold_subs(me, query_weight, "query_subs")
    own = call(
        functools.partial(input_own_kernel, parts),
        shape((slots, columns), BF16),
        (me, query_rows, value_rows, w_query, w_value),
        after=query_weight[:1],
        flops=weight_flops * 2 // parts,
        name="input_own",
    )
    query_weight = pass_round(query_weight, "seq")
    grad_wv = add_up(value_weight, F32, "value_sum", [own])
    grad_input, own_weight = call(
        input_sum_kernel,
        several(1, toks, columns) + several(1, piece, width_dev),
        (unsort, query_weight[0], own, *arrived),
        smem=(),
        scratch=[pltpu.VMEM((slots, columns), BF16)],
        flops=2 * toks * slots * columns,
        name="input_sum",
    )
    grad_wq = add_up([own_weight, *query_weight[1:]], F32, "query_sum")
    if groups > 1:
        centroid_grad = centroid_grad.reshape(groups, 2 * extra, width_dev)[:, :per_group]
        centroid_grad = centroid_grad.reshape(CLUSTERS, width_dev)
    return (grad_input, grad_wq, grad_wv, centroid_grad)


def solution(mesh):
    return jax.shard_map(
        on_device,
        mesh=mesh,
        in_specs=(
            P(("grp", "seq", "sub"), None),
            P(None, "head"),
            P(None, "head"),
            P(("grp", "seq", "sub"), "head"),
            P(("grp", "seq", "sub"), None),
        ),
        out_specs=(
            P(("grp", "seq", "sub"), "head"),
            P(("grp", "seq", "sub"), "head"),
            P(("grp", "seq", "sub"), "head"),
            P("grp", "head"),
        ),
        check_vma=False,
    )
```

```python
import functools

import jax
import jax.numpy as jnp
from jax import lax
from jax.experimental import pallas as pl
from jax.experimental.pallas import tpu as pltpu
from jax.sharding import PartitionSpec as P

HD = 64
CLUSTERS = 64
BLOCK_ROWS = 128
LANES = 128
UNROLL = 4
COUNT_ROWS = 16
SCALE = 0.5 * HD ** (-0.5)
F32 = jnp.float32
BF16 = jnp.bfloat16
OWNERS = ("seq", "sub")
GROUP_ROWS = UNROLL * BLOCK_ROWS
LEAD = 2


def iota(shape, dim):
    return lax.broadcasted_iota(jnp.int32, shape, dim)


def low_half(shape):
    return iota(shape, 1) < HD


def swap_halves(tile):
    return pltpu.roll(tile, HD, 1)


def dot(a, b):
    return jnp.dot(a, b, preferred_element_type=F32)


def dot_nt(a, b):
    return lax.dot_general(a, b, (((1,), (1,)), ((), ())), preferred_element_type=F32)


def ones_where(condition):
    return jnp.where(condition, 1.0, 0.0).astype(BF16)


def owner_of(me_ref, ahead, sizes):
    seq = lax.rem(me_ref[0] + ahead[0], jnp.int32(sizes[0]))
    sub = lax.rem(me_ref[1] + ahead[1], jnp.int32(sizes[1]))
    return seq * sizes[1] + sub


def source_of(me_ref, ahead, sizes):
    return owner_of(me_ref, ((sizes[0] - ahead[0]) % sizes[0], (sizes[1] - ahead[1]) % sizes[1]), sizes)


def steps_of(sizes):
    far = sorted(range(1, sizes[0]), key=lambda seq: -min(seq, sizes[0] - seq))
    subs = range(sizes[1])
    return [(0, 0)] + [(seq, sub) for seq in far for sub in subs] + [(0, sub) for sub in subs if sub]


def hand_out(by_owner_ref, out_refs, me_ref, sizes):
    for ahead, out_ref in zip(steps_of(sizes), out_refs):
        out_ref[...] = by_owner_ref[owner_of(me_ref, ahead, sizes)]


def slots_of(assign, groups, rows):
    toks = assign.shape[1]
    per_group = CLUSTERS // groups
    member = jnp.where(iota((CLUSTERS, toks), 0) == assign, 1.0, 0.0)
    member_b = member.astype(BF16)
    upto = ones_where(iota((LANES, LANES), 0) <= iota((LANES, LANES), 1))
    counts = jnp.zeros((CLUSTERS, 1), F32)
    running = []
    for first in range(0, toks, LANES):
        within = dot(member_b[:, first : first + LANES], upto)
        running.append(within + counts)
        counts = counts + within[:, LANES - 1 :]
    running = jnp.concatenate(running, axis=1)
    here, other = iota((CLUSTERS, CLUSTERS), 0), iota((CLUSTERS, CLUSTERS), 1)
    group_of = lambda index: lax.div(index, jnp.int32(per_group))
    earlier = ones_where((other < here) & (group_of(other) == group_of(here)))
    base = dot(earlier, jnp.broadcast_to(counts, (CLUSTERS, LANES)).astype(BF16))[:, :1]
    base = base + (group_of(iota((CLUSTERS, 1), 0)) * rows).astype(F32)
    slot = jnp.sum(member * (running - 1.0 + base), axis=0, keepdims=True).astype(jnp.int32)
    spread = jnp.concatenate([member_b, jnp.zeros((LANES - CLUSTERS, toks), BF16)], axis=0)
    return slot, dot_nt(jnp.ones((COUNT_ROWS, toks), BF16), spread).astype(BF16)


def arrivals(sizes, me_ref, refs):
    seqs, subs = sizes
    for ahead in steps_of(sizes):
        if ahead[1] == 0:
            piece = refs[ahead[0]][me_ref[1]]
        else:
            piece = refs[seqs + ahead[1] - 1][ahead[0]]
        yield source_of(me_ref, ahead, sizes), piece


def swap_kernel(sizes, me_ref, *refs):
    for k, out_ref in enumerate(refs[sizes[0] :]):
        sub = lax.rem(me_ref[1] + (k + 1), jnp.int32(sizes[1]))
        for seq in range(sizes[0]):
            out_ref[seq] = refs[seq][sub]


def beside(query, cotan):
    low = low_half(query.shape)
    even = jnp.where(low, query, swap_halves(cotan)).astype(BF16)
    return even, jnp.where(low, swap_halves(query), cotan).astype(BF16)


def load_rows(source, target, sems, fine):
    return [
        pltpu.make_async_copy(source.at[pl.ds(row, fine), :], target.at[pl.ds(row, fine), :], sems.at[row // fine])
        for row in range(0, target.shape[0], fine)
    ]


def project_far_kernel(sizes, groups, rows, heads, assign_ref, tokens_hbm, weight_hbm, cotan_hbm, *refs):
    out_refs, refs = refs[: sizes[1]], refs[sizes[1] :]
    slot_ref, tokens_ref, weight_ref, cotan_ref, mixed_ref, sems = refs
    toks = tokens_ref.shape[0]
    fine = min(256, toks)
    me = (lax.axis_index("seq"), lax.axis_index("sub"))
    owner = owner_of(me, steps_of(sizes)[1], sizes) - me[1]
    group, head = lax.div(owner, jnp.int32(heads)), lax.rem(owner, jnp.int32(heads))
    columns = pl.ds(pl.multiple_of(head * HD, LANES), sizes[1] * HD)
    loads = [
        load_rows(source, target, sems.at[kind], fine)
        for kind, (source, target) in enumerate(
            ((weight_hbm.at[:, columns], weight_ref), (tokens_hbm, tokens_ref), (cotan_hbm.at[:, columns], cotan_ref))
        )
    ]
    for load in loads:
        for copy in load:
            copy.start()
    slot, tallies = slots_of(assign_ref[...], groups, rows)
    slot_ref[...] = slot
    pick = ones_where(iota((rows, toks), 0) + group * rows == slot)
    for copy in loads[0] + loads[2]:
        copy.wait()
    step = min(512, toks)
    for first in range(0, toks, step):
        for copy in loads[1][first // fine : (first + step) // fine]:
            copy.wait()
        where = slice(first, first + step)
        query, cotan = dot(tokens_ref[where, :], weight_ref[...]), cotan_ref[where, :].astype(F32)
        for pair in range(sizes[1] // 2):
            pair_columns = slice(pair * LANES, (pair + 1) * LANES)
            even, odd = beside(query[:, pair_columns], cotan[:, pair_columns])
            mixed_ref[where, 2 * pair * LANES : (2 * pair + 1) * LANES] = even
            mixed_ref[where, (2 * pair + 1) * LANES : (2 * pair + 2) * LANES] = odd
    in_order = dot(pick, mixed_ref[...]).astype(BF16)
    for ahead, out_ref in enumerate(out_refs):
        sub = lax.rem(me[1] + ahead, jnp.int32(sizes[1]))
        for other in range(sizes[1]):

            @pl.when(sub == other)
            def _():
                out_ref[:rows, :] = in_order[:, other * LANES : (other + 1) * LANES]

        out_ref[rows:, :] = tallies


def project_query_kernel(sizes, groups, rows, me_ref, slot_ref, assign_ref, tokens_ref, weight_ref, cotan_ref, *rest):
    out_refs, (mixed_ref, sorted_ref) = rest[:-2], rest[-2:]
    toks = tokens_ref.shape[0]
    heads = weight_ref.shape[1] // HD
    step = min(512, toks)
    for first in range(0, toks, step):
        where = slice(first, first + step)
        query, cotan = dot(tokens_ref[where, :], weight_ref[...]), cotan_ref[where, :].astype(F32)
        for pair in range(heads // 2):
            columns = slice(pair * LANES, (pair + 1) * LANES)
            even, odd = beside(query[:, columns], cotan[:, columns])
            mixed_ref[where, 2 * pair * LANES : (2 * pair + 1) * LANES] = even
            mixed_ref[where, (2 * pair + 1) * LANES : (2 * pair + 2) * LANES] = odd
    part = min(512, rows)
    pieces = rows // part

    @pl.loop(0, groups * pieces)
    def _(i):
        group, piece = lax.div(i, jnp.int32(pieces)), lax.rem(i, jnp.int32(pieces))
        first = pl.multiple_of(piece * part, part)
        pick = ones_where(iota((part, toks), 0) + i * part == slot_ref[...])
        sorted_rows = dot(pick, mixed_ref[...]).astype(BF16)
        for head in range(heads):
            sorted_ref[group * heads + head, pl.ds(first, part), :] = sorted_rows[
                :, head * LANES : (head + 1) * LANES
            ]

    member = jnp.where(iota((LANES, toks), 0) == assign_ref[...], 1.0, 0.0).astype(BF16)
    tallies = dot_nt(jnp.ones((COUNT_ROWS, toks), BF16), member).astype(BF16)
    for owner in range(sorted_ref.shape[0]):
        sorted_ref[owner, rows:, :] = tallies
    steps = steps_of(sizes)
    for ahead, out_ref in zip(steps[:1] + steps[1 + sizes[1] :], out_refs):
        out_ref[...] = sorted_ref[owner_of(me_ref, ahead, sizes)]


def project_value_kernel(sizes, groups, rows, me_ref, slot_ref, tokens_ref, weight_ref, *rest):
    out_refs, (turned_ref, unsort_ref, value_ref, sorted_ref) = rest[:-4], rest[-4:]
    toks = tokens_ref.shape[0]
    heads = weight_ref.shape[1] // HD
    step = min(512, toks)

    @pl.loop(0, toks // step)
    def _(i):
        where = pl.ds(pl.multiple_of(i * step, step), step)
        value_ref[where, :] = dot(tokens_ref[where, :], weight_ref[...]).astype(BF16)

    half = rows // 2
    part = min(256, half)
    pieces = half // part

    @pl.loop(0, groups * pieces)
    def _(i):
        group, piece = lax.div(i, jnp.int32(pieces)), lax.rem(i, jnp.int32(pieces))
        first = pl.multiple_of(piece * part, part)
        index = iota((part, toks), 0) + group * rows + first
        upper = dot(ones_where(index == slot_ref[...]), value_ref[...])
        lower = dot(ones_where(index + half == slot_ref[...]), value_ref[...])
        low = low_half((part, LANES))
        for pair in range(heads // 2):
            up = upper[:, pair * LANES : (pair + 1) * LANES]
            down = lower[:, pair * LANES : (pair + 1) * LANES]
            even = jnp.where(low, up, swap_halves(down)).astype(BF16)
            odd = jnp.where(low, swap_halves(up), down).astype(BF16)
            sorted_ref[group * heads + 2 * pair, pl.ds(first, part), :] = even
            sorted_ref[group * heads + 2 * pair + 1, pl.ds(first, part), :] = odd

    hand_out(sorted_ref, out_refs, me_ref, sizes)
    turned = tokens_ref[...].T
    slots = unsort_ref.shape[1]
    part = min(256, slots)
    for i in range(slots // part):
        pick = ones_where(iota((part, toks), 0) + i * part == slot_ref[...])
        unsort_ref[:, i * part : (i + 1) * part] = pick.T
        turned_ref[:, i * part : (i + 1) * part] = dot_nt(turned, pick).astype(BF16)


def score(mixed):
    query = jnp.where(low_half(mixed.shape), mixed.astype(F32) * SCALE, 0.0).astype(BF16)
    return dot_nt(query, mixed)


def softmax_turned(scores):
    shape = scores.shape
    seen = iota(shape, 0) <= iota(shape, 1)
    scores = jnp.where(seen, scores, -jnp.inf)
    raised = jnp.exp(scores - jnp.max(scores, axis=0, keepdims=True))
    return raised * (1.0 / jnp.sum(raised, axis=0, keepdims=True))


def for_each_cluster(counts_ref, me_ref, place_ref, owners, per_group, body):
    for source in range(owners):
        place_ref[source] = 0

    def step(cluster, block):
        runs = []
        total = 0
        base = block * BLOCK_ROWS
        for source in range(owners):
            count = counts_ref[source, me_ref[3] + cluster]
            start = place_ref[source]
            runs.append((source, start, base + total))
            place_ref[source] = start + count
            total = total + count
        body(cluster, block, runs, base + total)
        return block + lax.shift_right_logical(total + (BLOCK_ROWS - 1), jnp.int32(7))

    return lax.fori_loop(0, per_group, step, jnp.int32(LEAD * UNROLL))


def gather_blocks(counts_ref, me_ref, place_ref, owners, per_group, slot_rows, wide_ref, block_ref):
    def body(cluster, block, runs, end):
        for source, start, row in runs:
            block_ref[pl.ds(row, slot_rows), :] = wide_ref[source, pl.ds(start, slot_rows), :]
        block_ref[pl.ds(end, BLOCK_ROWS), :] = jnp.zeros((BLOCK_ROWS, LANES), F32)

    blocks = for_each_cluster(counts_ref, me_ref, place_ref, owners, per_group, body)
    spare = pl.ds(pl.multiple_of(blocks * BLOCK_ROWS, BLOCK_ROWS), GROUP_ROWS)
    block_ref[spare, :] = jnp.zeros((GROUP_ROWS, LANES), F32)
    return blocks


def for_each_group(blocks, stages):
    first, second, third = stages
    groups = lax.div(blocks + (UNROLL - 1), jnp.int32(UNROLL))

    def step(i, carry):
        for slot in range(2):
            group = LEAD + 2 * i + slot
            third(group - 2, slot)
            second(group - 1, 1 - slot)
            first(group, slot)
        return carry

    lax.fori_loop(0, lax.shift_right_logical(groups + 1, jnp.int32(1)), step, 0)


def block_rows(group, ahead):
    return pl.ds(pl.multiple_of((group * UNROLL + ahead) * BLOCK_ROWS, BLOCK_ROWS), BLOCK_ROWS)


def tile_rows(ahead):
    return slice(ahead * BLOCK_ROWS, (ahead + 1) * BLOCK_ROWS)


def value_grad_kernel(sizes, per_group, slot_rows, me_ref, *refs):
    owners = sizes[0] * sizes[1]
    mixed_refs, out_refs, rest = refs[:owners], refs[owners : owners + sizes[0]], refs[owners + sizes[0] :]
    dense_ref, counts_out_ref, counts_ref, place_ref, wide_ref, block_ref, home_ref = rest[:7]
    score_refs, probs_refs = rest[7:9], rest[9:11]
    half = out_refs[0].shape[1]
    rows = 2 * half
    for ahead, mixed_ref in zip(steps_of(sizes), mixed_refs):
        source = source_of(me_ref, ahead, sizes)
        tail = mixed_ref[rows:, :].astype(F32).astype(jnp.int32)
        counts_out_ref[pl.ds(source, 1), :] = tail[:1, :]
        wide_ref[source, :rows, :] = mixed_ref[:rows, :].astype(F32)
        wide_ref[source, rows:, :] = jnp.zeros((slot_rows, LANES), F32)
    pltpu.sync_copy(counts_out_ref, counts_ref)
    blocks = gather_blocks(counts_ref, me_ref, place_ref, owners, per_group, slot_rows, wide_ref, block_ref)

    def first(group, slot):
        for ahead in range(UNROLL):
            where = block_rows(group, ahead)
            mixed = block_ref[where, :].astype(BF16)
            dense_ref[where, :] = mixed
            score_refs[slot][tile_rows(ahead), :] = score(mixed)

    def second(group, slot):
        for ahead in range(UNROLL):
            tile = tile_rows(ahead)
            probs_refs[slot][tile, :] = softmax_turned(score_refs[slot][tile, :]).astype(BF16)

    def third(group, slot):
        for ahead in range(UNROLL):
            where = block_rows(group, ahead)
            block_ref[where, :] = dot(probs_refs[slot][tile_rows(ahead), :], dense_ref[where, :])

    for_each_group(blocks, (first, second, third))

    def scatter(cluster, block, runs, end):
        for source, start, row in runs:
            wide_ref[source, pl.ds(start, slot_rows), :] = block_ref[pl.ds(row, slot_rows), :]

    for_each_cluster(counts_ref, me_ref, place_ref, owners, per_group, scatter)
    for ahead, out_ref in enumerate(out_refs):
        for sub in range(sizes[1]):
            source = owner_of(me_ref, (ahead, 0), sizes) - me_ref[1] + sub
            up, down = wide_ref[source, :half, :], wide_ref[source, half:rows, :]
            out_ref[sub] = jnp.where(low_half((half, LANES)), swap_halves(up), down).astype(BF16)


def query_grad_kernel(sizes, per_group, slot_rows, me_ref, counts_ref, dense_ref, *refs):
    owners = sizes[0] * sizes[1]
    mid = owners + sizes[0]
    value_refs, out_refs, rest = refs[:owners], refs[owners:mid], refs[mid:]
    place_ref, wide_ref, block_ref, sums_ref, centroid_ref = rest[:5]
    score_refs, grad_probs_refs, both_refs = rest[5:7], rest[7:9], rest[9:11]
    half = value_refs[0].shape[0]
    rows = 2 * half
    for ahead, value_ref in zip(steps_of(sizes), value_refs):
        source = source_of(me_ref, ahead, sizes)
        value = value_ref[...].astype(F32)
        wide_ref[source, :half, :] = swap_halves(value)
        wide_ref[source, half:rows, :] = value
        wide_ref[source, rows:, :] = jnp.zeros((slot_rows, LANES), F32)
    blocks = gather_blocks(counts_ref, me_ref, place_ref, owners, per_group, slot_rows, wide_ref, block_ref)

    def first(group, slot):
        for ahead in range(UNROLL):
            where, tile = block_rows(group, ahead), tile_rows(ahead)
            mixed = dense_ref[where, :]
            value = block_ref[where, :].astype(BF16)
            cotan = jnp.where(low_half(mixed.shape), jnp.zeros_like(mixed), mixed)
            score_refs[slot][tile, :] = score(mixed)
            grad_probs_refs[slot][tile, :] = dot_nt(value, cotan)

    def second(group, slot):
        for ahead in range(UNROLL):
            tile = tile_rows(ahead)
            probs = softmax_turned(score_refs[slot][tile, :])
            grad_probs = grad_probs_refs[slot][tile, :]
            probs_half = probs.astype(BF16).astype(F32)
            row_dot = jnp.sum(probs_half * grad_probs, axis=0, keepdims=True)
            grad_scores = (probs * (grad_probs - row_dot)).astype(BF16).astype(F32)
            both_refs[slot][tile, :] = (grad_scores + grad_scores.T).astype(BF16)

    def third(group, slot):
        for ahead in range(UNROLL):
            where = block_rows(group, ahead)
            grad = dot(both_refs[slot][tile_rows(ahead), :], dense_ref[where, :]) * SCALE
            grad = grad.astype(BF16).astype(F32)
            block_ref[where, :] = grad
            sums_ref[pl.ds(group * UNROLL + ahead, 1), :] = jnp.sum(grad, axis=0, keepdims=True)

    for_each_group(blocks, (first, second, third))
    most = (owners * slot_rows + BLOCK_ROWS - 1) // BLOCK_ROWS

    def scatter(cluster, block, runs, end):
        total = jnp.zeros((1, LANES), F32)
        for ahead in range(most):
            here = block + ahead
            total = total + jnp.where(here * BLOCK_ROWS < end, sums_ref[pl.ds(here, 1), :], 0.0)
        centroid_ref[pl.ds(cluster, 1), :] = total
        for source, start, row in runs:
            wide_ref[source, pl.ds(start, slot_rows), :] = block_ref[pl.ds(row, slot_rows), :]

    for_each_cluster(counts_ref, me_ref, place_ref, owners, per_group, scatter)
    extra = out_refs[0].shape[1] - half
    centroid = jnp.where(
        low_half((extra, LANES)), centroid_ref[:extra, :], swap_halves(centroid_ref[extra:, :])
    ).astype(BF16)
    for ahead, out_ref in enumerate(out_refs):
        for sub in range(sizes[1]):
            source = owner_of(me_ref, (ahead, 0), sizes) - me_ref[1] + sub
            up, down = wide_ref[source, :half, :], wide_ref[source, half:rows, :]
            out_ref[sub, :half, :] = jnp.where(low_half((half, LANES)), up, swap_halves(down)).astype(BF16)
            out_ref[sub, half:, :] = centroid


def unfold(home_ref, out_ref, heads, start, half, finish):
    low = low_half((half, LANES))
    for group in range(home_ref.shape[0] // heads):
        first = group * 2 * half
        for pair in range(heads // 2):
            even = home_ref[group * heads + 2 * pair, start : start + half, :].astype(F32)
            odd = home_ref[group * heads + 2 * pair + 1, start : start + half, :].astype(F32)
            columns = slice(pair * LANES, (pair + 1) * LANES)
            out_ref[first : first + half, columns] = finish(jnp.where(low, even, swap_halves(odd)))
            out_ref[first + half : first + 2 * half, columns] = finish(
                jnp.where(low, swap_halves(even), odd)
            )


def to_half(x):
    return x.astype(BF16)


def bring_home(sizes, heads, pieces, home_ref, rows_ref):
    for source, piece in pieces:
        home_ref[source] = piece
    unfold(home_ref, rows_ref, heads, 0, rows_ref.shape[0] * heads // home_ref.shape[0] // 2, to_half)


def weight_partial(sizes, me_ref, turned_ref, rows_ref, sub_refs):
    piece = turned_ref.shape[0] // (sizes[0] * sizes[1])
    for ahead, sub_ref in enumerate(sub_refs):
        sub = lax.rem(me_ref[1] + ahead, jnp.int32(sizes[1]))
        first = [pl.multiple_of((seq * sizes[1] + sub) * piece, piece) for seq in range(sizes[0])]
        turned = jnp.concatenate([turned_ref[pl.ds(row, piece), :] for row in first], axis=0)
        partial = dot(turned, rows_ref[...]).astype(BF16)
        for seq in range(sizes[0]):
            sub_ref[seq] = partial[seq * piece : (seq + 1) * piece, :]


def input_columns(me_ref, ahead, parts, width):
    columns = width // parts
    dest = lax.rem(me_ref[2] + ahead, jnp.int32(parts))
    return pl.ds(pl.multiple_of(dest * columns, columns), columns)


def value_home_kernel(sizes, heads, parts, me_ref, turned_ref, weight_ref, *refs):
    came = sizes[0] + sizes[1] - 1
    part_refs, refs = refs[:came], refs[came:]
    rows_ref, term_refs, refs = refs[0], refs[1:parts], refs[parts:]
    sub_refs, home_ref = refs[: sizes[1]], refs[sizes[1]]
    bring_home(sizes, heads, arrivals(sizes, me_ref, part_refs), home_ref, rows_ref)
    for k, term_ref in enumerate(term_refs):
        mine = input_columns(me_ref, k + 1, parts, weight_ref.shape[0])
        term_ref[...] = dot_nt(rows_ref[...], weight_ref[mine, :])
    weight_partial(sizes, me_ref, turned_ref, rows_ref, sub_refs)


def query_home_kernel(sizes, heads, factor, parts, me_ref, weight_ref, *refs):
    term_refs, refs = refs[: parts - 1], refs[parts - 1 :]
    came = sizes[0] + sizes[1] - 1
    part_refs, refs = refs[:came], refs[came:]
    out_refs, (rows_ref, centroid_ref, home_ref) = refs[: parts - 1], refs[parts - 1 :]
    bring_home(sizes, heads, arrivals(sizes, me_ref, part_refs), home_ref, rows_ref)
    for k, (term_ref, out_ref) in enumerate(zip(term_refs, out_refs)):
        mine = input_columns(me_ref, k + 1, parts, weight_ref.shape[0])
        out_ref[...] = (dot_nt(rows_ref[...], weight_ref[mine, :]) + term_ref[...]).astype(BF16)
    half = rows_ref.shape[0] * heads // home_ref.shape[0] // 2
    unfold(home_ref, centroid_ref, heads, half, home_ref.shape[1] - half, lambda x: x * factor)


def query_weight_kernel(sizes, me_ref, turned_ref, rows_ref, *sub_refs):
    weight_partial(sizes, me_ref, turned_ref, rows_ref, sub_refs)


def input_own_kernel(parts, me_ref, rows_ref, value_rows_ref, w_query_ref, w_value_ref, out_ref):
    mine = input_columns(me_ref, 0, parts, w_query_ref.shape[0])
    total = dot_nt(rows_ref[...], w_query_ref[mine, :]) + dot_nt(value_rows_ref[...], w_value_ref[mine, :])
    out_ref[...] = total.astype(BF16)


def fold_subs_kernel(me_ref, *refs):
    seqs = refs[0].shape[0]
    terms, out_refs = refs[:-seqs], refs[-seqs:]
    for ahead, out_ref in enumerate(out_refs):
        seq = lax.rem(me_ref[0] + ahead, jnp.int32(seqs))
        total = terms[0][seq].astype(F32)
        for term in terms[1:]:
            total = total + term[seq].astype(F32)
        out_ref[...] = total.astype(BF16)


def sum_kernel(*refs):
    total = refs[0][...].astype(F32)
    for ref in refs[1:-1]:
        total = total + ref[...].astype(F32)
    refs[-1][...] = total.astype(refs[-1].dtype)


def input_sum_kernel(unsort_ref, weight_ref, *refs):
    part_refs, out_ref, weight_out_ref, total_ref = refs[:-3], refs[-3], refs[-2], refs[-1]
    total = part_refs[0][...].astype(F32)
    for part_ref in part_refs[1:]:
        total = total + part_ref[...].astype(F32)
    total_ref[...] = total.astype(BF16)
    out_ref[...] = dot(unsort_ref[...], total_ref[...]).astype(BF16)
    weight_out_ref[...] = weight_ref[...]


def call(kernel, outs, inputs, smem=(0,), in_place=(), after=(), scratch=(), flops=0, vmem=24, name=None):
    def body(*refs):
        kernel(*refs[: len(inputs)], *refs[len(inputs) + len(after) :])

    def space(i):
        return pltpu.SMEM if i in smem else pl.ANY if i in in_place else pltpu.VMEM

    specs = [pl.BlockSpec(memory_space=space(i)) for i in range(len(inputs))]
    specs += [pl.BlockSpec(memory_space=pl.ANY)] * len(after)
    moved = sum(x.size * x.dtype.itemsize for x in inputs) + sum(
        x.size * x.dtype.itemsize for x in jax.tree.leaves(outs)
    )
    return pl.pallas_call(
        body,
        out_shape=outs,
        in_specs=specs,
        out_specs=jax.tree.map(lambda _: pl.BlockSpec(memory_space=pltpu.VMEM), outs),
        scratch_shapes=list(scratch),
        compiler_params=pltpu.CompilerParams(vmem_limit_bytes=vmem * 2**20),
        cost_estimate=pl.CostEstimate(flops=flops, bytes_accessed=moved, transcendentals=0),
        name=name,
    )(*inputs, *after)


def exchange(parts, sizes):
    out = []
    for ahead, part in zip(steps_of(sizes), parts):
        moves = [
            (
                seq * sizes[1] + sub,
                (seq + ahead[0]) % sizes[0] * sizes[1] + (sub + ahead[1]) % sizes[1],
            )
            for seq, sub in steps_of(sizes)
        ]
        out.append(part if ahead == (0, 0) else lax.ppermute(part, OWNERS, moves))
    return out


def shift(part, axis, ahead):
    size = lax.axis_size(axis)
    return lax.ppermute(part, axis, [(i, (i + ahead) % size) for i in range(size)])


def pass_round(parts, axis):
    return [parts[0]] + [shift(parts[ahead], axis, ahead) for ahead in range(1, len(parts))]


def exchange_by_chip(me, parts, sizes, name, after=()):
    came = pass_round(parts, "seq")
    swapped = call(
        functools.partial(swap_kernel, sizes),
        (jax.ShapeDtypeStruct((sizes[0], *parts[0].shape[1:]), BF16),) * (sizes[1] - 1),
        (me, *came),
        after=after,
        name=name,
    )
    return came + [shift(part, "sub", k + 1) for k, part in enumerate(swapped)]


def fold_subs(me, by_sub, name):
    seqs, piece, columns = by_sub[0].shape
    return call(
        fold_subs_kernel,
        (jax.ShapeDtypeStruct((piece, columns), BF16),) * seqs,
        (me, *pass_round(by_sub, "sub")),
        name=name,
    )


def add_up(terms, dtype, name, after=()):
    out = jax.ShapeDtypeStruct(terms[0].shape, dtype)
    return call(sum_kernel, out, tuple(terms), smem=(), after=after, name=name)


def on_device(tokens_in, w_query, w_value, cotangent, assignment):
    sizes = (lax.axis_size("seq"), lax.axis_size("sub"))
    owners = sizes[0] * sizes[1]
    parts = lax.axis_size("head")
    toks, width = tokens_in.shape
    width_dev = cotangent.shape[1]
    heads = width_dev // HD
    slot_rows = 2 * toks // CLUSTERS
    assert owners % heads == 0 and heads % 2 == 0
    groups = owners // heads
    per_group = CLUSTERS // groups
    rows = toks if groups == 1 else per_group * slot_rows
    half = rows // 2
    slots = groups * rows
    columns = width // parts
    capacity = (slot_rows * owners + BLOCK_ROWS - 1) // BLOCK_ROWS * BLOCK_ROWS
    extra = max(per_group // 2, 16)
    shape = jax.ShapeDtypeStruct
    seq, sub = lax.axis_index("seq"), lax.axis_index("sub")
    first = lax.div(seq * sizes[1] + sub, jnp.int32(heads)) * per_group
    me = jnp.stack([seq, sub, lax.axis_index("head"), first]).astype(jnp.int32)

    def several(count, *dims):
        return (shape(dims, BF16),) * count

    assign_row = assignment.reshape(1, toks)
    *far_mixed, slot_row = call(
        functools.partial(project_far_kernel, sizes, groups, rows, heads),
        several(sizes[1], rows + COUNT_ROWS, LANES) + (shape((1, toks), jnp.int32),),
        (assign_row, tokens_in, w_query, cotangent),
        smem=(),
        in_place=(1, 2, 3),
        scratch=[
            pltpu.VMEM((toks, width), BF16),
            pltpu.VMEM((width, sizes[1] * HD), BF16),
            pltpu.VMEM((toks, sizes[1] * HD), BF16),
            pltpu.VMEM((toks, sizes[1] * LANES), BF16),
            pltpu.SemaphoreType.DMA((3, max(toks, width) // min(256, toks))),
        ],
        flops=2 * toks * width * sizes[1] * HD + 2 * rows * toks * sizes[1] * LANES,
        vmem=60,
        name="project_far",
    )
    own_mixed, *near_mixed = call(
        functools.partial(project_query_kernel, sizes, groups, rows),
        several(owners - sizes[1], rows + COUNT_ROWS, LANES),
        (me, slot_row, assign_row, tokens_in, w_query, cotangent),
        scratch=[pltpu.VMEM((toks, 2 * width_dev), BF16), pltpu.VMEM((owners, rows + COUNT_ROWS, LANES), BF16)],
        flops=2 * toks * width * width_dev + 4 * slots * toks * width_dev,
        name="project_query",
    )
    send_mixed = [own_mixed, *far_mixed, *near_mixed]
    got_mixed = exchange(send_mixed, sizes)
    *send_value, turned, unsort = call(
        functools.partial(project_value_kernel, sizes, groups, rows),
        several(owners, half, LANES) + several(1, width, slots) + several(1, toks, slots),
        (me, slot_row, tokens_in, w_value),
        after=near_mixed[:1],
        scratch=[pltpu.VMEM((toks, width_dev), BF16), pltpu.VMEM((owners, half, LANES), BF16)],
        flops=2 * toks * width * width_dev + 2 * slots * toks * width_dev,
        name="project_value",
    )
    behind = [0, *range(3, owners), 2, 1][:owners]
    send_value = [lax.optimization_barrier((part, got_mixed[k]))[0] for part, k in zip(send_value, behind)]
    got_value = exchange(send_value, sizes)
    blocks = per_group * capacity // BLOCK_ROWS
    held = blocks + (LEAD + 4) * UNROLL
    block_flops = 2 * BLOCK_ROWS * BLOCK_ROWS * LANES
    tall = pltpu.VMEM((owners, rows + slot_rows, LANES), F32)
    dense_rows = pltpu.VMEM((held * BLOCK_ROWS, LANES), F32)
    group_f32 = pltpu.VMEM((GROUP_ROWS, BLOCK_ROWS), F32)
    group_b16 = pltpu.VMEM((GROUP_ROWS, BLOCK_ROWS), BF16)
    place = pltpu.SMEM((owners,), jnp.int32)
    *back_value, dense, counts = call(
        functools.partial(value_grad_kernel, sizes, per_group, slot_rows),
        several(sizes[0], sizes[1], half, LANES)
        + several(1, held * BLOCK_ROWS, LANES)
        + (shape((owners, LANES), jnp.int32),),
        (me, *got_mixed),
        after=[unsort],
        scratch=[pltpu.SMEM((owners, LANES), jnp.int32), place, tall, dense_rows, tall]
        + [group_f32] * 2
        + [group_b16] * 2,
        flops=4 * blocks * block_flops,
        vmem=48,
        name="value_grad",
    )
    back_value, _ = lax.optimization_barrier((back_value, got_value[1:]))
    back_query = call(
        functools.partial(query_grad_kernel, sizes, per_group, slot_rows),
        several(sizes[0], sizes[1], half + extra, LANES),
        (me, counts, dense, *got_value),
        smem=(0, 1),
        scratch=[place, tall, dense_rows, pltpu.VMEM((held, LANES), F32), pltpu.VMEM((2 * extra, LANES), F32)]
        + [group_f32] * 4
        + [group_b16] * 2,
        flops=6 * blocks * block_flops,
        vmem=48,
        name="query_grad",
    )
    home_query = exchange_by_chip(me, back_query, sizes, "swap_query")
    home_value = exchange_by_chip(me, back_value, sizes, "swap_value", back_query[:1])
    weight_flops = 2 * slots * width * width_dev
    home_flops = weight_flops // parts * (parts - 1)
    piece = width // owners
    sub_shapes = several(sizes[1], sizes[0], piece, width_dev)
    value_rows, *refs = call(
        functools.partial(value_home_kernel, sizes, heads, parts),
        several(1, slots, width_dev) + (shape((slots, columns), F32),) * (parts - 1) + sub_shapes,
        (me, turned, w_value, *home_value),
        scratch=[pltpu.VMEM((owners, half, LANES), BF16)],
        flops=weight_flops + home_flops,
        name="value_home",
    )
    value_terms, value_weight = refs[: parts - 1], refs[parts - 1 :]
    value_weight = fold_subs(me, value_weight, "value_subs")
    *partials, query_rows, centroid_grad = call(
        functools.partial(query_home_kernel, sizes, heads, (CLUSTERS / (toks * owners)) ** 0.5, parts),
        several(parts - 1, slots, columns)
        + several(1, slots, width_dev)
        + (shape((groups * 2 * extra, width_dev), F32),),
        (me, w_query, *value_terms, *home_query),
        scratch=[pltpu.VMEM((owners, half + extra, LANES), BF16)],
        flops=home_flops,
        name="query_home",
    )
    arrived = [shift(partial, "head", k + 1) for k, partial in enumerate(partials)]
    value_weight, _ = lax.optimization_barrier((value_weight, home_query))
    value_weight = pass_round(value_weight, "seq")
    query_weight = call(
        functools.partial(query_weight_kernel, sizes),
        sub_shapes,
        (me, turned, query_rows),
        flops=weight_flops,
        name="query_weight",
    )
    query_weight = fold_subs(me, query_weight, "query_subs")
    own = call(
        functools.partial(input_own_kernel, parts),
        shape((slots, columns), BF16),
        (me, query_rows, value_rows, w_query, w_value),
        after=query_weight[:1],
        flops=weight_flops * 2 // parts,
        name="input_own",
    )
    query_weight = pass_round(query_weight, "seq")
    grad_wv = add_up(value_weight, F32, "value_sum", [own])
    grad_input, own_weight = call(
        input_sum_kernel,
        several(1, toks, columns) + several(1, piece, width_dev),
        (unsort, query_weight[0], own, *arrived),
        smem=(),
        scratch=[pltpu.VMEM((slots, columns), BF16)],
        flops=2 * toks * slots * columns,
        name="input_sum",
    )
    grad_wq = add_up([own_weight, *query_weight[1:]], F32, "query_sum")
    if groups > 1:
        centroid_grad = centroid_grad.reshape(groups, 2 * extra, width_dev)[:, :per_group]
        centroid_grad = centroid_grad.reshape(CLUSTERS, width_dev)
    return (grad_input, grad_wq, grad_wv, centroid_grad)


def solution(mesh):
    return jax.shard_map(
        on_device,
        mesh=mesh,
        in_specs=(
            P(("grp", "seq", "sub"), None),
            P(None, "head"),
            P(None, "head"),
            P(("grp", "seq", "sub"), "head"),
            P(("grp", "seq", "sub"), None),
        ),
        out_specs=(
            P(("grp", "seq", "sub"), "head"),
            P(("grp", "seq", "sub"), "head"),
            P(("grp", "seq", "sub"), "head"),
            P("grp", "head"),
        ),
        check_vma=False,
    )
```

```python
import functools

import jax
import jax.numpy as jnp
from jax import lax
from jax.experimental import pallas as pl
from jax.experimental.pallas import tpu as pltpu
from jax.sharding import PartitionSpec as P

HD = 64
CLUSTERS = 64
BLOCK_ROWS = 128
LANES = 128
UNROLL = 4
COUNT_ROWS = 16
SCALE = 0.5 * HD ** (-0.5)
F32 = jnp.float32
BF16 = jnp.bfloat16
OWNERS = ("seq", "sub")
GROUP_ROWS = UNROLL * BLOCK_ROWS
LEAD = 2


def iota(shape, dim):
    return lax.broadcasted_iota(jnp.int32, shape, dim)


def low_half(shape):
    return iota(shape, 1) < HD


def swap_halves(tile):
    return pltpu.roll(tile, HD, 1)


def dot(a, b):
    return jnp.dot(a, b, preferred_element_type=F32)


def dot_nt(a, b):
    return lax.dot_general(a, b, (((1,), (1,)), ((), ())), preferred_element_type=F32)


def ones_where(condition):
    return jnp.where(condition, 1.0, 0.0).astype(BF16)


def owner_of(me_ref, ahead, sizes):
    seq = lax.rem(me_ref[0] + ahead[0], jnp.int32(sizes[0]))
    sub = lax.rem(me_ref[1] + ahead[1], jnp.int32(sizes[1]))
    return seq * sizes[1] + sub


def source_of(me_ref, ahead, sizes):
    return owner_of(me_ref, ((sizes[0] - ahead[0]) % sizes[0], (sizes[1] - ahead[1]) % sizes[1]), sizes)


def steps_of(sizes):
    far = sorted(range(1, sizes[0]), key=lambda seq: -min(seq, sizes[0] - seq))
    subs = range(sizes[1])
    return [(0, 0)] + [(seq, sub) for seq in far for sub in subs] + [(0, sub) for sub in subs if sub]


def hand_out(by_owner_ref, out_refs, me_ref, sizes):
    for ahead, out_ref in zip(steps_of(sizes), out_refs):
        out_ref[...] = by_owner_ref[owner_of(me_ref, ahead, sizes)]


def slots_of(assign, groups, rows):
    toks = assign.shape[1]
    per_group = CLUSTERS // groups
    member = jnp.where(iota((CLUSTERS, toks), 0) == assign, 1.0, 0.0)
    member_b = member.astype(BF16)
    upto = ones_where(iota((LANES, LANES), 0) <= iota((LANES, LANES), 1))
    counts = jnp.zeros((CLUSTERS, 1), F32)
    running = []
    for first in range(0, toks, LANES):
        within = dot(member_b[:, first : first + LANES], upto)
        running.append(within + counts)
        counts = counts + within[:, LANES - 1 :]
    running = jnp.concatenate(running, axis=1)
    here, other = iota((CLUSTERS, CLUSTERS), 0), iota((CLUSTERS, CLUSTERS), 1)
    group_of = lambda index: lax.div(index, jnp.int32(per_group))
    earlier = ones_where((other < here) & (group_of(other) == group_of(here)))
    base = dot(earlier, jnp.broadcast_to(counts, (CLUSTERS, LANES)).astype(BF16))[:, :1]
    base = base + (group_of(iota((CLUSTERS, 1), 0)) * rows).astype(F32)
    slot = jnp.sum(member * (running - 1.0 + base), axis=0, keepdims=True).astype(jnp.int32)
    spread = jnp.concatenate([member_b, jnp.zeros((LANES - CLUSTERS, toks), BF16)], axis=0)
    return slot, dot_nt(jnp.ones((COUNT_ROWS, toks), BF16), spread).astype(BF16)


def arrivals(sizes, me_ref, refs):
    seqs, subs = sizes
    for ahead in steps_of(sizes):
        if ahead[1] == 0:
            piece = refs[ahead[0]][me_ref[1]]
        else:
            piece = refs[seqs + ahead[1] - 1][ahead[0]]
        yield source_of(me_ref, ahead, sizes), piece


def swap_kernel(sizes, me_ref, *refs):
    for k, out_ref in enumerate(refs[sizes[0] :]):
        sub = lax.rem(me_ref[1] + (k + 1), jnp.int32(sizes[1]))
        for seq in range(sizes[0]):
            out_ref[seq] = refs[seq][sub]


def beside(query, cotan):
    low = low_half(query.shape)
    even = jnp.where(low, query, swap_halves(cotan)).astype(BF16)
    return even, jnp.where(low, swap_halves(query), cotan).astype(BF16)


def load_rows(source, target, sems, fine):
    return [
        pltpu.make_async_copy(source.at[pl.ds(row, fine), :], target.at[pl.ds(row, fine), :], sems.at[row // fine])
        for row in range(0, target.shape[0], fine)
    ]


def project_far_kernel(sizes, groups, rows, heads, assign_ref, tokens_hbm, weight_hbm, cotan_hbm, *refs):
    out_refs, refs = refs[: sizes[1]], refs[sizes[1] :]
    slot_ref, tokens_ref, weight_ref, cotan_ref, mixed_ref, sems = refs
    toks = tokens_ref.shape[0]
    fine = min(256, toks)
    me = (lax.axis_index("seq"), lax.axis_index("sub"))
    owner = owner_of(me, steps_of(sizes)[1], sizes) - me[1]
    group, head = lax.div(owner, jnp.int32(heads)), lax.rem(owner, jnp.int32(heads))
    columns = pl.ds(pl.multiple_of(head * HD, LANES), sizes[1] * HD)
    loads = [
        load_rows(source, target, sems.at[kind], fine)
        for kind, (source, target) in enumerate(
            ((weight_hbm.at[:, columns], weight_ref), (tokens_hbm, tokens_ref), (cotan_hbm.at[:, columns], cotan_ref))
        )
    ]
    for load in loads:
        for copy in load:
            copy.start()
    slot, tallies = slots_of(assign_ref[...], groups, rows)
    slot_ref[...] = slot
    pick = ones_where(iota((rows, toks), 0) + group * rows == slot)
    for copy in loads[0] + loads[2]:
        copy.wait()
    step = fine
    for first in range(0, toks, step):
        for copy in loads[1][first // fine : (first + step) // fine]:
            copy.wait()
        where = slice(first, first + step)
        query, cotan = dot(tokens_ref[where, :], weight_ref[...]), cotan_ref[where, :].astype(F32)
        for pair in range(sizes[1] // 2):
            pair_columns = slice(pair * LANES, (pair + 1) * LANES)
            even, odd = beside(query[:, pair_columns], cotan[:, pair_columns])
            mixed_ref[where, 2 * pair * LANES : (2 * pair + 1) * LANES] = even
            mixed_ref[where, (2 * pair + 1) * LANES : (2 * pair + 2) * LANES] = odd
    part = min(256, rows)
    for first in range(0, rows, part):
        where = slice(first, first + part)
        in_order = dot(pick[where, :], mixed_ref[...]).astype(BF16)
        for ahead, out_ref in enumerate(out_refs):
            sub = lax.rem(me[1] + ahead, jnp.int32(sizes[1]))
            piece = in_order[:, :LANES]
            for other in range(1, sizes[1]):
                piece = jnp.where(sub == other, in_order[:, other * LANES : (other + 1) * LANES], piece)
            out_ref[where, :] = piece
    for out_ref in out_refs:
        out_ref[rows:, :] = tallies


def project_query_kernel(sizes, groups, rows, me_ref, slot_ref, assign_ref, tokens_ref, weight_ref, cotan_ref, *rest):
    out_refs, (mixed_ref, sorted_ref) = rest[:-2], rest[-2:]
    toks = tokens_ref.shape[0]
    heads = weight_ref.shape[1] // HD
    step = min(512, toks)
    for first in range(0, toks, step):
        where = slice(first, first + step)
        query, cotan = dot(tokens_ref[where, :], weight_ref[...]), cotan_ref[where, :].astype(F32)
        for pair in range(heads // 2):
            columns = slice(pair * LANES, (pair + 1) * LANES)
            even, odd = beside(query[:, columns], cotan[:, columns])
            mixed_ref[where, 2 * pair * LANES : (2 * pair + 1) * LANES] = even
            mixed_ref[where, (2 * pair + 1) * LANES : (2 * pair + 2) * LANES] = odd
    part = min(512, rows)
    pieces = rows // part

    @pl.loop(0, groups * pieces)
    def _(i):
        group, piece = lax.div(i, jnp.int32(pieces)), lax.rem(i, jnp.int32(pieces))
        first = pl.multiple_of(piece * part, part)
        pick = ones_where(iota((part, toks), 0) + i * part == slot_ref[...])
        sorted_rows = dot(pick, mixed_ref[...]).astype(BF16)
        for head in range(heads):
            sorted_ref[group * heads + head, pl.ds(first, part), :] = sorted_rows[
                :, head * LANES : (head + 1) * LANES
            ]

    member = jnp.where(iota((LANES, toks), 0) == assign_ref[...], 1.0, 0.0).astype(BF16)
    tallies = dot_nt(jnp.ones((COUNT_ROWS, toks), BF16), member).astype(BF16)
    for owner in range(sorted_ref.shape[0]):
        sorted_ref[owner, rows:, :] = tallies
    steps = steps_of(sizes)
    for ahead, out_ref in zip(steps[:1] + steps[1 + sizes[1] :], out_refs):
        out_ref[...] = sorted_ref[owner_of(me_ref, ahead, sizes)]


def project_value_kernel(sizes, groups, rows, me_ref, slot_ref, tokens_ref, weight_ref, *rest):
    out_refs, (turned_ref, unsort_ref, value_ref, sorted_ref) = rest[:-4], rest[-4:]
    toks = tokens_ref.shape[0]
    heads = weight_ref.shape[1] // HD
    step = min(512, toks)

    @pl.loop(0, toks // step)
    def _(i):
        where = pl.ds(pl.multiple_of(i * step, step), step)
        value_ref[where, :] = dot(tokens_ref[where, :], weight_ref[...]).astype(BF16)

    half = rows // 2
    part = min(256, half)
    pieces = half // part

    @pl.loop(0, groups * pieces)
    def _(i):
        group, piece = lax.div(i, jnp.int32(pieces)), lax.rem(i, jnp.int32(pieces))
        first = pl.multiple_of(piece * part, part)
        index = iota((part, toks), 0) + group * rows + first
        upper = dot(ones_where(index == slot_ref[...]), value_ref[...])
        lower = dot(ones_where(index + half == slot_ref[...]), value_ref[...])
        low = low_half((part, LANES))
        for pair in range(heads // 2):
            up = upper[:, pair * LANES : (pair + 1) * LANES]
            down = lower[:, pair * LANES : (pair + 1) * LANES]
            even = jnp.where(low, up, swap_halves(down)).astype(BF16)
            odd = jnp.where(low, swap_halves(up), down).astype(BF16)
            sorted_ref[group * heads + 2 * pair, pl.ds(first, part), :] = even
            sorted_ref[group * heads + 2 * pair + 1, pl.ds(first, part), :] = odd

    hand_out(sorted_ref, out_refs, me_ref, sizes)
    turned = tokens_ref[...].T
    slots = unsort_ref.shape[1]
    part = min(256, slots)
    for i in range(slots // part):
        pick = ones_where(iota((part, toks), 0) + i * part == slot_ref[...])
        unsort_ref[:, i * part : (i + 1) * part] = pick.T
        turned_ref[:, i * part : (i + 1) * part] = dot_nt(turned, pick).astype(BF16)


def score(mixed):
    query = jnp.where(low_half(mixed.shape), mixed.astype(F32) * SCALE, 0.0).astype(BF16)
    return dot_nt(query, mixed)


def softmax_turned(scores):
    shape = scores.shape
    seen = iota(shape, 0) <= iota(shape, 1)
    scores = jnp.where(seen, scores, -jnp.inf)
    raised = jnp.exp(scores - jnp.max(scores, axis=0, keepdims=True))
    return raised * (1.0 / jnp.sum(raised, axis=0, keepdims=True))


def for_each_cluster(counts_ref, me_ref, place_ref, owners, per_group, body):
    for source in range(owners):
        place_ref[source] = 0

    def step(cluster, block):
        runs = []
        total = 0
        base = block * BLOCK_ROWS
        for source in range(owners):
            count = counts_ref[source, me_ref[3] + cluster]
            start = place_ref[source]
            runs.append((source, start, base + total))
            place_ref[source] = start + count
            total = total + count
        body(cluster, block, runs, base + total)
        return block + lax.shift_right_logical(total + (BLOCK_ROWS - 1), jnp.int32(7))

    return lax.fori_loop(0, per_group, step, jnp.int32(LEAD * UNROLL))


def gather_blocks(counts_ref, me_ref, place_ref, owners, per_group, slot_rows, wide_ref, block_ref):
    def body(cluster, block, runs, end):
        for source, start, row in runs:
            block_ref[pl.ds(row, slot_rows), :] = wide_ref[source, pl.ds(start, slot_rows), :]
        block_ref[pl.ds(end, BLOCK_ROWS), :] = jnp.zeros((BLOCK_ROWS, LANES), F32)

    blocks = for_each_cluster(counts_ref, me_ref, place_ref, owners, per_group, body)
    spare = pl.ds(pl.multiple_of(blocks * BLOCK_ROWS, BLOCK_ROWS), GROUP_ROWS)
    block_ref[spare, :] = jnp.zeros((GROUP_ROWS, LANES), F32)
    return blocks


def for_each_group(blocks, stages):
    first, second, third = stages
    groups = lax.div(blocks + (UNROLL - 1), jnp.int32(UNROLL))

    def step(i, carry):
        for slot in range(2):
            group = LEAD + 2 * i + slot
            third(group - 2, slot)
            second(group - 1, 1 - slot)
            first(group, slot)
        return carry

    lax.fori_loop(0, lax.shift_right_logical(groups + 1, jnp.int32(1)), step, 0)


def block_rows(group, ahead):
    return pl.ds(pl.multiple_of((group * UNROLL + ahead) * BLOCK_ROWS, BLOCK_ROWS), BLOCK_ROWS)


def tile_rows(ahead):
    return slice(ahead * BLOCK_ROWS, (ahead + 1) * BLOCK_ROWS)


def value_grad_kernel(sizes, per_group, slot_rows, me_ref, *refs):
    owners = sizes[0] * sizes[1]
    mixed_refs, out_refs, rest = refs[:owners], refs[owners : owners + sizes[0]], refs[owners + sizes[0] :]
    dense_ref, counts_out_ref, counts_ref, place_ref, wide_ref, block_ref, home_ref = rest[:7]
    score_refs, probs_refs = rest[7:9], rest[9:11]
    half = out_refs[0].shape[1]
    rows = 2 * half
    for ahead, mixed_ref in zip(steps_of(sizes), mixed_refs):
        source = source_of(me_ref, ahead, sizes)
        tail = mixed_ref[rows:, :].astype(F32).astype(jnp.int32)
        counts_out_ref[pl.ds(source, 1), :] = tail[:1, :]
        wide_ref[source, :rows, :] = mixed_ref[:rows, :].astype(F32)
        wide_ref[source, rows:, :] = jnp.zeros((slot_rows, LANES), F32)
    pltpu.sync_copy(counts_out_ref, counts_ref)
    blocks = gather_blocks(counts_ref, me_ref, place_ref, owners, per_group, slot_rows, wide_ref, block_ref)

    def first(group, slot):
        for ahead in range(UNROLL):
            where = block_rows(group, ahead)
            mixed = block_ref[where, :].astype(BF16)
            dense_ref[where, :] = mixed
            score_refs[slot][tile_rows(ahead), :] = score(mixed)

    def second(group, slot):
        for ahead in range(UNROLL):
            tile = tile_rows(ahead)
            probs_refs[slot][tile, :] = softmax_turned(score_refs[slot][tile, :]).astype(BF16)

    def third(group, slot):
        for ahead in range(UNROLL):
            where = block_rows(group, ahead)
            block_ref[where, :] = dot(probs_refs[slot][tile_rows(ahead), :], dense_ref[where, :])

    for_each_group(blocks, (first, second, third))

    def scatter(cluster, block, runs, end):
        for source, start, row in runs:
            wide_ref[source, pl.ds(start, slot_rows), :] = block_ref[pl.ds(row, slot_rows), :]

    for_each_cluster(counts_ref, me_ref, place_ref, owners, per_group, scatter)
    for ahead, out_ref in enumerate(out_refs):
        for sub in range(sizes[1]):
            source = owner_of(me_ref, (ahead, 0), sizes) - me_ref[1] + sub
            up, down = wide_ref[source, :half, :], wide_ref[source, half:rows, :]
            out_ref[sub] = jnp.where(low_half((half, LANES)), swap_halves(up), down).astype(BF16)


def query_grad_kernel(sizes, per_group, slot_rows, me_ref, counts_ref, dense_ref, *refs):
    owners = sizes[0] * sizes[1]
    mid = owners + sizes[0]
    value_refs, out_refs, rest = refs[:owners], refs[owners:mid], refs[mid:]
    place_ref, wide_ref, block_ref, sums_ref, centroid_ref = rest[:5]
    score_refs, grad_probs_refs, both_refs = rest[5:7], rest[7:9], rest[9:11]
    half = value_refs[0].shape[0]
    rows = 2 * half
    for ahead, value_ref in zip(steps_of(sizes), value_refs):
        source = source_of(me_ref, ahead, sizes)
        value = value_ref[...].astype(F32)
        wide_ref[source, :half, :] = swap_halves(value)
        wide_ref[source, half:rows, :] = value
        wide_ref[source, rows:, :] = jnp.zeros((slot_rows, LANES), F32)
    blocks = gather_blocks(counts_ref, me_ref, place_ref, owners, per_group, slot_rows, wide_ref, block_ref)

    def first(group, slot):
        for ahead in range(UNROLL):
            where, tile = block_rows(group, ahead), tile_rows(ahead)
            mixed = dense_ref[where, :]
            value = block_ref[where, :].astype(BF16)
            cotan = jnp.where(low_half(mixed.shape), jnp.zeros_like(mixed), mixed)
            score_refs[slot][tile, :] = score(mixed)
            grad_probs_refs[slot][tile, :] = dot_nt(value, cotan)

    def second(group, slot):
        for ahead in range(UNROLL):
            tile = tile_rows(ahead)
            probs = softmax_turned(score_refs[slot][tile, :])
            grad_probs = grad_probs_refs[slot][tile, :]
            probs_half = probs.astype(BF16).astype(F32)
            row_dot = jnp.sum(probs_half * grad_probs, axis=0, keepdims=True)
            grad_scores = (probs * (grad_probs - row_dot)).astype(BF16).astype(F32)
            both_refs[slot][tile, :] = (grad_scores + grad_scores.T).astype(BF16)

    def third(group, slot):
        for ahead in range(UNROLL):
            where = block_rows(group, ahead)
            grad = dot(both_refs[slot][tile_rows(ahead), :], dense_ref[where, :]) * SCALE
            grad = grad.astype(BF16).astype(F32)
            block_ref[where, :] = grad
            sums_ref[pl.ds(group * UNROLL + ahead, 1), :] = jnp.sum(grad, axis=0, keepdims=True)

    for_each_group(blocks, (first, second, third))
    most = (owners * slot_rows + BLOCK_ROWS - 1) // BLOCK_ROWS

    def scatter(cluster, block, runs, end):
        total = jnp.zeros((1, LANES), F32)
        for ahead in range(most):
            here = block + ahead
            total = total + jnp.where(here * BLOCK_ROWS < end, sums_ref[pl.ds(here, 1), :], 0.0)
        centroid_ref[pl.ds(cluster, 1), :] = total
        for source, start, row in runs:
            wide_ref[source, pl.ds(start, slot_rows), :] = block_ref[pl.ds(row, slot_rows), :]

    for_each_cluster(counts_ref, me_ref, place_ref, owners, per_group, scatter)
    extra = out_refs[0].shape[1] - half
    centroid = jnp.where(
        low_half((extra, LANES)), centroid_ref[:extra, :], swap_halves(centroid_ref[extra:, :])
    ).astype(BF16)
    for ahead, out_ref in enumerate(out_refs):
        for sub in range(sizes[1]):
            source = owner_of(me_ref, (ahead, 0), sizes) - me_ref[1] + sub
            up, down = wide_ref[source, :half, :], wide_ref[source, half:rows, :]
            out_ref[sub, :half, :] = jnp.where(low_half((half, LANES)), up, swap_halves(down)).astype(BF16)
            out_ref[sub, half:, :] = centroid


def unfold(home_ref, out_ref, heads, start, half, finish):
    low = low_half((half, LANES))
    for group in range(home_ref.shape[0] // heads):
        first = group * 2 * half
        for pair in range(heads // 2):
            even = home_ref[group * heads + 2 * pair, start : start + half, :].astype(F32)
            odd = home_ref[group * heads + 2 * pair + 1, start : start + half, :].astype(F32)
            columns = slice(pair * LANES, (pair + 1) * LANES)
            out_ref[first : first + half, columns] = finish(jnp.where(low, even, swap_halves(odd)))
            out_ref[first + half : first + 2 * half, columns] = finish(
                jnp.where(low, swap_halves(even), odd)
            )


def to_half(x):
    return x.astype(BF16)


def bring_home(sizes, heads, pieces, home_ref, rows_ref):
    for source, piece in pieces:
        home_ref[source] = piece
    unfold(home_ref, rows_ref, heads, 0, rows_ref.shape[0] * heads // home_ref.shape[0] // 2, to_half)


def weight_partial(sizes, me_ref, turned_ref, rows_ref, sub_refs):
    piece = turned_ref.shape[0] // (sizes[0] * sizes[1])
    for ahead, sub_ref in enumerate(sub_refs):
        sub = lax.rem(me_ref[1] + ahead, jnp.int32(sizes[1]))
        first = [pl.multiple_of((seq * sizes[1] + sub) * piece, piece) for seq in range(sizes[0])]
        turned = jnp.concatenate([turned_ref[pl.ds(row, piece), :] for row in first], axis=0)
        partial = dot(turned, rows_ref[...]).astype(BF16)
        for seq in range(sizes[0]):
            sub_ref[seq] = partial[seq * piece : (seq + 1) * piece, :]


def input_columns(me_ref, ahead, parts, width):
    columns = width // parts
    dest = lax.rem(me_ref[2] + ahead, jnp.int32(parts))
    return pl.ds(pl.multiple_of(dest * columns, columns), columns)


def value_home_kernel(sizes, heads, parts, me_ref, turned_ref, weight_ref, *refs):
    came = sizes[0] + sizes[1] - 1
    part_refs, refs = refs[:came], refs[came:]
    rows_ref, term_refs, refs = refs[0], refs[1:parts], refs[parts:]
    sub_refs, home_ref = refs[: sizes[1]], refs[sizes[1]]
    bring_home(sizes, heads, arrivals(sizes, me_ref, part_refs), home_ref, rows_ref)
    for k, term_ref in enumerate(term_refs):
        mine = input_columns(me_ref, k + 1, parts, weight_ref.shape[0])
        term_ref[...] = dot_nt(rows_ref[...], weight_ref[mine, :])
    weight_partial(sizes, me_ref, turned_ref, rows_ref, sub_refs)


def query_home_kernel(sizes, heads, factor, parts, me_ref, weight_ref, *refs):
    term_refs, refs = refs[: parts - 1], refs[parts - 1 :]
    came = sizes[0] + sizes[1] - 1
    part_refs, refs = refs[:came], refs[came:]
    out_refs, (rows_ref, centroid_ref, home_ref) = refs[: parts - 1], refs[parts - 1 :]
    bring_home(sizes, heads, arrivals(sizes, me_ref, part_refs), home_ref, rows_ref)
    for k, (term_ref, out_ref) in enumerate(zip(term_refs, out_refs)):
        mine = input_columns(me_ref, k + 1, parts, weight_ref.shape[0])
        step = min(256, rows_ref.shape[0])
        for first in range(0, rows_ref.shape[0], step):
            where = slice(first, first + step)
            out_ref[where, :] = (dot_nt(rows_ref[where, :], weight_ref[mine, :]) + term_ref[where, :]).astype(BF16)
    half = rows_ref.shape[0] * heads // home_ref.shape[0] // 2
    unfold(home_ref, centroid_ref, heads, half, home_ref.shape[1] - half, lambda x: x * factor)


def query_weight_kernel(sizes, me_ref, turned_ref, rows_ref, *sub_refs):
    weight_partial(sizes, me_ref, turned_ref, rows_ref, sub_refs)


def input_own_kernel(parts, me_ref, rows_ref, value_rows_ref, w_query_ref, w_value_ref, out_ref):
    mine = input_columns(me_ref, 0, parts, w_query_ref.shape[0])
    total = dot_nt(rows_ref[...], w_query_ref[mine, :]) + dot_nt(value_rows_ref[...], w_value_ref[mine, :])
    out_ref[...] = total.astype(BF16)


def fold_subs_kernel(me_ref, *refs):
    seqs = refs[0].shape[0]
    terms, out_refs = refs[:-seqs], refs[-seqs:]
    for ahead, out_ref in enumerate(out_refs):
        seq = lax.rem(me_ref[0] + ahead, jnp.int32(seqs))
        total = terms[0][seq].astype(F32)
        for term in terms[1:]:
            total = total + term[seq].astype(F32)
        out_ref[...] = total.astype(BF16)


def sum_kernel(*refs):
    total = refs[0][...].astype(F32)
    for ref in refs[1:-1]:
        total = total + ref[...].astype(F32)
    refs[-1][...] = total.astype(refs[-1].dtype)


def input_sum_kernel(unsort_ref, weight_ref, *refs):
    part_refs, out_ref, weight_out_ref, total_ref = refs[:-3], refs[-3], refs[-2], refs[-1]
    total = part_refs[0][...].astype(F32)
    for part_ref in part_refs[1:]:
        total = total + part_ref[...].astype(F32)
    total_ref[...] = total.astype(BF16)
    step = min(256, out_ref.shape[0])
    for first in range(0, out_ref.shape[0], step):
        where = slice(first, first + step)
        out_ref[where, :] = dot(unsort_ref[where, :], total_ref[...]).astype(BF16)
    weight_out_ref[...] = weight_ref[...]


def call(kernel, outs, inputs, smem=(0,), in_place=(), after=(), scratch=(), flops=0, vmem=24, name=None):
    def body(*refs):
        kernel(*refs[: len(inputs)], *refs[len(inputs) + len(after) :])

    def space(i):
        return pltpu.SMEM if i in smem else pl.ANY if i in in_place else pltpu.VMEM

    specs = [pl.BlockSpec(memory_space=space(i)) for i in range(len(inputs))]
    specs += [pl.BlockSpec(memory_space=pl.ANY)] * len(after)
    moved = sum(x.size * x.dtype.itemsize for x in inputs) + sum(
        x.size * x.dtype.itemsize for x in jax.tree.leaves(outs)
    )
    return pl.pallas_call(
        body,
        out_shape=outs,
        in_specs=specs,
        out_specs=jax.tree.map(lambda _: pl.BlockSpec(memory_space=pltpu.VMEM), outs),
        scratch_shapes=list(scratch),
        compiler_params=pltpu.CompilerParams(vmem_limit_bytes=vmem * 2**20),
        cost_estimate=pl.CostEstimate(flops=flops, bytes_accessed=moved, transcendentals=0),
        name=name,
    )(*inputs, *after)


def exchange(parts, sizes):
    out = []
    for ahead, part in zip(steps_of(sizes), parts):
        moves = [
            (
                seq * sizes[1] + sub,
                (seq + ahead[0]) % sizes[0] * sizes[1] + (sub + ahead[1]) % sizes[1],
            )
            for seq, sub in steps_of(sizes)
        ]
        out.append(part if ahead == (0, 0) else lax.ppermute(part, OWNERS, moves))
    return out


def shift(part, axis, ahead):
    size = lax.axis_size(axis)
    return lax.ppermute(part, axis, [(i, (i + ahead) % size) for i in range(size)])


def pass_round(parts, axis):
    return [parts[0]] + [shift(parts[ahead], axis, ahead) for ahead in range(1, len(parts))]


def exchange_by_chip(me, parts, sizes, name, after=()):
    came = pass_round(parts, "seq")
    swapped = call(
        functools.partial(swap_kernel, sizes),
        (jax.ShapeDtypeStruct((sizes[0], *parts[0].shape[1:]), BF16),) * (sizes[1] - 1),
        (me, *came),
        after=after,
        name=name,
    )
    return came + [shift(part, "sub", k + 1) for k, part in enumerate(swapped)]


def fold_subs(me, by_sub, name):
    seqs, piece, columns = by_sub[0].shape
    return call(
        fold_subs_kernel,
        (jax.ShapeDtypeStruct((piece, columns), BF16),) * seqs,
        (me, *pass_round(by_sub, "sub")),
        name=name,
    )


def add_up(terms, dtype, name, after=()):
    out = jax.ShapeDtypeStruct(terms[0].shape, dtype)
    return call(sum_kernel, out, tuple(terms), smem=(), after=after, name=name)


def on_device(tokens_in, w_query, w_value, cotangent, assignment):
    sizes = (lax.axis_size("seq"), lax.axis_size("sub"))
    owners = sizes[0] * sizes[1]
    parts = lax.axis_size("head")
    toks, width = tokens_in.shape
    width_dev = cotangent.shape[1]
    heads = width_dev // HD
    slot_rows = 2 * toks // CLUSTERS
    assert owners % heads == 0 and heads % 2 == 0
    groups = owners // heads
    per_group = CLUSTERS // groups
    rows = toks if groups == 1 else per_group * slot_rows
    half = rows // 2
    slots = groups * rows
    columns = width // parts
    capacity = (slot_rows * owners + BLOCK_ROWS - 1) // BLOCK_ROWS * BLOCK_ROWS
    extra = max(per_group // 2, 16)
    shape = jax.ShapeDtypeStruct
    seq, sub = lax.axis_index("seq"), lax.axis_index("sub")
    first = lax.div(seq * sizes[1] + sub, jnp.int32(heads)) * per_group
    me = jnp.stack([seq, sub, lax.axis_index("head"), first]).astype(jnp.int32)

    def several(count, *dims):
        return (shape(dims, BF16),) * count

    assign_row = assignment.reshape(1, toks)
    *far_mixed, slot_row = call(
        functools.partial(project_far_kernel, sizes, groups, rows, heads),
        several(sizes[1], rows + COUNT_ROWS, LANES) + (shape((1, toks), jnp.int32),),
        (assign_row, tokens_in, w_query, cotangent),
        smem=(),
        in_place=(1, 2, 3),
        scratch=[
            pltpu.VMEM((toks, width), BF16),
            pltpu.VMEM((width, sizes[1] * HD), BF16),
            pltpu.VMEM((toks, sizes[1] * HD), BF16),
            pltpu.VMEM((toks, sizes[1] * LANES), BF16),
            pltpu.SemaphoreType.DMA((3, max(toks, width) // min(256, toks))),
        ],
        flops=2 * toks * width * sizes[1] * HD + 2 * rows * toks * sizes[1] * LANES,
        vmem=60,
        name="project_far",
    )
    own_mixed, *near_mixed = call(
        functools.partial(project_query_kernel, sizes, groups, rows),
        several(owners - sizes[1], rows + COUNT_ROWS, LANES),
        (me, slot_row, assign_row, tokens_in, w_query, cotangent),
        scratch=[pltpu.VMEM((toks, 2 * width_dev), BF16), pltpu.VMEM((owners, rows + COUNT_ROWS, LANES), BF16)],
        flops=2 * toks * width * width_dev + 4 * slots * toks * width_dev,
        name="project_query",
    )
    send_mixed = [own_mixed, *far_mixed, *near_mixed]
    got_mixed = exchange(send_mixed, sizes)
    *send_value, turned, unsort = call(
        functools.partial(project_value_kernel, sizes, groups, rows),
        several(owners, half, LANES) + several(1, width, slots) + several(1, toks, slots),
        (me, slot_row, tokens_in, w_value),
        after=near_mixed[:1],
        scratch=[pltpu.VMEM((toks, width_dev), BF16), pltpu.VMEM((owners, half, LANES), BF16)],
        flops=2 * toks * width * width_dev + 2 * slots * toks * width_dev,
        name="project_value",
    )
    behind = [0, *range(3, owners), 2, 1][:owners]
    send_value = [lax.optimization_barrier((part, got_mixed[k]))[0] for part, k in zip(send_value, behind)]
    got_value = exchange(send_value, sizes)
    blocks = per_group * capacity // BLOCK_ROWS
    held = blocks + (LEAD + 4) * UNROLL
    block_flops = 2 * BLOCK_ROWS * BLOCK_ROWS * LANES
    tall = pltpu.VMEM((owners, rows + slot_rows, LANES), F32)
    dense_rows = pltpu.VMEM((held * BLOCK_ROWS, LANES), F32)
    group_f32 = pltpu.VMEM((GROUP_ROWS, BLOCK_ROWS), F32)
    group_b16 = pltpu.VMEM((GROUP_ROWS, BLOCK_ROWS), BF16)
    place = pltpu.SMEM((owners,), jnp.int32)
    *back_value, dense, counts = call(
        functools.partial(value_grad_kernel, sizes, per_group, slot_rows),
        several(sizes[0], sizes[1], half, LANES)
        + several(1, held * BLOCK_ROWS, LANES)
        + (shape((owners, LANES), jnp.int32),),
        (me, *got_mixed),
        after=[unsort],
        scratch=[pltpu.SMEM((owners, LANES), jnp.int32), place, tall, dense_rows, tall]
        + [group_f32] * 2
        + [group_b16] * 2,
        flops=4 * blocks * block_flops,
        vmem=48,
        name="value_grad",
    )
    back_value, _ = lax.optimization_barrier((back_value, got_value[1:]))
    back_query = call(
        functools.partial(query_grad_kernel, sizes, per_group, slot_rows),
        several(sizes[0], sizes[1], half + extra, LANES),
        (me, counts, dense, *got_value),
        smem=(0, 1),
        scratch=[place, tall, dense_rows, pltpu.VMEM((held, LANES), F32), pltpu.VMEM((2 * extra, LANES), F32)]
        + [group_f32] * 4
        + [group_b16] * 2,
        flops=6 * blocks * block_flops,
        vmem=48,
        name="query_grad",
    )
    home_query = exchange_by_chip(me, back_query, sizes, "swap_query")
    home_value = exchange_by_chip(me, back_value, sizes, "swap_value", back_query[:1])
    weight_flops = 2 * slots * width * width_dev
    home_flops = weight_flops // parts * (parts - 1)
    piece = width // owners
    sub_shapes = several(sizes[1], sizes[0], piece, width_dev)
    value_rows, *refs = call(
        functools.partial(value_home_kernel, sizes, heads, parts),
        several(1, slots, width_dev) + (shape((slots, columns), F32),) * (parts - 1) + sub_shapes,
        (me, turned, w_value, *home_value),
        scratch=[pltpu.VMEM((owners, half, LANES), BF16)],
        flops=weight_flops + home_flops,
        name="value_home",
    )
    value_terms, value_weight = refs[: parts - 1], refs[parts - 1 :]
    value_weight = fold_subs(me, value_weight, "value_subs")
    *partials, query_rows, centroid_grad = call(
        functools.partial(query_home_kernel, sizes, heads, (CLUSTERS / (toks * owners)) ** 0.5, parts),
        several(parts - 1, slots, columns)
        + several(1, slots, width_dev)
        + (shape((groups * 2 * extra, width_dev), F32),),
        (me, w_query, *value_terms, *home_query),
        scratch=[pltpu.VMEM((owners, half + extra, LANES), BF16)],
        flops=home_flops,
        name="query_home",
    )
    arrived = [shift(partial, "head", k + 1) for k, partial in enumerate(partials)]
    value_weight, _ = lax.optimization_barrier((value_weight, home_query))
    value_weight = pass_round(value_weight, "seq")
    query_weight = call(
        functools.partial(query_weight_kernel, sizes),
        sub_shapes,
        (me, turned, query_rows),
        flops=weight_flops,
        name="query_weight",
    )
    query_weight = fold_subs(me, query_weight, "query_subs")
    own = call(
        functools.partial(input_own_kernel, parts),
        shape((slots, columns), BF16),
        (me, query_rows, value_rows, w_query, w_value),
        after=query_weight[:1],
        flops=weight_flops * 2 // parts,
        name="input_own",
    )
    query_weight = pass_round(query_weight, "seq")
    grad_wv = add_up(value_weight, F32, "value_sum", [own])
    grad_input, own_weight = call(
        input_sum_kernel,
        several(1, toks, columns) + several(1, piece, width_dev),
        (unsort, query_weight[0], own, *arrived),
        smem=(),
        scratch=[pltpu.VMEM((slots, columns), BF16)],
        flops=2 * toks * slots * columns,
        name="input_sum",
    )
    grad_wq = add_up([own_weight, *query_weight[1:]], F32, "query_sum")
    if groups > 1:
        centroid_grad = centroid_grad.reshape(groups, 2 * extra, width_dev)[:, :per_group]
        centroid_grad = centroid_grad.reshape(CLUSTERS, width_dev)
    return (grad_input, grad_wq, grad_wv, centroid_grad)


def solution(mesh):
    return jax.shard_map(
        on_device,
        mesh=mesh,
        in_specs=(
            P(("grp", "seq", "sub"), None),
            P(None, "head"),
            P(None, "head"),
            P(("grp", "seq", "sub"), "head"),
            P(("grp", "seq", "sub"), None),
        ),
        out_specs=(
            P(("grp", "seq", "sub"), "head"),
            P(("grp", "seq", "sub"), "head"),
            P(("grp", "seq", "sub"), "head"),
            P("grp", "head"),
        ),
        check_vma=False,
    )
```

```python
import functools

import jax
import jax.numpy as jnp
from jax import lax
from jax.experimental import pallas as pl
from jax.experimental.pallas import tpu as pltpu
from jax.sharding import PartitionSpec as P

HD = 64
CLUSTERS = 64
BLOCK_ROWS = 128
LANES = 128
UNROLL = 4
COUNT_ROWS = 16
SCALE = 0.5 * HD ** (-0.5)
F32 = jnp.float32
BF16 = jnp.bfloat16
OWNERS = ("seq", "sub")
GROUP_ROWS = UNROLL * BLOCK_ROWS
LEAD = 2


def iota(shape, dim):
    return lax.broadcasted_iota(jnp.int32, shape, dim)


def low_half(shape):
    return iota(shape, 1) < HD


def swap_halves(tile):
    return pltpu.roll(tile, HD, 1)


def dot(a, b):
    return jnp.dot(a, b, preferred_element_type=F32)


def dot_nt(a, b):
    return lax.dot_general(a, b, (((1,), (1,)), ((), ())), preferred_element_type=F32)


def ones_where(condition):
    return jnp.where(condition, 1.0, 0.0).astype(BF16)


def owner_of(me_ref, ahead, sizes):
    seq = lax.rem(me_ref[0] + ahead[0], jnp.int32(sizes[0]))
    sub = lax.rem(me_ref[1] + ahead[1], jnp.int32(sizes[1]))
    return seq * sizes[1] + sub


def source_of(me_ref, ahead, sizes):
    return owner_of(me_ref, ((sizes[0] - ahead[0]) % sizes[0], (sizes[1] - ahead[1]) % sizes[1]), sizes)


def steps_of(sizes):
    far = sorted(range(1, sizes[0]), key=lambda seq: -min(seq, sizes[0] - seq))
    subs = range(sizes[1])
    return [(0, 0)] + [(seq, sub) for seq in far for sub in subs] + [(0, sub) for sub in subs if sub]


def hand_out(by_owner_ref, out_refs, me_ref, sizes):
    for ahead, out_ref in zip(steps_of(sizes), out_refs):
        out_ref[...] = by_owner_ref[owner_of(me_ref, ahead, sizes)]


def slots_of(assign, groups, rows):
    toks = assign.shape[1]
    per_group = CLUSTERS // groups
    member = jnp.where(iota((CLUSTERS, toks), 0) == assign, 1.0, 0.0)
    member_b = member.astype(BF16)
    upto = ones_where(iota((LANES, LANES), 0) <= iota((LANES, LANES), 1))
    counts = jnp.zeros((CLUSTERS, 1), F32)
    running = []
    for first in range(0, toks, LANES):
        within = dot(member_b[:, first : first + LANES], upto)
        running.append(within + counts)
        counts = counts + within[:, LANES - 1 :]
    running = jnp.concatenate(running, axis=1)
    here, other = iota((CLUSTERS, CLUSTERS), 0), iota((CLUSTERS, CLUSTERS), 1)
    group_of = lambda index: lax.div(index, jnp.int32(per_group))
    earlier = ones_where((other < here) & (group_of(other) == group_of(here)))
    base = dot(earlier, jnp.broadcast_to(counts, (CLUSTERS, LANES)).astype(BF16))[:, :1]
    base = base + (group_of(iota((CLUSTERS, 1), 0)) * rows).astype(F32)
    slot = jnp.sum(member * (running - 1.0 + base), axis=0, keepdims=True).astype(jnp.int32)
    spread = jnp.concatenate([member_b, jnp.zeros((LANES - CLUSTERS, toks), BF16)], axis=0)
    return slot, dot_nt(jnp.ones((COUNT_ROWS, toks), BF16), spread).astype(BF16)


def arrivals(sizes, me_ref, refs):
    seqs, subs = sizes
    for ahead in steps_of(sizes):
        if ahead[1] == 0:
            piece = refs[ahead[0]][me_ref[1]]
        else:
            piece = refs[seqs + ahead[1] - 1][ahead[0]]
        yield source_of(me_ref, ahead, sizes), piece


def swap_kernel(sizes, me_ref, *refs):
    for k, out_ref in enumerate(refs[sizes[0] :]):
        sub = lax.rem(me_ref[1] + (k + 1), jnp.int32(sizes[1]))
        for seq in range(sizes[0]):
            out_ref[seq] = refs[seq][sub]


def beside(query, cotan):
    low = low_half(query.shape)
    even = jnp.where(low, query, swap_halves(cotan)).astype(BF16)
    return even, jnp.where(low, swap_halves(query), cotan).astype(BF16)


def load_rows(source, target, sems, fine):
    return [
        pltpu.make_async_copy(source.at[pl.ds(row, fine), :], target.at[pl.ds(row, fine), :], sems.at[row // fine])
        for row in range(0, target.shape[0], fine)
    ]


def fold_halves(tile):
    half = tile.shape[0] // 2
    low = low_half((half, LANES))
    up, down = tile[:half], tile[half:]
    even = jnp.where(low, up, swap_halves(down)).astype(BF16)
    return even, jnp.where(low, swap_halves(up), down).astype(BF16)


def far_place(sizes, heads):
    me = (lax.axis_index("seq"), lax.axis_index("sub"))
    owner = owner_of(me, steps_of(sizes)[1], sizes) - me[1]
    head = lax.rem(owner, jnp.int32(heads))
    columns = pl.ds(pl.multiple_of(head * HD, LANES), sizes[1] * HD)
    return me[1], lax.div(owner, jnp.int32(heads)), columns


def give_pieces(pieces, sub, out_refs):
    for ahead, out_ref in enumerate(out_refs):
        dest = lax.rem(sub + ahead, jnp.int32(len(pieces)))
        chosen = pieces[0]
        for other in range(1, len(pieces)):
            chosen = jnp.where(dest == other, pieces[other], chosen)
        out_ref[: chosen.shape[0], :] = chosen


def cotan_far_kernel(sizes, groups, rows, heads, assign_ref, cotan_hbm, *refs):
    out_refs, (slot_ref, cotan_ref, sems) = refs[: sizes[1]], refs[sizes[1] :]
    toks = cotan_ref.shape[0]
    sub, group, columns = far_place(sizes, heads)
    load = load_rows(cotan_hbm.at[:, columns], cotan_ref, sems, min(256, toks))
    for copy in load:
        copy.start()
    slot, tallies = slots_of(assign_ref[...], groups, rows)
    slot_ref[...] = slot
    pick = ones_where(iota((rows, toks), 0) + group * rows == slot)
    for copy in load:
        copy.wait()
    pieces = []
    for first in range(0, sizes[1] * HD, LANES):
        pieces += fold_halves(dot(pick, cotan_ref[:, first : first + LANES]))
    give_pieces(pieces, sub, out_refs)
    for out_ref in out_refs:
        out_ref[rows // 2 :, :] = tallies


def query_far_kernel(sizes, groups, rows, heads, slot_ref, tokens_hbm, weight_hbm, *refs):
    out_refs, (tokens_ref, weight_ref, query_ref, sems) = refs[: sizes[1]], refs[sizes[1] :]
    toks = tokens_ref.shape[0]
    fine = min(256, toks)
    sub, group, columns = far_place(sizes, heads)
    weight = load_rows(weight_hbm.at[:, columns], weight_ref, sems.at[0], fine)
    tokens = load_rows(tokens_hbm, tokens_ref, sems.at[1], fine)
    for copy in weight + tokens:
        copy.start()
    pick = ones_where(iota((rows, toks), 0) + group * rows == slot_ref[...])
    for copy in weight:
        copy.wait()
    for index, copy in enumerate(tokens):
        copy.wait()
        where = slice(index * fine, (index + 1) * fine)
        query_ref[where, :] = dot(tokens_ref[where, :], weight_ref[...]).astype(BF16)
    pieces = []
    for first in range(0, sizes[1] * HD, LANES):
        pieces += fold_halves(dot(pick, query_ref[:, first : first + LANES]))
    give_pieces(pieces, sub, out_refs)


def project_query_kernel(sizes, groups, rows, me_ref, slot_ref, assign_ref, tokens_ref, weight_ref, cotan_ref, *rest):
    out_refs, (mixed_ref, sorted_ref) = rest[:-2], rest[-2:]
    toks = tokens_ref.shape[0]
    heads = weight_ref.shape[1] // HD
    step = min(512, toks)
    for first in range(0, toks, step):
        where = slice(first, first + step)
        query, cotan = dot(tokens_ref[where, :], weight_ref[...]), cotan_ref[where, :].astype(F32)
        for pair in range(heads // 2):
            columns = slice(pair * LANES, (pair + 1) * LANES)
            even, odd = beside(query[:, columns], cotan[:, columns])
            mixed_ref[where, 2 * pair * LANES : (2 * pair + 1) * LANES] = even
            mixed_ref[where, (2 * pair + 1) * LANES : (2 * pair + 2) * LANES] = odd
    part = min(512, rows)
    pieces = rows // part

    @pl.loop(0, groups * pieces)
    def _(i):
        group, piece = lax.div(i, jnp.int32(pieces)), lax.rem(i, jnp.int32(pieces))
        first = pl.multiple_of(piece * part, part)
        pick = ones_where(iota((part, toks), 0) + i * part == slot_ref[...])
        sorted_rows = dot(pick, mixed_ref[...]).astype(BF16)
        for head in range(heads):
            sorted_ref[group * heads + head, pl.ds(first, part), :] = sorted_rows[
                :, head * LANES : (head + 1) * LANES
            ]

    member = jnp.where(iota((LANES, toks), 0) == assign_ref[...], 1.0, 0.0).astype(BF16)
    tallies = dot_nt(jnp.ones((COUNT_ROWS, toks), BF16), member).astype(BF16)
    for owner in range(sorted_ref.shape[0]):
        sorted_ref[owner, rows:, :] = tallies
    steps = steps_of(sizes)
    for ahead, out_ref in zip(steps[:1] + steps[1 + sizes[1] :], out_refs):
        out_ref[...] = sorted_ref[owner_of(me_ref, ahead, sizes)]


def project_value_kernel(sizes, groups, rows, me_ref, slot_ref, tokens_ref, weight_ref, *rest):
    out_refs, (turned_ref, unsort_ref, value_ref, sorted_ref) = rest[:-4], rest[-4:]
    toks = tokens_ref.shape[0]
    heads = weight_ref.shape[1] // HD
    step = min(512, toks)

    @pl.loop(0, toks // step)
    def _(i):
        where = pl.ds(pl.multiple_of(i * step, step), step)
        value_ref[where, :] = dot(tokens_ref[where, :], weight_ref[...]).astype(BF16)

    half = rows // 2
    part = min(256, half)
    pieces = half // part

    @pl.loop(0, groups * pieces)
    def _(i):
        group, piece = lax.div(i, jnp.int32(pieces)), lax.rem(i, jnp.int32(pieces))
        first = pl.multiple_of(piece * part, part)
        index = iota((part, toks), 0) + group * rows + first
        upper = dot(ones_where(index == slot_ref[...]), value_ref[...])
        lower = dot(ones_where(index + half == slot_ref[...]), value_ref[...])
        low = low_half((part, LANES))
        for pair in range(heads // 2):
            up = upper[:, pair * LANES : (pair + 1) * LANES]
            down = lower[:, pair * LANES : (pair + 1) * LANES]
            even = jnp.where(low, up, swap_halves(down)).astype(BF16)
            odd = jnp.where(low, swap_halves(up), down).astype(BF16)
            sorted_ref[group * heads + 2 * pair, pl.ds(first, part), :] = even
            sorted_ref[group * heads + 2 * pair + 1, pl.ds(first, part), :] = odd

    hand_out(sorted_ref, out_refs, me_ref, sizes)
    turned = tokens_ref[...].T
    slots = unsort_ref.shape[1]
    part = min(256, slots)
    for i in range(slots // part):
        pick = ones_where(iota((part, toks), 0) + i * part == slot_ref[...])
        unsort_ref[:, i * part : (i + 1) * part] = pick.T
        turned_ref[:, i * part : (i + 1) * part] = dot_nt(turned, pick).astype(BF16)


def score(mixed):
    query = jnp.where(low_half(mixed.shape), mixed.astype(F32) * SCALE, 0.0).astype(BF16)
    return dot_nt(query, mixed)


def softmax_turned(scores):
    shape = scores.shape
    seen = iota(shape, 0) <= iota(shape, 1)
    scores = jnp.where(seen, scores, -jnp.inf)
    raised = jnp.exp(scores - jnp.max(scores, axis=0, keepdims=True))
    return raised * (1.0 / jnp.sum(raised, axis=0, keepdims=True))


def for_each_cluster(counts_ref, me_ref, place_ref, owners, per_group, body):
    for source in range(owners):
        place_ref[source] = 0

    def step(cluster, block):
        runs = []
        total = 0
        base = block * BLOCK_ROWS
        for source in range(owners):
            count = counts_ref[source, me_ref[3] + cluster]
            start = place_ref[source]
            runs.append((source, start, base + total))
            place_ref[source] = start + count
            total = total + count
        body(cluster, block, runs, base + total)
        return block + lax.shift_right_logical(total + (BLOCK_ROWS - 1), jnp.int32(7))

    return lax.fori_loop(0, per_group, step, jnp.int32(LEAD * UNROLL))


def gather_blocks(counts_ref, me_ref, place_ref, owners, per_group, slot_rows, wide_ref, block_ref):
    def body(cluster, block, runs, end):
        for source, start, row in runs:
            block_ref[pl.ds(row, slot_rows), :] = wide_ref[source, pl.ds(start, slot_rows), :]
        block_ref[pl.ds(end, BLOCK_ROWS), :] = jnp.zeros((BLOCK_ROWS, LANES), F32)

    blocks = for_each_cluster(counts_ref, me_ref, place_ref, owners, per_group, body)
    spare = pl.ds(pl.multiple_of(blocks * BLOCK_ROWS, BLOCK_ROWS), GROUP_ROWS)
    block_ref[spare, :] = jnp.zeros((GROUP_ROWS, LANES), F32)
    return blocks


def for_each_group(blocks, stages):
    first, second, third = stages
    groups = lax.div(blocks + (UNROLL - 1), jnp.int32(UNROLL))

    def step(i, carry):
        for slot in range(2):
            group = LEAD + 2 * i + slot
            third(group - 2, slot)
            second(group - 1, 1 - slot)
            first(group, slot)
        return carry

    lax.fori_loop(0, lax.shift_right_logical(groups + 1, jnp.int32(1)), step, 0)


def block_rows(group, ahead):
    return pl.ds(pl.multiple_of((group * UNROLL + ahead) * BLOCK_ROWS, BLOCK_ROWS), BLOCK_ROWS)


def tile_rows(ahead):
    return slice(ahead * BLOCK_ROWS, (ahead + 1) * BLOCK_ROWS)


def value_grad_kernel(sizes, per_group, slot_rows, me_ref, *refs):
    owners = sizes[0] * sizes[1]
    near, came = owners - sizes[1], owners + sizes[1]
    mixed_refs, far_refs = refs[:near], refs[near:came]
    out_refs, rest = refs[came : came + sizes[0]], refs[came + sizes[0] :]
    dense_ref, counts_out_ref, counts_ref, place_ref, wide_ref, block_ref, home_ref = rest[:7]
    score_refs, probs_refs = rest[7:9], rest[9:11]
    half = out_refs[0].shape[1]
    rows = 2 * half
    steps, subs = steps_of(sizes), sizes[1]
    low = low_half((half, LANES))
    for index, ahead in enumerate(steps):
        source = source_of(me_ref, ahead, sizes)
        if 1 <= index <= subs:
            cotan = far_refs[index - 1][:half, :].astype(F32)
            query = far_refs[index - 1 + subs][...].astype(F32)
            tail = far_refs[index - 1][half:, :]
            wide_ref[source, :half, :] = jnp.where(low, query, swap_halves(cotan))
            wide_ref[source, half:rows, :] = jnp.where(low, swap_halves(query), cotan)
        else:
            mixed_ref = mixed_refs[index if index == 0 else index - subs]
            tail = mixed_ref[rows:, :]
            wide_ref[source, :rows, :] = mixed_ref[:rows, :].astype(F32)
        counts_out_ref[pl.ds(source, 1), :] = tail.astype(F32).astype(jnp.int32)[:1, :]
        wide_ref[source, rows:, :] = jnp.zeros((slot_rows, LANES), F32)
    pltpu.sync_copy(counts_out_ref, counts_ref)
    blocks = gather_blocks(counts_ref, me_ref, place_ref, owners, per_group, slot_rows, wide_ref, block_ref)

    def first(group, slot):
        for ahead in range(UNROLL):
            where = block_rows(group, ahead)
            mixed = block_ref[where, :].astype(BF16)
            dense_ref[where, :] = mixed
            score_refs[slot][tile_rows(ahead), :] = score(mixed)

    def second(group, slot):
        for ahead in range(UNROLL):
            tile = tile_rows(ahead)
            probs_refs[slot][tile, :] = softmax_turned(score_refs[slot][tile, :]).astype(BF16)

    def third(group, slot):
        for ahead in range(UNROLL):
            where = block_rows(group, ahead)
            block_ref[where, :] = dot(probs_refs[slot][tile_rows(ahead), :], dense_ref[where, :])

    for_each_group(blocks, (first, second, third))

    def scatter(cluster, block, runs, end):
        for source, start, row in runs:
            wide_ref[source, pl.ds(start, slot_rows), :] = block_ref[pl.ds(row, slot_rows), :]

    for_each_cluster(counts_ref, me_ref, place_ref, owners, per_group, scatter)
    for ahead, out_ref in enumerate(out_refs):
        for sub in range(sizes[1]):
            source = owner_of(me_ref, (ahead, 0), sizes) - me_ref[1] + sub
            up, down = wide_ref[source, :half, :], wide_ref[source, half:rows, :]
            out_ref[sub] = jnp.where(low_half((half, LANES)), swap_halves(up), down).astype(BF16)


def query_grad_kernel(sizes, per_group, slot_rows, me_ref, counts_ref, dense_ref, *refs):
    owners = sizes[0] * sizes[1]
    mid = owners + sizes[0]
    value_refs, out_refs, rest = refs[:owners], refs[owners:mid], refs[mid:]
    place_ref, wide_ref, block_ref, sums_ref, centroid_ref = rest[:5]
    score_refs, grad_probs_refs, both_refs = rest[5:7], rest[7:9], rest[9:11]
    half = value_refs[0].shape[0]
    rows = 2 * half
    for ahead, value_ref in zip(steps_of(sizes), value_refs):
        source = source_of(me_ref, ahead, sizes)
        value = value_ref[...].astype(F32)
        wide_ref[source, :half, :] = swap_halves(value)
        wide_ref[source, half:rows, :] = value
        wide_ref[source, rows:, :] = jnp.zeros((slot_rows, LANES), F32)
    blocks = gather_blocks(counts_ref, me_ref, place_ref, owners, per_group, slot_rows, wide_ref, block_ref)

    def first(group, slot):
        for ahead in range(UNROLL):
            where, tile = block_rows(group, ahead), tile_rows(ahead)
            mixed = dense_ref[where, :]
            value = block_ref[where, :].astype(BF16)
            cotan = jnp.where(low_half(mixed.shape), jnp.zeros_like(mixed), mixed)
            score_refs[slot][tile, :] = score(mixed)
            grad_probs_refs[slot][tile, :] = dot_nt(value, cotan)

    def second(group, slot):
        for ahead in range(UNROLL):
            tile = tile_rows(ahead)
            probs = softmax_turned(score_refs[slot][tile, :])
            grad_probs = grad_probs_refs[slot][tile, :]
            probs_half = probs.astype(BF16).astype(F32)
            row_dot = jnp.sum(probs_half * grad_probs, axis=0, keepdims=True)
            grad_scores = (probs * (grad_probs - row_dot)).astype(BF16).astype(F32)
            both_refs[slot][tile, :] = (grad_scores + grad_scores.T).astype(BF16)

    def third(group, slot):
        for ahead in range(UNROLL):
            where = block_rows(group, ahead)
            grad = dot(both_refs[slot][tile_rows(ahead), :], dense_ref[where, :]) * SCALE
            grad = grad.astype(BF16).astype(F32)
            block_ref[where, :] = grad
            sums_ref[pl.ds(group * UNROLL + ahead, 1), :] = jnp.sum(grad, axis=0, keepdims=True)

    for_each_group(blocks, (first, second, third))
    most = (owners * slot_rows + BLOCK_ROWS - 1) // BLOCK_ROWS

    def scatter(cluster, block, runs, end):
        total = jnp.zeros((1, LANES), F32)
        for ahead in range(most):
            here = block + ahead
            total = total + jnp.where(here * BLOCK_ROWS < end, sums_ref[pl.ds(here, 1), :], 0.0)
        centroid_ref[pl.ds(cluster, 1), :] = total
        for source, start, row in runs:
            wide_ref[source, pl.ds(start, slot_rows), :] = block_ref[pl.ds(row, slot_rows), :]

    for_each_cluster(counts_ref, me_ref, place_ref, owners, per_group, scatter)
    extra = out_refs[0].shape[1] - half
    centroid = jnp.where(
        low_half((extra, LANES)), centroid_ref[:extra, :], swap_halves(centroid_ref[extra:, :])
    ).astype(BF16)
    for ahead, out_ref in enumerate(out_refs):
        for sub in range(sizes[1]):
            source = owner_of(me_ref, (ahead, 0), sizes) - me_ref[1] + sub
            up, down = wide_ref[source, :half, :], wide_ref[source, half:rows, :]
            out_ref[sub, :half, :] = jnp.where(low_half((half, LANES)), up, swap_halves(down)).astype(BF16)
            out_ref[sub, half:, :] = centroid


def unfold(home_ref, out_ref, heads, start, half, finish):
    low = low_half((half, LANES))
    for group in range(home_ref.shape[0] // heads):
        first = group * 2 * half
        for pair in range(heads // 2):
            even = home_ref[group * heads + 2 * pair, start : start + half, :].astype(F32)
            odd = home_ref[group * heads + 2 * pair + 1, start : start + half, :].astype(F32)
            columns = slice(pair * LANES, (pair + 1) * LANES)
            out_ref[first : first + half, columns] = finish(jnp.where(low, even, swap_halves(odd)))
            out_ref[first + half : first + 2 * half, columns] = finish(
                jnp.where(low, swap_halves(even), odd)
            )


def to_half(x):
    return x.astype(BF16)


def bring_home(sizes, heads, pieces, home_ref, rows_ref):
    for source, piece in pieces:
        home_ref[source] = piece
    unfold(home_ref, rows_ref, heads, 0, rows_ref.shape[0] * heads // home_ref.shape[0] // 2, to_half)


def weight_partial(sizes, me_ref, turned_ref, rows_ref, sub_refs):
    piece = turned_ref.shape[0] // (sizes[0] * sizes[1])
    for ahead, sub_ref in enumerate(sub_refs):
        sub = lax.rem(me_ref[1] + ahead, jnp.int32(sizes[1]))
        first = [pl.multiple_of((seq * sizes[1] + sub) * piece, piece) for seq in range(sizes[0])]
        turned = jnp.concatenate([turned_ref[pl.ds(row, piece), :] for row in first], axis=0)
        partial = dot(turned, rows_ref[...]).astype(BF16)
        for seq in range(sizes[0]):
            sub_ref[seq] = partial[seq * piece : (seq + 1) * piece, :]


def input_columns(me_ref, ahead, parts, width):
    columns = width // parts
    dest = lax.rem(me_ref[2] + ahead, jnp.int32(parts))
    return pl.ds(pl.multiple_of(dest * columns, columns), columns)


def value_home_kernel(sizes, heads, parts, me_ref, turned_ref, weight_ref, *refs):
    came = sizes[0] + sizes[1] - 1
    part_refs, refs = refs[:came], refs[came:]
    rows_ref, term_refs, refs = refs[0], refs[1:parts], refs[parts:]
    sub_refs, home_ref = refs[: sizes[1]], refs[sizes[1]]
    bring_home(sizes, heads, arrivals(sizes, me_ref, part_refs), home_ref, rows_ref)
    for k, term_ref in enumerate(term_refs):
        mine = input_columns(me_ref, k + 1, parts, weight_ref.shape[0])
        term_ref[...] = dot_nt(rows_ref[...], weight_ref[mine, :])
    weight_partial(sizes, me_ref, turned_ref, rows_ref, sub_refs)


def query_home_kernel(sizes, heads, factor, parts, me_ref, weight_ref, *refs):
    term_refs, refs = refs[: parts - 1], refs[parts - 1 :]
    came = sizes[0] + sizes[1] - 1
    part_refs, refs = refs[:came], refs[came:]
    out_refs, (rows_ref, centroid_ref, home_ref) = refs[: parts - 1], refs[parts - 1 :]
    bring_home(sizes, heads, arrivals(sizes, me_ref, part_refs), home_ref, rows_ref)
    for k, (term_ref, out_ref) in enumerate(zip(term_refs, out_refs)):
        mine = input_columns(me_ref, k + 1, parts, weight_ref.shape[0])
        step = min(256, rows_ref.shape[0])
        for first in range(0, rows_ref.shape[0], step):
            where = slice(first, first + step)
            out_ref[where, :] = (dot_nt(rows_ref[where, :], weight_ref[mine, :]) + term_ref[where, :]).astype(BF16)
    half = rows_ref.shape[0] * heads // home_ref.shape[0] // 2
    unfold(home_ref, centroid_ref, heads, half, home_ref.shape[1] - half, lambda x: x * factor)


def query_weight_kernel(sizes, me_ref, turned_ref, rows_ref, *sub_refs):
    weight_partial(sizes, me_ref, turned_ref, rows_ref, sub_refs)


def input_own_kernel(parts, me_ref, rows_ref, value_rows_ref, w_query_ref, w_value_ref, out_ref):
    mine = input_columns(me_ref, 0, parts, w_query_ref.shape[0])
    total = dot_nt(rows_ref[...], w_query_ref[mine, :]) + dot_nt(value_rows_ref[...], w_value_ref[mine, :])
    out_ref[...] = total.astype(BF16)


def fold_subs_kernel(me_ref, *refs):
    seqs = refs[0].shape[0]
    terms, out_refs = refs[:-seqs], refs[-seqs:]
    for ahead, out_ref in enumerate(out_refs):
        seq = lax.rem(me_ref[0] + ahead, jnp.int32(seqs))
        total = terms[0][seq].astype(F32)
        for term in terms[1:]:
            total = total + term[seq].astype(F32)
        out_ref[...] = total.astype(BF16)


def sum_kernel(*refs):
    total = refs[0][...].astype(F32)
    for ref in refs[1:-1]:
        total = total + ref[...].astype(F32)
    refs[-1][...] = total.astype(refs[-1].dtype)


def input_sum_kernel(unsort_ref, weight_ref, *refs):
    part_refs, out_ref, weight_out_ref, total_ref = refs[:-3], refs[-3], refs[-2], refs[-1]
    total = part_refs[0][...].astype(F32)
    for part_ref in part_refs[1:]:
        total = total + part_ref[...].astype(F32)
    total_ref[...] = total.astype(BF16)
    step = min(256, out_ref.shape[0])
    for first in range(0, out_ref.shape[0], step):
        where = slice(first, first + step)
        out_ref[where, :] = dot(unsort_ref[where, :], total_ref[...]).astype(BF16)
    weight_out_ref[...] = weight_ref[...]


def call(kernel, outs, inputs, smem=(0,), in_place=(), after=(), scratch=(), flops=0, vmem=24, name=None):
    def body(*refs):
        kernel(*refs[: len(inputs)], *refs[len(inputs) + len(after) :])

    def space(i):
        return pltpu.SMEM if i in smem else pl.ANY if i in in_place else pltpu.VMEM

    specs = [pl.BlockSpec(memory_space=space(i)) for i in range(len(inputs))]
    specs += [pl.BlockSpec(memory_space=pl.ANY)] * len(after)
    moved = sum(x.size * x.dtype.itemsize for x in inputs) + sum(
        x.size * x.dtype.itemsize for x in jax.tree.leaves(outs)
    )
    return pl.pallas_call(
        body,
        out_shape=outs,
        in_specs=specs,
        out_specs=jax.tree.map(lambda _: pl.BlockSpec(memory_space=pltpu.VMEM), outs),
        scratch_shapes=list(scratch),
        compiler_params=pltpu.CompilerParams(vmem_limit_bytes=vmem * 2**20),
        cost_estimate=pl.CostEstimate(flops=flops, bytes_accessed=moved, transcendentals=0),
        name=name,
    )(*inputs, *after)


def send(part, ahead, sizes):
    moves = [
        (seq * sizes[1] + sub, (seq + ahead[0]) % sizes[0] * sizes[1] + (sub + ahead[1]) % sizes[1])
        for seq, sub in steps_of(sizes)
    ]
    return part if ahead == (0, 0) else lax.ppermute(part, OWNERS, moves)


def exchange(parts, sizes):
    return [send(part, ahead, sizes) for ahead, part in zip(steps_of(sizes), parts)]


def shift(part, axis, ahead):
    size = lax.axis_size(axis)
    return lax.ppermute(part, axis, [(i, (i + ahead) % size) for i in range(size)])


def pass_round(parts, axis):
    return [parts[0]] + [shift(parts[ahead], axis, ahead) for ahead in range(1, len(parts))]


def exchange_by_chip(me, parts, sizes, name, after=()):
    came = pass_round(parts, "seq")
    swapped = call(
        functools.partial(swap_kernel, sizes),
        (jax.ShapeDtypeStruct((sizes[0], *parts[0].shape[1:]), BF16),) * (sizes[1] - 1),
        (me, *came),
        after=after,
        name=name,
    )
    return came + [shift(part, "sub", k + 1) for k, part in enumerate(swapped)]


def fold_subs(me, by_sub, name):
    seqs, piece, columns = by_sub[0].shape
    return call(
        fold_subs_kernel,
        (jax.ShapeDtypeStruct((piece, columns), BF16),) * seqs,
        (me, *pass_round(by_sub, "sub")),
        name=name,
    )


def add_up(terms, dtype, name, after=()):
    out = jax.ShapeDtypeStruct(terms[0].shape, dtype)
    return call(sum_kernel, out, tuple(terms), smem=(), after=after, name=name)


def on_device(tokens_in, w_query, w_value, cotangent, assignment):
    sizes = (lax.axis_size("seq"), lax.axis_size("sub"))
    owners = sizes[0] * sizes[1]
    parts = lax.axis_size("head")
    toks, width = tokens_in.shape
    width_dev = cotangent.shape[1]
    heads = width_dev // HD
    slot_rows = 2 * toks // CLUSTERS
    assert owners % heads == 0 and heads % 2 == 0
    groups = owners // heads
    per_group = CLUSTERS // groups
    rows = toks if groups == 1 else per_group * slot_rows
    half = rows // 2
    slots = groups * rows
    columns = width // parts
    capacity = (slot_rows * owners + BLOCK_ROWS - 1) // BLOCK_ROWS * BLOCK_ROWS
    extra = max(per_group // 2, 16)
    shape = jax.ShapeDtypeStruct
    seq, sub = lax.axis_index("seq"), lax.axis_index("sub")
    first = lax.div(seq * sizes[1] + sub, jnp.int32(heads)) * per_group
    me = jnp.stack([seq, sub, lax.axis_index("head"), first]).astype(jnp.int32)

    def several(count, *dims):
        return (shape(dims, BF16),) * count

    assign_row = assignment.reshape(1, toks)
    subs = sizes[1]
    far_columns = subs * HD
    loads = max(toks, width) // min(256, toks)
    *far_cotan, slot_row = call(
        functools.partial(cotan_far_kernel, sizes, groups, rows, heads),
        several(subs, half + COUNT_ROWS, LANES) + (shape((1, toks), jnp.int32),),
        (assign_row, cotangent),
        smem=(),
        in_place=(1,),
        scratch=[pltpu.VMEM((toks, far_columns), BF16), pltpu.SemaphoreType.DMA((loads,))],
        flops=2 * rows * toks * far_columns,
        vmem=60,
        name="cotan_far",
    )
    far_query = call(
        functools.partial(query_far_kernel, sizes, groups, rows, heads),
        several(subs, half, LANES),
        (slot_row, tokens_in, w_query),
        smem=(),
        in_place=(1, 2),
        scratch=[
            pltpu.VMEM((toks, width), BF16),
            pltpu.VMEM((width, far_columns), BF16),
            pltpu.VMEM((toks, far_columns), BF16),
            pltpu.SemaphoreType.DMA((2, loads)),
        ],
        flops=2 * toks * width * far_columns + 2 * rows * toks * far_columns,
        vmem=60,
        name="query_far",
    )
    steps = steps_of(sizes)
    far_cotan = [send(part, ahead, sizes) for ahead, part in zip(steps[1:], far_cotan)]
    far_query = [send(part, ahead, sizes) for ahead, part in zip(steps[1:], far_query)]
    own_mixed, *near_mixed = call(
        functools.partial(project_query_kernel, sizes, groups, rows),
        several(owners - sizes[1], rows + COUNT_ROWS, LANES),
        (me, slot_row, assign_row, tokens_in, w_query, cotangent),
        after=far_cotan,
        scratch=[pltpu.VMEM((toks, 2 * width_dev), BF16), pltpu.VMEM((owners, rows + COUNT_ROWS, LANES), BF16)],
        flops=2 * toks * width * width_dev + 4 * slots * toks * width_dev,
        name="project_query",
    )
    near_mixed = [send(part, ahead, sizes) for ahead, part in zip(steps[1 + subs :], near_mixed)]
    got_mixed = [own_mixed, *far_query, *near_mixed]
    *send_value, turned, unsort = call(
        functools.partial(project_value_kernel, sizes, groups, rows),
        several(owners, half, LANES) + several(1, width, slots) + several(1, toks, slots),
        (me, slot_row, tokens_in, w_value),
        after=[own_mixed],
        scratch=[pltpu.VMEM((toks, width_dev), BF16), pltpu.VMEM((owners, half, LANES), BF16)],
        flops=2 * toks * width * width_dev + 2 * slots * toks * width_dev,
        name="project_value",
    )
    behind = [0, *range(3, owners), 2, 1][:owners]
    send_value = [lax.optimization_barrier((part, got_mixed[k]))[0] for part, k in zip(send_value, behind)]
    got_value = exchange(send_value, sizes)
    blocks = per_group * capacity // BLOCK_ROWS
    held = blocks + (LEAD + 4) * UNROLL
    block_flops = 2 * BLOCK_ROWS * BLOCK_ROWS * LANES
    tall = pltpu.VMEM((owners, rows + slot_rows, LANES), F32)
    dense_rows = pltpu.VMEM((held * BLOCK_ROWS, LANES), F32)
    group_f32 = pltpu.VMEM((GROUP_ROWS, BLOCK_ROWS), F32)
    group_b16 = pltpu.VMEM((GROUP_ROWS, BLOCK_ROWS), BF16)
    place = pltpu.SMEM((owners,), jnp.int32)
    *back_value, dense, counts = call(
        functools.partial(value_grad_kernel, sizes, per_group, slot_rows),
        several(sizes[0], sizes[1], half, LANES)
        + several(1, held * BLOCK_ROWS, LANES)
        + (shape((owners, LANES), jnp.int32),),
        (me, own_mixed, *near_mixed, *far_cotan, *far_query),
        after=[unsort],
        scratch=[pltpu.SMEM((owners, LANES), jnp.int32), place, tall, dense_rows, tall]
        + [group_f32] * 2
        + [group_b16] * 2,
        flops=4 * blocks * block_flops,
        vmem=48,
        name="value_grad",
    )
    back_value, _ = lax.optimization_barrier((back_value, got_value[1:]))
    back_query = call(
        functools.partial(query_grad_kernel, sizes, per_group, slot_rows),
        several(sizes[0], sizes[1], half + extra, LANES),
        (me, counts, dense, *got_value),
        smem=(0, 1),
        scratch=[place, tall, dense_rows, pltpu.VMEM((held, LANES), F32), pltpu.VMEM((2 * extra, LANES), F32)]
        + [group_f32] * 4
        + [group_b16] * 2,
        flops=6 * blocks * block_flops,
        vmem=48,
        name="query_grad",
    )
    home_query = exchange_by_chip(me, back_query, sizes, "swap_query")
    home_value = exchange_by_chip(me, back_value, sizes, "swap_value", back_query[:1])
    weight_flops = 2 * slots * width * width_dev
    home_flops = weight_flops // parts * (parts - 1)
    piece = width // owners
    sub_shapes = several(sizes[1], sizes[0], piece, width_dev)
    value_rows, *refs = call(
        functools.partial(value_home_kernel, sizes, heads, parts),
        several(1, slots, width_dev) + (shape((slots, columns), F32),) * (parts - 1) + sub_shapes,
        (me, turned, w_value, *home_value),
        scratch=[pltpu.VMEM((owners, half, LANES), BF16)],
        flops=weight_flops + home_flops,
        name="value_home",
    )
    value_terms, value_weight = refs[: parts - 1], refs[parts - 1 :]
    value_weight = fold_subs(me, value_weight, "value_subs")
    *partials, query_rows, centroid_grad = call(
        functools.partial(query_home_kernel, sizes, heads, (CLUSTERS / (toks * owners)) ** 0.5, parts),
        several(parts - 1, slots, columns)
        + several(1, slots, width_dev)
        + (shape((groups * 2 * extra, width_dev), F32),),
        (me, w_query, *value_terms, *home_query),
        scratch=[pltpu.VMEM((owners, half + extra, LANES), BF16)],
        flops=home_flops,
        name="query_home",
    )
    arrived = [shift(partial, "head", k + 1) for k, partial in enumerate(partials)]
    value_weight, _ = lax.optimization_barrier((value_weight, home_query))
    value_weight = pass_round(value_weight, "seq")
    query_weight = call(
        functools.partial(query_weight_kernel, sizes),
        sub_shapes,
        (me, turned, query_rows),
        flops=weight_flops,
        name="query_weight",
    )
    query_weight = fold_subs(me, query_weight, "query_subs")
    own = call(
        functools.partial(input_own_kernel, parts),
        shape((slots, columns), BF16),
        (me, query_rows, value_rows, w_query, w_value),
        after=query_weight[:1],
        flops=weight_flops * 2 // parts,
        name="input_own",
    )
    query_weight = pass_round(query_weight, "seq")
    grad_wv = add_up(value_weight, F32, "value_sum", [own])
    grad_input, own_weight = call(
        input_sum_kernel,
        several(1, toks, columns) + several(1, piece, width_dev),
        (unsort, query_weight[0], own, *arrived),
        smem=(),
        scratch=[pltpu.VMEM((slots, columns), BF16)],
        flops=2 * toks * slots * columns,
        name="input_sum",
    )
    grad_wq = add_up([own_weight, *query_weight[1:]], F32, "query_sum")
    if groups > 1:
        centroid_grad = centroid_grad.reshape(groups, 2 * extra, width_dev)[:, :per_group]
        centroid_grad = centroid_grad.reshape(CLUSTERS, width_dev)
    return (grad_input, grad_wq, grad_wv, centroid_grad)


def solution(mesh):
    return jax.shard_map(
        on_device,
        mesh=mesh,
        in_specs=(
            P(("grp", "seq", "sub"), None),
            P(None, "head"),
            P(None, "head"),
            P(("grp", "seq", "sub"), "head"),
            P(("grp", "seq", "sub"), None),
        ),
        out_specs=(
            P(("grp", "seq", "sub"), "head"),
            P(("grp", "seq", "sub"), "head"),
            P(("grp", "seq", "sub"), "head"),
            P("grp", "head"),
        ),
        check_vma=False,
    )
```

```python
import functools

import jax
import jax.numpy as jnp
from jax import lax
from jax.experimental import pallas as pl
from jax.experimental.pallas import tpu as pltpu
from jax.sharding import PartitionSpec as P

HD = 64
CLUSTERS = 64
BLOCK_ROWS = 128
LANES = 128
UNROLL = 4
COUNT_ROWS = 16
SCALE = 0.5 * HD ** (-0.5)
F32 = jnp.float32
BF16 = jnp.bfloat16
OWNERS = ("seq", "sub")
GROUP_ROWS = UNROLL * BLOCK_ROWS
LEAD = 2


def iota(shape, dim):
    return lax.broadcasted_iota(jnp.int32, shape, dim)


def low_half(shape):
    return iota(shape, 1) < HD


def swap_halves(tile):
    return pltpu.roll(tile, HD, 1)


def dot(a, b):
    return jnp.dot(a, b, preferred_element_type=F32)


def dot_nt(a, b):
    return lax.dot_general(a, b, (((1,), (1,)), ((), ())), preferred_element_type=F32)


def ones_where(condition):
    return jnp.where(condition, 1.0, 0.0).astype(BF16)


def owner_of(me_ref, ahead, sizes):
    seq = lax.rem(me_ref[0] + ahead[0], jnp.int32(sizes[0]))
    sub = lax.rem(me_ref[1] + ahead[1], jnp.int32(sizes[1]))
    return seq * sizes[1] + sub


def source_of(me_ref, ahead, sizes):
    return owner_of(me_ref, ((sizes[0] - ahead[0]) % sizes[0], (sizes[1] - ahead[1]) % sizes[1]), sizes)


def steps_of(sizes):
    far = sorted(range(1, sizes[0]), key=lambda seq: -min(seq, sizes[0] - seq))
    subs = range(sizes[1])
    return [(0, 0)] + [(seq, sub) for seq in far for sub in subs] + [(0, sub) for sub in subs if sub]


def hand_out(by_owner_ref, out_refs, me_ref, sizes):
    for ahead, out_ref in zip(steps_of(sizes), out_refs):
        out_ref[...] = by_owner_ref[owner_of(me_ref, ahead, sizes)]


def slots_of(assign, groups, rows):
    toks = assign.shape[1]
    per_group = CLUSTERS // groups
    member = jnp.where(iota((CLUSTERS, toks), 0) == assign, 1.0, 0.0)
    member_b = member.astype(BF16)
    upto = ones_where(iota((LANES, LANES), 0) <= iota((LANES, LANES), 1))
    counts = jnp.zeros((CLUSTERS, 1), F32)
    running = []
    for first in range(0, toks, LANES):
        within = dot(member_b[:, first : first + LANES], upto)
        running.append(within + counts)
        counts = counts + within[:, LANES - 1 :]
    running = jnp.concatenate(running, axis=1)
    here, other = iota((CLUSTERS, CLUSTERS), 0), iota((CLUSTERS, CLUSTERS), 1)
    group_of = lambda index: lax.div(index, jnp.int32(per_group))
    earlier = ones_where((other < here) & (group_of(other) == group_of(here)))
    base = dot(earlier, jnp.broadcast_to(counts, (CLUSTERS, LANES)).astype(BF16))[:, :1]
    base = base + (group_of(iota((CLUSTERS, 1), 0)) * rows).astype(F32)
    slot = jnp.sum(member * (running - 1.0 + base), axis=0, keepdims=True).astype(jnp.int32)
    spread = jnp.concatenate([member_b, jnp.zeros((LANES - CLUSTERS, toks), BF16)], axis=0)
    return slot, dot_nt(jnp.ones((COUNT_ROWS, toks), BF16), spread).astype(BF16)


def arrivals(sizes, me_ref, refs):
    seqs, subs = sizes
    for ahead in steps_of(sizes):
        if ahead[1] == 0:
            piece = refs[ahead[0]][me_ref[1]]
        else:
            piece = refs[seqs + ahead[1] - 1][ahead[0]]
        yield source_of(me_ref, ahead, sizes), piece


def swap_kernel(sizes, me_ref, *refs):
    for k, out_ref in enumerate(refs[sizes[0] :]):
        sub = lax.rem(me_ref[1] + (k + 1), jnp.int32(sizes[1]))
        for seq in range(sizes[0]):
            out_ref[seq] = refs[seq][sub]


def beside(query, cotan):
    low = low_half(query.shape)
    even = jnp.where(low, query, swap_halves(cotan)).astype(BF16)
    return even, jnp.where(low, swap_halves(query), cotan).astype(BF16)


def load_rows(source, target, sems, fine):
    return [
        pltpu.make_async_copy(source.at[pl.ds(row, fine), :], target.at[pl.ds(row, fine), :], sems.at[row // fine])
        for row in range(0, target.shape[0], fine)
    ]


def fold_halves(tile):
    half = tile.shape[0] // 2
    low = low_half((half, LANES))
    up, down = tile[:half], tile[half:]
    even = jnp.where(low, up, swap_halves(down)).astype(BF16)
    return even, jnp.where(low, swap_halves(up), down).astype(BF16)


def far_place(sizes, heads):
    me = (lax.axis_index("seq"), lax.axis_index("sub"))
    owner = owner_of(me, steps_of(sizes)[1], sizes) - me[1]
    head = lax.rem(owner, jnp.int32(heads))
    columns = pl.ds(pl.multiple_of(head * HD, LANES), sizes[1] * HD)
    return me[1], lax.div(owner, jnp.int32(heads)), columns


def give_pieces(pieces, sub, out_refs):
    for ahead, out_ref in enumerate(out_refs):
        dest = lax.rem(sub + ahead, jnp.int32(len(pieces)))
        chosen = pieces[0]
        for other in range(1, len(pieces)):
            chosen = jnp.where(dest == other, pieces[other], chosen)
        out_ref[: chosen.shape[0], :] = chosen


def cotan_far_kernel(sizes, groups, rows, heads, assign_ref, cotan_hbm, *refs):
    out_refs, (slot_ref, cotan_ref, sems) = refs[: sizes[1]], refs[sizes[1] :]
    toks = cotan_ref.shape[0]
    sub, group, columns = far_place(sizes, heads)
    load = load_rows(cotan_hbm.at[:, columns], cotan_ref, sems, min(256, toks))
    for copy in load:
        copy.start()
    slot, tallies = slots_of(assign_ref[...], groups, rows)
    slot_ref[...] = slot
    pick = ones_where(iota((rows, toks), 0) + group * rows == slot)
    for copy in load:
        copy.wait()
    pieces = []
    for first in range(0, sizes[1] * HD, LANES):
        pieces += fold_halves(dot(pick, cotan_ref[:, first : first + LANES]))
    give_pieces(pieces, sub, out_refs)
    for out_ref in out_refs:
        out_ref[rows // 2 :, :] = tallies


def query_far_kernel(sizes, groups, rows, heads, slot_ref, tokens_hbm, weight_hbm, *refs):
    out_refs, (tokens_ref, weight_ref, query_ref, sems) = refs[: sizes[1]], refs[sizes[1] :]
    toks = tokens_ref.shape[0]
    fine = min(256, toks)
    sub, group, columns = far_place(sizes, heads)
    weight = load_rows(weight_hbm.at[:, columns], weight_ref, sems.at[0], fine)
    tokens = load_rows(tokens_hbm, tokens_ref, sems.at[1], fine)
    for copy in weight + tokens:
        copy.start()
    pick = ones_where(iota((rows, toks), 0) + group * rows == slot_ref[...])
    for copy in weight:
        copy.wait()
    for index, copy in enumerate(tokens):
        copy.wait()
        where = slice(index * fine, (index + 1) * fine)
        query_ref[where, :] = dot(tokens_ref[where, :], weight_ref[...]).astype(BF16)
    pieces = []
    for first in range(0, sizes[1] * HD, LANES):
        pieces += fold_halves(dot(pick, query_ref[:, first : first + LANES]))
    give_pieces(pieces, sub, out_refs)


def project_query_kernel(sizes, groups, rows, me_ref, slot_ref, assign_ref, tokens_ref, weight_ref, cotan_ref, *rest):
    out_refs, (mixed_ref, sorted_ref) = rest[:-2], rest[-2:]
    toks = tokens_ref.shape[0]
    heads = weight_ref.shape[1] // HD
    step = min(512, toks)
    for first in range(0, toks, step):
        where = slice(first, first + step)
        query, cotan = dot(tokens_ref[where, :], weight_ref[...]), cotan_ref[where, :].astype(F32)
        for pair in range(heads // 2):
            columns = slice(pair * LANES, (pair + 1) * LANES)
            even, odd = beside(query[:, columns], cotan[:, columns])
            mixed_ref[where, 2 * pair * LANES : (2 * pair + 1) * LANES] = even
            mixed_ref[where, (2 * pair + 1) * LANES : (2 * pair + 2) * LANES] = odd
    part = min(512, rows)
    pieces = rows // part

    @pl.loop(0, groups * pieces)
    def _(i):
        group, piece = lax.div(i, jnp.int32(pieces)), lax.rem(i, jnp.int32(pieces))
        first = pl.multiple_of(piece * part, part)
        pick = ones_where(iota((part, toks), 0) + i * part == slot_ref[...])
        sorted_rows = dot(pick, mixed_ref[...]).astype(BF16)
        for head in range(heads):
            sorted_ref[group * heads + head, pl.ds(first, part), :] = sorted_rows[
                :, head * LANES : (head + 1) * LANES
            ]

    member = jnp.where(iota((LANES, toks), 0) == assign_ref[...], 1.0, 0.0).astype(BF16)
    tallies = dot_nt(jnp.ones((COUNT_ROWS, toks), BF16), member).astype(BF16)
    for owner in range(sorted_ref.shape[0]):
        sorted_ref[owner, rows:, :] = tallies
    steps = steps_of(sizes)
    for ahead, out_ref in zip(steps[:1] + steps[1 + sizes[1] :], out_refs):
        out_ref[...] = sorted_ref[owner_of(me_ref, ahead, sizes)]


def project_value_kernel(sizes, groups, rows, me_ref, slot_ref, tokens_ref, weight_ref, *rest):
    out_refs, (turned_ref, unsort_ref, value_ref, sorted_ref) = rest[:-4], rest[-4:]
    toks = tokens_ref.shape[0]
    heads = weight_ref.shape[1] // HD
    step = min(512, toks)

    @pl.loop(0, toks // step)
    def _(i):
        where = pl.ds(pl.multiple_of(i * step, step), step)
        value_ref[where, :] = dot(tokens_ref[where, :], weight_ref[...]).astype(BF16)

    half = rows // 2
    part = min(256, half)
    pieces = half // part

    @pl.loop(0, groups * pieces)
    def _(i):
        group, piece = lax.div(i, jnp.int32(pieces)), lax.rem(i, jnp.int32(pieces))
        first = pl.multiple_of(piece * part, part)
        index = iota((part, toks), 0) + group * rows + first
        upper = dot(ones_where(index == slot_ref[...]), value_ref[...])
        lower = dot(ones_where(index + half == slot_ref[...]), value_ref[...])
        low = low_half((part, LANES))
        for pair in range(heads // 2):
            up = upper[:, pair * LANES : (pair + 1) * LANES]
            down = lower[:, pair * LANES : (pair + 1) * LANES]
            even = jnp.where(low, up, swap_halves(down)).astype(BF16)
            odd = jnp.where(low, swap_halves(up), down).astype(BF16)
            sorted_ref[group * heads + 2 * pair, pl.ds(first, part), :] = even
            sorted_ref[group * heads + 2 * pair + 1, pl.ds(first, part), :] = odd

    hand_out(sorted_ref, out_refs, me_ref, sizes)
    turned = tokens_ref[...].T
    slots = unsort_ref.shape[1]
    part = min(256, slots)
    for i in range(slots // part):
        pick = ones_where(iota((part, toks), 0) + i * part == slot_ref[...])
        unsort_ref[:, i * part : (i + 1) * part] = pick.T
        turned_ref[:, i * part : (i + 1) * part] = dot_nt(turned, pick).astype(BF16)


def score(mixed):
    query = jnp.where(low_half(mixed.shape), mixed.astype(F32) * SCALE, 0.0).astype(BF16)
    return dot_nt(query, mixed)


def softmax_turned(scores):
    shape = scores.shape
    seen = iota(shape, 0) <= iota(shape, 1)
    scores = jnp.where(seen, scores, -jnp.inf)
    raised = jnp.exp(scores - jnp.max(scores, axis=0, keepdims=True))
    return raised * (1.0 / jnp.sum(raised, axis=0, keepdims=True))


def for_each_cluster(counts_ref, me_ref, place_ref, owners, per_group, body):
    for source in range(owners):
        place_ref[source] = 0

    def step(cluster, block):
        runs = []
        total = 0
        base = block * BLOCK_ROWS
        for source in range(owners):
            count = counts_ref[source, me_ref[3] + cluster]
            start = place_ref[source]
            runs.append((source, start, base + total))
            place_ref[source] = start + count
            total = total + count
        body(cluster, block, runs, base + total)
        return block + lax.shift_right_logical(total + (BLOCK_ROWS - 1), jnp.int32(7))

    return lax.fori_loop(0, per_group, step, jnp.int32(LEAD * UNROLL))


def gather_blocks(counts_ref, me_ref, place_ref, owners, per_group, slot_rows, wide_ref, block_ref):
    def body(cluster, block, runs, end):
        for source, start, row in runs:
            block_ref[pl.ds(row, slot_rows), :] = wide_ref[source, pl.ds(start, slot_rows), :]
        block_ref[pl.ds(end, BLOCK_ROWS), :] = jnp.zeros((BLOCK_ROWS, LANES), F32)

    blocks = for_each_cluster(counts_ref, me_ref, place_ref, owners, per_group, body)
    spare = pl.ds(pl.multiple_of(blocks * BLOCK_ROWS, BLOCK_ROWS), GROUP_ROWS)
    block_ref[spare, :] = jnp.zeros((GROUP_ROWS, LANES), F32)
    return blocks


def for_each_group(blocks, stages):
    first, second, third = stages
    groups = lax.div(blocks + (UNROLL - 1), jnp.int32(UNROLL))

    def step(i, carry):
        for slot in range(2):
            group = LEAD + 2 * i + slot
            third(group - 2, slot)
            second(group - 1, 1 - slot)
            first(group, slot)
        return carry

    lax.fori_loop(0, lax.shift_right_logical(groups + 1, jnp.int32(1)), step, 0)


def block_rows(group, ahead):
    return pl.ds(pl.multiple_of((group * UNROLL + ahead) * BLOCK_ROWS, BLOCK_ROWS), BLOCK_ROWS)


def tile_rows(ahead):
    return slice(ahead * BLOCK_ROWS, (ahead + 1) * BLOCK_ROWS)


def value_grad_kernel(sizes, per_group, slot_rows, me_ref, *refs):
    owners = sizes[0] * sizes[1]
    near, came = owners - sizes[1], owners + sizes[1]
    mixed_refs, far_refs = refs[:near], refs[near:came]
    out_refs, rest = refs[came : came + sizes[0]], refs[came + sizes[0] :]
    dense_ref, counts_out_ref, counts_ref, place_ref, wide_ref, block_ref, home_ref = rest[:7]
    score_refs, probs_refs = rest[7:9], rest[9:11]
    half = out_refs[0].shape[1]
    rows = 2 * half
    steps, subs = steps_of(sizes), sizes[1]
    low = low_half((half, LANES))
    for index, ahead in enumerate(steps):
        source = source_of(me_ref, ahead, sizes)
        if 1 <= index <= subs:
            cotan = far_refs[index - 1][:half, :].astype(F32)
            query = far_refs[index - 1 + subs][...].astype(F32)
            tail = far_refs[index - 1][half:, :]
            wide_ref[source, :half, :] = jnp.where(low, query, swap_halves(cotan))
            wide_ref[source, half:rows, :] = jnp.where(low, swap_halves(query), cotan)
        else:
            mixed_ref = mixed_refs[index if index == 0 else index - subs]
            tail = mixed_ref[rows:, :]
            wide_ref[source, :rows, :] = mixed_ref[:rows, :].astype(F32)
        counts_out_ref[pl.ds(source, 1), :] = tail.astype(F32).astype(jnp.int32)[:1, :]
        wide_ref[source, rows:, :] = jnp.zeros((slot_rows, LANES), F32)
    pltpu.sync_copy(counts_out_ref, counts_ref)
    blocks = gather_blocks(counts_ref, me_ref, place_ref, owners, per_group, slot_rows, wide_ref, block_ref)

    def first(group, slot):
        for ahead in range(UNROLL):
            where = block_rows(group, ahead)
            mixed = block_ref[where, :].astype(BF16)
            dense_ref[where, :] = mixed
            score_refs[slot][tile_rows(ahead), :] = score(mixed)

    def second(group, slot):
        for ahead in range(UNROLL):
            tile = tile_rows(ahead)
            probs_refs[slot][tile, :] = softmax_turned(score_refs[slot][tile, :]).astype(BF16)

    def third(group, slot):
        for ahead in range(UNROLL):
            where = block_rows(group, ahead)
            block_ref[where, :] = dot(probs_refs[slot][tile_rows(ahead), :], dense_ref[where, :])

    for_each_group(blocks, (first, second, third))

    def scatter(cluster, block, runs, end):
        for source, start, row in runs:
            wide_ref[source, pl.ds(start, slot_rows), :] = block_ref[pl.ds(row, slot_rows), :]

    for_each_cluster(counts_ref, me_ref, place_ref, owners, per_group, scatter)
    for ahead, out_ref in enumerate(out_refs):
        for sub in range(sizes[1]):
            source = owner_of(me_ref, (ahead, 0), sizes) - me_ref[1] + sub
            up, down = wide_ref[source, :half, :], wide_ref[source, half:rows, :]
            out_ref[sub] = jnp.where(low_half((half, LANES)), swap_halves(up), down).astype(BF16)


def query_grad_kernel(sizes, per_group, slot_rows, me_ref, counts_ref, dense_ref, *refs):
    owners = sizes[0] * sizes[1]
    mid = owners + sizes[0]
    value_refs, out_refs, rest = refs[:owners], refs[owners:mid], refs[mid:]
    place_ref, wide_ref, block_ref, sums_ref, centroid_ref = rest[:5]
    score_refs, grad_probs_refs, both_refs = rest[5:7], rest[7:9], rest[9:11]
    half = value_refs[0].shape[0]
    rows = 2 * half
    for ahead, value_ref in zip(steps_of(sizes), value_refs):
        source = source_of(me_ref, ahead, sizes)
        value = value_ref[...].astype(F32)
        wide_ref[source, :half, :] = swap_halves(value)
        wide_ref[source, half:rows, :] = value
        wide_ref[source, rows:, :] = jnp.zeros((slot_rows, LANES), F32)
    blocks = gather_blocks(counts_ref, me_ref, place_ref, owners, per_group, slot_rows, wide_ref, block_ref)

    def first(group, slot):
        for ahead in range(UNROLL):
            where, tile = block_rows(group, ahead), tile_rows(ahead)
            mixed = dense_ref[where, :]
            value = block_ref[where, :].astype(BF16)
            cotan = jnp.where(low_half(mixed.shape), jnp.zeros_like(mixed), mixed)
            score_refs[slot][tile, :] = score(mixed)
            grad_probs_refs[slot][tile, :] = dot_nt(value, cotan)

    def second(group, slot):
        for ahead in range(UNROLL):
            tile = tile_rows(ahead)
            probs = softmax_turned(score_refs[slot][tile, :])
            grad_probs = grad_probs_refs[slot][tile, :]
            probs_half = probs.astype(BF16).astype(F32)
            row_dot = jnp.sum(probs_half * grad_probs, axis=0, keepdims=True)
            grad_scores = (probs * (grad_probs - row_dot)).astype(BF16).astype(F32)
            both_refs[slot][tile, :] = (grad_scores + grad_scores.T).astype(BF16)

    def third(group, slot):
        for ahead in range(UNROLL):
            where = block_rows(group, ahead)
            grad = dot(both_refs[slot][tile_rows(ahead), :], dense_ref[where, :]) * SCALE
            grad = grad.astype(BF16).astype(F32)
            block_ref[where, :] = grad
            sums_ref[pl.ds(group * UNROLL + ahead, 1), :] = jnp.sum(grad, axis=0, keepdims=True)

    for_each_group(blocks, (first, second, third))
    most = (owners * slot_rows + BLOCK_ROWS - 1) // BLOCK_ROWS

    def scatter(cluster, block, runs, end):
        total = jnp.zeros((1, LANES), F32)
        for ahead in range(most):
            here = block + ahead
            total = total + jnp.where(here * BLOCK_ROWS < end, sums_ref[pl.ds(here, 1), :], 0.0)
        centroid_ref[pl.ds(cluster, 1), :] = total
        for source, start, row in runs:
            wide_ref[source, pl.ds(start, slot_rows), :] = block_ref[pl.ds(row, slot_rows), :]

    for_each_cluster(counts_ref, me_ref, place_ref, owners, per_group, scatter)
    extra = out_refs[0].shape[1] - half
    centroid = jnp.where(
        low_half((extra, LANES)), centroid_ref[:extra, :], swap_halves(centroid_ref[extra:, :])
    ).astype(BF16)
    for ahead, out_ref in enumerate(out_refs):
        for sub in range(sizes[1]):
            source = owner_of(me_ref, (ahead, 0), sizes) - me_ref[1] + sub
            up, down = wide_ref[source, :half, :], wide_ref[source, half:rows, :]
            out_ref[sub, :half, :] = jnp.where(low_half((half, LANES)), up, swap_halves(down)).astype(BF16)
            out_ref[sub, half:, :] = centroid


def unfold(home_ref, out_ref, heads, start, half, finish):
    low = low_half((half, LANES))
    for group in range(home_ref.shape[0] // heads):
        first = group * 2 * half
        for pair in range(heads // 2):
            even = home_ref[group * heads + 2 * pair, start : start + half, :].astype(F32)
            odd = home_ref[group * heads + 2 * pair + 1, start : start + half, :].astype(F32)
            columns = slice(pair * LANES, (pair + 1) * LANES)
            out_ref[first : first + half, columns] = finish(jnp.where(low, even, swap_halves(odd)))
            out_ref[first + half : first + 2 * half, columns] = finish(
                jnp.where(low, swap_halves(even), odd)
            )


def to_half(x):
    return x.astype(BF16)


def bring_home(sizes, heads, pieces, home_ref, rows_ref):
    for source, piece in pieces:
        home_ref[source] = piece
    unfold(home_ref, rows_ref, heads, 0, rows_ref.shape[0] * heads // home_ref.shape[0] // 2, to_half)


def weight_partial(sizes, me_ref, turned_ref, rows_ref, sub_refs):
    piece = turned_ref.shape[0] // (sizes[0] * sizes[1])
    for ahead, sub_ref in enumerate(sub_refs):
        sub = lax.rem(me_ref[1] + ahead, jnp.int32(sizes[1]))
        first = [pl.multiple_of((seq * sizes[1] + sub) * piece, piece) for seq in range(sizes[0])]
        turned = jnp.concatenate([turned_ref[pl.ds(row, piece), :] for row in first], axis=0)
        partial = dot(turned, rows_ref[...]).astype(BF16)
        for seq in range(sizes[0]):
            sub_ref[seq] = partial[seq * piece : (seq + 1) * piece, :]


def input_columns(me_ref, ahead, parts, width):
    columns = width // parts
    dest = lax.rem(me_ref[2] + ahead, jnp.int32(parts))
    return pl.ds(pl.multiple_of(dest * columns, columns), columns)


def value_home_kernel(sizes, heads, parts, me_ref, turned_ref, weight_ref, *refs):
    came = sizes[0] + sizes[1] - 1
    part_refs, refs = refs[:came], refs[came:]
    rows_ref, term_refs, refs = refs[0], refs[1:parts], refs[parts:]
    sub_refs, home_ref = refs[: sizes[1]], refs[sizes[1]]
    bring_home(sizes, heads, arrivals(sizes, me_ref, part_refs), home_ref, rows_ref)
    for k, term_ref in enumerate(term_refs):
        mine = input_columns(me_ref, k + 1, parts, weight_ref.shape[0])
        term_ref[...] = dot_nt(rows_ref[...], weight_ref[mine, :])
    weight_partial(sizes, me_ref, turned_ref, rows_ref, sub_refs)


def query_home_kernel(sizes, heads, factor, parts, me_ref, weight_ref, *refs):
    term_refs, refs = refs[: parts - 1], refs[parts - 1 :]
    came = sizes[0] + sizes[1] - 1
    part_refs, refs = refs[:came], refs[came:]
    out_refs, (rows_ref, centroid_ref, home_ref) = refs[: parts - 1], refs[parts - 1 :]
    bring_home(sizes, heads, arrivals(sizes, me_ref, part_refs), home_ref, rows_ref)
    for k, (term_ref, out_ref) in enumerate(zip(term_refs, out_refs)):
        mine = input_columns(me_ref, k + 1, parts, weight_ref.shape[0])
        step = min(256, rows_ref.shape[0])
        for first in range(0, rows_ref.shape[0], step):
            where = slice(first, first + step)
            out_ref[where, :] = (dot_nt(rows_ref[where, :], weight_ref[mine, :]) + term_ref[where, :]).astype(BF16)
    half = rows_ref.shape[0] * heads // home_ref.shape[0] // 2
    unfold(home_ref, centroid_ref, heads, half, home_ref.shape[1] - half, lambda x: x * factor)


def query_weight_kernel(sizes, me_ref, turned_ref, rows_ref, *sub_refs):
    weight_partial(sizes, me_ref, turned_ref, rows_ref, sub_refs)


def input_own_kernel(parts, me_ref, rows_ref, value_rows_ref, w_query_ref, w_value_ref, out_ref):
    mine = input_columns(me_ref, 0, parts, w_query_ref.shape[0])
    total = dot_nt(rows_ref[...], w_query_ref[mine, :]) + dot_nt(value_rows_ref[...], w_value_ref[mine, :])
    out_ref[...] = total.astype(BF16)


def fold_subs_kernel(me_ref, *refs):
    seqs = refs[0].shape[0]
    terms, out_refs = refs[:-seqs], refs[-seqs:]
    for ahead, out_ref in enumerate(out_refs):
        seq = lax.rem(me_ref[0] + ahead, jnp.int32(seqs))
        total = terms[0][seq].astype(F32)
        for term in terms[1:]:
            total = total + term[seq].astype(F32)
        out_ref[...] = total.astype(BF16)


def sum_kernel(*refs):
    total = refs[0][...].astype(F32)
    for ref in refs[1:-1]:
        total = total + ref[...].astype(F32)
    refs[-1][...] = total.astype(refs[-1].dtype)


def input_sum_kernel(unsort_ref, weight_ref, *refs):
    part_refs, out_ref, weight_out_ref, total_ref = refs[:-3], refs[-3], refs[-2], refs[-1]
    total = part_refs[0][...].astype(F32)
    for part_ref in part_refs[1:]:
        total = total + part_ref[...].astype(F32)
    total_ref[...] = total.astype(BF16)
    step = min(256, out_ref.shape[0])
    for first in range(0, out_ref.shape[0], step):
        where = slice(first, first + step)
        out_ref[where, :] = dot(unsort_ref[where, :], total_ref[...]).astype(BF16)
    weight_out_ref[...] = weight_ref[...]


def call(kernel, outs, inputs, smem=(0,), in_place=(), after=(), scratch=(), flops=0, vmem=24, name=None):
    def body(*refs):
        kernel(*refs[: len(inputs)], *refs[len(inputs) + len(after) :])

    def space(i):
        return pltpu.SMEM if i in smem else pl.ANY if i in in_place else pltpu.VMEM

    specs = [pl.BlockSpec(memory_space=space(i)) for i in range(len(inputs))]
    specs += [pl.BlockSpec(memory_space=pl.ANY)] * len(after)
    moved = sum(x.size * x.dtype.itemsize for x in inputs) + sum(
        x.size * x.dtype.itemsize for x in jax.tree.leaves(outs)
    )
    return pl.pallas_call(
        body,
        out_shape=outs,
        in_specs=specs,
        out_specs=jax.tree.map(lambda _: pl.BlockSpec(memory_space=pltpu.VMEM), outs),
        scratch_shapes=list(scratch),
        compiler_params=pltpu.CompilerParams(vmem_limit_bytes=vmem * 2**20),
        cost_estimate=pl.CostEstimate(flops=flops, bytes_accessed=moved, transcendentals=0),
        name=name,
    )(*inputs, *after)


def send(part, ahead, sizes):
    moves = [
        (seq * sizes[1] + sub, (seq + ahead[0]) % sizes[0] * sizes[1] + (sub + ahead[1]) % sizes[1])
        for seq, sub in steps_of(sizes)
    ]
    return part if ahead == (0, 0) else lax.ppermute(part, OWNERS, moves)


def exchange(parts, sizes):
    return [send(part, ahead, sizes) for ahead, part in zip(steps_of(sizes), parts)]


def shift(part, axis, ahead):
    size = lax.axis_size(axis)
    return lax.ppermute(part, axis, [(i, (i + ahead) % size) for i in range(size)])


def pass_round(parts, axis):
    return [parts[0]] + [shift(parts[ahead], axis, ahead) for ahead in range(1, len(parts))]


def exchange_by_chip(me, parts, sizes, name, after=()):
    came = pass_round(parts, "seq")
    swapped = call(
        functools.partial(swap_kernel, sizes),
        (jax.ShapeDtypeStruct((sizes[0], *parts[0].shape[1:]), BF16),) * (sizes[1] - 1),
        (me, *came),
        after=after,
        name=name,
    )
    return came + [shift(part, "sub", k + 1) for k, part in enumerate(swapped)]


def fold_subs(me, by_sub, name):
    seqs, piece, columns = by_sub[0].shape
    return call(
        fold_subs_kernel,
        (jax.ShapeDtypeStruct((piece, columns), BF16),) * seqs,
        (me, *pass_round(by_sub, "sub")),
        name=name,
    )


def add_up(terms, dtype, name, after=()):
    out = jax.ShapeDtypeStruct(terms[0].shape, dtype)
    return call(sum_kernel, out, tuple(terms), smem=(), after=after, name=name)


def on_device(tokens_in, w_query, w_value, cotangent, assignment):
    sizes = (lax.axis_size("seq"), lax.axis_size("sub"))
    owners = sizes[0] * sizes[1]
    parts = lax.axis_size("head")
    toks, width = tokens_in.shape
    width_dev = cotangent.shape[1]
    heads = width_dev // HD
    slot_rows = 2 * toks // CLUSTERS
    assert owners % heads == 0 and heads % 2 == 0
    groups = owners // heads
    per_group = CLUSTERS // groups
    rows = toks if groups == 1 else per_group * slot_rows
    half = rows // 2
    slots = groups * rows
    columns = width // parts
    capacity = (slot_rows * owners + BLOCK_ROWS - 1) // BLOCK_ROWS * BLOCK_ROWS
    extra = max(per_group // 2, 16)
    shape = jax.ShapeDtypeStruct
    seq, sub = lax.axis_index("seq"), lax.axis_index("sub")
    first = lax.div(seq * sizes[1] + sub, jnp.int32(heads)) * per_group
    me = jnp.stack([seq, sub, lax.axis_index("head"), first]).astype(jnp.int32)

    def several(count, *dims):
        return (shape(dims, BF16),) * count

    assign_row = assignment.reshape(1, toks)
    subs = sizes[1]
    far_columns = subs * HD
    loads = max(toks, width) // min(256, toks)
    *far_cotan, slot_row = call(
        functools.partial(cotan_far_kernel, sizes, groups, rows, heads),
        several(subs, half + COUNT_ROWS, LANES) + (shape((1, toks), jnp.int32),),
        (assign_row, cotangent),
        smem=(),
        in_place=(1,),
        scratch=[pltpu.VMEM((toks, far_columns), BF16), pltpu.SemaphoreType.DMA((loads,))],
        flops=2 * rows * toks * far_columns,
        vmem=60,
        name="cotan_far",
    )
    far_query = call(
        functools.partial(query_far_kernel, sizes, groups, rows, heads),
        several(subs, half, LANES),
        (slot_row, tokens_in, w_query),
        smem=(),
        in_place=(1, 2),
        scratch=[
            pltpu.VMEM((toks, width), BF16),
            pltpu.VMEM((width, far_columns), BF16),
            pltpu.VMEM((toks, far_columns), BF16),
            pltpu.SemaphoreType.DMA((2, loads)),
        ],
        flops=2 * toks * width * far_columns + 2 * rows * toks * far_columns,
        vmem=60,
        name="query_far",
    )
    steps = steps_of(sizes)
    far_cotan = [send(part, ahead, sizes) for ahead, part in zip(steps[1:], far_cotan)]
    raw_query = far_query
    far_query = [send(part, ahead, sizes) for ahead, part in zip(steps[1:], far_query)]
    own_mixed, *near_mixed = call(
        functools.partial(project_query_kernel, sizes, groups, rows),
        several(owners - sizes[1], rows + COUNT_ROWS, LANES),
        (me, slot_row, assign_row, tokens_in, w_query, cotangent),
        after=raw_query[:1],
        scratch=[pltpu.VMEM((toks, 2 * width_dev), BF16), pltpu.VMEM((owners, rows + COUNT_ROWS, LANES), BF16)],
        flops=2 * toks * width * width_dev + 4 * slots * toks * width_dev,
        name="project_query",
    )
    near_mixed = [send(part, ahead, sizes) for ahead, part in zip(steps[1 + subs :], near_mixed)]
    got_mixed = [own_mixed, *far_query, *near_mixed]
    *send_value, turned, unsort = call(
        functools.partial(project_value_kernel, sizes, groups, rows),
        several(owners, half, LANES) + several(1, width, slots) + several(1, toks, slots),
        (me, slot_row, tokens_in, w_value),
        after=[own_mixed, *far_cotan],
        scratch=[pltpu.VMEM((toks, width_dev), BF16), pltpu.VMEM((owners, half, LANES), BF16)],
        flops=2 * toks * width * width_dev + 2 * slots * toks * width_dev,
        name="project_value",
    )
    behind = [0, *range(3, owners), 2, 1][:owners]
    send_value = [lax.optimization_barrier((part, got_mixed[k]))[0] for part, k in zip(send_value, behind)]
    got_value = exchange(send_value, sizes)
    blocks = per_group * capacity // BLOCK_ROWS
    held = blocks + (LEAD + 4) * UNROLL
    block_flops = 2 * BLOCK_ROWS * BLOCK_ROWS * LANES
    tall = pltpu.VMEM((owners, rows + slot_rows, LANES), F32)
    dense_rows = pltpu.VMEM((held * BLOCK_ROWS, LANES), F32)
    group_f32 = pltpu.VMEM((GROUP_ROWS, BLOCK_ROWS), F32)
    group_b16 = pltpu.VMEM((GROUP_ROWS, BLOCK_ROWS), BF16)
    place = pltpu.SMEM((owners,), jnp.int32)
    *back_value, dense, counts = call(
        functools.partial(value_grad_kernel, sizes, per_group, slot_rows),
        several(sizes[0], sizes[1], half, LANES)
        + several(1, held * BLOCK_ROWS, LANES)
        + (shape((owners, LANES), jnp.int32),),
        (me, own_mixed, *near_mixed, *far_cotan, *far_query),
        after=[unsort],
        scratch=[pltpu.SMEM((owners, LANES), jnp.int32), place, tall, dense_rows, tall]
        + [group_f32] * 2
        + [group_b16] * 2,
        flops=4 * blocks * block_flops,
        vmem=48,
        name="value_grad",
    )
    back_value, _ = lax.optimization_barrier((back_value, got_value[1:]))
    back_query = call(
        functools.partial(query_grad_kernel, sizes, per_group, slot_rows),
        several(sizes[0], sizes[1], half + extra, LANES),
        (me, counts, dense, *got_value),
        smem=(0, 1),
        scratch=[place, tall, dense_rows, pltpu.VMEM((held, LANES), F32), pltpu.VMEM((2 * extra, LANES), F32)]
        + [group_f32] * 4
        + [group_b16] * 2,
        flops=6 * blocks * block_flops,
        vmem=48,
        name="query_grad",
    )
    home_query = exchange_by_chip(me, back_query, sizes, "swap_query")
    home_value = exchange_by_chip(me, back_value, sizes, "swap_value", back_query[:1])
    weight_flops = 2 * slots * width * width_dev
    home_flops = weight_flops // parts * (parts - 1)
    piece = width // owners
    sub_shapes = several(sizes[1], sizes[0], piece, width_dev)
    value_rows, *refs = call(
        functools.partial(value_home_kernel, sizes, heads, parts),
        several(1, slots, width_dev) + (shape((slots, columns), F32),) * (parts - 1) + sub_shapes,
        (me, turned, w_value, *home_value),
        scratch=[pltpu.VMEM((owners, half, LANES), BF16)],
        flops=weight_flops + home_flops,
        name="value_home",
    )
    value_terms, value_weight = refs[: parts - 1], refs[parts - 1 :]
    value_weight = fold_subs(me, value_weight, "value_subs")
    *partials, query_rows, centroid_grad = call(
        functools.partial(query_home_kernel, sizes, heads, (CLUSTERS / (toks * owners)) ** 0.5, parts),
        several(parts - 1, slots, columns)
        + several(1, slots, width_dev)
        + (shape((groups * 2 * extra, width_dev), F32),),
        (me, w_query, *value_terms, *home_query),
        scratch=[pltpu.VMEM((owners, half + extra, LANES), BF16)],
        flops=home_flops,
        name="query_home",
    )
    arrived = [shift(partial, "head", k + 1) for k, partial in enumerate(partials)]
    value_weight, _ = lax.optimization_barrier((value_weight, home_query))
    value_weight = pass_round(value_weight, "seq")
    query_weight = call(
        functools.partial(query_weight_kernel, sizes),
        sub_shapes,
        (me, turned, query_rows),
        flops=weight_flops,
        name="query_weight",
    )
    query_weight = fold_subs(me, query_weight, "query_subs")
    own = call(
        functools.partial(input_own_kernel, parts),
        shape((slots, columns), BF16),
        (me, query_rows, value_rows, w_query, w_value),
        after=query_weight[:1],
        flops=weight_flops * 2 // parts,
        name="input_own",
    )
    query_weight = pass_round(query_weight, "seq")
    grad_wv = add_up(value_weight, F32, "value_sum", [own])
    grad_input, own_weight = call(
        input_sum_kernel,
        several(1, toks, columns) + several(1, piece, width_dev),
        (unsort, query_weight[0], own, *arrived),
        smem=(),
        scratch=[pltpu.VMEM((slots, columns), BF16)],
        flops=2 * toks * slots * columns,
        name="input_sum",
    )
    grad_wq = add_up([own_weight, *query_weight[1:]], F32, "query_sum")
    if groups > 1:
        centroid_grad = centroid_grad.reshape(groups, 2 * extra, width_dev)[:, :per_group]
        centroid_grad = centroid_grad.reshape(CLUSTERS, width_dev)
    return (grad_input, grad_wq, grad_wv, centroid_grad)


def solution(mesh):
    return jax.shard_map(
        on_device,
        mesh=mesh,
        in_specs=(
            P(("grp", "seq", "sub"), None),
            P(None, "head"),
            P(None, "head"),
            P(("grp", "seq", "sub"), "head"),
            P(("grp", "seq", "sub"), None),
        ),
        out_specs=(
            P(("grp", "seq", "sub"), "head"),
            P(("grp", "seq", "sub"), "head"),
            P(("grp", "seq", "sub"), "head"),
            P("grp", "head"),
        ),
        check_vma=False,
    )
```

```python
import functools

import jax
import jax.numpy as jnp
from jax import lax
from jax.experimental import pallas as pl
from jax.experimental.pallas import tpu as pltpu
from jax.sharding import PartitionSpec as P

HD = 64
CLUSTERS = 64
BLOCK_ROWS = 128
LANES = 128
UNROLL = 4
COUNT_ROWS = 16
SCALE = 0.5 * HD ** (-0.5)
F32 = jnp.float32
BF16 = jnp.bfloat16
OWNERS = ("seq", "sub")
GROUP_ROWS = UNROLL * BLOCK_ROWS
LEAD = 2


def iota(shape, dim):
    return lax.broadcasted_iota(jnp.int32, shape, dim)


def low_half(shape):
    return iota(shape, 1) < HD


def swap_halves(tile):
    return pltpu.roll(tile, HD, 1)


def dot(a, b):
    return jnp.dot(a, b, preferred_element_type=F32)


def dot_nt(a, b):
    return lax.dot_general(a, b, (((1,), (1,)), ((), ())), preferred_element_type=F32)


def ones_where(condition):
    return jnp.where(condition, 1.0, 0.0).astype(BF16)


def owner_of(me_ref, ahead, sizes):
    seq = lax.rem(me_ref[0] + ahead[0], jnp.int32(sizes[0]))
    sub = lax.rem(me_ref[1] + ahead[1], jnp.int32(sizes[1]))
    return seq * sizes[1] + sub


def source_of(me_ref, ahead, sizes):
    return owner_of(me_ref, ((sizes[0] - ahead[0]) % sizes[0], (sizes[1] - ahead[1]) % sizes[1]), sizes)


def steps_of(sizes):
    far = sorted(range(1, sizes[0]), key=lambda seq: -min(seq, sizes[0] - seq))
    subs = range(sizes[1])
    return [(0, 0)] + [(seq, sub) for seq in far for sub in subs] + [(0, sub) for sub in subs if sub]


def hand_out(by_owner_ref, out_refs, me_ref, sizes):
    for ahead, out_ref in zip(steps_of(sizes), out_refs):
        out_ref[...] = by_owner_ref[owner_of(me_ref, ahead, sizes)]


def slots_of(assign, groups, rows):
    toks = assign.shape[1]
    per_group = CLUSTERS // groups
    member = jnp.where(iota((CLUSTERS, toks), 0) == assign, 1.0, 0.0)
    member_b = member.astype(BF16)
    upto = ones_where(iota((LANES, LANES), 0) <= iota((LANES, LANES), 1))
    counts = jnp.zeros((CLUSTERS, 1), F32)
    running = []
    for first in range(0, toks, LANES):
        within = dot(member_b[:, first : first + LANES], upto)
        running.append(within + counts)
        counts = counts + within[:, LANES - 1 :]
    running = jnp.concatenate(running, axis=1)
    here, other = iota((CLUSTERS, CLUSTERS), 0), iota((CLUSTERS, CLUSTERS), 1)
    group_of = lambda index: lax.div(index, jnp.int32(per_group))
    earlier = ones_where((other < here) & (group_of(other) == group_of(here)))
    base = dot(earlier, jnp.broadcast_to(counts, (CLUSTERS, LANES)).astype(BF16))[:, :1]
    base = base + (group_of(iota((CLUSTERS, 1), 0)) * rows).astype(F32)
    slot = jnp.sum(member * (running - 1.0 + base), axis=0, keepdims=True).astype(jnp.int32)
    spread = jnp.concatenate([member_b, jnp.zeros((LANES - CLUSTERS, toks), BF16)], axis=0)
    return slot, dot_nt(jnp.ones((COUNT_ROWS, toks), BF16), spread).astype(BF16)


def arrivals(sizes, me_ref, refs):
    seqs, subs = sizes
    for ahead in steps_of(sizes):
        if ahead[1] == 0:
            piece = refs[ahead[0]][me_ref[1]]
        else:
            piece = refs[seqs + ahead[1] - 1][ahead[0]]
        yield source_of(me_ref, ahead, sizes), piece


def swap_kernel(sizes, me_ref, *refs):
    for k, out_ref in enumerate(refs[sizes[0] :]):
        sub = lax.rem(me_ref[1] + (k + 1), jnp.int32(sizes[1]))
        for seq in range(sizes[0]):
            out_ref[seq] = refs[seq][sub]


def beside(query, cotan):
    low = low_half(query.shape)
    even = jnp.where(low, query, swap_halves(cotan)).astype(BF16)
    return even, jnp.where(low, swap_halves(query), cotan).astype(BF16)


def load_rows(source, target, sems, fine):
    return [
        pltpu.make_async_copy(source.at[pl.ds(row, fine), :], target.at[pl.ds(row, fine), :], sems.at[row // fine])
        for row in range(0, target.shape[0], fine)
    ]


def project_far_kernel(sizes, groups, rows, heads, assign_ref, tokens_hbm, weight_hbm, cotan_hbm, *refs):
    out_refs, refs = refs[: sizes[1]], refs[sizes[1] :]
    slot_ref, tokens_ref, weight_ref, cotan_ref, mixed_ref, sems = refs
    toks = tokens_ref.shape[0]
    fine = min(256, toks)
    me = (lax.axis_index("seq"), lax.axis_index("sub"))
    owner = owner_of(me, steps_of(sizes)[1], sizes) - me[1]
    group, head = lax.div(owner, jnp.int32(heads)), lax.rem(owner, jnp.int32(heads))
    columns = pl.ds(pl.multiple_of(head * HD, LANES), sizes[1] * HD)
    loads = [
        load_rows(source, target, sems.at[kind], fine)
        for kind, (source, target) in enumerate(
            ((weight_hbm.at[:, columns], weight_ref), (tokens_hbm, tokens_ref), (cotan_hbm.at[:, columns], cotan_ref))
        )
    ]
    for load in loads:
        for copy in load:
            copy.start()
    slot, tallies = slots_of(assign_ref[...], groups, rows)
    slot_ref[...] = slot
    pick = ones_where(iota((rows, toks), 0) + group * rows == slot)
    for copy in loads[0] + loads[2]:
        copy.wait()
    step = fine
    for first in range(0, toks, step):
        for copy in loads[1][first // fine : (first + step) // fine]:
            copy.wait()
        where = slice(first, first + step)
        query, cotan = dot(tokens_ref[where, :], weight_ref[...]), cotan_ref[where, :].astype(F32)
        for pair in range(sizes[1] // 2):
            pair_columns = slice(pair * LANES, (pair + 1) * LANES)
            even, odd = beside(query[:, pair_columns], cotan[:, pair_columns])
            mixed_ref[where, 2 * pair * LANES : (2 * pair + 1) * LANES] = even
            mixed_ref[where, (2 * pair + 1) * LANES : (2 * pair + 2) * LANES] = odd
    part = min(256, rows)
    for first in range(0, rows, part):
        where = slice(first, first + part)
        in_order = dot(pick[where, :], mixed_ref[...]).astype(BF16)
        for ahead, out_ref in enumerate(out_refs):
            sub = lax.rem(me[1] + ahead, jnp.int32(sizes[1]))
            piece = in_order[:, :LANES]
            for other in range(1, sizes[1]):
                piece = jnp.where(sub == other, in_order[:, other * LANES : (other + 1) * LANES], piece)
            out_ref[where, :] = piece
    for out_ref in out_refs:
        out_ref[rows:, :] = tallies


def project_query_kernel(sizes, groups, rows, me_ref, slot_ref, assign_ref, tokens_ref, weight_ref, cotan_ref, *rest):
    out_refs, (mixed_ref, sorted_ref) = rest[:-2], rest[-2:]
    toks = tokens_ref.shape[0]
    heads = weight_ref.shape[1] // HD
    step = min(512, toks)
    for first in range(0, toks, step):
        where = slice(first, first + step)
        query, cotan = dot(tokens_ref[where, :], weight_ref[...]), cotan_ref[where, :].astype(F32)
        for pair in range(heads // 2):
            columns = slice(pair * LANES, (pair + 1) * LANES)
            even, odd = beside(query[:, columns], cotan[:, columns])
            mixed_ref[where, 2 * pair * LANES : (2 * pair + 1) * LANES] = even
            mixed_ref[where, (2 * pair + 1) * LANES : (2 * pair + 2) * LANES] = odd
    part = min(512, rows)
    pieces = rows // part

    @pl.loop(0, groups * pieces)
    def _(i):
        group, piece = lax.div(i, jnp.int32(pieces)), lax.rem(i, jnp.int32(pieces))
        first = pl.multiple_of(piece * part, part)
        pick = ones_where(iota((part, toks), 0) + i * part == slot_ref[...])
        sorted_rows = dot(pick, mixed_ref[...]).astype(BF16)
        for head in range(heads):
            sorted_ref[group * heads + head, pl.ds(first, part), :] = sorted_rows[
                :, head * LANES : (head + 1) * LANES
            ]

    member = jnp.where(iota((LANES, toks), 0) == assign_ref[...], 1.0, 0.0).astype(BF16)
    tallies = dot_nt(jnp.ones((COUNT_ROWS, toks), BF16), member).astype(BF16)
    for owner in range(sorted_ref.shape[0]):
        sorted_ref[owner, rows:, :] = tallies
    steps = steps_of(sizes)
    for ahead, out_ref in zip(steps[:1] + steps[1 + sizes[1] :], out_refs):
        out_ref[...] = sorted_ref[owner_of(me_ref, ahead, sizes)]


def project_value_kernel(sizes, groups, rows, me_ref, slot_ref, tokens_ref, weight_ref, *rest):
    out_refs, (turned_ref, unsort_ref, value_ref, sorted_ref) = rest[:-4], rest[-4:]
    toks = tokens_ref.shape[0]
    heads = weight_ref.shape[1] // HD
    step = min(512, toks)

    @pl.loop(0, toks // step)
    def _(i):
        where = pl.ds(pl.multiple_of(i * step, step), step)
        value_ref[where, :] = dot(tokens_ref[where, :], weight_ref[...]).astype(BF16)

    half = rows // 2
    part = min(256, half)
    pieces = half // part

    @pl.loop(0, groups * pieces)
    def _(i):
        group, piece = lax.div(i, jnp.int32(pieces)), lax.rem(i, jnp.int32(pieces))
        first = pl.multiple_of(piece * part, part)
        index = iota((part, toks), 0) + group * rows + first
        upper = dot(ones_where(index == slot_ref[...]), value_ref[...])
        lower = dot(ones_where(index + half == slot_ref[...]), value_ref[...])
        low = low_half((part, LANES))
        for pair in range(heads // 2):
            up = upper[:, pair * LANES : (pair + 1) * LANES]
            down = lower[:, pair * LANES : (pair + 1) * LANES]
            even = jnp.where(low, up, swap_halves(down)).astype(BF16)
            odd = jnp.where(low, swap_halves(up), down).astype(BF16)
            sorted_ref[group * heads + 2 * pair, pl.ds(first, part), :] = even
            sorted_ref[group * heads + 2 * pair + 1, pl.ds(first, part), :] = odd

    hand_out(sorted_ref, out_refs, me_ref, sizes)
    turned = tokens_ref[...].T
    slots = unsort_ref.shape[1]
    part = min(256, slots)
    for i in range(slots // part):
        pick = ones_where(iota((part, toks), 0) + i * part == slot_ref[...])
        unsort_ref[:, i * part : (i + 1) * part] = pick.T
        turned_ref[:, i * part : (i + 1) * part] = dot_nt(turned, pick).astype(BF16)


def score(mixed):
    query = jnp.where(low_half(mixed.shape), mixed.astype(F32) * SCALE, 0.0).astype(BF16)
    return dot_nt(query, mixed)


def softmax_turned(scores):
    shape = scores.shape
    seen = iota(shape, 0) <= iota(shape, 1)
    scores = jnp.where(seen, scores, -jnp.inf)
    raised = jnp.exp(scores - jnp.max(scores, axis=0, keepdims=True))
    return raised * (1.0 / jnp.sum(raised, axis=0, keepdims=True))


def for_each_cluster(counts_ref, me_ref, place_ref, owners, per_group, body):
    for source in range(owners):
        place_ref[source] = 0

    def step(cluster, block):
        runs = []
        total = 0
        base = block * BLOCK_ROWS
        for source in range(owners):
            count = counts_ref[source, me_ref[3] + cluster]
            start = place_ref[source]
            runs.append((source, start, base + total))
            place_ref[source] = start + count
            total = total + count
        body(cluster, block, runs, base + total)
        return block + lax.shift_right_logical(total + (BLOCK_ROWS - 1), jnp.int32(7))

    return lax.fori_loop(0, per_group, step, jnp.int32(LEAD * UNROLL))


def gather_blocks(counts_ref, me_ref, place_ref, owners, per_group, slot_rows, wide_ref, block_ref):
    def body(cluster, block, runs, end):
        for source, start, row in runs:
            block_ref[pl.ds(row, slot_rows), :] = wide_ref[source, pl.ds(start, slot_rows), :]
        block_ref[pl.ds(end, BLOCK_ROWS), :] = jnp.zeros((BLOCK_ROWS, LANES), F32)

    blocks = for_each_cluster(counts_ref, me_ref, place_ref, owners, per_group, body)
    spare = pl.ds(pl.multiple_of(blocks * BLOCK_ROWS, BLOCK_ROWS), GROUP_ROWS)
    block_ref[spare, :] = jnp.zeros((GROUP_ROWS, LANES), F32)
    return blocks


def for_each_group(blocks, stages):
    first, second, third = stages
    groups = lax.div(blocks + (UNROLL - 1), jnp.int32(UNROLL))

    def step(i, carry):
        for slot in range(2):
            group = LEAD + 2 * i + slot
            third(group - 2, slot)
            second(group - 1, 1 - slot)
            first(group, slot)
        return carry

    lax.fori_loop(0, lax.shift_right_logical(groups + 1, jnp.int32(1)), step, 0)


def block_rows(group, ahead):
    return pl.ds(pl.multiple_of((group * UNROLL + ahead) * BLOCK_ROWS, BLOCK_ROWS), BLOCK_ROWS)


def tile_rows(ahead):
    return slice(ahead * BLOCK_ROWS, (ahead + 1) * BLOCK_ROWS)


def value_grad_kernel(sizes, per_group, slot_rows, me_ref, *refs):
    owners = sizes[0] * sizes[1]
    mixed_refs, out_refs, rest = refs[:owners], refs[owners : owners + sizes[0]], refs[owners + sizes[0] :]
    dense_ref, counts_out_ref, counts_ref, place_ref, wide_ref, block_ref, home_ref = rest[:7]
    score_refs, probs_refs = rest[7:9], rest[9:11]
    half = out_refs[0].shape[1]
    rows = 2 * half
    for ahead, mixed_ref in zip(steps_of(sizes), mixed_refs):
        source = source_of(me_ref, ahead, sizes)
        tail = mixed_ref[rows:, :].astype(F32).astype(jnp.int32)
        counts_out_ref[pl.ds(source, 1), :] = tail[:1, :]
        wide_ref[source, :rows, :] = mixed_ref[:rows, :].astype(F32)
        wide_ref[source, rows:, :] = jnp.zeros((slot_rows, LANES), F32)
    pltpu.sync_copy(counts_out_ref, counts_ref)
    blocks = gather_blocks(counts_ref, me_ref, place_ref, owners, per_group, slot_rows, wide_ref, block_ref)

    def first(group, slot):
        for ahead in range(UNROLL):
            where = block_rows(group, ahead)
            mixed = block_ref[where, :].astype(BF16)
            dense_ref[where, :] = mixed
            score_refs[slot][tile_rows(ahead), :] = score(mixed)

    def second(group, slot):
        for ahead in range(UNROLL):
            tile = tile_rows(ahead)
            probs_refs[slot][tile, :] = softmax_turned(score_refs[slot][tile, :]).astype(BF16)

    def third(group, slot):
        for ahead in range(UNROLL):
            where = block_rows(group, ahead)
            block_ref[where, :] = dot(probs_refs[slot][tile_rows(ahead), :], dense_ref[where, :])

    for_each_group(blocks, (first, second, third))

    def scatter(cluster, block, runs, end):
        for source, start, row in runs:
            wide_ref[source, pl.ds(start, slot_rows), :] = block_ref[pl.ds(row, slot_rows), :]

    for_each_cluster(counts_ref, me_ref, place_ref, owners, per_group, scatter)
    for ahead, out_ref in enumerate(out_refs):
        for sub in range(sizes[1]):
            source = owner_of(me_ref, (ahead, 0), sizes) - me_ref[1] + sub
            up, down = wide_ref[source, :half, :], wide_ref[source, half:rows, :]
            out_ref[sub] = jnp.where(low_half((half, LANES)), swap_halves(up), down).astype(BF16)


def query_grad_kernel(sizes, per_group, slot_rows, me_ref, counts_ref, dense_ref, *refs):
    owners = sizes[0] * sizes[1]
    mid = owners + sizes[0]
    value_refs, out_refs, rest = refs[:owners], refs[owners:mid], refs[mid:]
    place_ref, wide_ref, block_ref, sums_ref, centroid_ref = rest[:5]
    score_refs, grad_probs_refs, both_refs = rest[5:7], rest[7:9], rest[9:11]
    half = value_refs[0].shape[0]
    rows = 2 * half
    for ahead, value_ref in zip(steps_of(sizes), value_refs):
        source = source_of(me_ref, ahead, sizes)
        value = value_ref[...].astype(F32)
        wide_ref[source, :half, :] = swap_halves(value)
        wide_ref[source, half:rows, :] = value
        wide_ref[source, rows:, :] = jnp.zeros((slot_rows, LANES), F32)
    blocks = gather_blocks(counts_ref, me_ref, place_ref, owners, per_group, slot_rows, wide_ref, block_ref)

    def first(group, slot):
        for ahead in range(UNROLL):
            where, tile = block_rows(group, ahead), tile_rows(ahead)
            mixed = dense_ref[where, :]
            value = block_ref[where, :].astype(BF16)
            cotan = jnp.where(low_half(mixed.shape), jnp.zeros_like(mixed), mixed)
            score_refs[slot][tile, :] = score(mixed)
            grad_probs_refs[slot][tile, :] = dot_nt(value, cotan)

    def second(group, slot):
        for ahead in range(UNROLL):
            tile = tile_rows(ahead)
            probs = softmax_turned(score_refs[slot][tile, :])
            grad_probs = grad_probs_refs[slot][tile, :]
            probs_half = probs.astype(BF16).astype(F32)
            row_dot = jnp.sum(probs_half * grad_probs, axis=0, keepdims=True)
            grad_scores = (probs * (grad_probs - row_dot)).astype(BF16).astype(F32)
            both_refs[slot][tile, :] = (grad_scores + grad_scores.T).astype(BF16)

    def third(group, slot):
        for ahead in range(UNROLL):
            where = block_rows(group, ahead)
            grad = dot(both_refs[slot][tile_rows(ahead), :], dense_ref[where, :]) * SCALE
            grad = grad.astype(BF16).astype(F32)
            block_ref[where, :] = grad
            sums_ref[pl.ds(group * UNROLL + ahead, 1), :] = jnp.sum(grad, axis=0, keepdims=True)

    for_each_group(blocks, (first, second, third))
    most = (owners * slot_rows + BLOCK_ROWS - 1) // BLOCK_ROWS

    def scatter(cluster, block, runs, end):
        total = jnp.zeros((1, LANES), F32)
        for ahead in range(most):
            here = block + ahead
            total = total + jnp.where(here * BLOCK_ROWS < end, sums_ref[pl.ds(here, 1), :], 0.0)
        centroid_ref[pl.ds(cluster, 1), :] = total
        for source, start, row in runs:
            wide_ref[source, pl.ds(start, slot_rows), :] = block_ref[pl.ds(row, slot_rows), :]

    for_each_cluster(counts_ref, me_ref, place_ref, owners, per_group, scatter)
    extra = out_refs[0].shape[1] - half
    centroid = jnp.where(
        low_half((extra, LANES)), centroid_ref[:extra, :], swap_halves(centroid_ref[extra:, :])
    ).astype(BF16)
    for ahead, out_ref in enumerate(out_refs):
        for sub in range(sizes[1]):
            source = owner_of(me_ref, (ahead, 0), sizes) - me_ref[1] + sub
            up, down = wide_ref[source, :half, :], wide_ref[source, half:rows, :]
            out_ref[sub, :half, :] = jnp.where(low_half((half, LANES)), up, swap_halves(down)).astype(BF16)
            out_ref[sub, half:, :] = centroid


def unfold(home_ref, out_ref, heads, start, half, finish):
    low = low_half((half, LANES))
    for group in range(home_ref.shape[0] // heads):
        first = group * 2 * half
        for pair in range(heads // 2):
            even = home_ref[group * heads + 2 * pair, start : start + half, :].astype(F32)
            odd = home_ref[group * heads + 2 * pair + 1, start : start + half, :].astype(F32)
            columns = slice(pair * LANES, (pair + 1) * LANES)
            out_ref[first : first + half, columns] = finish(jnp.where(low, even, swap_halves(odd)))
            out_ref[first + half : first + 2 * half, columns] = finish(
                jnp.where(low, swap_halves(even), odd)
            )


def to_half(x):
    return x.astype(BF16)


def bring_home(sizes, heads, pieces, home_ref, rows_ref):
    for source, piece in pieces:
        home_ref[source] = piece
    unfold(home_ref, rows_ref, heads, 0, rows_ref.shape[0] * heads // home_ref.shape[0] // 2, to_half)


def weight_partial(sizes, me_ref, turned_ref, rows_ref, sub_refs):
    piece = turned_ref.shape[0] // (sizes[0] * sizes[1])
    for ahead, sub_ref in enumerate(sub_refs):
        sub = lax.rem(me_ref[1] + ahead, jnp.int32(sizes[1]))
        first = [pl.multiple_of((seq * sizes[1] + sub) * piece, piece) for seq in range(sizes[0])]
        turned = jnp.concatenate([turned_ref[pl.ds(row, piece), :] for row in first], axis=0)
        partial = dot(turned, rows_ref[...]).astype(BF16)
        for seq in range(sizes[0]):
            sub_ref[seq] = partial[seq * piece : (seq + 1) * piece, :]


def input_columns(me_ref, ahead, parts, width):
    columns = width // parts
    dest = lax.rem(me_ref[2] + ahead, jnp.int32(parts))
    return pl.ds(pl.multiple_of(dest * columns, columns), columns)


def value_home_kernel(sizes, heads, parts, me_ref, turned_ref, weight_ref, *refs):
    came = sizes[0] + sizes[1] - 1
    part_refs, refs = refs[:came], refs[came:]
    rows_ref, term_refs, refs = refs[0], refs[1:parts], refs[parts:]
    sub_refs, home_ref = refs[: sizes[1]], refs[sizes[1]]
    bring_home(sizes, heads, arrivals(sizes, me_ref, part_refs), home_ref, rows_ref)
    for k, term_ref in enumerate(term_refs):
        mine = input_columns(me_ref, k + 1, parts, weight_ref.shape[0])
        term_ref[...] = dot_nt(rows_ref[...], weight_ref[mine, :])
    weight_partial(sizes, me_ref, turned_ref, rows_ref, sub_refs)


def query_home_kernel(sizes, heads, factor, parts, me_ref, weight_ref, *refs):
    term_refs, refs = refs[: parts - 1], refs[parts - 1 :]
    came = sizes[0] + sizes[1] - 1
    part_refs, refs = refs[:came], refs[came:]
    out_refs, (rows_ref, centroid_ref, home_ref) = refs[: parts - 1], refs[parts - 1 :]
    bring_home(sizes, heads, arrivals(sizes, me_ref, part_refs), home_ref, rows_ref)
    for k, (term_ref, out_ref) in enumerate(zip(term_refs, out_refs)):
        mine = input_columns(me_ref, k + 1, parts, weight_ref.shape[0])
        step = min(256, rows_ref.shape[0])
        for first in range(0, rows_ref.shape[0], step):
            where = slice(first, first + step)
            out_ref[where, :] = (dot_nt(rows_ref[where, :], weight_ref[mine, :]) + term_ref[where, :]).astype(BF16)
    half = rows_ref.shape[0] * heads // home_ref.shape[0] // 2
    unfold(home_ref, centroid_ref, heads, half, home_ref.shape[1] - half, lambda x: x * factor)


def query_weight_kernel(sizes, me_ref, turned_ref, rows_ref, *refs):
    term_refs, sub_refs, seq_refs = refs[: sizes[1]], refs[sizes[1] : 2 * sizes[1]], refs[2 * sizes[1] :]
    fold_subs_kernel(me_ref, *term_refs, *seq_refs)
    weight_partial(sizes, me_ref, turned_ref, rows_ref, sub_refs)


def input_own_kernel(parts, me_ref, rows_ref, value_rows_ref, w_query_ref, w_value_ref, out_ref):
    mine = input_columns(me_ref, 0, parts, w_query_ref.shape[0])
    total = dot_nt(rows_ref[...], w_query_ref[mine, :]) + dot_nt(value_rows_ref[...], w_value_ref[mine, :])
    out_ref[...] = total.astype(BF16)


def fold_subs_kernel(me_ref, *refs):
    seqs = refs[0].shape[0]
    terms, out_refs = refs[:-seqs], refs[-seqs:]
    for ahead, out_ref in enumerate(out_refs):
        seq = lax.rem(me_ref[0] + ahead, jnp.int32(seqs))
        total = terms[0][seq].astype(F32)
        for term in terms[1:]:
            total = total + term[seq].astype(F32)
        out_ref[...] = total.astype(BF16)


def sum_kernel(*refs):
    total = refs[0][...].astype(F32)
    for ref in refs[1:-1]:
        total = total + ref[...].astype(F32)
    refs[-1][...] = total.astype(refs[-1].dtype)


def input_sum_kernel(unsort_ref, weight_ref, *refs):
    part_refs, out_ref, weight_out_ref, total_ref = refs[:-3], refs[-3], refs[-2], refs[-1]
    total = part_refs[0][...].astype(F32)
    for part_ref in part_refs[1:]:
        total = total + part_ref[...].astype(F32)
    total_ref[...] = total.astype(BF16)
    step = min(256, out_ref.shape[0])
    for first in range(0, out_ref.shape[0], step):
        where = slice(first, first + step)
        out_ref[where, :] = dot(unsort_ref[where, :], total_ref[...]).astype(BF16)
    weight_out_ref[...] = weight_ref[...]


def call(kernel, outs, inputs, smem=(0,), in_place=(), after=(), scratch=(), flops=0, vmem=24, name=None):
    def body(*refs):
        kernel(*refs[: len(inputs)], *refs[len(inputs) + len(after) :])

    def space(i):
        return pltpu.SMEM if i in smem else pl.ANY if i in in_place else pltpu.VMEM

    specs = [pl.BlockSpec(memory_space=space(i)) for i in range(len(inputs))]
    specs += [pl.BlockSpec(memory_space=pl.ANY)] * len(after)
    moved = sum(x.size * x.dtype.itemsize for x in inputs) + sum(
        x.size * x.dtype.itemsize for x in jax.tree.leaves(outs)
    )
    return pl.pallas_call(
        body,
        out_shape=outs,
        in_specs=specs,
        out_specs=jax.tree.map(lambda _: pl.BlockSpec(memory_space=pltpu.VMEM), outs),
        scratch_shapes=list(scratch),
        compiler_params=pltpu.CompilerParams(vmem_limit_bytes=vmem * 2**20),
        cost_estimate=pl.CostEstimate(flops=flops, bytes_accessed=moved, transcendentals=0),
        name=name,
    )(*inputs, *after)


def exchange(parts, sizes):
    out = []
    for ahead, part in zip(steps_of(sizes), parts):
        moves = [
            (
                seq * sizes[1] + sub,
                (seq + ahead[0]) % sizes[0] * sizes[1] + (sub + ahead[1]) % sizes[1],
            )
            for seq, sub in steps_of(sizes)
        ]
        out.append(part if ahead == (0, 0) else lax.ppermute(part, OWNERS, moves))
    return out


def shift(part, axis, ahead):
    size = lax.axis_size(axis)
    return lax.ppermute(part, axis, [(i, (i + ahead) % size) for i in range(size)])


def pass_round(parts, axis):
    return [parts[0]] + [shift(parts[ahead], axis, ahead) for ahead in range(1, len(parts))]


def exchange_by_chip(me, parts, sizes, name, after=()):
    came = pass_round(parts, "seq")
    swapped = call(
        functools.partial(swap_kernel, sizes),
        (jax.ShapeDtypeStruct((sizes[0], *parts[0].shape[1:]), BF16),) * (sizes[1] - 1),
        (me, *came),
        after=after,
        name=name,
    )
    return came + [shift(part, "sub", k + 1) for k, part in enumerate(swapped)]


def fold_subs(me, by_sub, name):
    seqs, piece, columns = by_sub[0].shape
    return call(
        fold_subs_kernel,
        (jax.ShapeDtypeStruct((piece, columns), BF16),) * seqs,
        (me, *pass_round(by_sub, "sub")),
        name=name,
    )


def add_up(terms, dtype, name, after=()):
    out = jax.ShapeDtypeStruct(terms[0].shape, dtype)
    return call(sum_kernel, out, tuple(terms), smem=(), after=after, name=name)


def on_device(tokens_in, w_query, w_value, cotangent, assignment):
    sizes = (lax.axis_size("seq"), lax.axis_size("sub"))
    owners = sizes[0] * sizes[1]
    parts = lax.axis_size("head")
    toks, width = tokens_in.shape
    width_dev = cotangent.shape[1]
    heads = width_dev // HD
    slot_rows = 2 * toks // CLUSTERS
    assert owners % heads == 0 and heads % 2 == 0
    groups = owners // heads
    per_group = CLUSTERS // groups
    rows = toks if groups == 1 else per_group * slot_rows
    half = rows // 2
    slots = groups * rows
    columns = width // parts
    capacity = (slot_rows * owners + BLOCK_ROWS - 1) // BLOCK_ROWS * BLOCK_ROWS
    extra = max(per_group // 2, 16)
    shape = jax.ShapeDtypeStruct
    seq, sub = lax.axis_index("seq"), lax.axis_index("sub")
    first = lax.div(seq * sizes[1] + sub, jnp.int32(heads)) * per_group
    me = jnp.stack([seq, sub, lax.axis_index("head"), first]).astype(jnp.int32)

    def several(count, *dims):
        return (shape(dims, BF16),) * count

    assign_row = assignment.reshape(1, toks)
    *far_mixed, slot_row = call(
        functools.partial(project_far_kernel, sizes, groups, rows, heads),
        several(sizes[1], rows + COUNT_ROWS, LANES) + (shape((1, toks), jnp.int32),),
        (assign_row, tokens_in, w_query, cotangent),
        smem=(),
        in_place=(1, 2, 3),
        scratch=[
            pltpu.VMEM((toks, width), BF16),
            pltpu.VMEM((width, sizes[1] * HD), BF16),
            pltpu.VMEM((toks, sizes[1] * HD), BF16),
            pltpu.VMEM((toks, sizes[1] * LANES), BF16),
            pltpu.SemaphoreType.DMA((3, max(toks, width) // min(256, toks))),
        ],
        flops=2 * toks * width * sizes[1] * HD + 2 * rows * toks * sizes[1] * LANES,
        vmem=60,
        name="project_far",
    )
    own_mixed, *near_mixed = call(
        functools.partial(project_query_kernel, sizes, groups, rows),
        several(owners - sizes[1], rows + COUNT_ROWS, LANES),
        (me, slot_row, assign_row, tokens_in, w_query, cotangent),
        scratch=[pltpu.VMEM((toks, 2 * width_dev), BF16), pltpu.VMEM((owners, rows + COUNT_ROWS, LANES), BF16)],
        flops=2 * toks * width * width_dev + 4 * slots * toks * width_dev,
        name="project_query",
    )
    send_mixed = [own_mixed, *far_mixed, *near_mixed]
    got_mixed = exchange(send_mixed, sizes)
    *send_value, turned, unsort = call(
        functools.partial(project_value_kernel, sizes, groups, rows),
        several(owners, half, LANES) + several(1, width, slots) + several(1, toks, slots),
        (me, slot_row, tokens_in, w_value),
        after=near_mixed[:1],
        scratch=[pltpu.VMEM((toks, width_dev), BF16), pltpu.VMEM((owners, half, LANES), BF16)],
        flops=2 * toks * width * width_dev + 2 * slots * toks * width_dev,
        name="project_value",
    )
    behind = [0, *range(3, owners), 2, 1][:owners]
    send_value = [lax.optimization_barrier((part, got_mixed[k]))[0] for part, k in zip(send_value, behind)]
    got_value = exchange(send_value, sizes)
    blocks = per_group * capacity // BLOCK_ROWS
    held = blocks + (LEAD + 4) * UNROLL
    block_flops = 2 * BLOCK_ROWS * BLOCK_ROWS * LANES
    tall = pltpu.VMEM((owners, rows + slot_rows, LANES), F32)
    dense_rows = pltpu.VMEM((held * BLOCK_ROWS, LANES), F32)
    group_f32 = pltpu.VMEM((GROUP_ROWS, BLOCK_ROWS), F32)
    group_b16 = pltpu.VMEM((GROUP_ROWS, BLOCK_ROWS), BF16)
    place = pltpu.SMEM((owners,), jnp.int32)
    *back_value, dense, counts = call(
        functools.partial(value_grad_kernel, sizes, per_group, slot_rows),
        several(sizes[0], sizes[1], half, LANES)
        + several(1, held * BLOCK_ROWS, LANES)
        + (shape((owners, LANES), jnp.int32),),
        (me, *got_mixed),
        after=[unsort],
        scratch=[pltpu.SMEM((owners, LANES), jnp.int32), place, tall, dense_rows, tall]
        + [group_f32] * 2
        + [group_b16] * 2,
        flops=4 * blocks * block_flops,
        vmem=48,
        name="value_grad",
    )
    back_value, _ = lax.optimization_barrier((back_value, got_value[1:]))
    back_query = call(
        functools.partial(query_grad_kernel, sizes, per_group, slot_rows),
        several(sizes[0], sizes[1], half + extra, LANES),
        (me, counts, dense, *got_value),
        smem=(0, 1),
        scratch=[place, tall, dense_rows, pltpu.VMEM((held, LANES), F32), pltpu.VMEM((2 * extra, LANES), F32)]
        + [group_f32] * 4
        + [group_b16] * 2,
        flops=6 * blocks * block_flops,
        vmem=48,
        name="query_grad",
    )
    home_query = exchange_by_chip(me, back_query, sizes, "swap_query")
    home_value = exchange_by_chip(me, back_value, sizes, "swap_value", back_query[:1])
    weight_flops = 2 * slots * width * width_dev
    home_flops = weight_flops // parts * (parts - 1)
    piece = width // owners
    sub_shapes = several(sizes[1], sizes[0], piece, width_dev)
    value_rows, *refs = call(
        functools.partial(value_home_kernel, sizes, heads, parts),
        several(1, slots, width_dev) + (shape((slots, columns), F32),) * (parts - 1) + sub_shapes,
        (me, turned, w_value, *home_value),
        scratch=[pltpu.VMEM((owners, half, LANES), BF16)],
        flops=weight_flops + home_flops,
        name="value_home",
    )
    value_terms, value_weight = refs[: parts - 1], refs[parts - 1 :]
    value_weight = pass_round(value_weight, "sub")
    *partials, query_rows, centroid_grad = call(
        functools.partial(query_home_kernel, sizes, heads, (CLUSTERS / (toks * owners)) ** 0.5, parts),
        several(parts - 1, slots, columns)
        + several(1, slots, width_dev)
        + (shape((groups * 2 * extra, width_dev), F32),),
        (me, w_query, *value_terms, *home_query),
        scratch=[pltpu.VMEM((owners, half + extra, LANES), BF16)],
        flops=home_flops,
        name="query_home",
    )
    arrived = [shift(partial, "head", k + 1) for k, partial in enumerate(partials)]
    refs = call(
        functools.partial(query_weight_kernel, sizes),
        sub_shapes + several(sizes[0], piece, width_dev),
        (me, turned, query_rows, *value_weight),
        flops=weight_flops,
        name="query_weight",
    )
    query_weight, value_weight = refs[: sizes[1]], pass_round(refs[sizes[1] :], "seq")
    query_weight = fold_subs(me, query_weight, "query_subs")
    own = call(
        functools.partial(input_own_kernel, parts),
        shape((slots, columns), BF16),
        (me, query_rows, value_rows, w_query, w_value),
        after=query_weight[:1],
        flops=weight_flops * 2 // parts,
        name="input_own",
    )
    query_weight = pass_round(query_weight, "seq")
    grad_wv = add_up(value_weight, F32, "value_sum", [own])
    grad_input, own_weight = call(
        input_sum_kernel,
        several(1, toks, columns) + several(1, piece, width_dev),
        (unsort, query_weight[0], own, *arrived),
        smem=(),
        scratch=[pltpu.VMEM((slots, columns), BF16)],
        flops=2 * toks * slots * columns,
        name="input_sum",
    )
    grad_wq = add_up([own_weight, *query_weight[1:]], F32, "query_sum")
    if groups > 1:
        centroid_grad = centroid_grad.reshape(groups, 2 * extra, width_dev)[:, :per_group]
        centroid_grad = centroid_grad.reshape(CLUSTERS, width_dev)
    return (grad_input, grad_wq, grad_wv, centroid_grad)


def solution(mesh):
    return jax.shard_map(
        on_device,
        mesh=mesh,
        in_specs=(
            P(("grp", "seq", "sub"), None),
            P(None, "head"),
            P(None, "head"),
            P(("grp", "seq", "sub"), "head"),
            P(("grp", "seq", "sub"), None),
        ),
        out_specs=(
            P(("grp", "seq", "sub"), "head"),
            P(("grp", "seq", "sub"), "head"),
            P(("grp", "seq", "sub"), "head"),
            P("grp", "head"),
        ),
        check_vma=False,
    )
```

```python
import functools

import jax
import jax.numpy as jnp
from jax import lax
from jax.experimental import pallas as pl
from jax.experimental.pallas import tpu as pltpu
from jax.sharding import PartitionSpec as P

HD = 64
CLUSTERS = 64
BLOCK_ROWS = 128
LANES = 128
UNROLL = 4
COUNT_ROWS = 16
SCALE = 0.5 * HD ** (-0.5)
F32 = jnp.float32
BF16 = jnp.bfloat16
OWNERS = ("seq", "sub")
GROUP_ROWS = UNROLL * BLOCK_ROWS
LEAD = 2


def iota(shape, dim):
    return lax.broadcasted_iota(jnp.int32, shape, dim)


def low_half(shape):
    return iota(shape, 1) < HD


def swap_halves(tile):
    return pltpu.roll(tile, HD, 1)


def dot(a, b):
    return jnp.dot(a, b, preferred_element_type=F32)


def dot_nt(a, b):
    return lax.dot_general(a, b, (((1,), (1,)), ((), ())), preferred_element_type=F32)


def ones_where(condition):
    return jnp.where(condition, 1.0, 0.0).astype(BF16)


def owner_of(me_ref, ahead, sizes):
    seq = lax.rem(me_ref[0] + ahead[0], jnp.int32(sizes[0]))
    sub = lax.rem(me_ref[1] + ahead[1], jnp.int32(sizes[1]))
    return seq * sizes[1] + sub


def source_of(me_ref, ahead, sizes):
    return owner_of(me_ref, ((sizes[0] - ahead[0]) % sizes[0], (sizes[1] - ahead[1]) % sizes[1]), sizes)


def steps_of(sizes):
    far = sorted(range(1, sizes[0]), key=lambda seq: -min(seq, sizes[0] - seq))
    subs = range(sizes[1])
    return [(0, 0)] + [(seq, sub) for seq in far for sub in subs] + [(0, sub) for sub in subs if sub]


def hand_out(by_owner_ref, out_refs, me_ref, sizes):
    for ahead, out_ref in zip(steps_of(sizes), out_refs):
        out_ref[...] = by_owner_ref[owner_of(me_ref, ahead, sizes)]


def slots_of(assign, groups, rows):
    toks = assign.shape[1]
    per_group = CLUSTERS // groups
    member = jnp.where(iota((CLUSTERS, toks), 0) == assign, 1.0, 0.0)
    member_b = member.astype(BF16)
    upto = ones_where(iota((LANES, LANES), 0) <= iota((LANES, LANES), 1))
    counts = jnp.zeros((CLUSTERS, 1), F32)
    running = []
    for first in range(0, toks, LANES):
        within = dot(member_b[:, first : first + LANES], upto)
        running.append(within + counts)
        counts = counts + within[:, LANES - 1 :]
    running = jnp.concatenate(running, axis=1)
    here, other = iota((CLUSTERS, CLUSTERS), 0), iota((CLUSTERS, CLUSTERS), 1)
    group_of = lambda index: lax.div(index, jnp.int32(per_group))
    earlier = ones_where((other < here) & (group_of(other) == group_of(here)))
    base = dot(earlier, jnp.broadcast_to(counts, (CLUSTERS, LANES)).astype(BF16))[:, :1]
    base = base + (group_of(iota((CLUSTERS, 1), 0)) * rows).astype(F32)
    slot = jnp.sum(member * (running - 1.0 + base), axis=0, keepdims=True).astype(jnp.int32)
    spread = jnp.concatenate([member_b, jnp.zeros((LANES - CLUSTERS, toks), BF16)], axis=0)
    return slot, dot_nt(jnp.ones((COUNT_ROWS, toks), BF16), spread).astype(BF16)


def arrivals(sizes, me_ref, refs):
    seqs, subs = sizes
    for ahead in steps_of(sizes):
        if ahead[1] == 0:
            piece = refs[ahead[0]][me_ref[1]]
        else:
            piece = refs[seqs + ahead[1] - 1][ahead[0]]
        yield source_of(me_ref, ahead, sizes), piece


def swap_kernel(sizes, me_ref, *refs):
    for k, out_ref in enumerate(refs[sizes[0] :]):
        sub = lax.rem(me_ref[1] + (k + 1), jnp.int32(sizes[1]))
        for seq in range(sizes[0]):
            out_ref[seq] = refs[seq][sub]


def beside(query, cotan):
    low = low_half(query.shape)
    even = jnp.where(low, query, swap_halves(cotan)).astype(BF16)
    return even, jnp.where(low, swap_halves(query), cotan).astype(BF16)


def load_rows(source, target, sems, fine):
    return [
        pltpu.make_async_copy(source.at[pl.ds(row, fine), :], target.at[pl.ds(row, fine), :], sems.at[row // fine])
        for row in range(0, target.shape[0], fine)
    ]


def project_far_kernel(sizes, groups, rows, heads, assign_ref, tokens_hbm, weight_hbm, cotan_hbm, *refs):
    out_refs, refs = refs[: sizes[1]], refs[sizes[1] :]
    slot_ref, tokens_ref, weight_ref, cotan_ref, mixed_ref, sems = refs
    toks = tokens_ref.shape[0]
    fine = min(256, toks)
    me = (lax.axis_index("seq"), lax.axis_index("sub"))
    owner = owner_of(me, steps_of(sizes)[1], sizes) - me[1]
    group, head = lax.div(owner, jnp.int32(heads)), lax.rem(owner, jnp.int32(heads))
    columns = pl.ds(pl.multiple_of(head * HD, LANES), sizes[1] * HD)
    loads = [
        load_rows(source, target, sems.at[kind], fine)
        for kind, (source, target) in enumerate(
            ((weight_hbm.at[:, columns], weight_ref), (tokens_hbm, tokens_ref), (cotan_hbm.at[:, columns], cotan_ref))
        )
    ]
    for load in loads:
        for copy in load:
            copy.start()
    slot, tallies = slots_of(assign_ref[...], groups, rows)
    slot_ref[...] = slot
    pick = ones_where(iota((rows, toks), 0) + group * rows == slot)
    for copy in loads[0] + loads[2]:
        copy.wait()
    step = fine
    for first in range(0, toks, step):
        for copy in loads[1][first // fine : (first + step) // fine]:
            copy.wait()
        where = slice(first, first + step)
        query, cotan = dot(tokens_ref[where, :], weight_ref[...]), cotan_ref[where, :].astype(F32)
        for pair in range(sizes[1] // 2):
            pair_columns = slice(pair * LANES, (pair + 1) * LANES)
            even, odd = beside(query[:, pair_columns], cotan[:, pair_columns])
            mixed_ref[where, 2 * pair * LANES : (2 * pair + 1) * LANES] = even
            mixed_ref[where, (2 * pair + 1) * LANES : (2 * pair + 2) * LANES] = odd
    part = min(256, rows)
    for first in range(0, rows, part):
        where = slice(first, first + part)
        in_order = dot(pick[where, :], mixed_ref[...]).astype(BF16)
        for ahead, out_ref in enumerate(out_refs):
            sub = lax.rem(me[1] + ahead, jnp.int32(sizes[1]))
            piece = in_order[:, :LANES]
            for other in range(1, sizes[1]):
                piece = jnp.where(sub == other, in_order[:, other * LANES : (other + 1) * LANES], piece)
            out_ref[where, :] = piece
    for out_ref in out_refs:
        out_ref[rows:, :] = tallies


def project_query_kernel(sizes, groups, rows, me_ref, slot_ref, assign_ref, tokens_ref, weight_ref, cotan_ref, *rest):
    out_refs, (mixed_ref, sorted_ref) = rest[:-2], rest[-2:]
    toks = tokens_ref.shape[0]
    heads = weight_ref.shape[1] // HD
    step = min(512, toks)
    for first in range(0, toks, step):
        where = slice(first, first + step)
        query, cotan = dot(tokens_ref[where, :], weight_ref[...]), cotan_ref[where, :].astype(F32)
        for pair in range(heads // 2):
            columns = slice(pair * LANES, (pair + 1) * LANES)
            even, odd = beside(query[:, columns], cotan[:, columns])
            mixed_ref[where, 2 * pair * LANES : (2 * pair + 1) * LANES] = even
            mixed_ref[where, (2 * pair + 1) * LANES : (2 * pair + 2) * LANES] = odd
    part = min(512, rows)
    pieces = rows // part

    @pl.loop(0, groups * pieces)
    def _(i):
        group, piece = lax.div(i, jnp.int32(pieces)), lax.rem(i, jnp.int32(pieces))
        first = pl.multiple_of(piece * part, part)
        pick = ones_where(iota((part, toks), 0) + i * part == slot_ref[...])
        sorted_rows = dot(pick, mixed_ref[...]).astype(BF16)
        for head in range(heads):
            sorted_ref[group * heads + head, pl.ds(first, part), :] = sorted_rows[
                :, head * LANES : (head + 1) * LANES
            ]

    member = jnp.where(iota((LANES, toks), 0) == assign_ref[...], 1.0, 0.0).astype(BF16)
    tallies = dot_nt(jnp.ones((COUNT_ROWS, toks), BF16), member).astype(BF16)
    for owner in range(sorted_ref.shape[0]):
        sorted_ref[owner, rows:, :] = tallies
    steps = steps_of(sizes)
    for ahead, out_ref in zip(steps[:1] + steps[1 + sizes[1] :], out_refs):
        out_ref[...] = sorted_ref[owner_of(me_ref, ahead, sizes)]


def project_value_kernel(sizes, groups, rows, me_ref, slot_ref, tokens_ref, weight_ref, *rest):
    out_refs, (turned_ref, unsort_ref, value_ref, sorted_ref) = rest[:-4], rest[-4:]
    toks = tokens_ref.shape[0]
    heads = weight_ref.shape[1] // HD
    step = min(512, toks)

    @pl.loop(0, toks // step)
    def _(i):
        where = pl.ds(pl.multiple_of(i * step, step), step)
        value_ref[where, :] = dot(tokens_ref[where, :], weight_ref[...]).astype(BF16)

    half = rows // 2
    part = min(256, half)
    pieces = half // part

    @pl.loop(0, groups * pieces)
    def _(i):
        group, piece = lax.div(i, jnp.int32(pieces)), lax.rem(i, jnp.int32(pieces))
        first = pl.multiple_of(piece * part, part)
        index = iota((part, toks), 0) + group * rows + first
        upper = dot(ones_where(index == slot_ref[...]), value_ref[...])
        lower = dot(ones_where(index + half == slot_ref[...]), value_ref[...])
        low = low_half((part, LANES))
        for pair in range(heads // 2):
            up = upper[:, pair * LANES : (pair + 1) * LANES]
            down = lower[:, pair * LANES : (pair + 1) * LANES]
            even = jnp.where(low, up, swap_halves(down)).astype(BF16)
            odd = jnp.where(low, swap_halves(up), down).astype(BF16)
            sorted_ref[group * heads + 2 * pair, pl.ds(first, part), :] = even
            sorted_ref[group * heads + 2 * pair + 1, pl.ds(first, part), :] = odd

    hand_out(sorted_ref, out_refs, me_ref, sizes)
    turned = tokens_ref[...].T
    slots = unsort_ref.shape[1]
    part = min(256, slots)
    for i in range(slots // part):
        pick = ones_where(iota((part, toks), 0) + i * part == slot_ref[...])
        unsort_ref[:, i * part : (i + 1) * part] = pick.T
        turned_ref[:, i * part : (i + 1) * part] = dot_nt(turned, pick).astype(BF16)


def score(mixed):
    query = jnp.where(low_half(mixed.shape), mixed.astype(F32) * SCALE, 0.0).astype(BF16)
    return dot_nt(query, mixed)


def softmax_turned(scores):
    shape = scores.shape
    seen = iota(shape, 0) <= iota(shape, 1)
    scores = jnp.where(seen, scores, -jnp.inf)
    raised = jnp.exp(scores - jnp.max(scores, axis=0, keepdims=True))
    return raised * (1.0 / jnp.sum(raised, axis=0, keepdims=True))


def for_each_cluster(counts_ref, me_ref, place_ref, owners, per_group, body):
    for source in range(owners):
        place_ref[source] = 0

    def step(cluster, block):
        runs = []
        total = 0
        base = block * BLOCK_ROWS
        for source in range(owners):
            count = counts_ref[source, me_ref[3] + cluster]
            start = place_ref[source]
            runs.append((source, start, base + total))
            place_ref[source] = start + count
            total = total + count
        body(cluster, block, runs, base + total)
        return block + lax.shift_right_logical(total + (BLOCK_ROWS - 1), jnp.int32(7))

    return lax.fori_loop(0, per_group, step, jnp.int32(LEAD * UNROLL))


def gather_blocks(counts_ref, me_ref, place_ref, owners, per_group, slot_rows, wide_ref, block_ref):
    def body(cluster, block, runs, end):
        for source, start, row in runs:
            block_ref[pl.ds(row, slot_rows), :] = wide_ref[source, pl.ds(start, slot_rows), :]
        block_ref[pl.ds(end, BLOCK_ROWS), :] = jnp.zeros((BLOCK_ROWS, LANES), F32)

    blocks = for_each_cluster(counts_ref, me_ref, place_ref, owners, per_group, body)
    spare = pl.ds(pl.multiple_of(blocks * BLOCK_ROWS, BLOCK_ROWS), GROUP_ROWS)
    block_ref[spare, :] = jnp.zeros((GROUP_ROWS, LANES), F32)
    return blocks


def for_each_group(blocks, stages):
    first, second, third = stages
    groups = lax.div(blocks + (UNROLL - 1), jnp.int32(UNROLL))

    def step(i, carry):
        for slot in range(2):
            group = LEAD + 2 * i + slot
            third(group - 2, slot)
            second(group - 1, 1 - slot)
            first(group, slot)
        return carry

    lax.fori_loop(0, lax.shift_right_logical(groups + 1, jnp.int32(1)), step, 0)


def block_rows(group, ahead):
    return pl.ds(pl.multiple_of((group * UNROLL + ahead) * BLOCK_ROWS, BLOCK_ROWS), BLOCK_ROWS)


def tile_rows(ahead):
    return slice(ahead * BLOCK_ROWS, (ahead + 1) * BLOCK_ROWS)


def value_grad_kernel(sizes, per_group, slot_rows, me_ref, *refs):
    owners = sizes[0] * sizes[1]
    mixed_refs, out_refs, rest = refs[:owners], refs[owners : owners + sizes[0]], refs[owners + sizes[0] :]
    dense_ref, counts_out_ref, counts_ref, place_ref, wide_ref, block_ref, home_ref = rest[:7]
    score_refs, probs_refs = rest[7:9], rest[9:11]
    half = out_refs[0].shape[1]
    rows = 2 * half
    for ahead, mixed_ref in zip(steps_of(sizes), mixed_refs):
        source = source_of(me_ref, ahead, sizes)
        tail = mixed_ref[rows:, :].astype(F32).astype(jnp.int32)
        counts_out_ref[pl.ds(source, 1), :] = tail[:1, :]
        wide_ref[source, :rows, :] = mixed_ref[:rows, :].astype(F32)
        wide_ref[source, rows:, :] = jnp.zeros((slot_rows, LANES), F32)
    pltpu.sync_copy(counts_out_ref, counts_ref)
    blocks = gather_blocks(counts_ref, me_ref, place_ref, owners, per_group, slot_rows, wide_ref, block_ref)

    def first(group, slot):
        for ahead in range(UNROLL):
            where = block_rows(group, ahead)
            mixed = block_ref[where, :].astype(BF16)
            dense_ref[where, :] = mixed
            score_refs[slot][tile_rows(ahead), :] = score(mixed)

    def second(group, slot):
        for ahead in range(UNROLL):
            tile = tile_rows(ahead)
            probs_refs[slot][tile, :] = softmax_turned(score_refs[slot][tile, :]).astype(BF16)

    def third(group, slot):
        for ahead in range(UNROLL):
            where = block_rows(group, ahead)
            block_ref[where, :] = dot(probs_refs[slot][tile_rows(ahead), :], dense_ref[where, :])

    for_each_group(blocks, (first, second, third))

    def scatter(cluster, block, runs, end):
        for source, start, row in runs:
            wide_ref[source, pl.ds(start, slot_rows), :] = block_ref[pl.ds(row, slot_rows), :]

    for_each_cluster(counts_ref, me_ref, place_ref, owners, per_group, scatter)
    for ahead, out_ref in enumerate(out_refs):
        for sub in range(sizes[1]):
            source = owner_of(me_ref, (ahead, 0), sizes) - me_ref[1] + sub
            up, down = wide_ref[source, :half, :], wide_ref[source, half:rows, :]
            out_ref[sub] = jnp.where(low_half((half, LANES)), swap_halves(up), down).astype(BF16)


def query_grad_kernel(sizes, per_group, slot_rows, me_ref, counts_ref, dense_ref, *refs):
    owners = sizes[0] * sizes[1]
    mid = owners + sizes[0]
    value_refs, out_refs, rest = refs[:owners], refs[owners:mid], refs[mid:]
    place_ref, wide_ref, block_ref, sums_ref, centroid_ref = rest[:5]
    score_refs, grad_probs_refs, both_refs = rest[5:7], rest[7:9], rest[9:11]
    half = value_refs[0].shape[0]
    rows = 2 * half
    for ahead, value_ref in zip(steps_of(sizes), value_refs):
        source = source_of(me_ref, ahead, sizes)
        value = value_ref[...].astype(F32)
        wide_ref[source, :half, :] = swap_halves(value)
        wide_ref[source, half:rows, :] = value
        wide_ref[source, rows:, :] = jnp.zeros((slot_rows, LANES), F32)
    blocks = gather_blocks(counts_ref, me_ref, place_ref, owners, per_group, slot_rows, wide_ref, block_ref)

    def first(group, slot):
        for ahead in range(UNROLL):
            where, tile = block_rows(group, ahead), tile_rows(ahead)
            mixed = dense_ref[where, :]
            value = block_ref[where, :].astype(BF16)
            cotan = jnp.where(low_half(mixed.shape), jnp.zeros_like(mixed), mixed)
            score_refs[slot][tile, :] = score(mixed)
            grad_probs_refs[slot][tile, :] = dot_nt(value, cotan)

    def second(group, slot):
        for ahead in range(UNROLL):
            tile = tile_rows(ahead)
            probs = softmax_turned(score_refs[slot][tile, :])
            grad_probs = grad_probs_refs[slot][tile, :]
            probs_half = probs.astype(BF16).astype(F32)
            row_dot = jnp.sum(probs_half * grad_probs, axis=0, keepdims=True)
            grad_scores = (probs * (grad_probs - row_dot)).astype(BF16).astype(F32)
            both_refs[slot][tile, :] = (grad_scores + grad_scores.T).astype(BF16)

    def third(group, slot):
        for ahead in range(UNROLL):
            where = block_rows(group, ahead)
            grad = dot(both_refs[slot][tile_rows(ahead), :], dense_ref[where, :]) * SCALE
            grad = grad.astype(BF16).astype(F32)
            block_ref[where, :] = grad
            sums_ref[pl.ds(group * UNROLL + ahead, 1), :] = jnp.sum(grad, axis=0, keepdims=True)

    for_each_group(blocks, (first, second, third))
    most = (owners * slot_rows + BLOCK_ROWS - 1) // BLOCK_ROWS

    def scatter(cluster, block, runs, end):
        total = jnp.zeros((1, LANES), F32)
        for ahead in range(most):
            here = block + ahead
            total = total + jnp.where(here * BLOCK_ROWS < end, sums_ref[pl.ds(here, 1), :], 0.0)
        centroid_ref[pl.ds(cluster, 1), :] = total
        for source, start, row in runs:
            wide_ref[source, pl.ds(start, slot_rows), :] = block_ref[pl.ds(row, slot_rows), :]

    for_each_cluster(counts_ref, me_ref, place_ref, owners, per_group, scatter)
    extra = out_refs[0].shape[1] - half
    centroid = jnp.where(
        low_half((extra, LANES)), centroid_ref[:extra, :], swap_halves(centroid_ref[extra:, :])
    ).astype(BF16)
    for ahead, out_ref in enumerate(out_refs):
        for sub in range(sizes[1]):
            source = owner_of(me_ref, (ahead, 0), sizes) - me_ref[1] + sub
            up, down = wide_ref[source, :half, :], wide_ref[source, half:rows, :]
            out_ref[sub, :half, :] = jnp.where(low_half((half, LANES)), up, swap_halves(down)).astype(BF16)
            out_ref[sub, half:, :] = centroid


def unfold(home_ref, out_ref, heads, start, half, finish):
    low = low_half((half, LANES))
    for group in range(home_ref.shape[0] // heads):
        first = group * 2 * half
        for pair in range(heads // 2):
            even = home_ref[group * heads + 2 * pair, start : start + half, :].astype(F32)
            odd = home_ref[group * heads + 2 * pair + 1, start : start + half, :].astype(F32)
            columns = slice(pair * LANES, (pair + 1) * LANES)
            out_ref[first : first + half, columns] = finish(jnp.where(low, even, swap_halves(odd)))
            out_ref[first + half : first + 2 * half, columns] = finish(
                jnp.where(low, swap_halves(even), odd)
            )


def to_half(x):
    return x.astype(BF16)


def bring_home(sizes, heads, pieces, home_ref, rows_ref):
    for source, piece in pieces:
        home_ref[source] = piece
    unfold(home_ref, rows_ref, heads, 0, rows_ref.shape[0] * heads // home_ref.shape[0] // 2, to_half)


def weight_partial(sizes, me_ref, turned_ref, rows_ref, sub_refs):
    piece = turned_ref.shape[0] // (sizes[0] * sizes[1])
    for ahead, sub_ref in enumerate(sub_refs):
        sub = lax.rem(me_ref[1] + ahead, jnp.int32(sizes[1]))
        first = [pl.multiple_of((seq * sizes[1] + sub) * piece, piece) for seq in range(sizes[0])]
        turned = jnp.concatenate([turned_ref[pl.ds(row, piece), :] for row in first], axis=0)
        partial = dot(turned, rows_ref[...]).astype(BF16)
        for seq in range(sizes[0]):
            sub_ref[seq] = partial[seq * piece : (seq + 1) * piece, :]


def input_columns(me_ref, ahead, parts, width):
    columns = width // parts
    dest = lax.rem(me_ref[2] + ahead, jnp.int32(parts))
    return pl.ds(pl.multiple_of(dest * columns, columns), columns)


def value_home_kernel(sizes, heads, parts, me_ref, turned_ref, weight_ref, *refs):
    came = sizes[0] + sizes[1] - 1
    part_refs, refs = refs[:came], refs[came:]
    rows_ref, term_refs, refs = refs[0], refs[1:parts], refs[parts:]
    sub_refs, home_ref = refs[: sizes[1]], refs[sizes[1]]
    bring_home(sizes, heads, arrivals(sizes, me_ref, part_refs), home_ref, rows_ref)
    for k, term_ref in enumerate(term_refs):
        mine = input_columns(me_ref, k + 1, parts, weight_ref.shape[0])
        term_ref[...] = dot_nt(rows_ref[...], weight_ref[mine, :])
    weight_partial(sizes, me_ref, turned_ref, rows_ref, sub_refs)


def query_home_kernel(sizes, heads, factor, parts, me_ref, weight_ref, *refs):
    term_refs, refs = refs[: parts - 1], refs[parts - 1 :]
    came = sizes[0] + sizes[1] - 1
    part_refs, refs = refs[:came], refs[came:]
    out_refs, (rows_ref, centroid_ref, home_ref) = refs[: parts - 1], refs[parts - 1 :]
    bring_home(sizes, heads, arrivals(sizes, me_ref, part_refs), home_ref, rows_ref)
    for k, (term_ref, out_ref) in enumerate(zip(term_refs, out_refs)):
        mine = input_columns(me_ref, k + 1, parts, weight_ref.shape[0])
        step = min(256, rows_ref.shape[0])
        for first in range(0, rows_ref.shape[0], step):
            where = slice(first, first + step)
            out_ref[where, :] = (dot_nt(rows_ref[where, :], weight_ref[mine, :]) + term_ref[where, :]).astype(BF16)
    half = rows_ref.shape[0] * heads // home_ref.shape[0] // 2
    unfold(home_ref, centroid_ref, heads, half, home_ref.shape[1] - half, lambda x: x * factor)


def query_weight_kernel(sizes, me_ref, turned_ref, rows_ref, *refs):
    term_refs, sub_refs, seq_refs = refs[: sizes[1]], refs[sizes[1] : 2 * sizes[1]], refs[2 * sizes[1] :]
    fold_subs_kernel(me_ref, *term_refs, *seq_refs)
    weight_partial(sizes, me_ref, turned_ref, rows_ref, sub_refs)


def input_own_kernel(parts, me_ref, rows_ref, value_rows_ref, w_query_ref, w_value_ref, out_ref):
    mine = input_columns(me_ref, 0, parts, w_query_ref.shape[0])
    total = dot_nt(rows_ref[...], w_query_ref[mine, :]) + dot_nt(value_rows_ref[...], w_value_ref[mine, :])
    out_ref[...] = total.astype(BF16)


def fold_subs_kernel(me_ref, *refs):
    seqs = refs[0].shape[0]
    terms, out_refs = refs[:-seqs], refs[-seqs:]
    for ahead, out_ref in enumerate(out_refs):
        seq = lax.rem(me_ref[0] + ahead, jnp.int32(seqs))
        total = terms[0][seq].astype(F32)
        for term in terms[1:]:
            total = total + term[seq].astype(F32)
        out_ref[...] = total.astype(BF16)


def sum_kernel(*refs):
    total = refs[0][...].astype(F32)
    for ref in refs[1:-1]:
        total = total + ref[...].astype(F32)
    refs[-1][...] = total.astype(refs[-1].dtype)


def input_sum_kernel(unsort_ref, weight_ref, *refs):
    part_refs, out_ref, weight_out_ref, total_ref = refs[:-3], refs[-3], refs[-2], refs[-1]
    total = part_refs[0][...].astype(F32)
    for part_ref in part_refs[1:]:
        total = total + part_ref[...].astype(F32)
    total_ref[...] = total.astype(BF16)
    step = min(256, out_ref.shape[0])
    for first in range(0, out_ref.shape[0], step):
        where = slice(first, first + step)
        out_ref[where, :] = dot(unsort_ref[where, :], total_ref[...]).astype(BF16)
    weight_out_ref[...] = weight_ref[...]


def call(kernel, outs, inputs, smem=(0,), in_place=(), after=(), scratch=(), flops=0, vmem=24, name=None):
    def body(*refs):
        kernel(*refs[: len(inputs)], *refs[len(inputs) + len(after) :])

    def space(i):
        return pltpu.SMEM if i in smem else pl.ANY if i in in_place else pltpu.VMEM

    specs = [pl.BlockSpec(memory_space=space(i)) for i in range(len(inputs))]
    specs += [pl.BlockSpec(memory_space=pl.ANY)] * len(after)
    moved = sum(x.size * x.dtype.itemsize for x in inputs) + sum(
        x.size * x.dtype.itemsize for x in jax.tree.leaves(outs)
    )
    return pl.pallas_call(
        body,
        out_shape=outs,
        in_specs=specs,
        out_specs=jax.tree.map(lambda _: pl.BlockSpec(memory_space=pltpu.VMEM), outs),
        scratch_shapes=list(scratch),
        compiler_params=pltpu.CompilerParams(vmem_limit_bytes=vmem * 2**20),
        cost_estimate=pl.CostEstimate(flops=flops, bytes_accessed=moved, transcendentals=0),
        name=name,
    )(*inputs, *after)


def exchange(parts, sizes):
    out = []
    for ahead, part in zip(steps_of(sizes), parts):
        moves = [
            (
                seq * sizes[1] + sub,
                (seq + ahead[0]) % sizes[0] * sizes[1] + (sub + ahead[1]) % sizes[1],
            )
            for seq, sub in steps_of(sizes)
        ]
        out.append(part if ahead == (0, 0) else lax.ppermute(part, OWNERS, moves))
    return out


def shift(part, axis, ahead):
    size = lax.axis_size(axis)
    return lax.ppermute(part, axis, [(i, (i + ahead) % size) for i in range(size)])


def pass_round(parts, axis):
    return [parts[0]] + [shift(parts[ahead], axis, ahead) for ahead in range(1, len(parts))]


def far_first(terms):
    size = len(terms)
    return [terms[0]] + [terms[k] for k in sorted(range(1, size), key=lambda k: -min(k, size - k))]


def exchange_by_chip(me, parts, sizes, name, after=()):
    came = pass_round(parts, "seq")
    swapped = call(
        functools.partial(swap_kernel, sizes),
        (jax.ShapeDtypeStruct((sizes[0], *parts[0].shape[1:]), BF16),) * (sizes[1] - 1),
        (me, *came),
        after=after,
        name=name,
    )
    return came + [shift(part, "sub", k + 1) for k, part in enumerate(swapped)]


def fold_subs(me, by_sub, name):
    seqs, piece, columns = by_sub[0].shape
    return call(
        fold_subs_kernel,
        (jax.ShapeDtypeStruct((piece, columns), BF16),) * seqs,
        (me, *pass_round(by_sub, "sub")),
        name=name,
    )


def add_up(terms, dtype, name, after=()):
    out = jax.ShapeDtypeStruct(terms[0].shape, dtype)
    return call(sum_kernel, out, tuple(terms), smem=(), after=after, name=name)


def on_device(tokens_in, w_query, w_value, cotangent, assignment):
    sizes = (lax.axis_size("seq"), lax.axis_size("sub"))
    owners = sizes[0] * sizes[1]
    parts = lax.axis_size("head")
    toks, width = tokens_in.shape
    width_dev = cotangent.shape[1]
    heads = width_dev // HD
    slot_rows = 2 * toks // CLUSTERS
    assert owners % heads == 0 and heads % 2 == 0
    groups = owners // heads
    per_group = CLUSTERS // groups
    rows = toks if groups == 1 else per_group * slot_rows
    half = rows // 2
    slots = groups * rows
    columns = width // parts
    capacity = (slot_rows * owners + BLOCK_ROWS - 1) // BLOCK_ROWS * BLOCK_ROWS
    extra = max(per_group // 2, 16)
    shape = jax.ShapeDtypeStruct
    seq, sub = lax.axis_index("seq"), lax.axis_index("sub")
    first = lax.div(seq * sizes[1] + sub, jnp.int32(heads)) * per_group
    me = jnp.stack([seq, sub, lax.axis_index("head"), first]).astype(jnp.int32)

    def several(count, *dims):
        return (shape(dims, BF16),) * count

    assign_row = assignment.reshape(1, toks)
    *far_mixed, slot_row = call(
        functools.partial(project_far_kernel, sizes, groups, rows, heads),
        several(sizes[1], rows + COUNT_ROWS, LANES) + (shape((1, toks), jnp.int32),),
        (assign_row, tokens_in, w_query, cotangent),
        smem=(),
        in_place=(1, 2, 3),
        scratch=[
            pltpu.VMEM((toks, width), BF16),
            pltpu.VMEM((width, sizes[1] * HD), BF16),
            pltpu.VMEM((toks, sizes[1] * HD), BF16),
            pltpu.VMEM((toks, sizes[1] * LANES), BF16),
            pltpu.SemaphoreType.DMA((3, max(toks, width) // min(256, toks))),
        ],
        flops=2 * toks * width * sizes[1] * HD + 2 * rows * toks * sizes[1] * LANES,
        vmem=60,
        name="project_far",
    )
    own_mixed, *near_mixed = call(
        functools.partial(project_query_kernel, sizes, groups, rows),
        several(owners - sizes[1], rows + COUNT_ROWS, LANES),
        (me, slot_row, assign_row, tokens_in, w_query, cotangent),
        scratch=[pltpu.VMEM((toks, 2 * width_dev), BF16), pltpu.VMEM((owners, rows + COUNT_ROWS, LANES), BF16)],
        flops=2 * toks * width * width_dev + 4 * slots * toks * width_dev,
        name="project_query",
    )
    send_mixed = [own_mixed, *far_mixed, *near_mixed]
    got_mixed = exchange(send_mixed, sizes)
    *send_value, turned, unsort = call(
        functools.partial(project_value_kernel, sizes, groups, rows),
        several(owners, half, LANES) + several(1, width, slots) + several(1, toks, slots),
        (me, slot_row, tokens_in, w_value),
        after=near_mixed[:1],
        scratch=[pltpu.VMEM((toks, width_dev), BF16), pltpu.VMEM((owners, half, LANES), BF16)],
        flops=2 * toks * width * width_dev + 2 * slots * toks * width_dev,
        name="project_value",
    )
    behind = [0, *range(3, owners), 2, 1][:owners]
    send_value = [lax.optimization_barrier((part, got_mixed[k]))[0] for part, k in zip(send_value, behind)]
    got_value = exchange(send_value, sizes)
    blocks = per_group * capacity // BLOCK_ROWS
    held = blocks + (LEAD + 4) * UNROLL
    block_flops = 2 * BLOCK_ROWS * BLOCK_ROWS * LANES
    tall = pltpu.VMEM((owners, rows + slot_rows, LANES), F32)
    dense_rows = pltpu.VMEM((held * BLOCK_ROWS, LANES), F32)
    group_f32 = pltpu.VMEM((GROUP_ROWS, BLOCK_ROWS), F32)
    group_b16 = pltpu.VMEM((GROUP_ROWS, BLOCK_ROWS), BF16)
    place = pltpu.SMEM((owners,), jnp.int32)
    *back_value, dense, counts = call(
        functools.partial(value_grad_kernel, sizes, per_group, slot_rows),
        several(sizes[0], sizes[1], half, LANES)
        + several(1, held * BLOCK_ROWS, LANES)
        + (shape((owners, LANES), jnp.int32),),
        (me, *got_mixed),
        after=[unsort],
        scratch=[pltpu.SMEM((owners, LANES), jnp.int32), place, tall, dense_rows, tall]
        + [group_f32] * 2
        + [group_b16] * 2,
        flops=4 * blocks * block_flops,
        vmem=48,
        name="value_grad",
    )
    back_value, _ = lax.optimization_barrier((back_value, got_value[1:]))
    back_query = call(
        functools.partial(query_grad_kernel, sizes, per_group, slot_rows),
        several(sizes[0], sizes[1], half + extra, LANES),
        (me, counts, dense, *got_value),
        smem=(0, 1),
        scratch=[place, tall, dense_rows, pltpu.VMEM((held, LANES), F32), pltpu.VMEM((2 * extra, LANES), F32)]
        + [group_f32] * 4
        + [group_b16] * 2,
        flops=6 * blocks * block_flops,
        vmem=48,
        name="query_grad",
    )
    home_query = exchange_by_chip(me, back_query, sizes, "swap_query")
    home_value = exchange_by_chip(me, back_value, sizes, "swap_value", back_query[:1])
    weight_flops = 2 * slots * width * width_dev
    home_flops = weight_flops // parts * (parts - 1)
    piece = width // owners
    sub_shapes = several(sizes[1], sizes[0], piece, width_dev)
    value_rows, *refs = call(
        functools.partial(value_home_kernel, sizes, heads, parts),
        several(1, slots, width_dev) + (shape((slots, columns), F32),) * (parts - 1) + sub_shapes,
        (me, turned, w_value, *home_value),
        scratch=[pltpu.VMEM((owners, half, LANES), BF16)],
        flops=weight_flops + home_flops,
        name="value_home",
    )
    value_terms, value_weight = refs[: parts - 1], refs[parts - 1 :]
    value_weight = pass_round(value_weight, "sub")
    *partials, query_rows, centroid_grad = call(
        functools.partial(query_home_kernel, sizes, heads, (CLUSTERS / (toks * owners)) ** 0.5, parts),
        several(parts - 1, slots, columns)
        + several(1, slots, width_dev)
        + (shape((groups * 2 * extra, width_dev), F32),),
        (me, w_query, *value_terms, *home_query),
        scratch=[pltpu.VMEM((owners, half + extra, LANES), BF16)],
        flops=home_flops,
        name="query_home",
    )
    arrived = [shift(partial, "head", k + 1) for k, partial in enumerate(partials)]
    refs = call(
        functools.partial(query_weight_kernel, sizes),
        sub_shapes + several(sizes[0], piece, width_dev),
        (me, turned, query_rows, *value_weight),
        flops=weight_flops,
        name="query_weight",
    )
    query_weight, value_weight = refs[: sizes[1]], far_first(pass_round(refs[sizes[1] :], "seq"))
    query_weight = fold_subs(me, query_weight, "query_subs")
    own = call(
        functools.partial(input_own_kernel, parts),
        shape((slots, columns), BF16),
        (me, query_rows, value_rows, w_query, w_value),
        after=query_weight[:1],
        flops=weight_flops * 2 // parts,
        name="input_own",
    )
    query_weight = far_first(pass_round(query_weight, "seq"))
    grad_wv = add_up(value_weight, F32, "value_sum", [own])
    grad_input, own_weight = call(
        input_sum_kernel,
        several(1, toks, columns) + several(1, piece, width_dev),
        (unsort, query_weight[0], own, *arrived),
        smem=(),
        scratch=[pltpu.VMEM((slots, columns), BF16)],
        flops=2 * toks * slots * columns,
        name="input_sum",
    )
    grad_wq = add_up([own_weight, *query_weight[1:]], F32, "query_sum")
    if groups > 1:
        centroid_grad = centroid_grad.reshape(groups, 2 * extra, width_dev)[:, :per_group]
        centroid_grad = centroid_grad.reshape(CLUSTERS, width_dev)
    return (grad_input, grad_wq, grad_wv, centroid_grad)


def solution(mesh):
    return jax.shard_map(
        on_device,
        mesh=mesh,
        in_specs=(
            P(("grp", "seq", "sub"), None),
            P(None, "head"),
            P(None, "head"),
            P(("grp", "seq", "sub"), "head"),
            P(("grp", "seq", "sub"), None),
        ),
        out_specs=(
            P(("grp", "seq", "sub"), "head"),
            P(("grp", "seq", "sub"), "head"),
            P(("grp", "seq", "sub"), "head"),
            P("grp", "head"),
        ),
        check_vma=False,
    )
```
